32 devices in a mesh: dp: 4 (over y, x), fsdp: 8 (over z, core).
Axes of the slice: x: 2, y: 2, z: 4, core: 2. Of those that a mesh axis runs over, the one named last changes fastest.
Arguments:
- tokens: bfloat16 [96, 256, 1152], P(('dp', 'fsdp')), may hold values from -6 to 6
- timesteps: int32 [96], P(('dp', 'fsdp')), may hold values from 0 to 999
- labels: int32 [96], P(('dp', 'fsdp')), may hold values from 0 to 999
- head_mask: int32 [96, 16], P(('dp', 'fsdp')), may hold values 0 or 1
- keep_mask: int32 [96, 256], P(('dp', 'fsdp')), may hold values from 0 to 1, as said below
- cotangent: bfloat16 [96, 256, 1152], P(('dp', 'fsdp')), may hold values from -6 to 6
- time_weight: bfloat16 [256, 1152], P('fsdp'), may hold values from -0.375 to 0.375
- class_table: bfloat16 [1000, 1152], P(None, 'fsdp'), may hold values from -6 to 6
- ada_weight: bfloat16 [1152, 6912], P(None, 'fsdp'), may hold values from -0.1875 to 0.1875
- head_router: bfloat16 [1152, 16], P('fsdp'), may hold values from -0.1875 to 0.1875
- qkv_weight: bfloat16 [1152, 3456], P('fsdp'), may hold values from -0.1875 to 0.1875
- proj_weight: bfloat16 [1152, 1152], P('fsdp'), may hold values from -0.5 to 0.5
- fc1_weight: bfloat16 [1152, 4608], P('fsdp'), may hold values from -0.1875 to 0.1875
- fc2_weight: bfloat16 [4608, 1152], P('fsdp'), may hold values from -0.1875 to 0.1875
- token_router: bfloat16 [1152, 1], P('fsdp'), may hold values from -0.1875 to 0.1875
Outputs:
- output: bfloat16 [96, 256, 1152], P(('dp', 'fsdp'))
- grad_tokens: float32 [96, 256, 1152], P(('dp', 'fsdp'))
- grad_time_weight: float32 [256, 1152], P('fsdp')
- grad_class_table: float32 [1000, 1152], P(None, 'fsdp')
- grad_ada_weight: float32 [1152, 6912], P(None, 'fsdp')
- grad_head_router: float32 [1152, 16], P('fsdp')
- grad_qkv_weight: float32 [1152, 3456], P('fsdp')
- grad_proj_weight: float32 [1152, 1152], P('fsdp')
- grad_fc1_weight: float32 [1152, 4608], P('fsdp')
- grad_fc2_weight: float32 [4608, 1152], P('fsdp')
- grad_token_router: float32 [1152, 1], P('fsdp')
The draws below stay inside these ranges and needn't reach their ends.
Inputs may be any that keep to these rules, and one draw needn't show every extreme that they name: `keep_mask`: each image keeps between one fifth (rounded up) and all of its 256 tokens.
All inputs are finite; a program needn't handle non-finite values. No bound on the sum of `head_mask` on one device may be relied on, other than what follows from the above.
Results may differ from the reference program's by a relative error of at most 0.02.
Values may be sent and summed in bfloat16 or wider, within the bound.
A program may use at most 256 MiB of HBM per device.

```python
import math
import jax
import jax.numpy as jnp
from jax import lax

D = 1152
H = 16
FF = 4608
NCLASS = 1000
FREQ = 256
SEQ = 256
IMG_DEV = 3
IMAGES = 96


def draw_keep_mask(key, part):
    key = jax.random.fold_in(key, 7)
    count_key, order_key = jax.random.split(key)
    least = max(1, (SEQ + 4) // 5)
    counts = jax.random.randint(count_key, (IMAGES, 1), least, SEQ + 1)
    order_keys = jax.random.split(order_key, IMAGES)
    ranks = jax.vmap(lambda single: jax.random.permutation(single, SEQ))(order_keys)
    return (ranks < counts).astype(jnp.int32)


def with_ends(entries, own_key, smallest, high):
    dims = entries.shape
    index_at = [jax.random.randint(jax.random.fold_in(own_key, axis), (), 0, dims[axis]) for axis in range(len(dims))]
    entries = entries.at[tuple(index_at)].set(smallest)
    longest = dims.index(max(dims))
    index_at[longest] = (index_at[longest] + 1) % dims[longest]
    return entries.at[tuple(index_at)].set(high)


def level_of(own_key, extent, cuts, low, top_value):
    def one(dim, blocks):
        heights = jax.random.uniform(jax.random.fold_in(jax.random.fold_in(own_key, 6), dim), (blocks,), jnp.float32, low / len(cuts), top_value / len(cuts))
        return jnp.repeat(jnp.exp(heights), extent[dim] // blocks).reshape((-1,) + (1,) * (len(extent) - dim - 1))

    level = one(*cuts[0])
    for cut in cuts[1:]:
        level = level * one(*cut)
    return level


def bell_draw(key, extent, scale, most, cuts=(), held_as=jnp.bfloat16):
    entries = scale * jax.random.normal(key, extent, jnp.float32)
    if cuts:
        entries = entries * level_of(key, extent, cuts, -0.22, 0.18)
    return jnp.clip(entries, -most, most).astype(held_as)


def setup_inputs(seed: int = 0) -> dict:
    seeds = jax.random.split(jax.random.key(seed), 16)
    tokens = bell_draw(seeds[0], (IMAGES, SEQ, D), 1.0, 6.0, ((0, 32),))
    timesteps = with_ends(jax.random.randint(seeds[1], (IMAGES,), 0, 1000), jax.random.fold_in(seeds[1], 1), 0, 999).astype(jnp.int32)
    labels = with_ends(jax.random.randint(seeds[2], (IMAGES,), 0, NCLASS), jax.random.fold_in(seeds[2], 1), 0, NCLASS - 1).astype(jnp.int32)
    head_mask = with_ends((jax.random.randint(seeds[3], (IMAGES, H), 0, 4) < 3).astype(jnp.int32), jax.random.fold_in(seeds[3], 1), 0, 1)
    keep_mask = draw_keep_mask(jax.random.fold_in(seeds[15], 71), 0)
    cotangent = bell_draw(seeds[5], (IMAGES, SEQ, D), 1.0, 6.0, ((0, 32),))
    time_weight = bell_draw(seeds[6], (FREQ, D), FREQ ** -0.5, 0.375, ((0, 8),))
    class_table = bell_draw(seeds[7], (NCLASS, D), 1.0, 6.0, ((1, 8),))
    ada_weight = bell_draw(seeds[8], (D, 6 * D), D ** -0.5, 0.1875, ((1, 8),))
    head_router = bell_draw(seeds[9], (D, H), D ** -0.5, 0.1875, ((0, 8),))
    qkv_weight = bell_draw(seeds[10], (D, 3 * D), D ** -0.5, 0.1875, ((0, 8),))
    proj_weight = bell_draw(seeds[11], (D, D), (D // 8) ** -0.5, 0.5, ((0, 8),))
    fc1_weight = bell_draw(seeds[12], (D, FF), D ** -0.5, 0.1875, ((0, 8),))
    fc2_weight = bell_draw(seeds[13], (FF, D), (FF // 4) ** -0.5, 0.1875, ((0, 8),))
    token_router = bell_draw(seeds[14], (D, 1), D ** -0.5, 0.1875, ((0, 8),))
    return {"tokens": tokens, "timesteps": timesteps, "labels": labels, "head_mask": head_mask, "keep_mask": keep_mask, "cotangent": cotangent, "time_weight": time_weight, "class_table": class_table, "ada_weight": ada_weight, "head_router": head_router, "qkv_weight": qkv_weight, "proj_weight": proj_weight, "fc1_weight": fc1_weight, "fc2_weight": fc2_weight, "token_router": token_router}


EPSILON = 1e-06

@jax.custom_vjp
def low(v):
    return lax.optimization_barrier(v.astype(jnp.bfloat16)).astype(jnp.float32)

@jax.custom_vjp
def low_back(v):
    return v

def low_keep(v):
    return (low(v), None)

def low_pass(kept, grad):
    return (grad,)

def back_keep(v):
    return (v, None)

def back_low(kept, grad):
    return (low(grad),)
low.defvjp(low_keep, low_pass)
low_back.defvjp(back_keep, back_low)

def product(spec, left, right):
    return jnp.einsum(spec, left, right, precision=lax.Precision.HIGHEST)

def sinusoid(steps):
    half = FREQ // 2
    freqs = jnp.exp(-math.log(10000.0) * jnp.arange(half, dtype=jnp.float32) / half)
    angles = steps.astype(jnp.float32)[:, None] * freqs[None, :]
    return jnp.concatenate([jnp.cos(angles), jnp.sin(angles)], axis=1)

def layer_norm(value):
    centered = value - lax.optimization_barrier(jnp.mean(value, axis=-1, keepdims=True))
    return centered * lax.rsqrt(lax.optimization_barrier(jnp.mean(centered * centered, axis=-1, keepdims=True)) + EPSILON)

def forward(inputs, time_weight, class_table, ada_weight, head_router, qkv_weight, proj_weight, fc1_weight, fc2_weight, token_router, embedded, labels, head_mask, keep_mask):
    images, seq, width = inputs.shape
    heads = head_mask.shape[-1]
    size = width // heads
    pre_cond = low_back(product('if,fd->id', low(embedded), time_weight) + jnp.take(class_table, labels, axis=0))
    cond = low(jax.nn.silu(pre_cond))
    modulation = low_back(product('id,de->ie', cond, ada_weight))
    shift_one, scale_one, gate_one, shift_two, scale_two, gate_two = jnp.split(modulation[:, None, :], 6, axis=2)
    head_gates = head_mask * jax.nn.sigmoid(low_back(product('id,dh->ih', cond, head_router)))
    h_one = low(layer_norm(inputs) * (1.0 + scale_one) + shift_one)
    triple = low(low_back(product('isd,de->ise', h_one, qkv_weight)))
    query = triple[..., :width].reshape(images, seq, heads, size)
    keys = triple[..., width:2 * width].reshape(images, seq, heads, size)
    values = triple[..., 2 * width:].reshape(images, seq, heads, size)
    scores = low_back(product('ishe,ithe->ihst', query, keys)) * size ** (-0.5)
    probs = low(jax.nn.softmax(scores, axis=-1))
    attended = low_back(product('ihst,ithe->ishe', probs, values))
    mixed = low(low_back(attended * head_gates[:, None, :, None])).reshape(images, seq, width)
    attn = low_back(product('isd,de->ise', mixed, proj_weight))
    middle = inputs + gate_one * attn
    h_two = low(layer_norm(middle) * (1.0 + scale_two) + shift_two)
    rate = jax.nn.sigmoid(low_back(product('isd,de->ise', h_two, token_router)))
    upward = low_back(product('isd,de->ise', h_two, fc1_weight))
    active = low(jax.nn.gelu(upward, approximate=True))
    downward = low_back(product('isf,fd->isd', active, fc2_weight))
    return middle + gate_two * (keep_mask[..., None] * rate) * downward

def reference(tokens, timesteps, labels, head_mask, keep_mask, cotangent, time_weight, class_table, ada_weight, head_router, qkv_weight, proj_weight, fc1_weight, fc2_weight, token_router):
    weights = tuple((w.astype(jnp.float32) for w in (time_weight, class_table, ada_weight, head_router, qkv_weight, proj_weight, fc1_weight, fc2_weight, token_router)))
    groups = IMAGES // IMG_DEV

    def regroup(array):
        return array.reshape((groups, IMG_DEV) + array.shape[1:])

    def one_group(totals, pieces):
        inputs, steps, label_group, mask_group, keep_group, grad_group = pieces
        embedded = sinusoid(steps)

        def run(value, *params):
            return forward(value, *params, embedded, label_group, mask_group.astype(jnp.float32), keep_group.astype(jnp.float32))
        result, pull = jax.vjp(run, inputs.astype(jnp.float32), *weights)
        grads = pull(grad_group.astype(jnp.float32))
        totals = tuple((total + grad for total, grad in zip(totals, grads[1:])))
        return (totals, (result.astype(jnp.bfloat16), grads[0]))
    start = tuple((jnp.zeros(w.shape, jnp.float32) for w in weights))
    totals, (results, grad_inputs) = lax.scan(one_group, start, (regroup(tokens), regroup(timesteps), regroup(labels), regroup(head_mask), regroup(keep_mask), regroup(cotangent)))
    return (results.reshape(tokens.shape), grad_inputs.reshape(tokens.shape), totals[0], totals[1], totals[2], totals[3], totals[4], totals[5], totals[6], totals[7], totals[8])
```

```python
from functools import partial
import math

import jax
import jax.numpy as jnp
from jax import lax
from jax.experimental import pallas as pl
from jax.experimental.pallas import tpu as pltpu
from jax.sharding import PartitionSpec as P

EPSILON = 1e-06
MESH = pl.DeviceIdType.MESH
QUARTERS = 4


def sinusoid(steps, entries):
    half = entries // 2
    freqs = jnp.exp(-math.log(10000.0) * jnp.arange(half, dtype=jnp.float32) / half)
    angles = steps.astype(jnp.float32)[:, None] * freqs[None, :]
    return jnp.concatenate([jnp.cos(angles), jnp.sin(angles)], axis=1)


def layer_norm(value):
    centered = value - jnp.mean(value, axis=-1, keepdims=True)
    return centered * lax.rsqrt(jnp.mean(centered * centered, axis=-1, keepdims=True) + EPSILON)


def norm_back(value, grad):
    _, pull = jax.vjp(layer_norm, value)
    return pull(grad)[0]


def matmul(left, right):
    return jnp.dot(left, right, preferred_element_type=jnp.float32)


def times_rows(left, right):
    return lax.dot_general(
        left, right, (((0,), (0,)), ((), ())), preferred_element_type=jnp.float32
    )


def times_back(left, right):
    return lax.dot_general(
        left, right, (((1,), (1,)), ((), ())), preferred_element_type=jnp.float32
    )


class Place:
    def __init__(self, ring):
        self.ring = ring
        d = lax.axis_index("dp")
        f = lax.axis_index("fsdp")
        self.d, self.f = d, f
        self.z = f // 2
        self.c = f % 2
        self.q = d % QUARTERS
        dx = d + 1 - 2 * (d % 2)
        dy = d + 2 - 4 * ((d // 2) % 2)
        self.qx = dx % QUARTERS
        self.qy = dy % QUARTERS
        self.qd = (self.qx + self.qy - self.q + QUARTERS) % QUARTERS
        self.core = (d, f + 1 - 2 * (f % 2))
        self.x = (dx, f)
        self.y = (dy, f)
        self.up = (d, ((self.z + 1) % ring) * 2 + self.c)
        self.down = (d, ((self.z + ring - 1) % ring) * 2 + self.c)

    def shard(self, back):
        return ((self.z + self.ring - back) % self.ring) * 2 + self.c

    def greet(self):
        barrier = pltpu.get_barrier_semaphore()
        near = [self.core, self.x, self.y, self.up, self.down]
        for other in near:
            pl.semaphore_signal(barrier, inc=1, device_id=other, device_id_type=MESH)
        pl.semaphore_wait(barrier, len(near))


def remote(src, dst, send, recv, device):
    return pltpu.make_async_remote_copy(
        src_ref=src, dst_ref=dst, send_sem=send, recv_sem=recv, device_id=device, device_id_type=MESH
    )


def cut(width):
    first = ((width // 128 + 1) // 2) * 128
    return (0, first), (first, width - first)


def view(ref, lead, q, width, part=None):
    start, size = (0, width) if part is None else part
    flat = ref.shape[-1] != width
    if flat:
        column = pl.multiple_of(q * width + start, 128)
        return ref.at[(*lead, slice(None), pl.ds(column, size))]
    return ref.at[(*lead, q, slice(None), pl.ds(start, size))]


def gather_kernel(ring, width, *refs):
    weights = 3
    shards, fulls = refs[:weights], refs[weights : 2 * weights]
    (own_sem, core_s, core_r, ring_s, ring_r, x_s, x_r, y_s, y_r, a_s, a_r, b_s, b_r) = refs[2 * weights :]
    at = Place(ring)
    part_a, part_b = cut(width)
    at.greet()
    sent, landed = [], []

    def go(copy):
        copy.start()
        sent.append(copy)
        return copy

    def ring_copy(k, step):
        index = at.shard(step - 1)
        if step == 1:
            src = view(shards[k], (), at.q, width)
        else:
            src = view(fulls[k], (index,), at.q, width)
        return remote(src, view(fulls[k], (index,), at.q, width), ring_s.at[k, step - 1], ring_r.at[k, step - 1], at.up)

    items = [(k, step) for k in range(weights) for step in range(1, ring)]
    rings = {items[0]: go(ring_copy(*items[0]))}
    locals_ = []
    for k in range(weights):
        copy = pltpu.make_async_copy(shards[k], fulls[k].at[at.f], own_sem.at[k])
        copy.start()
        locals_.append(copy)
        landed.append(go(remote(shards[k], fulls[k].at[at.f], core_s.at[k, 0], core_r.at[k, 0], at.core)))
    flights = {}
    for turn in range(len(items) + 2):
        if turn < len(items):
            k, step = items[turn]
            rings[k, step].wait_recv()
            if turn + 1 < len(items):
                rings[items[turn + 1]] = go(ring_copy(*items[turn + 1]))
            mine = view(fulls[k], (at.shard(step),), at.q, width)
            flights[turn] = (
                go(remote(mine, mine, x_s.at[k, step - 1], x_r.at[k, step - 1], at.x)),
                go(remote(mine, mine, y_s.at[k, step - 1], y_r.at[k, step - 1], at.y)),
            )
        if 0 <= turn - 1 < len(items):
            k, step = items[turn - 1]
            by_x, by_y = flights[turn - 1]
            by_x.wait_recv()
            half = view(fulls[k], (at.shard(step),), at.qx, width, part_a)
            first = go(remote(half, half, a_s.at[k, step - 1], a_r.at[k, step - 1], at.y))
            by_y.wait_recv()
            half = view(fulls[k], (at.shard(step),), at.qy, width, part_b)
            second = go(remote(half, half, b_s.at[k, step - 1], b_r.at[k, step - 1], at.x))
            flights[turn - 1] = (first, second)
        if 0 <= turn - 2 < len(items):
            k, step = items[turn - 2]
            for copy in flights[turn - 2]:
                copy.wait_recv()
            whole = fulls[k].at[at.shard(step)]
            landed.append(go(remote(whole, whole, core_s.at[k, step], core_r.at[k, step], at.core)))
    for copy in landed:
        copy.wait_recv()
    for copy in locals_:
        copy.wait()
    for copy in sent:
        copy.wait_send()


def gather_weights(shards, width, fsdp):
    ring = fsdp // 2
    dma = pltpu.SemaphoreType.DMA
    steps = dma((3, ring - 1))
    return pl.pallas_call(
        partial(gather_kernel, ring, width),
        out_shape=[jax.ShapeDtypeStruct((fsdp, *s.shape), s.dtype) for s in shards],
        in_specs=[pl.BlockSpec(memory_space=pl.ANY)] * 3,
        out_specs=[pl.BlockSpec(memory_space=pl.ANY)] * 3,
        scratch_shapes=[dma((3,)), dma((3, ring)), dma((3, ring))] + [steps] * 10,
        compiler_params=pltpu.CompilerParams(collective_id=0, has_side_effects=True),
        name="gather",
    )(*shards)


def reduce_kernel(ring, width, *refs):
    weights = 3
    terms, outs = refs[:weights], refs[weights : 2 * weights]
    (
        own, pair, first_a, first_b, second_a, second_b, hops, done,
        load, core_s, core_r, xa_s, xa_r, yb_s, yb_r, ya_s, ya_r, xb_s, xb_r, ring_s, ring_r,
        end_s, end_r, out_sem,
    ) = refs[2 * weights :]
    at = Place(ring)
    part_a, part_b = cut(width)
    cols_a, cols_b = pl.ds(*part_a), pl.ds(*part_b)
    rows = slice(None)
    sent = []

    def go(copy):
        copy.start()
        sent.append(copy)
        return copy

    at.greet()
    items = [(k, j) for k in range(weights) for j in range(ring)]
    loads, pairs = {}, {}
    other = 1 - 2 * at.c
    for k, j in items:
        back = (j + 1) % ring
        mine = at.shard(back)
        loads[k, j] = []
        for q in range(QUARTERS):
            copy = pltpu.make_async_copy(view(terms[k], (mine,), q, width), own.at[k, j, q], load.at[k, j, q])
            copy.start()
            loads[k, j].append(copy)
        pairs[k, j] = [
            go(remote(view(terms[k], (mine + other,), q, width), pair.at[k, j, q], core_s.at[k, j, q], core_r.at[k, j, q], at.core))
            for q in range(QUARTERS)
        ]
    flights, rings, ends = {}, {}, {}

    def stage_one(k, j):
        for q in range(QUARTERS):
            loads[k, j][q].wait()
            pairs[k, j][q].wait_recv()
            own[k, j, q] = own[k, j, q] + pair[k, j, q]
        flights[k, j] = [
            go(remote(own.at[k, j, at.qx, rows, cols_a], first_a.at[k, j, 0], xa_s.at[k, j, 0], xa_r.at[k, j, 0], at.x)),
            go(remote(own.at[k, j, at.qd, rows, cols_a], first_a.at[k, j, 1], xa_s.at[k, j, 1], xa_r.at[k, j, 1], at.x)),
            go(remote(own.at[k, j, at.qy, rows, cols_b], first_b.at[k, j, 0], yb_s.at[k, j, 0], yb_r.at[k, j, 0], at.y)),
            go(remote(own.at[k, j, at.qd, rows, cols_b], first_b.at[k, j, 1], yb_s.at[k, j, 1], yb_r.at[k, j, 1], at.y)),
        ]

    def stage_two(k, j):
        one, two, three, four = flights[k, j]
        two.wait_recv()
        own[k, j, at.qy, :, cols_a] = own[k, j, at.qy, :, cols_a] + first_a[k, j, 1]
        next_a = go(remote(own.at[k, j, at.qy, rows, cols_a], second_a.at[k, j], ya_s.at[k, j], ya_r.at[k, j], at.y))
        four.wait_recv()
        own[k, j, at.qx, :, cols_b] = own[k, j, at.qx, :, cols_b] + first_b[k, j, 1]
        next_b = go(remote(own.at[k, j, at.qx, rows, cols_b], second_b.at[k, j], xb_s.at[k, j], xb_r.at[k, j], at.x))
        one.wait_recv()
        own[k, j, at.q, :, cols_a] = own[k, j, at.q, :, cols_a] + first_a[k, j, 0]
        three.wait_recv()
        own[k, j, at.q, :, cols_b] = own[k, j, at.q, :, cols_b] + first_b[k, j, 0]
        flights[k, j] = [next_a, next_b]

    def stage_three(k, j):
        for copy in flights[k, j]:
            copy.wait_recv()
        own[k, j, at.q, :, cols_a] = own[k, j, at.q, :, cols_a] + second_a[k, j]
        own[k, j, at.q, :, cols_b] = own[k, j, at.q, :, cols_b] + second_b[k, j]
        if j > 0:
            rings[k, j - 1].wait_recv()
            own[k, j, at.q] = own[k, j, at.q] + hops[k, j - 1]
        if j < ring - 1:
            rings[k, j] = go(remote(own.at[k, j, at.q], hops.at[k, j], ring_s.at[k, j], ring_r.at[k, j], at.up))
            return
        done[k, at.q] = own[k, j, at.q]
        mine = done.at[k, at.q]
        ends[k] = [
            go(remote(mine, mine, end_s.at[k, 0], end_r.at[k, 0], at.x)),
            go(remote(mine, mine, end_s.at[k, 1], end_r.at[k, 1], at.y)),
        ]

    def stage_four(k):
        by_x, by_y = ends[k]
        by_x.wait_recv()
        half = done.at[k, at.qx, rows, cols_a]
        first = go(remote(half, half, end_s.at[k, 2], end_r.at[k, 2], at.y))
        by_y.wait_recv()
        half = done.at[k, at.qy, rows, cols_b]
        second = go(remote(half, half, end_s.at[k, 3], end_r.at[k, 3], at.x))
        ends[k] = [first, second]

    outgoing = []

    def stage_five(k):
        for copy in ends[k]:
            copy.wait_recv()
        copy = pltpu.make_async_copy(done.at[k], outs[k], out_sem.at[k])
        copy.start()
        outgoing.append(copy)

    for turn in range(len(items) + 4):
        if turn < len(items):
            stage_one(*items[turn])
        if 0 <= turn - 1 < len(items):
            stage_two(*items[turn - 1])
        if 0 <= turn - 2 < len(items):
            stage_three(*items[turn - 2])
        if 0 <= turn - 3 < len(items) and items[turn - 3][1] == ring - 1:
            stage_four(items[turn - 3][0])
        if 0 <= turn - 4 < len(items) and items[turn - 4][1] == ring - 1:
            stage_five(items[turn - 4][0])
    for copy in outgoing:
        copy.wait()
    for copy in sent:
        copy.wait_send()


def reduce_terms(terms, rows, width, fsdp):
    ring = fsdp // 2
    dma = pltpu.SemaphoreType.DMA
    low = jnp.bfloat16
    (_, size_a), (_, size_b) = cut(width)
    vmem = pltpu.VMEM
    scratch = [
        vmem((3, ring, QUARTERS, rows, width), low),
        vmem((3, ring, QUARTERS, rows, width), low),
        vmem((3, ring, 2, rows, size_a), low),
        vmem((3, ring, 2, rows, size_b), low),
        vmem((3, ring, rows, size_a), low),
        vmem((3, ring, rows, size_b), low),
        vmem((3, ring - 1, rows, width), low),
        vmem((3, QUARTERS, rows, width), low),
    ]
    sems = (
        [dma((3, ring, QUARTERS))] * 3
        + [dma((3, ring, 2))] * 4
        + [dma((3, ring))] * 4
        + [dma((3, ring - 1))] * 2
        + [dma((3, 4))] * 2
        + [dma((3,))]
    )
    return pl.pallas_call(
        partial(reduce_kernel, ring, width),
        out_shape=[jax.ShapeDtypeStruct((QUARTERS, rows, width), low)] * 3,
        in_specs=[pl.BlockSpec(memory_space=pl.ANY)] * 3,
        out_specs=[pl.BlockSpec(memory_space=pl.ANY)] * 3,
        scratch_shapes=scratch + sems,
        compiler_params=pltpu.CompilerParams(
            collective_id=1, has_side_effects=True, vmem_limit_bytes=60 * 2**20
        ),
        name="reduce",
    )(*terms)


def body(
    dp,
    fsdp,
    tokens,
    timesteps,
    labels,
    head_mask,
    keep_mask,
    cotangent,
    time_weight,
    class_table,
    ada_weight,
    head_router,
    qkv_weight,
    proj_weight,
    fc1_weight,
    fc2_weight,
    token_router,
):
    images, seq, width = tokens.shape
    heads = head_mask.shape[1]
    size = width // heads
    scale = size ** (-0.5)
    count = images * seq
    rows = qkv_weight.shape[0]
    hidden = fc1_weight.shape[1]
    entries = time_weight.shape[0] * fsdp
    group = images * fsdp
    me_dp, me_fsdp = lax.axis_index("dp"), lax.axis_index("fsdp")
    everyone = ("dp", "fsdp")

    joint_full, fc1_full, fc2_full = gather_weights(
        [
            jnp.concatenate([qkv_weight, proj_weight], axis=1),
            fc1_weight,
            fc2_weight.reshape(QUARTERS, rows, width),
        ],
        width,
        fsdp,
    )
    joint_full = joint_full.reshape(width, 4 * width)
    triple, merger = joint_full[:, : 3 * width], joint_full[:, 3 * width :]
    expand = fc1_full.reshape(width, hidden)
    shrink = fc2_full.reshape(hidden, width)

    asked = lax.all_gather(jnp.stack([timesteps, labels], axis=1), everyone, axis=0, tiled=True)
    all_steps, all_labels = asked[:, 0], asked[:, 1]
    packed = jnp.concatenate(
        [time_weight.reshape(-1), head_router.reshape(-1), token_router.reshape(-1)]
    )
    parts = lax.all_gather(packed, "fsdp", axis=0, tiled=False)
    cut_one = time_weight.size
    cut_two = cut_one + head_router.size
    time_full = parts[:, :cut_one].reshape(entries, width)
    chooser = parts[:, cut_one:cut_two].reshape(width, heads)
    picker = parts[:, cut_two:].reshape(width, 1)

    table_rows = jnp.arange(class_table.shape[0], dtype=jnp.int32)
    all_rows = (all_labels[:, None] == table_rows[None, :]).astype(jnp.bfloat16)
    group_rows = lax.dynamic_slice_in_dim(all_rows, me_dp * group, group, axis=0)
    picked = matmul(group_rows, class_table).astype(jnp.bfloat16)
    class_part = lax.all_to_all(picked, "fsdp", split_axis=0, concat_axis=1, tiled=True)
    all_embedded = sinusoid(all_steps, entries).astype(jnp.bfloat16)
    embedded = sinusoid(timesteps, entries).astype(jnp.bfloat16)
    pre_cond = matmul(embedded, time_full) + class_part.astype(jnp.float32)
    cond = jax.nn.silu(pre_cond).astype(jnp.bfloat16)
    all_cond = lax.all_gather(cond, everyone, axis=0, tiled=True)
    group_cond = lax.dynamic_slice_in_dim(all_cond, me_dp * group, group, axis=0)
    modulation = lax.all_to_all(
        matmul(group_cond, ada_weight), "fsdp", split_axis=0, concat_axis=1, tiled=True
    )
    shift_one, scale_one, gate_one, shift_two, scale_two, gate_two = jnp.split(
        modulation[:, None, :], 6, axis=2
    )
    router_sig = jax.nn.sigmoid(matmul(cond, chooser))
    mask_float = head_mask.astype(jnp.float32)
    head_gates = mask_float * router_sig
    inputs = tokens.astype(jnp.float32)
    normed_one = layer_norm(inputs)
    flat_one = (
        (normed_one * (1.0 + scale_one) + shift_one).astype(jnp.bfloat16).reshape(count, width)
    )
    joint = matmul(flat_one, triple).astype(jnp.bfloat16)
    query = joint[:, :width].reshape(images, seq, heads, size)
    keys = joint[:, width : 2 * width].reshape(images, seq, heads, size)
    values = joint[:, 2 * width :].reshape(images, seq, heads, size)
    raw = jnp.einsum("ishe,ithe->ihst", query, keys, preferred_element_type=jnp.float32) * scale
    peak = jnp.max(raw, axis=-1, keepdims=True)
    expo = jnp.exp(raw - peak)
    total = jnp.sum(expo, axis=-1, keepdims=True)
    log_total = peak + jnp.log(total)
    probs_low = (expo / total).astype(jnp.bfloat16)
    attended = jnp.einsum("ihst,ithe->ishe", probs_low, values, preferred_element_type=jnp.float32)
    mixed = (attended * head_gates[:, None, :, None]).astype(jnp.bfloat16).reshape(count, width)
    attn = matmul(mixed, merger).reshape(images, seq, width)
    middle = inputs + gate_one * attn
    normed_two = layer_norm(middle)
    flat_two = (
        (normed_two * (1.0 + scale_two) + shift_two).astype(jnp.bfloat16).reshape(count, width)
    )
    rate = jax.nn.sigmoid(matmul(flat_two, picker)).reshape(images, seq, 1)
    upward = matmul(flat_two, expand)
    active = jax.nn.gelu(upward, approximate=True).astype(jnp.bfloat16)
    downward = matmul(active, shrink).reshape(images, seq, width)
    kept = keep_mask.astype(jnp.float32)[:, :, None]
    kept_rate = kept * rate
    output = (middle + gate_two * kept_rate * downward).astype(jnp.bfloat16)
    grad_out = cotangent.astype(jnp.float32)
    grad_gate_two = jnp.sum(grad_out * kept_rate * downward, axis=1)
    grad_down = (grad_out * gate_two * kept_rate).astype(jnp.bfloat16).reshape(count, width)
    grad_rate = jnp.sum(grad_out * gate_two * downward, axis=-1, keepdims=True) * kept
    grad_logit = (grad_rate * rate * (1.0 - rate)).astype(jnp.bfloat16).reshape(count, 1)
    grad_shrink = times_rows(active, grad_down).astype(jnp.bfloat16)
    _, gelu_pull = jax.vjp(partial(jax.nn.gelu, approximate=True), upward)
    grad_up = gelu_pull(times_back(grad_down, shrink))[0].astype(jnp.bfloat16)
    grad_expand = times_rows(flat_two, grad_up).astype(jnp.bfloat16)
    grad_picker = times_rows(grad_logit, flat_two)
    grad_h_two = (times_back(grad_up, expand) + times_back(grad_logit, picker)).reshape(
        images, seq, width
    )
    grad_shift_two = jnp.sum(grad_h_two, axis=1)
    grad_scale_two = jnp.sum(grad_h_two * normed_two, axis=1)
    grad_middle = grad_out + norm_back(middle, grad_h_two * (1.0 + scale_two))
    grad_gate_one = jnp.sum(grad_middle * attn, axis=1)
    grad_attn = (grad_middle * gate_one).astype(jnp.bfloat16).reshape(count, width)
    grad_merger = times_rows(mixed, grad_attn).astype(jnp.bfloat16)
    grad_mixed = (
        times_back(grad_attn, merger).astype(jnp.bfloat16).reshape(images, seq, heads, size)
    )
    grad_gates = jnp.sum(grad_mixed * attended, axis=(1, 3))
    grad_router = (grad_gates * mask_float * router_sig * (1.0 - router_sig)).astype(jnp.bfloat16)
    grad_attended = (grad_mixed * head_gates[:, None, :, None]).astype(jnp.bfloat16)
    again_raw = (
        jnp.einsum("ishe,ithe->ihst", query, keys, preferred_element_type=jnp.float32) * scale
    )
    probs = jnp.exp(again_raw - log_total)
    grad_values = jnp.einsum(
        "ihst,ishe->ithe",
        probs.astype(jnp.bfloat16),
        grad_attended,
        preferred_element_type=jnp.float32,
    )
    grad_probs = jnp.einsum(
        "ishe,ithe->ihst", grad_attended, values, preferred_element_type=jnp.float32
    )
    inner = jnp.sum(grad_probs * probs, axis=-1, keepdims=True)
    grad_scores = (probs * (grad_probs - inner) * scale).astype(jnp.bfloat16)
    grad_query = jnp.einsum(
        "ihst,ithe->ishe", grad_scores, keys, preferred_element_type=jnp.float32
    )
    grad_keys = jnp.einsum(
        "ihst,ishe->ithe", grad_scores, query, preferred_element_type=jnp.float32
    )
    grad_joint = jnp.concatenate(
        [
            grad_query.reshape(count, width),
            grad_keys.reshape(count, width),
            grad_values.reshape(count, width),
        ],
        axis=1,
    ).astype(jnp.bfloat16)
    grad_triple = times_rows(flat_one, grad_joint).astype(jnp.bfloat16)
    grad_h_one = times_back(grad_joint, triple).reshape(images, seq, width)
    grad_shift_one = jnp.sum(grad_h_one, axis=1)
    grad_scale_one = jnp.sum(grad_h_one * normed_one, axis=1)
    grad_inputs = grad_middle + norm_back(inputs, grad_h_one * (1.0 + scale_one))
    grad_modulation = jnp.concatenate(
        [
            grad_shift_one,
            grad_scale_one,
            grad_gate_one,
            grad_shift_two,
            grad_scale_two,
            grad_gate_two,
        ],
        axis=1,
    ).astype(jnp.bfloat16)

    sums = reduce_terms(
        [
            jnp.concatenate([grad_triple, grad_merger], axis=1).reshape(fsdp, rows, 4 * width),
            grad_expand.reshape(fsdp, rows, hidden),
            grad_shrink.reshape(fsdp, QUARTERS, rows, width),
        ],
        rows,
        width,
        fsdp,
    )
    if dp > QUARTERS:
        parts = list(sums)
        for hop in range(QUARTERS, dp, QUARTERS):
            pairs = [(i, (i + hop) % dp) for i in range(dp)]
            parts = [
                part.astype(jnp.float32) + lax.ppermute(s, "dp", pairs).astype(jnp.float32)
                for part, s in zip(parts, sums)
            ]
        sums = parts
    sums = [s.astype(jnp.float32) for s in sums]
    sum_triple = jnp.concatenate([sums[0][0], sums[0][1], sums[0][2]], axis=1)
    sum_merger = sums[0][3]
    sum_expand = jnp.concatenate([sums[1][i] for i in range(QUARTERS)], axis=1)
    sum_shrink = sums[2].reshape(QUARTERS * rows, width)

    group_grad = lax.all_to_all(grad_modulation, "fsdp", split_axis=1, concat_axis=0, tiled=True)
    all_grad = lax.all_gather(group_grad, "dp", axis=0, tiled=True)
    sum_ada = times_rows(all_cond, all_grad)
    grad_cond = lax.psum_scatter(
        times_back(group_grad, ada_weight), "fsdp", scatter_dimension=0, tiled=True
    )
    grad_cond = grad_cond + times_back(grad_router, chooser)
    _, silu_pull = jax.vjp(jax.nn.silu, pre_cond)
    grad_pre = silu_pull(grad_cond)[0].astype(jnp.bfloat16)
    both = lax.all_gather(
        jnp.concatenate([grad_pre, grad_router], axis=1), everyone, axis=0, tiled=True
    )
    all_pre, all_router = both[:, :width], both[:, width:]
    sum_time = times_rows(
        lax.dynamic_slice_in_dim(all_embedded, me_fsdp * (entries // fsdp), entries // fsdp, axis=1),
        all_pre,
    )
    sum_table = times_rows(
        all_rows, lax.dynamic_slice_in_dim(all_pre, me_fsdp * rows, rows, axis=1)
    )
    sum_chooser = times_rows(
        lax.dynamic_slice_in_dim(all_cond, me_fsdp * rows, rows, axis=1), all_router
    )
    all_picker = lax.all_gather(grad_picker, everyone, axis=0, tiled=True)
    sum_picker = lax.dynamic_slice_in_dim(
        jnp.sum(all_picker, axis=0), me_fsdp * rows, rows, axis=0
    )[:, None]
    return (
        output,
        grad_inputs,
        sum_time,
        sum_table,
        sum_ada,
        sum_chooser,
        sum_triple,
        sum_merger,
        sum_expand,
        sum_shrink,
        sum_picker,
    )


def solution(mesh):
    images = P(("dp", "fsdp"), None, None)
    pairs = P(("dp", "fsdp"), None)
    single = P(("dp", "fsdp"))
    by_row, by_column = P("fsdp", None), P(None, "fsdp")
    in_specs = (
        images, single, single, pairs, pairs, images,
        by_row, by_column, by_column, by_row, by_row, by_row, by_row, by_row, by_row,
    )
    out_specs = (
        images, images,
        by_row, by_column, by_column, by_row, by_row, by_row, by_row, by_row, by_row,
    )
    return jax.shard_map(
        partial(body, mesh.shape["dp"], mesh.shape["fsdp"]),
        mesh=mesh, in_specs=in_specs, out_specs=out_specs, check_vma=False,
    )
```

```python
from functools import partial
import math

import jax
import jax.numpy as jnp
from jax import lax
from jax.experimental import pallas as pl
from jax.experimental.pallas import tpu as pltpu
from jax.sharding import PartitionSpec as P

EPSILON = 1e-06
MESH = pl.DeviceIdType.MESH
QUARTERS = 4


def sinusoid(steps, entries):
    half = entries // 2
    freqs = jnp.exp(-math.log(10000.0) * jnp.arange(half, dtype=jnp.float32) / half)
    angles = steps.astype(jnp.float32)[:, None] * freqs[None, :]
    return jnp.concatenate([jnp.cos(angles), jnp.sin(angles)], axis=1)


def layer_norm(value):
    centered = value - jnp.mean(value, axis=-1, keepdims=True)
    return centered * lax.rsqrt(jnp.mean(centered * centered, axis=-1, keepdims=True) + EPSILON)


def norm_back(value, grad):
    _, pull = jax.vjp(layer_norm, value)
    return pull(grad)[0]


def matmul(left, right):
    return jnp.dot(left, right, preferred_element_type=jnp.float32)


def times_rows(left, right):
    return lax.dot_general(
        left, right, (((0,), (0,)), ((), ())), preferred_element_type=jnp.float32
    )


def times_back(left, right):
    return lax.dot_general(
        left, right, (((1,), (1,)), ((), ())), preferred_element_type=jnp.float32
    )


class Place:
    def __init__(self, dp, fsdp):
        ring = fsdp // 2
        self.dp, self.fsdp, self.ring = dp, fsdp, ring
        d = lax.axis_index("dp")
        f = lax.axis_index("fsdp")
        self.d, self.f = d, f
        self.z = f // 2
        self.c = f % 2
        self.q = d % QUARTERS
        dx = d + 1 - 2 * (d % 2)
        dy = d + 2 - 4 * ((d // 2) % 2)
        self.qx = dx % QUARTERS
        self.qy = dy % QUARTERS
        self.qd = (self.qx + self.qy - self.q + QUARTERS) % QUARTERS
        self.core = (d, f + 1 - 2 * (f % 2))
        self.x = (dx, f)
        self.y = (dy, f)
        self.up = (d, ((self.z + 1) % ring) * 2 + self.c)
        self.down = (d, ((self.z + ring - 1) % ring) * 2 + self.c)

    def shard(self, back):
        return ((self.z + self.ring - back) % self.ring) * 2 + self.c

    def mates(self):
        return [(self.d, (self.f + offset) % self.fsdp) for offset in range(1, self.fsdp)]

    def cousins(self):
        return [((self.d + offset) % self.dp, self.f) for offset in range(1, self.dp)]

    def greet(self):
        barrier = pltpu.get_barrier_semaphore()
        near = self.mates() + self.cousins()
        for other in near:
            pl.semaphore_signal(barrier, inc=1, device_id=other, device_id_type=MESH)
        pl.semaphore_wait(barrier, len(near))


def remote(src, dst, send, recv, device):
    return pltpu.make_async_remote_copy(
        src_ref=src, dst_ref=dst, send_sem=send, recv_sem=recv, device_id=device, device_id_type=MESH
    )


class Swap:
    def __init__(self, partners, send, recv):
        self.partners, self.send, self.recv = partners, send, recv
        self.copies = []

    def start(self, source, landing):
        for i, device in enumerate(self.partners):
            copy = remote(source(device), landing, self.send.at[i], self.recv.at[i], device)
            copy.start()
            self.copies.append(copy)

    def arrived(self):
        for copy in self.copies:
            copy.wait_recv()

    def left(self):
        for copy in self.copies:
            copy.wait_send()


def cut(width):
    first = ((width // 128 + 1) // 2) * 128
    return (0, first), (first, width - first)


def view(ref, lead, q, width, part=None):
    start, size = (0, width) if part is None else part
    flat = ref.shape[-1] != width
    if flat:
        column = pl.multiple_of(q * width + start, 128)
        return ref.at[(*lead, slice(None), pl.ds(column, size))]
    return ref.at[(*lead, q, slice(None), pl.ds(start, size))]


def gather_kernel(dp, fsdp, width, *refs):
    weights = 3
    ring = fsdp // 2
    shards, refs = refs[:weights], refs[weights:]
    ask_ref, time_ref, table_ref, ada_ref, router_ref = refs[:5]
    refs = refs[5:]
    fulls, refs = refs[:weights], refs[weights:]
    pre_ref, mod_ref, routers_ref, all_cond_ref, all_ask_ref = refs[:5]
    refs = refs[5:]
    asks, parts, mine_in, conds, columns = refs[:5]
    refs = refs[5:]
    (own_sem, core_s, core_r, ring_s, ring_r, x_s, x_r, y_s, y_r, a_s, a_r, b_s, b_r) = refs[:13]
    mate_s, mate_r, cousin_s, cousin_r, small_sem = refs[13:]
    at = Place(dp, fsdp)
    part_a, part_b = cut(width)
    at.greet()
    sent, landed = [], []
    mates, cousins = at.mates(), at.cousins()
    swaps = [Swap(mates, mate_s.at[i], mate_r.at[i]) for i in range(5)]
    far = [Swap(cousins, cousin_s.at[i], cousin_r.at[i]) for i in range(2)]
    pad = ask_ref.shape[0]
    group = fsdp * pad
    rows = table_ref.shape[1]

    def go(copy):
        copy.start()
        sent.append(copy)
        return copy

    def ring_copy(k, step):
        index = at.shard(step - 1)
        if step == 1:
            src = view(shards[k], (), at.q, width)
        else:
            src = view(fulls[k], (index,), at.q, width)
        return remote(src, view(fulls[k], (index,), at.q, width), ring_s.at[k, step - 1], ring_r.at[k, step - 1], at.up)

    small = []

    def keep(src, dst):
        copy = pltpu.make_async_copy(src, dst, small_sem.at[len(small)])
        copy.start()
        small.append(copy)

    def cond_one():
        swaps[0].arrived()
        asks[at.f] = ask_ref[...]
        every = asks[...].reshape(group, asks.shape[2])
        entries = every.shape[1] - 128
        own_rows = time_ref.shape[0]
        lanes = lax.broadcasted_iota(jnp.int32, (group, entries), 1)
        held = (lanes >= at.f * own_rows) & (lanes < (at.f + 1) * own_rows)
        embedded = jnp.where(held, every[:, :entries], 0.0).astype(jnp.bfloat16)
        stacked = jnp.concatenate([time_ref[...]] * fsdp, axis=0)
        label = every[:, entries : entries + 1].astype(jnp.int32)
        classes = table_ref.shape[0]
        picks = (label == lax.broadcasted_iota(jnp.int32, (group, classes), 1)).astype(jnp.float32)
        picked = matmul(picks.astype(jnp.bfloat16), table_ref[...]).astype(jnp.bfloat16)
        spot = lax.broadcasted_iota(jnp.int32, (rows, width), 1)
        line = lax.broadcasted_iota(jnp.int32, (rows, width), 0)
        place = (spot == line + at.f * rows).astype(jnp.float32).astype(jnp.bfloat16)
        partial_sum = matmul(embedded, stacked) + matmul(picked, place)
        parts[...] = partial_sum.reshape(fsdp, pad, width)
        swaps[1].start(lambda device: parts.at[device[1]], mine_in.at[at.f])
        far[1].start(lambda device: asks, all_ask_ref.at[at.d])
        keep(asks, all_ask_ref.at[at.d])

    def cond_two():
        swaps[1].arrived()
        mine_in[at.f] = parts[at.f]
        pre_cond = jnp.sum(mine_in[...], axis=0)
        pre_ref[...] = pre_cond
        conds[at.f] = (pre_cond * jax.nn.sigmoid(pre_cond)).astype(jnp.bfloat16).astype(jnp.float32)
        swaps[2].start(lambda device: conds.at[at.f], conds.at[at.f])

    def cond_three():
        swaps[2].arrived()
        every = conds[...].reshape(group, width).astype(jnp.bfloat16)
        columns[...] = matmul(every, ada_ref[...]).reshape(columns.shape)
        swaps[3].start(lambda device: columns.at[device[1]], mod_ref.at[at.f])
        far[0].start(lambda device: conds, all_cond_ref.at[at.d])
        keep(conds, all_cond_ref.at[at.d])
        keep(columns.at[at.f], mod_ref.at[at.f])

    extra = {0: cond_one, 1: cond_two, 2: cond_three}
    swaps[0].start(lambda device: ask_ref, asks.at[at.f])
    swaps[4].start(lambda device: router_ref, routers_ref.at[at.f])
    keep(router_ref, routers_ref.at[at.f])

    items = [(k, step) for k in range(weights) for step in range(1, ring)]
    rings = {items[0]: go(ring_copy(*items[0]))}
    locals_ = []
    for k in range(weights):
        copy = pltpu.make_async_copy(shards[k], fulls[k].at[at.f], own_sem.at[k])
        copy.start()
        locals_.append(copy)
        landed.append(go(remote(shards[k], fulls[k].at[at.f], core_s.at[k, 0], core_r.at[k, 0], at.core)))
    flights = {}
    for turn in range(len(items) + 2):
        if turn < len(items):
            k, step = items[turn]
            rings[k, step].wait_recv()
            if turn + 1 < len(items):
                rings[items[turn + 1]] = go(ring_copy(*items[turn + 1]))
            mine = view(fulls[k], (at.shard(step),), at.q, width)
            flights[turn] = (
                go(remote(mine, mine, x_s.at[k, step - 1], x_r.at[k, step - 1], at.x)),
                go(remote(mine, mine, y_s.at[k, step - 1], y_r.at[k, step - 1], at.y)),
            )
        if 0 <= turn - 1 < len(items):
            k, step = items[turn - 1]
            by_x, by_y = flights[turn - 1]
            by_x.wait_recv()
            half = view(fulls[k], (at.shard(step),), at.qx, width, part_a)
            first = go(remote(half, half, a_s.at[k, step - 1], a_r.at[k, step - 1], at.y))
            by_y.wait_recv()
            half = view(fulls[k], (at.shard(step),), at.qy, width, part_b)
            second = go(remote(half, half, b_s.at[k, step - 1], b_r.at[k, step - 1], at.x))
            flights[turn - 1] = (first, second)
        if 0 <= turn - 2 < len(items):
            k, step = items[turn - 2]
            for copy in flights[turn - 2]:
                copy.wait_recv()
            whole = fulls[k].at[at.shard(step)]
            landed.append(go(remote(whole, whole, core_s.at[k, step], core_r.at[k, step], at.core)))
        if turn in extra:
            extra[turn]()
    for swap in (swaps[3], swaps[4], far[0], far[1]):
        swap.arrived()
    for copy in landed:
        copy.wait_recv()
    for copy in locals_ + small:
        copy.wait()
    for swap in swaps + far:
        swap.left()
    for copy in sent:
        copy.wait_send()


def gather_weights(shards, asked, time_weight, class_table, ada_weight, routers, width, dp, fsdp):
    ring = fsdp // 2
    dma = pltpu.SemaphoreType.DMA
    vmem = pltpu.VMEM
    f32 = jnp.float32
    steps = dma((3, ring - 1))
    pad, asking = asked.shape
    columns = ada_weight.shape[1]
    out = jax.ShapeDtypeStruct
    any_space, in_vmem = pl.BlockSpec(memory_space=pl.ANY), pl.BlockSpec(memory_space=vmem)
    return pl.pallas_call(
        partial(gather_kernel, dp, fsdp, width),
        out_shape=[out((fsdp, *s.shape), s.dtype) for s in shards]
        + [
            out((pad, width), f32),
            out((fsdp, pad, columns), f32),
            out((fsdp, *routers.shape), routers.dtype),
            out((dp, fsdp, pad, width), f32),
            out((dp, fsdp, pad, asking), f32),
        ],
        in_specs=[any_space] * 3 + [in_vmem] * 5,
        out_specs=[any_space] * 3 + [in_vmem] + [any_space] * 4,
        scratch_shapes=[
            vmem((fsdp, pad, asking), f32),
            vmem((fsdp, pad, width), f32),
            vmem((fsdp, pad, width), f32),
            vmem((fsdp, pad, width), f32),
            vmem((fsdp, pad, columns), f32),
        ]
        + [dma((3,)), dma((3, ring)), dma((3, ring))]
        + [steps] * 10
        + [dma((5, fsdp - 1))] * 2
        + [dma((2, dp - 1))] * 2
        + [dma((4,))],
        compiler_params=pltpu.CompilerParams(
            collective_id=0, has_side_effects=True, vmem_limit_bytes=32 * 2**20
        ),
        name="gather",
    )(*shards, asked, time_weight, class_table, ada_weight, routers)


def reduce_kernel(dp, fsdp, width, *refs):
    weights = 3
    ring = fsdp // 2
    terms, refs = refs[:weights], refs[weights:]
    gm_ref, ada_ref, routed_ref, pre_ref, last_ref = refs[:5]
    refs = refs[5:]
    outs, refs = refs[:weights], refs[weights:]
    all_gm_ref, all_pre_ref = refs[:2]
    refs = refs[2:]
    (
        own, pair, first_a, first_b, second_a, second_b, hops, done, gms, parts, mine_in, pres,
        load, core_s, core_r, xa_s, xa_r, yb_s, yb_r, ya_s, ya_r, xb_s, xb_r, ring_s, ring_r,
        end_s, end_r, out_sem, mate_s, mate_r, cousin_s, cousin_r, small_sem,
    ) = refs
    at = Place(dp, fsdp)
    part_a, part_b = cut(width)
    cols_a, cols_b = pl.ds(*part_a), pl.ds(*part_b)
    rows = slice(None)
    sent = []

    def go(copy):
        copy.start()
        sent.append(copy)
        return copy

    at.greet()
    items = [(k, j) for k in range(weights) for j in range(ring)]
    loads, pairs = {}, {}
    other = 1 - 2 * at.c
    for k, j in items:
        back = (j + 1) % ring
        mine = at.shard(back)
        loads[k, j] = []
        for q in range(QUARTERS):
            copy = pltpu.make_async_copy(view(terms[k], (mine,), q, width), own.at[k, j, q], load.at[k, j, q])
            copy.start()
            loads[k, j].append(copy)
        pairs[k, j] = [
            go(remote(view(terms[k], (mine + other,), q, width), pair.at[k, j, q], core_s.at[k, j, q], core_r.at[k, j, q], at.core))
            for q in range(QUARTERS)
        ]
    flights, rings, ends = {}, {}, {}

    mates, cousins = at.mates(), at.cousins()
    swaps = [Swap(mates, mate_s.at[i], mate_r.at[i]) for i in range(3)]
    far = [Swap(cousins, cousin_s.at[i], cousin_r.at[i]) for i in range(2)]
    pad = pre_ref.shape[0]
    small = []

    def keep(src, dst):
        copy = pltpu.make_async_copy(src, dst, small_sem.at[len(small)])
        copy.start()
        small.append(copy)

    def cond_one():
        swaps[0].arrived()
        gms[at.f] = gm_ref[at.f]
        every = gms[...].reshape(fsdp * pad, gms.shape[2]).astype(jnp.bfloat16)
        parts[...] = times_back(every, ada_ref[...]).reshape(parts.shape)
        swaps[1].start(lambda device: parts.at[device[1]], mine_in.at[at.f])
        far[0].start(lambda device: gms, all_gm_ref.at[at.d])
        keep(gms, all_gm_ref.at[at.d])

    def cond_two():
        swaps[1].arrived()
        mine_in[at.f] = parts[at.f]
        grad_cond = jnp.sum(mine_in[...], axis=0) + routed_ref[...]
        pre_cond = pre_ref[...]
        sig = jax.nn.sigmoid(pre_cond)
        grad_pre = grad_cond * (sig * (1.0 + pre_cond * (1.0 - sig)))
        grad_pre = grad_pre.astype(jnp.bfloat16).astype(jnp.float32)
        pres[at.f, :, :width] = grad_pre + last_ref[:, :width]
        pres[at.f, :, width:] = last_ref[:, width:]
        swaps[2].start(lambda device: pres.at[at.f], pres.at[at.f])

    def cond_three():
        swaps[2].arrived()
        far[1].start(lambda device: pres, all_pre_ref.at[at.d])
        keep(pres, all_pre_ref.at[at.d])

    extra = {1: cond_one, 3: cond_two, 5: cond_three}
    swaps[0].start(lambda device: gm_ref.at[device[1]], gms.at[at.f])

    def stage_one(k, j):
        for q in range(QUARTERS):
            loads[k, j][q].wait()
            pairs[k, j][q].wait_recv()
            own[k, j, q] = own[k, j, q] + pair[k, j, q]
        flights[k, j] = [
            go(remote(own.at[k, j, at.qx, rows, cols_a], first_a.at[k, j, 0], xa_s.at[k, j, 0], xa_r.at[k, j, 0], at.x)),
            go(remote(own.at[k, j, at.qd, rows, cols_a], first_a.at[k, j, 1], xa_s.at[k, j, 1], xa_r.at[k, j, 1], at.x)),
            go(remote(own.at[k, j, at.qy, rows, cols_b], first_b.at[k, j, 0], yb_s.at[k, j, 0], yb_r.at[k, j, 0], at.y)),
            go(remote(own.at[k, j, at.qd, rows, cols_b], first_b.at[k, j, 1], yb_s.at[k, j, 1], yb_r.at[k, j, 1], at.y)),
        ]

    def stage_two(k, j):
        one, two, three, four = flights[k, j]
        two.wait_recv()
        own[k, j, at.qy, :, cols_a] = own[k, j, at.qy, :, cols_a] + first_a[k, j, 1]
        next_a = go(remote(own.at[k, j, at.qy, rows, cols_a], second_a.at[k, j], ya_s.at[k, j], ya_r.at[k, j], at.y))
        four.wait_recv()
        own[k, j, at.qx, :, cols_b] = own[k, j, at.qx, :, cols_b] + first_b[k, j, 1]
        next_b = go(remote(own.at[k, j, at.qx, rows, cols_b], second_b.at[k, j], xb_s.at[k, j], xb_r.at[k, j], at.x))
        one.wait_recv()
        own[k, j, at.q, :, cols_a] = own[k, j, at.q, :, cols_a] + first_a[k, j, 0]
        three.wait_recv()
        own[k, j, at.q, :, cols_b] = own[k, j, at.q, :, cols_b] + first_b[k, j, 0]
        flights[k, j] = [next_a, next_b]

    def stage_three(k, j):
        for copy in flights[k, j]:
            copy.wait_recv()
        own[k, j, at.q, :, cols_a] = own[k, j, at.q, :, cols_a] + second_a[k, j]
        own[k, j, at.q, :, cols_b] = own[k, j, at.q, :, cols_b] + second_b[k, j]
        if j > 0:
            rings[k, j - 1].wait_recv()
            own[k, j, at.q] = own[k, j, at.q] + hops[k, j - 1]
        if j < ring - 1:
            rings[k, j] = go(remote(own.at[k, j, at.q], hops.at[k, j], ring_s.at[k, j], ring_r.at[k, j], at.up))
            return
        done[k, at.q] = own[k, j, at.q]
        mine = done.at[k, at.q]
        ends[k] = [
            go(remote(mine, mine, end_s.at[k, 0], end_r.at[k, 0], at.x)),
            go(remote(mine, mine, end_s.at[k, 1], end_r.at[k, 1], at.y)),
        ]

    def stage_four(k):
        by_x, by_y = ends[k]
        by_x.wait_recv()
        half = done.at[k, at.qx, rows, cols_a]
        first = go(remote(half, half, end_s.at[k, 2], end_r.at[k, 2], at.y))
        by_y.wait_recv()
        half = done.at[k, at.qy, rows, cols_b]
        second = go(remote(half, half, end_s.at[k, 3], end_r.at[k, 3], at.x))
        ends[k] = [first, second]

    outgoing = []

    def stage_five(k):
        for copy in ends[k]:
            copy.wait_recv()
        copy = pltpu.make_async_copy(done.at[k], outs[k], out_sem.at[k])
        copy.start()
        outgoing.append(copy)

    for turn in range(len(items) + 4):
        if turn < len(items):
            stage_one(*items[turn])
        if 0 <= turn - 1 < len(items):
            stage_two(*items[turn - 1])
        if 0 <= turn - 2 < len(items):
            stage_three(*items[turn - 2])
        if 0 <= turn - 3 < len(items) and items[turn - 3][1] == ring - 1:
            stage_four(items[turn - 3][0])
        if 0 <= turn - 4 < len(items) and items[turn - 4][1] == ring - 1:
            stage_five(items[turn - 4][0])
        if turn in extra:
            extra[turn]()
    for swap in far:
        swap.arrived()
    for copy in outgoing + small:
        copy.wait()
    for swap in swaps + far:
        swap.left()
    for copy in sent:
        copy.wait_send()


def reduce_terms(terms, grad_modulation, ada_weight, routed, pre_cond, last, rows, width, dp, fsdp):
    ring = fsdp // 2
    dma = pltpu.SemaphoreType.DMA
    low = jnp.bfloat16
    (_, size_a), (_, size_b) = cut(width)
    vmem = pltpu.VMEM
    f32 = jnp.float32
    pad = pre_cond.shape[0]
    out = jax.ShapeDtypeStruct
    any_space, in_vmem = pl.BlockSpec(memory_space=pl.ANY), pl.BlockSpec(memory_space=vmem)
    scratch = [
        vmem((3, ring, QUARTERS, rows, width), low),
        vmem((3, ring, QUARTERS, rows, width), low),
        vmem((3, ring, 2, rows, size_a), low),
        vmem((3, ring, 2, rows, size_b), low),
        vmem((3, ring, rows, size_a), low),
        vmem((3, ring, rows, size_b), low),
        vmem((3, ring - 1, rows, width), low),
        vmem((3, QUARTERS, rows, width), low),
        vmem(grad_modulation.shape, f32),
        vmem((fsdp, pad, width), f32),
        vmem((fsdp, pad, width), f32),
        vmem((fsdp, *last.shape), f32),
    ]
    sems = (
        [dma((3, ring, QUARTERS))] * 3
        + [dma((3, ring, 2))] * 4
        + [dma((3, ring))] * 4
        + [dma((3, ring - 1))] * 2
        + [dma((3, 4))] * 2
        + [dma((3,))]
        + [dma((3, fsdp - 1))] * 2
        + [dma((2, dp - 1))] * 2
        + [dma((2,))]
    )
    return pl.pallas_call(
        partial(reduce_kernel, dp, fsdp, width),
        out_shape=[out((QUARTERS, rows, width), low)] * 3
        + [out((dp, *grad_modulation.shape), f32), out((dp, fsdp, *last.shape), f32)],
        in_specs=[any_space] * 3 + [in_vmem] * 5,
        out_specs=[any_space] * 5,
        scratch_shapes=scratch + sems,
        compiler_params=pltpu.CompilerParams(
            collective_id=1, has_side_effects=True, vmem_limit_bytes=60 * 2**20
        ),
        name="reduce",
    )(*terms, grad_modulation, ada_weight, routed, pre_cond, last)


def body(
    dp,
    fsdp,
    tokens,
    timesteps,
    labels,
    head_mask,
    keep_mask,
    cotangent,
    time_weight,
    class_table,
    ada_weight,
    head_router,
    qkv_weight,
    proj_weight,
    fc1_weight,
    fc2_weight,
    token_router,
):
    images, seq, width = tokens.shape
    heads = head_mask.shape[1]
    size = width // heads
    scale = size ** (-0.5)
    count = images * seq
    rows = qkv_weight.shape[0]
    hidden = fc1_weight.shape[1]
    entries = time_weight.shape[0] * fsdp
    me_fsdp = lax.axis_index("fsdp")
    pad = (images // 8 + 1) * 8

    def padded(array, value=0.0):
        return jnp.pad(array, ((0, pad - images), (0, 0)), constant_values=value)

    embedded = sinusoid(timesteps, entries).astype(jnp.bfloat16)
    asked = jnp.concatenate(
        [
            padded(embedded.astype(jnp.float32)),
            padded(jnp.broadcast_to(labels.astype(jnp.float32)[:, None], (images, 128)), -1.0),
        ],
        axis=1,
    )
    routers = jnp.pad(
        jnp.concatenate([head_router, token_router], axis=1), ((0, 0), (0, 127 - heads))
    )
    joint_full, fc1_full, fc2_full, pre_cond_pad, modulation, routers_full, all_cond, all_asked = gather_weights(
        [
            jnp.concatenate([qkv_weight, proj_weight], axis=1),
            fc1_weight,
            fc2_weight.reshape(QUARTERS, rows, width),
        ],
        asked,
        time_weight,
        class_table,
        ada_weight,
        routers,
        width,
        dp,
        fsdp,
    )
    joint_full = joint_full.reshape(width, 4 * width)
    triple, merger = joint_full[:, : 3 * width], joint_full[:, 3 * width :]
    expand = fc1_full.reshape(width, hidden)
    shrink = fc2_full.reshape(hidden, width)
    routers_full = routers_full.reshape(width, 128)
    chooser, picker = routers_full[:, :heads], routers_full[:, heads : heads + 1]
    everyone = dp * fsdp * pad
    all_cond = all_cond.reshape(everyone, width).astype(jnp.bfloat16)
    all_asked = all_asked.reshape(everyone, asked.shape[1])
    pre_cond = pre_cond_pad[:images]
    cond = jax.nn.silu(pre_cond).astype(jnp.bfloat16)
    modulation = modulation[:, :images].transpose(1, 0, 2).reshape(images, 6 * width)
    shift_one, scale_one, gate_one, shift_two, scale_two, gate_two = jnp.split(
        modulation[:, None, :], 6, axis=2
    )
    router_sig = jax.nn.sigmoid(matmul(cond, chooser))
    mask_float = head_mask.astype(jnp.float32)
    head_gates = mask_float * router_sig
    inputs = tokens.astype(jnp.float32)
    normed_one = layer_norm(inputs)
    flat_one = (
        (normed_one * (1.0 + scale_one) + shift_one).astype(jnp.bfloat16).reshape(count, width)
    )
    joint = matmul(flat_one, triple).astype(jnp.bfloat16)
    query = joint[:, :width].reshape(images, seq, heads, size)
    keys = joint[:, width : 2 * width].reshape(images, seq, heads, size)
    values = joint[:, 2 * width :].reshape(images, seq, heads, size)
    raw = jnp.einsum("ishe,ithe->ihst", query, keys, preferred_element_type=jnp.float32) * scale
    peak = jnp.max(raw, axis=-1, keepdims=True)
    expo = jnp.exp(raw - peak)
    total = jnp.sum(expo, axis=-1, keepdims=True)
    log_total = peak + jnp.log(total)
    probs_low = (expo / total).astype(jnp.bfloat16)
    attended = jnp.einsum("ihst,ithe->ishe", probs_low, values, preferred_element_type=jnp.float32)
    mixed = (attended * head_gates[:, None, :, None]).astype(jnp.bfloat16).reshape(count, width)
    attn = matmul(mixed, merger).reshape(images, seq, width)
    middle = inputs + gate_one * attn
    normed_two = layer_norm(middle)
    flat_two = (
        (normed_two * (1.0 + scale_two) + shift_two).astype(jnp.bfloat16).reshape(count, width)
    )
    rate = jax.nn.sigmoid(matmul(flat_two, picker)).reshape(images, seq, 1)
    upward = matmul(flat_two, expand)
    active = jax.nn.gelu(upward, approximate=True).astype(jnp.bfloat16)
    downward = matmul(active, shrink).reshape(images, seq, width)
    kept = keep_mask.astype(jnp.float32)[:, :, None]
    kept_rate = kept * rate
    output = (middle + gate_two * kept_rate * downward).astype(jnp.bfloat16)
    grad_out = cotangent.astype(jnp.float32)
    grad_gate_two = jnp.sum(grad_out * kept_rate * downward, axis=1)
    grad_down = (grad_out * gate_two * kept_rate).astype(jnp.bfloat16).reshape(count, width)
    grad_rate = jnp.sum(grad_out * gate_two * downward, axis=-1, keepdims=True) * kept
    grad_logit = (grad_rate * rate * (1.0 - rate)).astype(jnp.bfloat16).reshape(count, 1)
    grad_shrink = times_rows(active, grad_down).astype(jnp.bfloat16)
    _, gelu_pull = jax.vjp(partial(jax.nn.gelu, approximate=True), upward)
    grad_up = gelu_pull(times_back(grad_down, shrink))[0].astype(jnp.bfloat16)
    grad_expand = times_rows(flat_two, grad_up).astype(jnp.bfloat16)
    grad_picker = times_rows(grad_logit, flat_two)
    grad_h_two = (times_back(grad_up, expand) + times_back(grad_logit, picker)).reshape(
        images, seq, width
    )
    grad_shift_two = jnp.sum(grad_h_two, axis=1)
    grad_scale_two = jnp.sum(grad_h_two * normed_two, axis=1)
    grad_middle = grad_out + norm_back(middle, grad_h_two * (1.0 + scale_two))
    grad_gate_one = jnp.sum(grad_middle * attn, axis=1)
    grad_attn = (grad_middle * gate_one).astype(jnp.bfloat16).reshape(count, width)
    grad_merger = times_rows(mixed, grad_attn).astype(jnp.bfloat16)
    grad_mixed = (
        times_back(grad_attn, merger).astype(jnp.bfloat16).reshape(images, seq, heads, size)
    )
    grad_gates = jnp.sum(grad_mixed * attended, axis=(1, 3))
    grad_router = (grad_gates * mask_float * router_sig * (1.0 - router_sig)).astype(jnp.bfloat16)
    grad_attended = (grad_mixed * head_gates[:, None, :, None]).astype(jnp.bfloat16)
    again_raw = (
        jnp.einsum("ishe,ithe->ihst", query, keys, preferred_element_type=jnp.float32) * scale
    )
    probs = jnp.exp(again_raw - log_total)
    grad_values = jnp.einsum(
        "ihst,ishe->ithe",
        probs.astype(jnp.bfloat16),
        grad_attended,
        preferred_element_type=jnp.float32,
    )
    grad_probs = jnp.einsum(
        "ishe,ithe->ihst", grad_attended, values, preferred_element_type=jnp.float32
    )
    inner = jnp.sum(grad_probs * probs, axis=-1, keepdims=True)
    grad_scores = (probs * (grad_probs - inner) * scale).astype(jnp.bfloat16)
    grad_query = jnp.einsum(
        "ihst,ithe->ishe", grad_scores, keys, preferred_element_type=jnp.float32
    )
    grad_keys = jnp.einsum(
        "ihst,ishe->ithe", grad_scores, query, preferred_element_type=jnp.float32
    )
    grad_joint = jnp.concatenate(
        [
            grad_query.reshape(count, width),
            grad_keys.reshape(count, width),
            grad_values.reshape(count, width),
        ],
        axis=1,
    ).astype(jnp.bfloat16)
    grad_triple = times_rows(flat_one, grad_joint).astype(jnp.bfloat16)
    grad_h_one = times_back(grad_joint, triple).reshape(images, seq, width)
    grad_shift_one = jnp.sum(grad_h_one, axis=1)
    grad_scale_one = jnp.sum(grad_h_one * normed_one, axis=1)
    grad_inputs = grad_middle + norm_back(inputs, grad_h_one * (1.0 + scale_one))
    grad_modulation = jnp.concatenate(
        [
            grad_shift_one,
            grad_scale_one,
            grad_gate_one,
            grad_shift_two,
            grad_scale_two,
            grad_gate_two,
        ],
        axis=1,
    ).astype(jnp.bfloat16)

    last = jnp.concatenate(
        [
            jnp.pad(grad_picker, ((pad - 1, 0), (0, 0))),
            padded(jnp.pad(grad_router.astype(jnp.float32), ((0, 0), (0, 128 - heads)))),
        ],
        axis=1,
    )
    *sums, all_grad, all_pre = reduce_terms(
        [
            jnp.concatenate([grad_triple, grad_merger], axis=1).reshape(fsdp, rows, 4 * width),
            grad_expand.reshape(fsdp, rows, hidden),
            grad_shrink.reshape(fsdp, QUARTERS, rows, width),
        ],
        padded(grad_modulation.astype(jnp.float32)).reshape(pad, fsdp, -1).transpose(1, 0, 2),
        ada_weight,
        padded(times_back(grad_router, chooser)),
        pre_cond_pad,
        last,
        rows,
        width,
        dp,
        fsdp,
    )
    if dp > QUARTERS:
        parts = list(sums)
        for hop in range(QUARTERS, dp, QUARTERS):
            pairs = [(i, (i + hop) % dp) for i in range(dp)]
            parts = [
                part.astype(jnp.float32) + lax.ppermute(s, "dp", pairs).astype(jnp.float32)
                for part, s in zip(parts, sums)
            ]
        sums = parts
    sums = [s.astype(jnp.float32) for s in sums]
    sum_triple = jnp.concatenate([sums[0][0], sums[0][1], sums[0][2]], axis=1)
    sum_merger = sums[0][3]
    sum_expand = jnp.concatenate([sums[1][i] for i in range(QUARTERS)], axis=1)
    sum_shrink = sums[2].reshape(QUARTERS * rows, width)

    sum_ada = times_rows(all_cond, all_grad.reshape(everyone, -1).astype(jnp.bfloat16))
    sum_picker = lax.dynamic_slice_in_dim(
        jnp.sum(all_pre[:, :, pad - 1, :width], axis=(0, 1)), me_fsdp * rows, rows, axis=0
    )[:, None]
    is_image = (jnp.arange(pad) < images)[None, None, :, None]
    all_pre = jnp.where(is_image, all_pre, 0.0).reshape(everyone, -1).astype(jnp.bfloat16)
    all_router = all_pre[:, width : width + heads]
    all_pre = all_pre[:, :width]
    own_entries = entries // fsdp
    all_embedded = lax.dynamic_slice_in_dim(
        all_asked[:, :entries], me_fsdp * own_entries, own_entries, axis=1
    ).astype(jnp.bfloat16)
    classes = jnp.arange(class_table.shape[0], dtype=jnp.float32)
    all_rows = (all_asked[:, entries : entries + 1] == classes[None, :]).astype(jnp.bfloat16)
    sum_time = times_rows(all_embedded, all_pre)
    sum_table = times_rows(
        all_rows, lax.dynamic_slice_in_dim(all_pre, me_fsdp * rows, rows, axis=1)
    )
    sum_chooser = times_rows(
        lax.dynamic_slice_in_dim(all_cond, me_fsdp * rows, rows, axis=1), all_router
    )
    return (
        output,
        grad_inputs,
        sum_time,
        sum_table,
        sum_ada,
        sum_chooser,
        sum_triple,
        sum_merger,
        sum_expand,
        sum_shrink,
        sum_picker,
    )


def solution(mesh):
    images = P(("dp", "fsdp"), None, None)
    pairs = P(("dp", "fsdp"), None)
    single = P(("dp", "fsdp"))
    by_row, by_column = P("fsdp", None), P(None, "fsdp")
    in_specs = (
        images, single, single, pairs, pairs, images,
        by_row, by_column, by_column, by_row, by_row, by_row, by_row, by_row, by_row,
    )
    out_specs = (
        images, images,
        by_row, by_column, by_column, by_row, by_row, by_row, by_row, by_row, by_row,
    )
    return jax.shard_map(
        partial(body, mesh.shape["dp"], mesh.shape["fsdp"]),
        mesh=mesh, in_specs=in_specs, out_specs=out_specs, check_vma=False,
    )
```

```python
from functools import partial
import math

import jax
import jax.numpy as jnp
from jax import lax
from jax.experimental import pallas as pl
from jax.experimental.pallas import tpu as pltpu
from jax.sharding import PartitionSpec as P

EPSILON = 1e-06
MESH = pl.DeviceIdType.MESH
QUARTERS = 4


def sinusoid(steps, entries):
    half = entries // 2
    freqs = jnp.exp(-math.log(10000.0) * jnp.arange(half, dtype=jnp.float32) / half)
    angles = steps.astype(jnp.float32)[:, None] * freqs[None, :]
    return jnp.concatenate([jnp.cos(angles), jnp.sin(angles)], axis=1)


def layer_norm(value):
    centered = value - jnp.mean(value, axis=-1, keepdims=True)
    return centered * lax.rsqrt(jnp.mean(centered * centered, axis=-1, keepdims=True) + EPSILON)


def norm_back(value, grad):
    _, pull = jax.vjp(layer_norm, value)
    return pull(grad)[0]


def matmul(left, right):
    return jnp.dot(left, right, preferred_element_type=jnp.float32)


def times_rows(left, right):
    return lax.dot_general(
        left, right, (((0,), (0,)), ((), ())), preferred_element_type=jnp.float32
    )


def times_back(left, right):
    return lax.dot_general(
        left, right, (((1,), (1,)), ((), ())), preferred_element_type=jnp.float32
    )


class Place:
    def __init__(self, dp, fsdp):
        ring = fsdp // 2
        self.dp, self.fsdp, self.ring = dp, fsdp, ring
        d = lax.axis_index("dp")
        f = lax.axis_index("fsdp")
        self.d, self.f = d, f
        self.z = f // 2
        self.c = f % 2
        self.q = d % QUARTERS
        dx = d + 1 - 2 * (d % 2)
        dy = d + 2 - 4 * ((d // 2) % 2)
        self.qx = dx % QUARTERS
        self.qy = dy % QUARTERS
        self.qd = (self.qx + self.qy - self.q + QUARTERS) % QUARTERS
        self.core = (d, f + 1 - 2 * (f % 2))
        self.x = (dx, f)
        self.y = (dy, f)
        self.up = (d, ((self.z + 1) % ring) * 2 + self.c)
        self.down = (d, ((self.z + ring - 1) % ring) * 2 + self.c)

    def shard(self, back):
        return ((self.z + self.ring - back) % self.ring) * 2 + self.c

    def mates(self):
        return [(self.d, (self.f + offset) % self.fsdp) for offset in range(1, self.fsdp)]

    def cousins(self):
        return [((self.d + offset) % self.dp, self.f) for offset in range(1, self.dp)]

    def greet(self):
        barrier = pltpu.get_barrier_semaphore()
        near = self.mates() + self.cousins()
        for other in near:
            pl.semaphore_signal(barrier, inc=1, device_id=other, device_id_type=MESH)
        pl.semaphore_wait(barrier, len(near))


def remote(src, dst, send, recv, device):
    return pltpu.make_async_remote_copy(
        src_ref=src, dst_ref=dst, send_sem=send, recv_sem=recv, device_id=device, device_id_type=MESH
    )


class Swap:
    def __init__(self, partners, send, recv):
        self.partners, self.send, self.recv = partners, send, recv
        self.copies = []

    def start(self, source, landing):
        for i, device in enumerate(self.partners):
            copy = remote(source(device), landing, self.send.at[i], self.recv.at[i], device)
            copy.start()
            self.copies.append(copy)

    def arrived(self):
        for copy in self.copies:
            copy.wait_recv()

    def left(self):
        for copy in self.copies:
            copy.wait_send()


def cut(width):
    first = ((width // 128 + 1) // 2) * 128
    return (0, first), (first, width - first)


def view(ref, lead, q, width, part=None):
    start, size = (0, width) if part is None else part
    flat = ref.shape[-1] != width
    if flat:
        column = pl.multiple_of(q * width + start, 128)
        return ref.at[(*lead, slice(None), pl.ds(column, size))]
    return ref.at[(*lead, q, slice(None), pl.ds(start, size))]


def gather_kernel(dp, fsdp, width, *refs):
    weights = 3
    ring = fsdp // 2
    shards, refs = refs[:weights], refs[weights:]
    ask_ref, time_ref, table_ref, ada_ref, router_ref = refs[:5]
    refs = refs[5:]
    fulls, refs = refs[:weights], refs[weights:]
    pre_ref, mod_ref, routers_ref, all_cond_ref, all_ask_ref = refs[:5]
    refs = refs[5:]
    asks, parts, mine_in, conds, columns = refs[:5]
    refs = refs[5:]
    (own_sem, core_s, core_r, ring_s, ring_r, x_s, x_r, y_s, y_r, a_s, a_r, b_s, b_r) = refs[:13]
    mate_s, mate_r, cousin_s, cousin_r, small_sem = refs[13:]
    at = Place(dp, fsdp)
    part_a, part_b = cut(width)
    at.greet()
    sent, landed = [], []
    mates, cousins = at.mates(), at.cousins()
    swaps = [Swap(mates, mate_s.at[i], mate_r.at[i]) for i in range(5)]
    far = [Swap(cousins, cousin_s.at[i], cousin_r.at[i]) for i in range(2)]
    pad = ask_ref.shape[0]
    group = fsdp * pad
    rows = table_ref.shape[1]

    def go(copy):
        copy.start()
        sent.append(copy)
        return copy

    def ring_copy(k, step):
        index = at.shard(step - 1)
        if step == 1:
            src = view(shards[k], (), at.q, width)
        else:
            src = view(fulls[k], (index,), at.q, width)
        return remote(src, view(fulls[k], (index,), at.q, width), ring_s.at[k, step - 1], ring_r.at[k, step - 1], at.up)

    small = []

    def keep(src, dst):
        copy = pltpu.make_async_copy(src, dst, small_sem.at[len(small)])
        copy.start()
        small.append(copy)

    def cond_one():
        swaps[0].arrived()
        asks[at.f] = ask_ref[...]
        every = asks[...].reshape(group, asks.shape[2])
        entries = every.shape[1] - 128
        own_rows = time_ref.shape[0]
        lanes = lax.broadcasted_iota(jnp.int32, (group, entries), 1)
        held = (lanes >= at.f * own_rows) & (lanes < (at.f + 1) * own_rows)
        embedded = jnp.where(held, every[:, :entries], 0.0).astype(jnp.bfloat16)
        stacked = jnp.concatenate([time_ref[...]] * fsdp, axis=0)
        label = every[:, entries : entries + 1].astype(jnp.int32)
        classes = table_ref.shape[0]
        picks = (label == lax.broadcasted_iota(jnp.int32, (group, classes), 1)).astype(jnp.float32)
        picked = matmul(picks.astype(jnp.bfloat16), table_ref[...]).astype(jnp.bfloat16)
        spot = lax.broadcasted_iota(jnp.int32, (rows, width), 1)
        line = lax.broadcasted_iota(jnp.int32, (rows, width), 0)
        place = (spot == line + at.f * rows).astype(jnp.float32).astype(jnp.bfloat16)
        partial_sum = matmul(embedded, stacked) + matmul(picked, place)
        parts[...] = partial_sum.reshape(fsdp, pad, width)
        swaps[1].start(lambda device: parts.at[device[1]], mine_in.at[at.f])
        far[1].start(lambda device: asks, all_ask_ref.at[at.d])
        keep(asks, all_ask_ref.at[at.d])

    def cond_two():
        swaps[1].arrived()
        mine_in[at.f] = parts[at.f]
        pre_cond = jnp.sum(mine_in[...], axis=0)
        pre_ref[...] = pre_cond
        conds[at.f] = (pre_cond * jax.nn.sigmoid(pre_cond)).astype(jnp.bfloat16).astype(jnp.float32)
        swaps[2].start(lambda device: conds.at[at.f], conds.at[at.f])

    def cond_three():
        swaps[2].arrived()
        every = conds[...].reshape(group, width).astype(jnp.bfloat16)
        columns[...] = matmul(every, ada_ref[...]).reshape(columns.shape)
        swaps[3].start(lambda device: columns.at[device[1]], mod_ref.at[at.f])
        far[0].start(lambda device: conds, all_cond_ref.at[at.d])
        keep(conds, all_cond_ref.at[at.d])
        keep(columns.at[at.f], mod_ref.at[at.f])

    extra = {0: cond_one, 1: cond_two, 2: cond_three}
    swaps[0].start(lambda device: ask_ref, asks.at[at.f])
    swaps[4].start(lambda device: router_ref, routers_ref.at[at.f])
    keep(router_ref, routers_ref.at[at.f])

    items = [(k, step) for k in range(weights) for step in range(1, ring)]
    rings = {items[0]: go(ring_copy(*items[0]))}
    locals_ = []
    for k in range(weights):
        copy = pltpu.make_async_copy(shards[k], fulls[k].at[at.f], own_sem.at[k])
        copy.start()
        locals_.append(copy)
        landed.append(go(remote(shards[k], fulls[k].at[at.f], core_s.at[k, 0], core_r.at[k, 0], at.core)))
    flights = {}
    for turn in range(len(items) + 2):
        if turn < len(items):
            k, step = items[turn]
            rings[k, step].wait_recv()
            if turn + 1 < len(items):
                rings[items[turn + 1]] = go(ring_copy(*items[turn + 1]))
            mine = view(fulls[k], (at.shard(step),), at.q, width)
            flights[turn] = (
                go(remote(mine, mine, x_s.at[k, step - 1], x_r.at[k, step - 1], at.x)),
                go(remote(mine, mine, y_s.at[k, step - 1], y_r.at[k, step - 1], at.y)),
            )
        if 0 <= turn - 1 < len(items):
            k, step = items[turn - 1]
            by_x, by_y = flights[turn - 1]
            by_x.wait_recv()
            half = view(fulls[k], (at.shard(step),), at.qx, width, part_a)
            first = go(remote(half, half, a_s.at[k, step - 1], a_r.at[k, step - 1], at.y))
            by_y.wait_recv()
            half = view(fulls[k], (at.shard(step),), at.qy, width, part_b)
            second = go(remote(half, half, b_s.at[k, step - 1], b_r.at[k, step - 1], at.x))
            flights[turn - 1] = (first, second)
        if 0 <= turn - 2 < len(items):
            k, step = items[turn - 2]
            for copy in flights[turn - 2]:
                copy.wait_recv()
            whole = fulls[k].at[at.shard(step)]
            landed.append(go(remote(whole, whole, core_s.at[k, step], core_r.at[k, step], at.core)))
        if turn in extra:
            extra[turn]()
    for swap in (swaps[3], swaps[4], far[0], far[1]):
        swap.arrived()
    for copy in landed:
        copy.wait_recv()
    for copy in locals_ + small:
        copy.wait()
    for swap in swaps + far:
        swap.left()
    for copy in sent:
        copy.wait_send()


def gather_weights(shards, asked, time_weight, class_table, ada_weight, routers, width, dp, fsdp):
    ring = fsdp // 2
    dma = pltpu.SemaphoreType.DMA
    vmem = pltpu.VMEM
    f32 = jnp.float32
    steps = dma((3, ring - 1))
    pad, asking = asked.shape
    columns = ada_weight.shape[1]
    out = jax.ShapeDtypeStruct
    any_space, in_vmem = pl.BlockSpec(memory_space=pl.ANY), pl.BlockSpec(memory_space=vmem)
    return pl.pallas_call(
        partial(gather_kernel, dp, fsdp, width),
        out_shape=[out((fsdp, *s.shape), s.dtype) for s in shards]
        + [
            out((pad, width), f32),
            out((fsdp, pad, columns), f32),
            out((fsdp, *routers.shape), routers.dtype),
            out((dp, fsdp, pad, width), f32),
            out((dp, fsdp, pad, asking), f32),
        ],
        in_specs=[any_space] * 3 + [in_vmem] * 5,
        out_specs=[any_space] * 3 + [in_vmem] + [any_space] * 4,
        scratch_shapes=[
            vmem((fsdp, pad, asking), f32),
            vmem((fsdp, pad, width), f32),
            vmem((fsdp, pad, width), f32),
            vmem((fsdp, pad, width), f32),
            vmem((fsdp, pad, columns), f32),
        ]
        + [dma((3,)), dma((3, ring)), dma((3, ring))]
        + [steps] * 10
        + [dma((5, fsdp - 1))] * 2
        + [dma((2, dp - 1))] * 2
        + [dma((4,))],
        compiler_params=pltpu.CompilerParams(
            collective_id=0, has_side_effects=True, vmem_limit_bytes=32 * 2**20
        ),
        name="gather",
    )(*shards, asked, time_weight, class_table, ada_weight, routers)


def reduce_kernel(dp, fsdp, width, *refs):
    weights = 3
    ring = fsdp // 2
    terms, refs = refs[:weights], refs[weights:]
    gm_ref, ada_ref, routed_ref, pre_ref, last_ref = refs[:5]
    refs = refs[5:]
    outs, refs = refs[:weights], refs[weights:]
    all_gm_ref, all_pre_ref = refs[:2]
    refs = refs[2:]
    (
        own, pair, first_a, first_b, second_a, second_b, hops, done, gms, parts, mine_in, pres,
        load, core_s, core_r, xa_s, xa_r, yb_s, yb_r, ya_s, ya_r, xb_s, xb_r, ring_s, ring_r,
        end_s, end_r, out_sem, mate_s, mate_r, cousin_s, cousin_r, small_sem,
    ) = refs
    at = Place(dp, fsdp)
    part_a, part_b = cut(width)
    cols_a, cols_b = pl.ds(*part_a), pl.ds(*part_b)
    rows = slice(None)
    sent = []

    def go(copy):
        copy.start()
        sent.append(copy)
        return copy

    at.greet()
    items = [(k, j) for k in range(weights) for j in range(ring)]
    loads, pairs = {}, {}
    other = 1 - 2 * at.c
    for k, j in items:
        back = (j + 1) % ring
        mine = at.shard(back)
        loads[k, j] = []
        for q in range(QUARTERS):
            copy = pltpu.make_async_copy(view(terms[k], (mine,), q, width), own.at[k, j, q], load.at[k, j, q])
            copy.start()
            loads[k, j].append(copy)
        pairs[k, j] = [
            go(remote(view(terms[k], (mine + other,), q, width), pair.at[k, j, q], core_s.at[k, j, q], core_r.at[k, j, q], at.core))
            for q in range(QUARTERS)
        ]
    flights, rings, ends = {}, {}, {}

    mates, cousins = at.mates(), at.cousins()
    swaps = [Swap(mates, mate_s.at[i], mate_r.at[i]) for i in range(3)]
    far = [Swap(cousins, cousin_s.at[i], cousin_r.at[i]) for i in range(2)]
    pad = pre_ref.shape[0]
    small = []

    def keep(src, dst):
        copy = pltpu.make_async_copy(src, dst, small_sem.at[len(small)])
        copy.start()
        small.append(copy)

    def cond_one():
        swaps[0].arrived()
        gms[at.f] = gm_ref[at.f]
        every = gms[...].reshape(fsdp * pad, gms.shape[2]).astype(jnp.bfloat16)
        parts[...] = times_back(every, ada_ref[...]).reshape(parts.shape)
        swaps[1].start(lambda device: parts.at[device[1]], mine_in.at[at.f])
        far[0].start(lambda device: gms, all_gm_ref.at[at.d])
        keep(gms, all_gm_ref.at[at.d])

    def cond_two():
        swaps[1].arrived()
        mine_in[at.f] = parts[at.f]
        grad_cond = jnp.sum(mine_in[...], axis=0) + routed_ref[...]
        pre_cond = pre_ref[...]
        sig = jax.nn.sigmoid(pre_cond)
        grad_pre = grad_cond * (sig * (1.0 + pre_cond * (1.0 - sig)))
        grad_pre = grad_pre.astype(jnp.bfloat16).astype(jnp.float32)
        pres[at.f, :, :width] = grad_pre + last_ref[:, :width]
        pres[at.f, :, width:] = last_ref[:, width:]
        swaps[2].start(lambda device: pres.at[at.f], pres.at[at.f])

    def cond_three():
        swaps[2].arrived()
        far[1].start(lambda device: pres, all_pre_ref.at[at.d])
        keep(pres, all_pre_ref.at[at.d])

    extra = {1: cond_one, 3: cond_two, 5: cond_three}
    swaps[0].start(lambda device: gm_ref.at[device[1]], gms.at[at.f])

    def stage_one(k, j):
        for q in range(QUARTERS):
            loads[k, j][q].wait()
            pairs[k, j][q].wait_recv()
            own[k, j, q] = own[k, j, q] + pair[k, j, q]
        flights[k, j] = [
            go(remote(own.at[k, j, at.qx, rows, cols_a], first_a.at[k, j, 0], xa_s.at[k, j, 0], xa_r.at[k, j, 0], at.x)),
            go(remote(own.at[k, j, at.qd, rows, cols_a], first_a.at[k, j, 1], xa_s.at[k, j, 1], xa_r.at[k, j, 1], at.x)),
            go(remote(own.at[k, j, at.qy, rows, cols_b], first_b.at[k, j, 0], yb_s.at[k, j, 0], yb_r.at[k, j, 0], at.y)),
            go(remote(own.at[k, j, at.qd, rows, cols_b], first_b.at[k, j, 1], yb_s.at[k, j, 1], yb_r.at[k, j, 1], at.y)),
        ]

    def stage_two(k, j):
        one, two, three, four = flights[k, j]
        two.wait_recv()
        own[k, j, at.qy, :, cols_a] = own[k, j, at.qy, :, cols_a] + first_a[k, j, 1]
        next_a = go(remote(own.at[k, j, at.qy, rows, cols_a], second_a.at[k, j], ya_s.at[k, j], ya_r.at[k, j], at.y))
        four.wait_recv()
        own[k, j, at.qx, :, cols_b] = own[k, j, at.qx, :, cols_b] + first_b[k, j, 1]
        next_b = go(remote(own.at[k, j, at.qx, rows, cols_b], second_b.at[k, j], xb_s.at[k, j], xb_r.at[k, j], at.x))
        one.wait_recv()
        own[k, j, at.q, :, cols_a] = own[k, j, at.q, :, cols_a] + first_a[k, j, 0]
        three.wait_recv()
        own[k, j, at.q, :, cols_b] = own[k, j, at.q, :, cols_b] + first_b[k, j, 0]
        flights[k, j] = [next_a, next_b]

    def stage_three(k, j):
        for copy in flights[k, j]:
            copy.wait_recv()
        own[k, j, at.q, :, cols_a] = own[k, j, at.q, :, cols_a] + second_a[k, j]
        own[k, j, at.q, :, cols_b] = own[k, j, at.q, :, cols_b] + second_b[k, j]
        if j > 0:
            rings[k, j - 1].wait_recv()
            own[k, j, at.q] = own[k, j, at.q] + hops[k, j - 1]
        if j < ring - 1:
            rings[k, j] = go(remote(own.at[k, j, at.q], hops.at[k, j], ring_s.at[k, j], ring_r.at[k, j], at.up))
            return
        done[k, at.q] = own[k, j, at.q]
        mine = done.at[k, at.q]
        ends[k] = [
            go(remote(mine, mine, end_s.at[k, 0], end_r.at[k, 0], at.x)),
            go(remote(mine, mine, end_s.at[k, 1], end_r.at[k, 1], at.y)),
        ]

    def stage_four(k):
        by_x, by_y = ends[k]
        by_x.wait_recv()
        half = done.at[k, at.qx, rows, cols_a]
        first = go(remote(half, half, end_s.at[k, 2], end_r.at[k, 2], at.y))
        by_y.wait_recv()
        half = done.at[k, at.qy, rows, cols_b]
        second = go(remote(half, half, end_s.at[k, 3], end_r.at[k, 3], at.x))
        ends[k] = [first, second]

    outgoing = []

    def stage_five(k):
        for copy in ends[k]:
            copy.wait_recv()
        copy = pltpu.make_async_copy(done.at[k], outs[k], out_sem.at[k])
        copy.start()
        outgoing.append(copy)

    for turn in range(len(items) + 4):
        if turn < len(items):
            stage_one(*items[turn])
        if 0 <= turn - 1 < len(items):
            stage_two(*items[turn - 1])
        if 0 <= turn - 2 < len(items):
            stage_three(*items[turn - 2])
        if 0 <= turn - 3 < len(items) and items[turn - 3][1] == ring - 1:
            stage_four(items[turn - 3][0])
        if 0 <= turn - 4 < len(items) and items[turn - 4][1] == ring - 1:
            stage_five(items[turn - 4][0])
        if turn in extra:
            extra[turn]()
    for swap in far:
        swap.arrived()
    for copy in outgoing + small:
        copy.wait()
    for swap in swaps + far:
        swap.left()
    for copy in sent:
        copy.wait_send()


def reduce_terms(terms, grad_modulation, ada_weight, routed, pre_cond, last, rows, width, dp, fsdp):
    ring = fsdp // 2
    dma = pltpu.SemaphoreType.DMA
    low = jnp.bfloat16
    (_, size_a), (_, size_b) = cut(width)
    vmem = pltpu.VMEM
    f32 = jnp.float32
    pad = pre_cond.shape[0]
    out = jax.ShapeDtypeStruct
    any_space, in_vmem = pl.BlockSpec(memory_space=pl.ANY), pl.BlockSpec(memory_space=vmem)
    scratch = [
        vmem((3, ring, QUARTERS, rows, width), low),
        vmem((3, ring, QUARTERS, rows, width), low),
        vmem((3, ring, 2, rows, size_a), low),
        vmem((3, ring, 2, rows, size_b), low),
        vmem((3, ring, rows, size_a), low),
        vmem((3, ring, rows, size_b), low),
        vmem((3, ring - 1, rows, width), low),
        vmem((3, QUARTERS, rows, width), low),
        vmem(grad_modulation.shape, f32),
        vmem((fsdp, pad, width), f32),
        vmem((fsdp, pad, width), f32),
        vmem((fsdp, *last.shape), f32),
    ]
    sems = (
        [dma((3, ring, QUARTERS))] * 3
        + [dma((3, ring, 2))] * 4
        + [dma((3, ring))] * 4
        + [dma((3, ring - 1))] * 2
        + [dma((3, 4))] * 2
        + [dma((3,))]
        + [dma((3, fsdp - 1))] * 2
        + [dma((2, dp - 1))] * 2
        + [dma((2,))]
    )
    return pl.pallas_call(
        partial(reduce_kernel, dp, fsdp, width),
        out_shape=[out((QUARTERS, rows, width), low)] * 3
        + [out((dp, *grad_modulation.shape), f32), out((dp, fsdp, *last.shape), f32)],
        in_specs=[any_space] * 3 + [in_vmem] * 5,
        out_specs=[any_space] * 5,
        scratch_shapes=scratch + sems,
        compiler_params=pltpu.CompilerParams(
            collective_id=1, has_side_effects=True, vmem_limit_bytes=60 * 2**20
        ),
        name="reduce",
    )(*terms, grad_modulation, ada_weight, routed, pre_cond, last)


def window(head, size):
    low = head * size // 128 * 128
    high = -(-(head + 1) * size // 128) * 128
    spot = low + lax.broadcasted_iota(jnp.int32, (1, high - low), 1)
    own = ((spot >= head * size) & (spot < (head + 1) * size)).astype(jnp.float32).astype(jnp.bfloat16)
    return low, high - low, own


def attend_image(joint, gates, mixed, lse, image, seq, heads):
    width = mixed.shape[1]
    size = width // heads
    scale = size ** (-0.5)
    lines = pl.ds(pl.multiple_of(image * seq, seq), seq)
    mixed[lines, :] = jnp.zeros((seq, width), mixed.dtype)
    for head in range(heads):
        low, wide, own = window(head, size)
        query = joint[lines, pl.ds(low, wide)] * own
        keys = joint[lines, pl.ds(width + low, wide)]
        values = joint[lines, pl.ds(2 * width + low, wide)] * own
        raw = times_back(keys, query) * scale
        peak = jnp.max(raw, axis=0, keepdims=True)
        expo = jnp.exp(raw - peak)
        total = jnp.sum(expo, axis=0, keepdims=True)
        lse[image, head : head + 1, :] = peak + jnp.log(total)
        probs = (expo * (1.0 / total)).astype(jnp.bfloat16)
        attended = times_rows(probs, values) * gates[image, 0, head]
        mixed[lines, pl.ds(low, wide)] = mixed[lines, pl.ds(low, wide)] + attended.astype(jnp.bfloat16)


def attend_back_image(joint, grad_mixed, gates, lse, grad_joint, grad_gates, image, seq, heads):
    width = grad_mixed.shape[1]
    size = width // heads
    scale = size ** (-0.5)
    lines = pl.ds(pl.multiple_of(image * seq, seq), seq)
    grad_joint[lines, :] = jnp.zeros((seq, 3 * width), grad_joint.dtype)

    def put(column, wide, value):
        here = pl.ds(column, wide)
        grad_joint[lines, here] = grad_joint[lines, here] + value.astype(jnp.bfloat16)

    for head in range(heads):
        low, wide, own = window(head, size)
        query = joint[lines, pl.ds(low, wide)] * own
        keys = joint[lines, pl.ds(width + low, wide)] * own
        values = joint[lines, pl.ds(2 * width + low, wide)]
        grad = grad_mixed[lines, pl.ds(low, wide)] * own
        gate = gates[image, 0, head]
        probs = jnp.exp(times_back(keys, query) * scale - lse[image, head : head + 1, :])
        put(2 * width + low, wide, matmul(probs.astype(jnp.bfloat16), (grad.astype(jnp.float32) * gate).astype(jnp.bfloat16)))
        grad_probs = times_back(values, grad)
        inner = jnp.sum(grad_probs * probs, axis=0, keepdims=True)
        grad_gates[image, head : head + 1, :] = inner
        grad_scores = (probs * (grad_probs - inner) * (gate * scale)).astype(jnp.bfloat16)
        put(low, wide, times_rows(grad_scores, keys))
        put(width + low, wide, matmul(grad_scores, query))


def attend(joint, gates, seq):
    images, heads = gates.shape
    def kernel(j, g, m, l):
        attend_image(j, g, m, l, 0, seq, heads)
    n = joint.shape[1]
    return pl.pallas_call(
        kernel, grid=(images,),
        out_shape=[jax.ShapeDtypeStruct((joint.shape[0], n // 3), jnp.bfloat16), jax.ShapeDtypeStruct((images, heads, seq), jnp.float32)],
        in_specs=[
            pl.BlockSpec((seq, n), lambda i: (i, 0)),
            pl.BlockSpec((1, 1, heads), lambda i: (i, 0, 0), memory_space=pltpu.SMEM),
        ],
        out_specs=[pl.BlockSpec((seq, n // 3), lambda i: (i, 0)), pl.BlockSpec((1, heads, seq), lambda i: (i, 0, 0))],
        compiler_params=pltpu.CompilerParams(vmem_limit_bytes=48*2**20),
        name="attend",
    )(joint, gates[:, None, :])
def attend_back(joint, grad_mixed, gates, lse, seq):
    images, heads = gates.shape
    n = joint.shape[1]
    def kernel(j, gm, g, l, gj, gg):
        attend_back_image(j, gm, g, l, gj, gg, 0, seq, heads)
    gj, gg = pl.pallas_call(
        kernel, grid=(images,),
        out_shape=[jax.ShapeDtypeStruct(joint.shape, jnp.bfloat16), jax.ShapeDtypeStruct((images, heads, seq), jnp.float32)],
        in_specs=[pl.BlockSpec((seq, n), lambda i: (i, 0)), pl.BlockSpec((seq, n//3), lambda i: (i, 0)), pl.BlockSpec((1, 1, heads), lambda i: (i, 0, 0), memory_space=pltpu.SMEM), pl.BlockSpec((1, heads, seq), lambda i: (i, 0, 0))],
        out_specs=[pl.BlockSpec((seq, n), lambda i: (i, 0)), pl.BlockSpec((1, heads, seq), lambda i: (i, 0, 0))],
        compiler_params=pltpu.CompilerParams(vmem_limit_bytes=48*2**20),
        name="attend_back",
    )(joint, grad_mixed, gates[:, None, :], lse)
    return gj, jnp.sum(gg, axis=-1)


def body(
    dp,
    fsdp,
    tokens,
    timesteps,
    labels,
    head_mask,
    keep_mask,
    cotangent,
    time_weight,
    class_table,
    ada_weight,
    head_router,
    qkv_weight,
    proj_weight,
    fc1_weight,
    fc2_weight,
    token_router,
):
    images, seq, width = tokens.shape
    heads = head_mask.shape[1]
    count = images * seq
    rows = qkv_weight.shape[0]
    hidden = fc1_weight.shape[1]
    entries = time_weight.shape[0] * fsdp
    me_fsdp = lax.axis_index("fsdp")
    pad = (images // 8 + 1) * 8

    def padded(array, value=0.0):
        return jnp.pad(array, ((0, pad - images), (0, 0)), constant_values=value)

    embedded = sinusoid(timesteps, entries).astype(jnp.bfloat16)
    asked = jnp.concatenate(
        [
            padded(embedded.astype(jnp.float32)),
            padded(jnp.broadcast_to(labels.astype(jnp.float32)[:, None], (images, 128)), -1.0),
        ],
        axis=1,
    )
    routers = jnp.pad(
        jnp.concatenate([head_router, token_router], axis=1), ((0, 0), (0, 127 - heads))
    )
    joint_full, fc1_full, fc2_full, pre_cond_pad, modulation, routers_full, all_cond, all_asked = gather_weights(
        [
            jnp.concatenate([qkv_weight, proj_weight], axis=1),
            fc1_weight,
            fc2_weight.reshape(QUARTERS, rows, width),
        ],
        asked,
        time_weight,
        class_table,
        ada_weight,
        routers,
        width,
        dp,
        fsdp,
    )
    joint_full = joint_full.reshape(width, 4 * width)
    triple, merger = joint_full[:, : 3 * width], joint_full[:, 3 * width :]
    expand = fc1_full.reshape(width, hidden)
    shrink = fc2_full.reshape(hidden, width)
    routers_full = routers_full.reshape(width, 128)
    chooser, picker = routers_full[:, :heads], routers_full[:, heads : heads + 1]
    everyone = dp * fsdp * pad
    all_cond = all_cond.reshape(everyone, width).astype(jnp.bfloat16)
    all_asked = all_asked.reshape(everyone, asked.shape[1])
    pre_cond = pre_cond_pad[:images]
    cond = jax.nn.silu(pre_cond).astype(jnp.bfloat16)
    modulation = modulation[:, :images].transpose(1, 0, 2).reshape(images, 6 * width)
    shift_one, scale_one, gate_one, shift_two, scale_two, gate_two = jnp.split(
        modulation[:, None, :], 6, axis=2
    )
    router_sig = jax.nn.sigmoid(matmul(cond, chooser))
    mask_float = head_mask.astype(jnp.float32)
    head_gates = mask_float * router_sig
    inputs = tokens.astype(jnp.float32)
    normed_one = layer_norm(inputs)
    flat_one = (
        (normed_one * (1.0 + scale_one) + shift_one).astype(jnp.bfloat16).reshape(count, width)
    )
    joint = matmul(flat_one, triple).astype(jnp.bfloat16)
    mixed, log_total = attend(joint, head_gates, seq)
    attn = matmul(mixed, merger).reshape(images, seq, width)
    middle = inputs + gate_one * attn
    normed_two = layer_norm(middle)
    flat_two = (
        (normed_two * (1.0 + scale_two) + shift_two).astype(jnp.bfloat16).reshape(count, width)
    )
    rate = jax.nn.sigmoid(matmul(flat_two, picker)).reshape(images, seq, 1)
    upward = matmul(flat_two, expand)
    active = jax.nn.gelu(upward, approximate=True).astype(jnp.bfloat16)
    downward = matmul(active, shrink).reshape(images, seq, width)
    kept = keep_mask.astype(jnp.float32)[:, :, None]
    kept_rate = kept * rate
    output = (middle + gate_two * kept_rate * downward).astype(jnp.bfloat16)
    grad_out = cotangent.astype(jnp.float32)
    grad_gate_two = jnp.sum(grad_out * kept_rate * downward, axis=1)
    grad_down = (grad_out * gate_two * kept_rate).astype(jnp.bfloat16).reshape(count, width)
    grad_rate = jnp.sum(grad_out * gate_two * downward, axis=-1, keepdims=True) * kept
    grad_logit = (grad_rate * rate * (1.0 - rate)).astype(jnp.bfloat16).reshape(count, 1)
    grad_shrink = times_rows(active, grad_down).astype(jnp.bfloat16)
    _, gelu_pull = jax.vjp(partial(jax.nn.gelu, approximate=True), upward)
    grad_up = gelu_pull(times_back(grad_down, shrink))[0].astype(jnp.bfloat16)
    grad_expand = times_rows(flat_two, grad_up).astype(jnp.bfloat16)
    grad_picker = times_rows(grad_logit, flat_two)
    grad_h_two = (times_back(grad_up, expand) + times_back(grad_logit, picker)).reshape(
        images, seq, width
    )
    grad_shift_two = jnp.sum(grad_h_two, axis=1)
    grad_scale_two = jnp.sum(grad_h_two * normed_two, axis=1)
    grad_middle = grad_out + norm_back(middle, grad_h_two * (1.0 + scale_two))
    grad_gate_one = jnp.sum(grad_middle * attn, axis=1)
    grad_attn = (grad_middle * gate_one).astype(jnp.bfloat16).reshape(count, width)
    grad_merger = times_rows(mixed, grad_attn).astype(jnp.bfloat16)
    grad_mixed = times_back(grad_attn, merger).astype(jnp.bfloat16)
    grad_joint, grad_gates = attend_back(joint, grad_mixed, head_gates, log_total, seq)
    grad_router = (grad_gates * mask_float * router_sig * (1.0 - router_sig)).astype(jnp.bfloat16)
    grad_triple = times_rows(flat_one, grad_joint).astype(jnp.bfloat16)
    grad_h_one = times_back(grad_joint, triple).reshape(images, seq, width)
    grad_shift_one = jnp.sum(grad_h_one, axis=1)
    grad_scale_one = jnp.sum(grad_h_one * normed_one, axis=1)
    grad_inputs = grad_middle + norm_back(inputs, grad_h_one * (1.0 + scale_one))
    grad_modulation = jnp.concatenate(
        [
            grad_shift_one,
            grad_scale_one,
            grad_gate_one,
            grad_shift_two,
            grad_scale_two,
            grad_gate_two,
        ],
        axis=1,
    ).astype(jnp.bfloat16)

    last = jnp.concatenate(
        [
            jnp.pad(grad_picker, ((pad - 1, 0), (0, 0))),
            padded(jnp.pad(grad_router.astype(jnp.float32), ((0, 0), (0, 128 - heads)))),
        ],
        axis=1,
    )
    *sums, all_grad, all_pre = reduce_terms(
        [
            jnp.concatenate([grad_triple, grad_merger], axis=1).reshape(fsdp, rows, 4 * width),
            grad_expand.reshape(fsdp, rows, hidden),
            grad_shrink.reshape(fsdp, QUARTERS, rows, width),
        ],
        padded(grad_modulation.astype(jnp.float32)).reshape(pad, fsdp, -1).transpose(1, 0, 2),
        ada_weight,
        padded(times_back(grad_router, chooser)),
        pre_cond_pad,
        last,
        rows,
        width,
        dp,
        fsdp,
    )
    if dp > QUARTERS:
        parts = list(sums)
        for hop in range(QUARTERS, dp, QUARTERS):
            pairs = [(i, (i + hop) % dp) for i in range(dp)]
            parts = [
                part.astype(jnp.float32) + lax.ppermute(s, "dp", pairs).astype(jnp.float32)
                for part, s in zip(parts, sums)
            ]
        sums = parts
    sums = [s.astype(jnp.float32) for s in sums]
    sum_triple = jnp.concatenate([sums[0][0], sums[0][1], sums[0][2]], axis=1)
    sum_merger = sums[0][3]
    sum_expand = jnp.concatenate([sums[1][i] for i in range(QUARTERS)], axis=1)
    sum_shrink = sums[2].reshape(QUARTERS * rows, width)

    sum_ada = times_rows(all_cond, all_grad.reshape(everyone, -1).astype(jnp.bfloat16))
    sum_picker = lax.dynamic_slice_in_dim(
        jnp.sum(all_pre[:, :, pad - 1, :width], axis=(0, 1)), me_fsdp * rows, rows, axis=0
    )[:, None]
    is_image = (jnp.arange(pad) < images)[None, None, :, None]
    all_pre = jnp.where(is_image, all_pre, 0.0).reshape(everyone, -1).astype(jnp.bfloat16)
    all_router = all_pre[:, width : width + heads]
    all_pre = all_pre[:, :width]
    own_entries = entries // fsdp
    all_embedded = lax.dynamic_slice_in_dim(
        all_asked[:, :entries], me_fsdp * own_entries, own_entries, axis=1
    ).astype(jnp.bfloat16)
    classes = jnp.arange(class_table.shape[0], dtype=jnp.float32)
    all_rows = (all_asked[:, entries : entries + 1] == classes[None, :]).astype(jnp.bfloat16)
    sum_time = times_rows(all_embedded, all_pre)
    sum_table = times_rows(
        all_rows, lax.dynamic_slice_in_dim(all_pre, me_fsdp * rows, rows, axis=1)
    )
    sum_chooser = times_rows(
        lax.dynamic_slice_in_dim(all_cond, me_fsdp * rows, rows, axis=1), all_router
    )
    return (
        output,
        grad_inputs,
        sum_time,
        sum_table,
        sum_ada,
        sum_chooser,
        sum_triple,
        sum_merger,
        sum_expand,
        sum_shrink,
        sum_picker,
    )


def solution(mesh):
    images = P(("dp", "fsdp"), None, None)
    pairs = P(("dp", "fsdp"), None)
    single = P(("dp", "fsdp"))
    by_row, by_column = P("fsdp", None), P(None, "fsdp")
    in_specs = (
        images, single, single, pairs, pairs, images,
        by_row, by_column, by_column, by_row, by_row, by_row, by_row, by_row, by_row,
    )
    out_specs = (
        images, images,
        by_row, by_column, by_column, by_row, by_row, by_row, by_row, by_row, by_row,
    )
    return jax.shard_map(
        partial(body, mesh.shape["dp"], mesh.shape["fsdp"]),
        mesh=mesh, in_specs=in_specs, out_specs=out_specs, check_vma=False,
    )
```

```python
from functools import partial
import math

import jax
import jax.numpy as jnp
from jax import lax
from jax.experimental import pallas as pl
from jax.experimental.pallas import tpu as pltpu
from jax.sharding import PartitionSpec as P

EPSILON = 1e-06
MESH = pl.DeviceIdType.MESH
QUARTERS = 4


def sinusoid(steps, entries):
    half = entries // 2
    freqs = jnp.exp(-math.log(10000.0) * jnp.arange(half, dtype=jnp.float32) / half)
    angles = steps.astype(jnp.float32)[:, None] * freqs[None, :]
    return jnp.concatenate([jnp.cos(angles), jnp.sin(angles)], axis=1)


def layer_norm(value):
    centered = value - jnp.mean(value, axis=-1, keepdims=True)
    return centered * lax.rsqrt(jnp.mean(centered * centered, axis=-1, keepdims=True) + EPSILON)


def norm_back(value, grad):
    _, pull = jax.vjp(layer_norm, value)
    return pull(grad)[0]


def matmul(left, right):
    return jnp.dot(left, right, preferred_element_type=jnp.float32)


def times_rows(left, right):
    return lax.dot_general(
        left, right, (((0,), (0,)), ((), ())), preferred_element_type=jnp.float32
    )


def times_back(left, right):
    return lax.dot_general(
        left, right, (((1,), (1,)), ((), ())), preferred_element_type=jnp.float32
    )


class Place:
    def __init__(self, dp, fsdp):
        ring = fsdp // 2
        self.dp, self.fsdp, self.ring = dp, fsdp, ring
        d = lax.axis_index("dp")
        f = lax.axis_index("fsdp")
        self.d, self.f = d, f
        self.z = f // 2
        self.c = f % 2
        self.q = d % QUARTERS
        dx = d + 1 - 2 * (d % 2)
        dy = d + 2 - 4 * ((d // 2) % 2)
        self.qx = dx % QUARTERS
        self.qy = dy % QUARTERS
        self.qd = (self.qx + self.qy - self.q + QUARTERS) % QUARTERS
        self.core = (d, f + 1 - 2 * (f % 2))
        self.x = (dx, f)
        self.y = (dy, f)
        self.up = (d, ((self.z + 1) % ring) * 2 + self.c)
        self.down = (d, ((self.z + ring - 1) % ring) * 2 + self.c)

    def shard(self, back):
        return ((self.z + self.ring - back) % self.ring) * 2 + self.c

    def mates(self):
        return [(self.d, (self.f + offset) % self.fsdp) for offset in range(1, self.fsdp)]

    def cousins(self):
        return [((self.d + offset) % self.dp, self.f) for offset in range(1, self.dp)]

    def greet(self):
        barrier = pltpu.get_barrier_semaphore()
        near = self.mates() + self.cousins()
        for other in near:
            pl.semaphore_signal(barrier, inc=1, device_id=other, device_id_type=MESH)
        pl.semaphore_wait(barrier, len(near))


def remote(src, dst, send, recv, device):
    return pltpu.make_async_remote_copy(
        src_ref=src, dst_ref=dst, send_sem=send, recv_sem=recv, device_id=device, device_id_type=MESH
    )


class Swap:
    def __init__(self, partners, send, recv):
        self.partners, self.send, self.recv = partners, send, recv
        self.copies = []

    def start(self, source, landing):
        for i, device in enumerate(self.partners):
            copy = remote(source(device), landing, self.send.at[i], self.recv.at[i], device)
            copy.start()
            self.copies.append(copy)

    def arrived(self):
        for copy in self.copies:
            copy.wait_recv()

    def left(self):
        for copy in self.copies:
            copy.wait_send()


def cut(width):
    first = ((width // 128 + 1) // 2) * 128
    return (0, first), (first, width - first)


def view(ref, lead, q, width, part=None):
    start, size = (0, width) if part is None else part
    flat = ref.shape[-1] != width
    if flat:
        column = pl.multiple_of(q * width + start, 128)
        return ref.at[(*lead, slice(None), pl.ds(column, size))]
    return ref.at[(*lead, q, slice(None), pl.ds(start, size))]


def gather_kernel(dp, fsdp, width, *refs):
    weights = 3
    ring = fsdp // 2
    shards, refs = refs[:weights], refs[weights:]
    ask_ref, time_ref, table_ref, ada_ref, router_ref = refs[:5]
    refs = refs[5:]
    fulls, refs = refs[:weights], refs[weights:]
    pre_ref, mod_ref, routers_ref, all_cond_ref, all_ask_ref = refs[:5]
    refs = refs[5:]
    asks, parts, mine_in, conds, columns = refs[:5]
    refs = refs[5:]
    (own_sem, core_s, core_r, ring_s, ring_r, x_s, x_r, y_s, y_r, a_s, a_r, b_s, b_r) = refs[:13]
    mate_s, mate_r, cousin_s, cousin_r, small_sem = refs[13:]
    at = Place(dp, fsdp)
    part_a, part_b = cut(width)
    at.greet()
    sent, landed = [], []
    mates, cousins = at.mates(), at.cousins()
    swaps = [Swap(mates, mate_s.at[i], mate_r.at[i]) for i in range(5)]
    far = [Swap(cousins, cousin_s.at[i], cousin_r.at[i]) for i in range(2)]
    pad = ask_ref.shape[0]
    group = fsdp * pad
    rows = table_ref.shape[1]

    def go(copy):
        copy.start()
        sent.append(copy)
        return copy

    def ring_copy(k, step):
        index = at.shard(step - 1)
        if step == 1:
            src = view(shards[k], (), at.q, width)
        else:
            src = view(fulls[k], (index,), at.q, width)
        return remote(src, view(fulls[k], (index,), at.q, width), ring_s.at[k, step - 1], ring_r.at[k, step - 1], at.up)

    small = []

    def keep(src, dst):
        copy = pltpu.make_async_copy(src, dst, small_sem.at[len(small)])
        copy.start()
        small.append(copy)

    def cond_one():
        swaps[0].arrived()
        asks[at.f] = ask_ref[...]
        every = asks[...].reshape(group, asks.shape[2])
        entries = every.shape[1] - 128
        own_rows = time_ref.shape[0]
        lanes = lax.broadcasted_iota(jnp.int32, (group, entries), 1)
        held = (lanes >= at.f * own_rows) & (lanes < (at.f + 1) * own_rows)
        embedded = jnp.where(held, every[:, :entries], 0.0).astype(jnp.bfloat16)
        stacked = jnp.concatenate([time_ref[...]] * fsdp, axis=0)
        label = every[:, entries : entries + 1].astype(jnp.int32)
        classes = table_ref.shape[0]
        picks = (label == lax.broadcasted_iota(jnp.int32, (group, classes), 1)).astype(jnp.float32)
        picked = matmul(picks.astype(jnp.bfloat16), table_ref[...]).astype(jnp.bfloat16)
        spot = lax.broadcasted_iota(jnp.int32, (rows, width), 1)
        line = lax.broadcasted_iota(jnp.int32, (rows, width), 0)
        place = (spot == line + at.f * rows).astype(jnp.float32).astype(jnp.bfloat16)
        partial_sum = matmul(embedded, stacked) + matmul(picked, place)
        parts[...] = partial_sum.reshape(fsdp, pad, width)
        swaps[1].start(lambda device: parts.at[device[1]], mine_in.at[at.f])
        far[1].start(lambda device: asks, all_ask_ref.at[at.d])
        keep(asks, all_ask_ref.at[at.d])

    def cond_two():
        swaps[1].arrived()
        mine_in[at.f] = parts[at.f]
        pre_cond = jnp.sum(mine_in[...], axis=0)
        pre_ref[...] = pre_cond
        conds[at.f] = (pre_cond * jax.nn.sigmoid(pre_cond)).astype(jnp.bfloat16).astype(jnp.float32)
        swaps[2].start(lambda device: conds.at[at.f], conds.at[at.f])

    def cond_three():
        swaps[2].arrived()
        every = conds[...].reshape(group, width).astype(jnp.bfloat16)
        columns[...] = matmul(every, ada_ref[...]).reshape(columns.shape)
        swaps[3].start(lambda device: columns.at[device[1]], mod_ref.at[at.f])
        far[0].start(lambda device: conds, all_cond_ref.at[at.d])
        keep(conds, all_cond_ref.at[at.d])
        keep(columns.at[at.f], mod_ref.at[at.f])

    extra = {0: cond_one, 1: cond_two, 2: cond_three}
    swaps[0].start(lambda device: ask_ref, asks.at[at.f])
    swaps[4].start(lambda device: router_ref, routers_ref.at[at.f])
    keep(router_ref, routers_ref.at[at.f])

    items = [(k, step) for k in range(weights) for step in range(1, ring)]
    rings = {items[0]: go(ring_copy(*items[0]))}
    locals_ = []
    for k in range(weights):
        copy = pltpu.make_async_copy(shards[k], fulls[k].at[at.f], own_sem.at[k])
        copy.start()
        locals_.append(copy)
        landed.append(go(remote(shards[k], fulls[k].at[at.f], core_s.at[k, 0], core_r.at[k, 0], at.core)))
    flights = {}
    for turn in range(len(items) + 2):
        if turn < len(items):
            k, step = items[turn]
            rings[k, step].wait_recv()
            if turn + 1 < len(items):
                rings[items[turn + 1]] = go(ring_copy(*items[turn + 1]))
            mine = view(fulls[k], (at.shard(step),), at.q, width)
            flights[turn] = (
                go(remote(mine, mine, x_s.at[k, step - 1], x_r.at[k, step - 1], at.x)),
                go(remote(mine, mine, y_s.at[k, step - 1], y_r.at[k, step - 1], at.y)),
            )
        if 0 <= turn - 1 < len(items):
            k, step = items[turn - 1]
            by_x, by_y = flights[turn - 1]
            by_x.wait_recv()
            half = view(fulls[k], (at.shard(step),), at.qx, width, part_a)
            first = go(remote(half, half, a_s.at[k, step - 1], a_r.at[k, step - 1], at.y))
            by_y.wait_recv()
            half = view(fulls[k], (at.shard(step),), at.qy, width, part_b)
            second = go(remote(half, half, b_s.at[k, step - 1], b_r.at[k, step - 1], at.x))
            flights[turn - 1] = (first, second)
        if 0 <= turn - 2 < len(items):
            k, step = items[turn - 2]
            for copy in flights[turn - 2]:
                copy.wait_recv()
            whole = fulls[k].at[at.shard(step)]
            landed.append(go(remote(whole, whole, core_s.at[k, step], core_r.at[k, step], at.core)))
        if turn in extra:
            extra[turn]()
    for swap in (swaps[3], swaps[4], far[0], far[1]):
        swap.arrived()
    for copy in landed:
        copy.wait_recv()
    for copy in locals_ + small:
        copy.wait()
    for swap in swaps + far:
        swap.left()
    for copy in sent:
        copy.wait_send()


def gather_weights(shards, asked, time_weight, class_table, ada_weight, routers, width, dp, fsdp):
    ring = fsdp // 2
    dma = pltpu.SemaphoreType.DMA
    vmem = pltpu.VMEM
    f32 = jnp.float32
    steps = dma((3, ring - 1))
    pad, asking = asked.shape
    columns = ada_weight.shape[1]
    out = jax.ShapeDtypeStruct
    any_space, in_vmem = pl.BlockSpec(memory_space=pl.ANY), pl.BlockSpec(memory_space=vmem)
    return pl.pallas_call(
        partial(gather_kernel, dp, fsdp, width),
        out_shape=[out((fsdp, *s.shape), s.dtype) for s in shards]
        + [
            out((pad, width), f32),
            out((fsdp, pad, columns), f32),
            out((fsdp, *routers.shape), routers.dtype),
            out((dp, fsdp, pad, width), f32),
            out((dp, fsdp, pad, asking), f32),
        ],
        in_specs=[any_space] * 3 + [in_vmem] * 5,
        out_specs=[any_space] * 3 + [in_vmem] + [any_space] * 4,
        scratch_shapes=[
            vmem((fsdp, pad, asking), f32),
            vmem((fsdp, pad, width), f32),
            vmem((fsdp, pad, width), f32),
            vmem((fsdp, pad, width), f32),
            vmem((fsdp, pad, columns), f32),
        ]
        + [dma((3,)), dma((3, ring)), dma((3, ring))]
        + [steps] * 10
        + [dma((5, fsdp - 1))] * 2
        + [dma((2, dp - 1))] * 2
        + [dma((4,))],
        compiler_params=pltpu.CompilerParams(
            collective_id=0, has_side_effects=True, vmem_limit_bytes=32 * 2**20
        ),
        name="gather",
    )(*shards, asked, time_weight, class_table, ada_weight, routers)


def window(head, size):
    low = head * size // 128 * 128
    high = -(-(head + 1) * size // 128) * 128
    spot = low + lax.broadcasted_iota(jnp.int32, (1, high - low), 1)
    own = ((spot >= head * size) & (spot < (head + 1) * size)).astype(jnp.float32).astype(jnp.bfloat16)
    return low, high - low, own


def attend_image(joint, gates, mixed, lse, image, seq, heads):
    width = mixed.shape[1]
    size = width // heads
    scale = size ** (-0.5)
    lines = pl.ds(pl.multiple_of(image * seq, seq), seq)
    mixed[lines, :] = jnp.zeros((seq, width), mixed.dtype)
    for head in range(heads):
        low, wide, own = window(head, size)
        query = joint[lines, pl.ds(low, wide)] * own
        keys = joint[lines, pl.ds(width + low, wide)]
        values = joint[lines, pl.ds(2 * width + low, wide)] * own
        raw = times_back(keys, query) * scale
        peak = jnp.max(raw, axis=0, keepdims=True)
        expo = jnp.exp(raw - peak)
        total = jnp.sum(expo, axis=0, keepdims=True)
        lse[image, head : head + 1, :] = peak + jnp.log(total)
        probs = (expo * (1.0 / total)).astype(jnp.bfloat16)
        attended = times_rows(probs, values) * gates[image, 0, head]
        mixed[lines, pl.ds(low, wide)] = mixed[lines, pl.ds(low, wide)] + attended.astype(jnp.bfloat16)


def attend_back_image(joint, grad_mixed, gates, lse, grad_joint, grad_gates, image, seq, heads, span):
    width = grad_mixed.shape[1]
    size = width // heads
    scale = size ** (-0.5)
    if span[0] == 0:
        grad_joint[...] = jnp.zeros((seq, 3 * width), grad_joint.dtype)

    def put(column, wide, value):
        here = pl.ds(column, wide)
        grad_joint[:, here] = grad_joint[:, here] + value.astype(jnp.bfloat16)

    for head in span:
        low, wide, own = window(head, size)
        query = joint[:, pl.ds(low, wide)] * own
        keys = joint[:, pl.ds(width + low, wide)] * own
        values = joint[:, pl.ds(2 * width + low, wide)]
        grad = grad_mixed[:, pl.ds(low, wide)] * own
        gate = gates[image, 0, head]
        probs = jnp.exp(times_back(keys, query) * scale - lse[image, head : head + 1, :])
        put(2 * width + low, wide, matmul(probs.astype(jnp.bfloat16), (grad.astype(jnp.float32) * gate).astype(jnp.bfloat16)))
        grad_probs = times_back(values, grad)
        inner = jnp.sum(grad_probs * probs, axis=0, keepdims=True)
        grad_gates[image, head : head + 1, :] = inner
        grad_scores = (probs * (grad_probs - inner) * (gate * scale)).astype(jnp.bfloat16)
        put(low, wide, times_rows(grad_scores, keys))
        put(width + low, wide, matmul(grad_scores, query))


def attend(joint, gates, seq):
    images, heads = gates.shape
    def kernel(j, g, m, l):
        attend_image(j, g, m, l, 0, seq, heads)
    n = joint.shape[1]
    return pl.pallas_call(
        kernel, grid=(images,),
        out_shape=[jax.ShapeDtypeStruct((joint.shape[0], n // 3), jnp.bfloat16), jax.ShapeDtypeStruct((images, heads, seq), jnp.float32)],
        in_specs=[
            pl.BlockSpec((seq, n), lambda i: (i, 0)),
            pl.BlockSpec((1, 1, heads), lambda i: (i, 0, 0), memory_space=pltpu.SMEM),
        ],
        out_specs=[pl.BlockSpec((seq, n // 3), lambda i: (i, 0)), pl.BlockSpec((1, heads, seq), lambda i: (i, 0, 0))],
        compiler_params=pltpu.CompilerParams(vmem_limit_bytes=48*2**20),
        name="attend",
    )(joint, gates[:, None, :])
def thirds(width):
    tiles = width // 128
    a, b = tiles // 3, tiles // 3
    c = tiles - a - b
    sizes = [a, b, (c + 1) // 2, c // 2]
    starts = [sum(sizes[:i]) for i in range(4)]
    return [(128 * s, 128 * n) for s, n in zip(starts, sizes)]


OWN_SLOTS = 5
PAIR_SLOTS = 3


class Reducer:
    def __init__(self, at, piece, outs, scratch, width):
        self.at, self.piece, self.outs, self.width = at, piece, outs, width
        (
            self.own, self.pair, self.first_a, self.first_b, self.second_a, self.second_b,
            self.hops, self.hops_c, self.flat_a, self.flat_b, self.last_a, self.last_b, self.done,
            self.own_in, self.core_s, self.core_r, self.fa_s, self.fa_r, self.fb_s, self.fb_r,
            self.sa_s, self.sa_r, self.sb_s, self.sb_r, self.hop_s, self.hop_r, self.hopc_s, self.hopc_r,
            self.ca_s, self.ca_r, self.cb_s, self.cb_r, self.end_s, self.end_r, self.out_sem, self.credit,
        ) = scratch
        self.ring = at.ring
        self.total = 3 * self.ring
        self.sent, self.flights = {}, {}
        self.loose, self.outgoing = [], []
        self.cols = [pl.ds(*part) for part in thirds(width)]
        a, b = thirds(width)[1]
        self.cols_ab = pl.ds(0, a + b)
        self.cols_c = pl.ds(a + b, width - a - b)

    @staticmethod
    def scratch(rows, width, fsdp):
        ring = fsdp // 2
        total = 3 * ring
        low, vmem, dma = jnp.bfloat16, pltpu.VMEM, pltpu.SemaphoreType.DMA
        a, b, c, d = [size for _, size in thirds(width)]
        arrays = [
            vmem((OWN_SLOTS, QUARTERS, rows, width), low),
            vmem((PAIR_SLOTS, QUARTERS, rows, width), low),
            vmem((total, 2, rows, a), low),
            vmem((total, 2, rows, b), low),
            vmem((total, rows, a), low),
            vmem((total, rows, b), low),
            vmem((3, ring - 1, rows, a + b), low),
            vmem((3, ring - 1, QUARTERS, rows, c + d), low),
            vmem((3, 2, rows, c), low),
            vmem((3, 2, rows, d), low),
            vmem((3, rows, c), low),
            vmem((3, rows, d), low),
            vmem((3, QUARTERS, rows, width), low),
        ]
        sems = (
            [dma((total, QUARTERS))] * 3
            + [dma((total, 2))] * 4
            + [dma((total,))] * 4
            + [dma((3, ring - 1))] * 4
            + [dma((3, 3))] * 4
            + [dma((3, 4))] * 2
            + [dma((3,))]
            + [pltpu.SemaphoreType.REGULAR]
        )
        return arrays + sems

    def go(self, n, *parts):
        copy = remote(*parts)
        copy.start()
        self.sent.setdefault(n, []).append(copy)
        return copy

    def prefetch(self, n):
        at = self.at
        k, j = divmod(n, self.ring)
        slot, pair_slot = n % OWN_SLOTS, n % PAIR_SLOTS
        for copy in self.sent.pop(n - OWN_SLOTS, []):
            copy.wait_send()
        mine = at.shard((j + 1) % self.ring)
        other = mine + 1 - 2 * at.c
        if n >= PAIR_SLOTS:
            pl.semaphore_wait(self.credit, 1)
        loads, pairs = [], []
        for q in range(QUARTERS):
            copy = pltpu.make_async_copy(self.piece(k, mine, q), self.own.at[slot, q], self.own_in.at[n, q])
            copy.start()
            loads.append(copy)
            copy = remote(self.piece(k, other, q), self.pair.at[pair_slot, q], self.core_s.at[n, q], self.core_r.at[n, q], at.core)
            copy.start()
            pairs.append(copy)
        self.loose += pairs
        self.flights[n] = (loads, pairs)

    def plane_first(self, n, slot, cols_a, cols_b, land_a, land_b, sems):
        at, own = self.at, self.own
        rows = slice(None)
        (sa, ra), (sb, rb) = sems
        return [
            self.go(n, own.at[slot, at.qd, rows, cols_a], land_a.at[1], sa.at[1], ra.at[1], at.x),
            self.go(n, own.at[slot, at.qd, rows, cols_b], land_b.at[1], sb.at[1], rb.at[1], at.y),
            self.go(n, own.at[slot, at.qx, rows, cols_a], land_a.at[0], sa.at[0], ra.at[0], at.x),
            self.go(n, own.at[slot, at.qy, rows, cols_b], land_b.at[0], sb.at[0], rb.at[0], at.y),
        ]

    def plane_second(self, n, slot, copies, cols_a, cols_b, land_a, land_b, next_a, next_b, sems):
        at, own = self.at, self.own
        rows = slice(None)
        one_d, two_d, one, two = copies
        (sa, ra), (sb, rb) = sems
        one_d.wait_recv()
        own[slot, at.qy, :, cols_a] = own[slot, at.qy, :, cols_a] + land_a[1]
        on_a = self.go(n, own.at[slot, at.qy, rows, cols_a], next_a, sa, ra, at.y)
        two_d.wait_recv()
        own[slot, at.qx, :, cols_b] = own[slot, at.qx, :, cols_b] + land_b[1]
        on_b = self.go(n, own.at[slot, at.qx, rows, cols_b], next_b, sb, rb, at.x)
        one.wait_recv()
        own[slot, at.q, :, cols_a] = own[slot, at.q, :, cols_a] + land_a[0]
        two.wait_recv()
        own[slot, at.q, :, cols_b] = own[slot, at.q, :, cols_b] + land_b[0]
        return [on_a, on_b]

    def plane_third(self, slot, copies, cols_a, cols_b, next_a, next_b):
        at, own = self.at, self.own
        for copy in copies:
            copy.wait_recv()
        own[slot, at.q, :, cols_a] = own[slot, at.q, :, cols_a] + next_a[...]
        own[slot, at.q, :, cols_b] = own[slot, at.q, :, cols_b] + next_b[...]

    def one(self, n):
        at, own, pair = self.at, self.own, self.pair
        k, j = divmod(n, self.ring)
        slot, pair_slot = n % OWN_SLOTS, n % PAIR_SLOTS
        loads, pairs = self.flights[n]
        for q in range(QUARTERS):
            loads[q].wait()
            pairs[q].wait_recv()

        @pl.loop(0, QUARTERS)
        def _(q):
            own[slot, q] = own[slot, q] + pair[pair_slot, q]

        if n + PAIR_SLOTS < self.total:
            pl.semaphore_signal(self.credit, inc=1, device_id=at.core, device_id_type=MESH)
        a, b, c, d = self.cols
        self.flights[n] = self.plane_first(
            n, slot, a, b, self.first_a.at[n], self.first_b.at[n],
            ((self.fa_s.at[n], self.fa_r.at[n]), (self.fb_s.at[n], self.fb_r.at[n])),
        )
        if j > 0:
            self.flights[k, "c"].wait_recv()

            @pl.loop(0, QUARTERS)
            def _(q):
                own[slot, q, :, self.cols_c] = own[slot, q, :, self.cols_c] + self.hops_c[k, j - 1, q]

        rows = slice(None)
        if j < self.ring - 1:
            self.flights[k, "c"] = self.go(
                n, own.at[slot, rows, rows, self.cols_c], self.hops_c.at[k, j], self.hopc_s.at[k, j], self.hopc_r.at[k, j], at.up
            )
        else:
            self.flights[k, "flat"] = self.plane_first(
                n, slot, c, d, self.flat_a.at[k], self.flat_b.at[k],
                ((self.ca_s.at[k], self.ca_r.at[k]), (self.cb_s.at[k], self.cb_r.at[k])),
            )

    def two(self, n):
        k, j = divmod(n, self.ring)
        slot = n % OWN_SLOTS
        a, b, c, d = self.cols
        self.flights[n] = self.plane_second(
            n, slot, self.flights[n], a, b, self.first_a.at[n], self.first_b.at[n], self.second_a.at[n], self.second_b.at[n],
            ((self.sa_s.at[n], self.sa_r.at[n]), (self.sb_s.at[n], self.sb_r.at[n])),
        )
        if j == self.ring - 1:
            self.flights[k, "flat"] = self.plane_second(
                n, slot, self.flights[k, "flat"], c, d, self.flat_a.at[k], self.flat_b.at[k], self.last_a.at[k], self.last_b.at[k],
                ((self.ca_s.at[k, 2], self.ca_r.at[k, 2]), (self.cb_s.at[k, 2], self.cb_r.at[k, 2])),
            )

    def three(self, n):
        at, own = self.at, self.own
        k, j = divmod(n, self.ring)
        slot = n % OWN_SLOTS
        a, b, c, d = self.cols
        rows = slice(None)
        self.plane_third(slot, self.flights[n], a, b, self.second_a.at[n], self.second_b.at[n])
        if j > 0:
            self.flights[k, "ab"].wait_recv()
            own[slot, at.q, :, self.cols_ab] = own[slot, at.q, :, self.cols_ab] + self.hops[k, j - 1]
        if j < self.ring - 1:
            self.flights[k, "ab"] = self.go(
                n, own.at[slot, at.q, rows, self.cols_ab], self.hops.at[k, j], self.hop_s.at[k, j], self.hop_r.at[k, j], at.up
            )
            return
        self.plane_third(slot, self.flights[k, "flat"], c, d, self.last_a.at[k], self.last_b.at[k])
        self.done[k, at.q] = own[slot, at.q]
        mine = self.done.at[k, at.q]
        self.flights[k, "end"] = [
            self.keep(remote(mine, mine, self.end_s.at[k, 0], self.end_r.at[k, 0], at.x)),
            self.keep(remote(mine, mine, self.end_s.at[k, 1], self.end_r.at[k, 1], at.y)),
        ]

    def keep(self, copy):
        copy.start()
        self.loose.append(copy)
        return copy

    def four(self, k):
        at, done = self.at, self.done
        (start_a, size_a), (start_b, size_b) = cut(self.width)
        rows = slice(None)
        by_x, by_y = self.flights[k, "end"]
        by_x.wait_recv()
        half = done.at[k, at.qx, rows, pl.ds(start_a, size_a)]
        first = self.keep(remote(half, half, self.end_s.at[k, 2], self.end_r.at[k, 2], at.y))
        by_y.wait_recv()
        half = done.at[k, at.qy, rows, pl.ds(start_b, size_b)]
        second = self.keep(remote(half, half, self.end_s.at[k, 3], self.end_r.at[k, 3], at.x))
        self.flights[k, "end"] = [first, second]

    def five(self, k):
        for copy in self.flights[k, "end"]:
            copy.wait_recv()
        copy = pltpu.make_async_copy(self.done.at[k], self.outs[k], self.out_sem.at[k])
        copy.start()
        self.outgoing.append(copy)

    def turn(self, t, first, last):
        items = last - first
        if t + 2 < items:
            self.prefetch(first + t + 2)
        if t < items:
            self.one(first + t)
        if 0 <= t - 1 < items:
            self.two(first + t - 1)
        if 0 <= t - 2 < items:
            self.three(first + t - 2)
        for lag, stage in ((3, self.four), (4, self.five)):
            n = first + t - lag
            if first <= n < last and n % self.ring == self.ring - 1:
                stage(n // self.ring)

    def finish(self):
        for copy in self.outgoing:
            copy.wait()
        for copies in self.sent.values():
            for copy in copies:
                copy.wait_send()
        for copy in self.loose:
            copy.wait_send()


def back_kernel(dp, fsdp, width, images, seq, heads, *refs):
    ring = fsdp // 2
    fc2_ref, fc1_ref, proj_ref, joint_ref, mixed_ref, h1_ref, tokens_ref, middle_ref, weight_ref = refs[:9]
    lse_ref, gates_ref, vectors_ref, scales_ref, factor_ref, routers_ref, ada_ref, pre_ref, picker_ref = refs[9:18]
    refs = refs[18:]
    outs, refs = refs[:3], refs[3:]
    all_gm_ref, all_pre_ref, grad_tokens_ref, triple_ref = refs[:4]
    refs = refs[4:]
    joint, mixed, h1, middle, grad_joint, stage, total, inner, gm_row, gms, parts, mine_in, pres = refs[:13]
    in_sem, out_sem, mate_s, mate_r, cousin_s, cousin_r = refs[13:19]
    at = Place(dp, fsdp)
    at.greet()
    rows = fc1_ref.shape[1]
    count = images * seq
    pad = pre_ref.shape[0]

    def piece(k, index, q):
        if k == 0:
            return fc2_ref.at[index, q]
        if k == 1:
            return fc1_ref.at[index, :, pl.ds(q * width, width)]
        line = pl.ds(pl.multiple_of(index * rows, 8), rows)
        if q == 3:
            return proj_ref.at[line, :]
        return triple_ref.at[q, line, :]

    work = Reducer(at, piece, outs, refs[19:], width)
    moves, fetched = {}, []

    def fetch(name, src, dst):
        copy = pltpu.make_async_copy(src, dst, in_sem.at[len(fetched)])
        copy.start()
        fetched.append(copy)
        moves.setdefault(name, []).append(copy)

    def have(name):
        for copy in moves.pop(name):
            copy.wait()

    def store(name, src, dst, i):
        copy = pltpu.make_async_copy(src, dst, out_sem.at[i])
        copy.start()
        moves[name] = [copy]

    work.prefetch(0)
    work.prefetch(1)

    def lines(image):
        return pl.ds(image * seq, seq)

    fetch("mixed", mixed_ref, mixed)
    fetch("joint0", joint_ref.at[lines(0)], joint.at[0])
    fetch("h1", h1_ref, h1)
    inner[...] = jnp.zeros_like(inner)
    gm_row[...] = jnp.zeros_like(gm_row)

    def attention(image, half):
        slot = image % 2
        if half == 0:
            if image == 0:
                have("mixed")
            have("joint" + str(image))
            if image + 1 < images:
                fetch("joint" + str(image + 1), joint_ref.at[lines(image + 1)], joint.at[1 - slot])
        span = range(0, heads // 2) if half == 0 else range(heads // 2, heads)
        attend_back_image(
            joint.at[slot], mixed.at[lines(image)], gates_ref, lse_ref, grad_joint.at[lines(image)], inner, image, seq, heads, span
        )

    def weigh(q):
        if q == 0:
            have("h1")
            fetch("tokens", tokens_ref, mixed)
        slot = q % 2
        if q >= 2:
            have("out" + str(q - 2))

        @pl.loop(0, width // 128)
        def _(m):
            line = pl.ds(pl.multiple_of(m * 128, 128), 128)
            stage[slot, line, :] = times_rows(h1[:, line], grad_joint[:, pl.ds(q * width, width)]).astype(jnp.bfloat16)

        store("out" + str(q), stage.at[slot], triple_ref.at[q], q)

    def bring_weight(q):
        for f in range(fsdp):
            fetch("w" + str(q), weight_ref.at[f, :, pl.ds(q * width, width)], stage.at[q % 2, pl.ds(f * rows, rows), :])

    def wait_terms():
        for q in (1, 2):
            have("out" + str(q))
        bring_weight(0)
        bring_weight(1)
        fetch("middle0", middle_ref.at[lines(0)], middle.at[0])

    def spread(q):
        slot = q % 2
        have("w" + str(q))

        @pl.loop(0, images)
        def _(image):
            line = pl.ds(pl.multiple_of(image * seq, seq), seq)
            value = times_back(grad_joint[line, pl.ds(q * width, width)], stage[slot])
            if q == 0:
                total[line, :] = value
            else:
                total[line, :] = total[line, :] + value

        if q == 0:
            bring_weight(2)

    def norm(image):
        slot = image % 2
        if image == 0:
            have("tokens")
        have("middle" + str(image))
        if image + 1 < images:
            if image >= 1:
                have("done" + str(image - 1))
            fetch("middle" + str(image + 1), middle_ref.at[lines(image + 1)], middle.at[1 - slot])
        scale = 1.0 + scales_ref[image : image + 1, :]
        step = 32

        def chunk(i, sums):
            shift, gain = sums
            line = pl.ds(pl.multiple_of(image * seq + i * step, step), step)
            here = pl.ds(pl.multiple_of(i * step, step), step)
            value = mixed[line, :].astype(jnp.float32)
            grad = total[line, :]
            centered = value - jnp.mean(value, axis=-1, keepdims=True)
            inverse = lax.rsqrt(jnp.mean(centered * centered, axis=-1, keepdims=True) + EPSILON)
            normed = centered * inverse
            through = grad * scale
            back = through - jnp.mean(through, axis=-1, keepdims=True)
            back = back - normed * jnp.mean(through * normed, axis=-1, keepdims=True)
            middle[slot, here, :] = middle[slot, here, :] + inverse * back
            return (
                shift + jnp.sum(grad, axis=0, keepdims=True),
                gain + jnp.sum(grad * normed, axis=0, keepdims=True),
            )

        zero = jnp.zeros((1, width), jnp.float32)
        shift, gain = lax.fori_loop(0, seq // step, chunk, (zero, zero))
        store("done" + str(image), middle.at[slot], grad_tokens_ref.at[lines(image)], 3 + image)
        gm_row[image : image + 1, :width] = shift
        gm_row[image : image + 1, width : 2 * width] = gain

    mates, cousins = at.mates(), at.cousins()
    swaps = [Swap(mates, mate_s.at[i], mate_r.at[i]) for i in range(3)]
    far = [Swap(cousins, cousin_s.at[i], cousin_r.at[i]) for i in range(2)]
    small = []

    def keep(src, dst):
        copy = pltpu.make_async_copy(src, dst, out_sem.at[3 + images + len(small)])
        copy.start()
        small.append(copy)

    held = gms.shape[3]

    def tail_zero():
        gm_row[:, 2 * width :] = vectors_ref[...]
        for f in range(fsdp):
            gms[0, f] = gm_row[:, f * held : (f + 1) * held].astype(jnp.bfloat16).astype(jnp.float32)
        swaps[0].start(lambda device: gms.at[0, device[1]], gms.at[1, at.f])

    def tail_one():
        swaps[0].arrived()
        gms[1, at.f] = gms[0, at.f]
        every = gms[1].reshape(fsdp * pad, held).astype(jnp.bfloat16)
        parts[...] = times_back(every, ada_ref[...]).reshape(parts.shape)
        swaps[1].start(lambda device: parts.at[device[1]], mine_in.at[at.f])
        far[0].start(lambda device: gms.at[1], all_gm_ref.at[at.d])
        keep(gms.at[1], all_gm_ref.at[at.d])

    def tail_two():
        line = lax.broadcasted_iota(jnp.int32, (pad, 128), 0)
        gated = jnp.zeros((pad, 128), jnp.float32)
        for image in range(images):
            summed = lax.dot_general(
                jnp.ones((pad, seq), jnp.float32), inner[image], (((1,), (1,)), ((), ())),
                preferred_element_type=jnp.float32, precision=lax.Precision.HIGHEST,
            )
            gated = jnp.where(line == image, summed, gated)
        router = (gated * factor_ref[...]).astype(jnp.bfloat16)
        swaps[1].arrived()
        mine_in[at.f] = parts[at.f]
        grad_cond = jnp.sum(mine_in[...], axis=0) + times_back(router, routers_ref[...])
        pre_cond = pre_ref[...]
        sig = jax.nn.sigmoid(pre_cond)
        grad_pre = grad_cond * (sig * (1.0 + pre_cond * (1.0 - sig)))
        grad_pre = grad_pre.astype(jnp.bfloat16).astype(jnp.float32)
        pres[at.f, :, :width] = grad_pre + picker_ref[...]
        pres[at.f, :, width:] = router.astype(jnp.float32)
        swaps[2].start(lambda device: pres.at[at.f], pres.at[at.f])

    def tail_three():
        swaps[2].arrived()
        far[1].start(lambda device: pres, all_pre_ref.at[at.d])
        keep(pres, all_pre_ref.at[at.d])

    early = [partial(attention, image, half) for image in range(images) for half in range(2)]
    early += [partial(weigh, q) for q in range(3)] + [wait_terms]
    late = [partial(spread, q) for q in range(3)] + [partial(norm, image) for image in range(images)]
    late += [tail_zero, tail_one, tail_two, tail_three]
    split = 2 * ring

    def plan(turns, steps, turn):
        done = 0
        for t in range(turns):
            turn(t)
            upto = -(-len(steps) * (t + 1) // turns)
            for step in steps[done:upto]:
                step()
            done = upto

    plan(split + 4, early, lambda t: work.turn(t, 0, split))
    work.prefetch(split)
    work.prefetch(split + 1)
    plan(ring + 4, late, lambda t: work.turn(t, split, split + ring))
    for swap in far:
        swap.arrived()
    for copy in small:
        copy.wait()
    for image in range(max(images - 2, 0), images):
        have("done" + str(image))
    for swap in swaps + far:
        swap.left()
    work.finish()


def back_half(
    terms, joint, grad_mixed, flat_one, tokens, grad_middle, joint_full, log_total, gates, vectors, scales, factor,
    routers, ada_weight, pre_cond, picker, width, images, seq, dp, fsdp,
):
    rows = terms[1].shape[1]
    heads = gates.shape[1]
    count = images * seq
    pad = pre_cond.shape[0]
    columns = ada_weight.shape[1]
    dma, vmem = pltpu.SemaphoreType.DMA, pltpu.VMEM
    low, f32 = jnp.bfloat16, jnp.float32
    out = jax.ShapeDtypeStruct
    any_space, in_vmem = pl.BlockSpec(memory_space=pl.ANY), pl.BlockSpec(memory_space=vmem)
    in_smem = pl.BlockSpec(memory_space=pltpu.SMEM)
    return pl.pallas_call(
        partial(back_kernel, dp, fsdp, width, images, seq, heads),
        out_shape=[out((QUARTERS, rows, width), low)] * 3
        + [
            out((dp, fsdp, pad, columns), f32),
            out((dp, fsdp, pad, width + 128), f32),
            out((count, width), f32),
            out((3, width, width), low),
        ],
        in_specs=[any_space] * 9 + [in_vmem, in_smem] + [in_vmem] * 7,
        out_specs=[any_space] * 7,
        scratch_shapes=[
            vmem((2, seq, 3 * width), low),
            vmem((count, width), low),
            vmem((count, width), low),
            vmem((2, seq, width), f32),
            vmem((count, 3 * width), low),
            vmem((2, width, width), low),
            vmem((count, width), f32),
            vmem((images, 128, seq), f32),
            vmem((pad, 6 * width), f32),
            vmem((2, fsdp, pad, columns), f32),
            vmem((fsdp, pad, width), f32),
            vmem((fsdp, pad, width), f32),
            vmem((fsdp, pad, width + 128), f32),
            dma((3 * fsdp + 3 + 2 * images,)),
            dma((5 + images,)),
            dma((3, fsdp - 1)),
            dma((3, fsdp - 1)),
            dma((2, dp - 1)),
            dma((2, dp - 1)),
        ]
        + Reducer.scratch(rows, width, fsdp),
        compiler_params=pltpu.CompilerParams(
            collective_id=1, has_side_effects=True, vmem_limit_bytes=60 * 2**20
        ),
        name="back",
    )(
        *terms, joint, grad_mixed, flat_one, tokens, grad_middle, joint_full, log_total, gates[:, None, :], vectors, scales,
        factor, routers, ada_weight, pre_cond, picker,
    )


def body(
    dp,
    fsdp,
    tokens,
    timesteps,
    labels,
    head_mask,
    keep_mask,
    cotangent,
    time_weight,
    class_table,
    ada_weight,
    head_router,
    qkv_weight,
    proj_weight,
    fc1_weight,
    fc2_weight,
    token_router,
):
    images, seq, width = tokens.shape
    heads = head_mask.shape[1]
    count = images * seq
    rows = qkv_weight.shape[0]
    hidden = fc1_weight.shape[1]
    entries = time_weight.shape[0] * fsdp
    me_fsdp = lax.axis_index("fsdp")
    pad = (images // 8 + 1) * 8

    def padded(array, value=0.0):
        return jnp.pad(array, ((0, pad - images), (0, 0)), constant_values=value)

    embedded = sinusoid(timesteps, entries).astype(jnp.bfloat16)
    asked = jnp.concatenate(
        [
            padded(embedded.astype(jnp.float32)),
            padded(jnp.broadcast_to(labels.astype(jnp.float32)[:, None], (images, 128)), -1.0),
        ],
        axis=1,
    )
    routers = jnp.pad(
        jnp.concatenate([head_router, token_router], axis=1), ((0, 0), (0, 127 - heads))
    )
    joint_blocks, fc1_full, fc2_full, pre_cond_pad, modulation, routers_full, all_cond, all_asked = gather_weights(
        [
            jnp.concatenate([qkv_weight, proj_weight], axis=1),
            fc1_weight,
            fc2_weight.reshape(QUARTERS, rows, width),
        ],
        asked,
        time_weight,
        class_table,
        ada_weight,
        routers,
        width,
        dp,
        fsdp,
    )
    joint_full = joint_blocks.reshape(width, 4 * width)
    triple, merger = joint_full[:, : 3 * width], joint_full[:, 3 * width :]
    expand = fc1_full.reshape(width, hidden)
    shrink = fc2_full.reshape(hidden, width)
    routers_full = routers_full.reshape(width, 128)
    chooser, picker = routers_full[:, :heads], routers_full[:, heads : heads + 1]
    everyone = dp * fsdp * pad
    all_cond = all_cond.reshape(everyone, width).astype(jnp.bfloat16)
    all_asked = all_asked.reshape(everyone, asked.shape[1])
    pre_cond = pre_cond_pad[:images]
    cond = jax.nn.silu(pre_cond).astype(jnp.bfloat16)
    modulation = modulation[:, :images].transpose(1, 0, 2).reshape(images, 6 * width)
    shift_one, scale_one, gate_one, shift_two, scale_two, gate_two = jnp.split(
        modulation[:, None, :], 6, axis=2
    )
    router_sig = jax.nn.sigmoid(matmul(cond, chooser))
    mask_float = head_mask.astype(jnp.float32)
    head_gates = mask_float * router_sig
    inputs = tokens.astype(jnp.float32)
    normed_one = layer_norm(inputs)
    flat_one = (
        (normed_one * (1.0 + scale_one) + shift_one).astype(jnp.bfloat16).reshape(count, width)
    )
    joint = matmul(flat_one, triple).astype(jnp.bfloat16)
    mixed, log_total = attend(joint, head_gates, seq)
    attn = matmul(mixed, merger).reshape(images, seq, width)
    middle = inputs + gate_one * attn
    normed_two = layer_norm(middle)
    flat_two = (
        (normed_two * (1.0 + scale_two) + shift_two).astype(jnp.bfloat16).reshape(count, width)
    )
    rate = jax.nn.sigmoid(matmul(flat_two, picker)).reshape(images, seq, 1)
    upward = matmul(flat_two, expand)
    active = jax.nn.gelu(upward, approximate=True).astype(jnp.bfloat16)
    downward = matmul(active, shrink).reshape(images, seq, width)
    kept = keep_mask.astype(jnp.float32)[:, :, None]
    kept_rate = kept * rate
    output = (middle + gate_two * kept_rate * downward).astype(jnp.bfloat16)
    grad_out = cotangent.astype(jnp.float32)
    grad_gate_two = jnp.sum(grad_out * kept_rate * downward, axis=1)
    grad_down = (grad_out * gate_two * kept_rate).astype(jnp.bfloat16).reshape(count, width)
    grad_rate = jnp.sum(grad_out * gate_two * downward, axis=-1, keepdims=True) * kept
    grad_logit = (grad_rate * rate * (1.0 - rate)).astype(jnp.bfloat16).reshape(count, 1)
    grad_shrink = times_rows(active, grad_down).astype(jnp.bfloat16)
    _, gelu_pull = jax.vjp(partial(jax.nn.gelu, approximate=True), upward)
    grad_up = gelu_pull(times_back(grad_down, shrink))[0].astype(jnp.bfloat16)
    grad_expand = times_rows(flat_two, grad_up).astype(jnp.bfloat16)
    grad_picker = times_rows(grad_logit, flat_two)
    grad_h_two = (times_back(grad_up, expand) + times_back(grad_logit, picker)).reshape(
        images, seq, width
    )
    grad_shift_two = jnp.sum(grad_h_two, axis=1)
    grad_scale_two = jnp.sum(grad_h_two * normed_two, axis=1)
    grad_middle = grad_out + norm_back(middle, grad_h_two * (1.0 + scale_two))
    grad_gate_one = jnp.sum(grad_middle * attn, axis=1)
    grad_attn = (grad_middle * gate_one).astype(jnp.bfloat16).reshape(count, width)
    grad_merger = times_rows(mixed, grad_attn).astype(jnp.bfloat16)
    grad_mixed = times_back(grad_attn, merger).astype(jnp.bfloat16)
    vectors = jnp.concatenate([grad_gate_one, grad_shift_two, grad_scale_two, grad_gate_two], axis=1)
    *sums, all_grad, all_pre, grad_inputs, _ = back_half(
        [
            grad_shrink.reshape(fsdp, QUARTERS, rows, width),
            grad_expand.reshape(fsdp, rows, hidden),
            grad_merger,
        ],
        joint,
        grad_mixed,
        flat_one,
        tokens.reshape(count, width),
        grad_middle.reshape(count, width),
        joint_blocks,
        log_total,
        head_gates,
        padded(vectors),
        padded(scale_one[:, 0]),
        padded(jnp.pad(mask_float * router_sig * (1.0 - router_sig), ((0, 0), (0, 128 - heads)))),
        routers_full,
        ada_weight,
        pre_cond_pad,
        jnp.pad(grad_picker, ((pad - 1, 0), (0, 0))),
        width,
        images,
        seq,
        dp,
        fsdp,
    )
    grad_inputs = grad_inputs.reshape(images, seq, width)
    if dp > QUARTERS:
        parts = list(sums)
        for hop in range(QUARTERS, dp, QUARTERS):
            pairs = [(i, (i + hop) % dp) for i in range(dp)]
            parts = [
                part.astype(jnp.float32) + lax.ppermute(s, "dp", pairs).astype(jnp.float32)
                for part, s in zip(parts, sums)
            ]
        sums = parts
    sums = [s.astype(jnp.float32) for s in sums]
    sum_triple = jnp.concatenate([sums[2][0], sums[2][1], sums[2][2]], axis=1)
    sum_merger = sums[2][3]
    sum_expand = jnp.concatenate([sums[1][i] for i in range(QUARTERS)], axis=1)
    sum_shrink = sums[0].reshape(QUARTERS * rows, width)

    sum_ada = times_rows(all_cond, all_grad.reshape(everyone, -1).astype(jnp.bfloat16))
    sum_picker = lax.dynamic_slice_in_dim(
        jnp.sum(all_pre[:, :, pad - 1, :width], axis=(0, 1)), me_fsdp * rows, rows, axis=0
    )[:, None]
    is_image = (jnp.arange(pad) < images)[None, None, :, None]
    all_pre = jnp.where(is_image, all_pre, 0.0).reshape(everyone, -1).astype(jnp.bfloat16)
    all_router = all_pre[:, width : width + heads]
    all_pre = all_pre[:, :width]
    own_entries = entries // fsdp
    all_embedded = lax.dynamic_slice_in_dim(
        all_asked[:, :entries], me_fsdp * own_entries, own_entries, axis=1
    ).astype(jnp.bfloat16)
    classes = jnp.arange(class_table.shape[0], dtype=jnp.float32)
    all_rows = (all_asked[:, entries : entries + 1] == classes[None, :]).astype(jnp.bfloat16)
    sum_time = times_rows(all_embedded, all_pre)
    sum_table = times_rows(
        all_rows, lax.dynamic_slice_in_dim(all_pre, me_fsdp * rows, rows, axis=1)
    )
    sum_chooser = times_rows(
        lax.dynamic_slice_in_dim(all_cond, me_fsdp * rows, rows, axis=1), all_router
    )
    return (
        output,
        grad_inputs,
        sum_time,
        sum_table,
        sum_ada,
        sum_chooser,
        sum_triple,
        sum_merger,
        sum_expand,
        sum_shrink,
        sum_picker,
    )


def solution(mesh):
    images = P(("dp", "fsdp"), None, None)
    pairs = P(("dp", "fsdp"), None)
    single = P(("dp", "fsdp"))
    by_row, by_column = P("fsdp", None), P(None, "fsdp")
    in_specs = (
        images, single, single, pairs, pairs, images,
        by_row, by_column, by_column, by_row, by_row, by_row, by_row, by_row, by_row,
    )
    out_specs = (
        images, images,
        by_row, by_column, by_column, by_row, by_row, by_row, by_row, by_row, by_row,
    )
    return jax.shard_map(
        partial(body, mesh.shape["dp"], mesh.shape["fsdp"]),
        mesh=mesh, in_specs=in_specs, out_specs=out_specs, check_vma=False,
    )
```

```python
from functools import partial
import math

import jax
import jax.numpy as jnp
from jax import lax
from jax.experimental import pallas as pl
from jax.experimental.pallas import tpu as pltpu
from jax.sharding import PartitionSpec as P

EPSILON = 1e-06
MESH = pl.DeviceIdType.MESH
QUARTERS = 4
DIGIT = 256


def sinusoid(steps, entries):
    half = entries // 2
    freqs = jnp.exp(-math.log(10000.0) * jnp.arange(half, dtype=jnp.float32) / half)
    angles = steps.astype(jnp.float32)[:, None] * freqs[None, :]
    return jnp.concatenate([jnp.cos(angles), jnp.sin(angles)], axis=1)


def layer_norm(value):
    centered = value - jnp.mean(value, axis=-1, keepdims=True)
    return centered * lax.rsqrt(jnp.mean(centered * centered, axis=-1, keepdims=True) + EPSILON)


def norm_back(value, grad):
    _, pull = jax.vjp(layer_norm, value)
    return pull(grad)[0]


def matmul(left, right):
    return jnp.dot(left, right, preferred_element_type=jnp.float32)


def times_rows(left, right):
    return lax.dot_general(
        left, right, (((0,), (0,)), ((), ())), preferred_element_type=jnp.float32
    )


def times_back(left, right):
    return lax.dot_general(
        left, right, (((1,), (1,)), ((), ())), preferred_element_type=jnp.float32
    )


class Place:
    def __init__(self, dp, fsdp):
        ring = fsdp // 2
        self.dp, self.fsdp, self.ring = dp, fsdp, ring
        d = lax.axis_index("dp")
        f = lax.axis_index("fsdp")
        self.d, self.f = d, f
        self.z = f // 2
        self.c = f % 2
        self.q = d % QUARTERS
        dx = d + 1 - 2 * (d % 2)
        dy = d + 2 - 4 * ((d // 2) % 2)
        self.qx = dx % QUARTERS
        self.qy = dy % QUARTERS
        self.qd = (self.qx + self.qy - self.q + QUARTERS) % QUARTERS
        self.core = (d, f + 1 - 2 * (f % 2))
        self.x = (dx, f)
        self.y = (dy, f)
        self.up = (d, ((self.z + 1) % ring) * 2 + self.c)
        self.down = (d, ((self.z + ring - 1) % ring) * 2 + self.c)

    def shard(self, back):
        return ((self.z + self.ring - back) % self.ring) * 2 + self.c

    def mates(self):
        return [(self.d, (self.f + offset) % self.fsdp) for offset in range(1, self.fsdp)]

    def cousins(self):
        return [((self.d + offset) % self.dp, self.f) for offset in range(1, self.dp)]

    def greet(self):
        barrier = pltpu.get_barrier_semaphore()
        near = self.mates() + self.cousins()
        for other in near:
            pl.semaphore_signal(barrier, inc=1, device_id=other, device_id_type=MESH)
        pl.semaphore_wait(barrier, len(near))


def remote(src, dst, send, recv, device):
    return pltpu.make_async_remote_copy(
        src_ref=src, dst_ref=dst, send_sem=send, recv_sem=recv, device_id=device, device_id_type=MESH
    )


class Swap:
    def __init__(self, partners, send, recv):
        self.partners, self.send, self.recv = partners, send, recv
        self.copies = []

    def start(self, source, landing):
        for i, device in enumerate(self.partners):
            copy = remote(source(device), landing, self.send.at[i], self.recv.at[i], device)
            copy.start()
            self.copies.append(copy)

    def arrived(self):
        for copy in self.copies:
            copy.wait_recv()

    def left(self):
        for copy in self.copies:
            copy.wait_send()


def cut(width):
    first = ((width // 128 + 1) // 2) * 128
    return (0, first), (first, width - first)


def view(ref, lead, q, width, part=None):
    start, size = (0, width) if part is None else part
    flat = ref.shape[-1] != width
    if flat:
        column = pl.multiple_of(q * width + start, 128)
        return ref.at[(*lead, slice(None), pl.ds(column, size))]
    return ref.at[(*lead, q, slice(None), pl.ds(start, size))]


def gather_kernel(dp, fsdp, width, *refs):
    weights = 3
    ring = fsdp // 2
    shards, refs = refs[:weights], refs[weights:]
    ask_ref, time_ref, table_ref, ada_ref, router_ref = refs[:5]
    refs = refs[5:]
    fulls, refs = refs[:weights], refs[weights:]
    pre_ref, mod_ref, routers_ref, all_cond_ref, all_ask_ref = refs[:5]
    refs = refs[5:]
    asks, parts, mine_in, conds, columns = refs[:5]
    refs = refs[5:]
    (own_sem, core_s, core_r, ring_s, ring_r, x_s, x_r, y_s, y_r, a_s, a_r, b_s, b_r) = refs[:13]
    mate_s, mate_r, cousin_s, cousin_r, small_sem = refs[13:]
    at = Place(dp, fsdp)
    part_a, part_b = cut(width)
    at.greet()
    sent, landed = [], []
    mates, cousins = at.mates(), at.cousins()
    swaps = [Swap(mates, mate_s.at[i], mate_r.at[i]) for i in range(5)]
    far = [Swap(cousins, cousin_s.at[i], cousin_r.at[i]) for i in range(2)]
    pad = ask_ref.shape[0]
    group = fsdp * pad
    rows = table_ref.shape[1]

    def go(copy):
        copy.start()
        sent.append(copy)
        return copy

    def ring_copy(k, step):
        index = at.shard(step - 1)
        if step == 1:
            src = view(shards[k], (), at.q, width)
        else:
            src = view(fulls[k], (index,), at.q, width)
        return remote(src, view(fulls[k], (index,), at.q, width), ring_s.at[k, step - 1], ring_r.at[k, step - 1], at.up)

    small = []

    def keep(src, dst):
        copy = pltpu.make_async_copy(src, dst, small_sem.at[len(small)])
        copy.start()
        small.append(copy)

    def cond_one():
        swaps[0].arrived()
        asks[at.f] = ask_ref[...]
        every = asks[...].astype(jnp.float32).reshape(group, asks.shape[2])
        entries = every.shape[1] - 128
        own_rows = time_ref.shape[0]
        lanes = lax.broadcasted_iota(jnp.int32, (group, entries), 1)
        held = (lanes >= at.f * own_rows) & (lanes < (at.f + 1) * own_rows)
        embedded = jnp.where(held, every[:, :entries], 0.0).astype(jnp.bfloat16)
        stacked = jnp.concatenate([time_ref[...]] * fsdp, axis=0)
        label = (every[:, entries : entries + 1] * DIGIT + every[:, entries + 1 : entries + 2]).astype(jnp.int32)
        classes = table_ref.shape[0]
        picks = (label == lax.broadcasted_iota(jnp.int32, (group, classes), 1)).astype(jnp.float32)
        picked = matmul(picks.astype(jnp.bfloat16), table_ref[...]).astype(jnp.bfloat16)
        spot = lax.broadcasted_iota(jnp.int32, (rows, width), 1)
        line = lax.broadcasted_iota(jnp.int32, (rows, width), 0)
        place = (spot == line + at.f * rows).astype(jnp.float32).astype(jnp.bfloat16)
        partial_sum = matmul(embedded, stacked) + matmul(picked, place)
        parts[...] = partial_sum.reshape(fsdp, pad, width)
        swaps[1].start(lambda device: parts.at[device[1]], mine_in.at[at.f])
        far[1].start(lambda device: asks, all_ask_ref.at[at.d])
        keep(asks, all_ask_ref.at[at.d])

    def cond_two():
        swaps[1].arrived()
        mine_in[at.f] = parts[at.f]
        pre_cond = jnp.sum(mine_in[...], axis=0)
        pre_ref[...] = pre_cond
        conds[at.f] = (pre_cond * jax.nn.sigmoid(pre_cond)).astype(jnp.bfloat16)
        swaps[2].start(lambda device: conds.at[at.f], conds.at[at.f])

    def cond_three():
        swaps[2].arrived()
        every = conds[...].astype(jnp.float32).reshape(group, width).astype(jnp.bfloat16)
        columns[...] = matmul(every, ada_ref[...]).reshape(columns.shape)
        swaps[3].start(lambda device: columns.at[device[1]], mod_ref.at[at.f])
        far[0].start(lambda device: conds, all_cond_ref.at[at.d])
        keep(conds, all_cond_ref.at[at.d])
        keep(columns.at[at.f], mod_ref.at[at.f])

    extra = {0: cond_one, 1: cond_two, 2: cond_three}
    swaps[0].start(lambda device: ask_ref, asks.at[at.f])
    swaps[4].start(lambda device: router_ref, routers_ref.at[at.f])
    keep(router_ref, routers_ref.at[at.f])

    items = [(k, step) for k in range(weights) for step in range(1, ring)]
    rings = {items[0]: go(ring_copy(*items[0]))}
    locals_ = []
    for k in range(weights):
        copy = pltpu.make_async_copy(shards[k], fulls[k].at[at.f], own_sem.at[k])
        copy.start()
        locals_.append(copy)
        landed.append(go(remote(shards[k], fulls[k].at[at.f], core_s.at[k, 0], core_r.at[k, 0], at.core)))
    flights = {}
    for turn in range(len(items) + 2):
        if turn < len(items):
            k, step = items[turn]
            rings[k, step].wait_recv()
            if turn + 1 < len(items):
                rings[items[turn + 1]] = go(ring_copy(*items[turn + 1]))
            mine = view(fulls[k], (at.shard(step),), at.q, width)
            flights[turn] = (
                go(remote(mine, mine, x_s.at[k, step - 1], x_r.at[k, step - 1], at.x)),
                go(remote(mine, mine, y_s.at[k, step - 1], y_r.at[k, step - 1], at.y)),
            )
        if 0 <= turn - 1 < len(items):
            k, step = items[turn - 1]
            by_x, by_y = flights[turn - 1]
            by_x.wait_recv()
            half = view(fulls[k], (at.shard(step),), at.qx, width, part_a)
            first = go(remote(half, half, a_s.at[k, step - 1], a_r.at[k, step - 1], at.y))
            by_y.wait_recv()
            half = view(fulls[k], (at.shard(step),), at.qy, width, part_b)
            second = go(remote(half, half, b_s.at[k, step - 1], b_r.at[k, step - 1], at.x))
            flights[turn - 1] = (first, second)
        if 0 <= turn - 2 < len(items):
            k, step = items[turn - 2]
            for copy in flights[turn - 2]:
                copy.wait_recv()
            whole = fulls[k].at[at.shard(step)]
            landed.append(go(remote(whole, whole, core_s.at[k, step], core_r.at[k, step], at.core)))
        if turn in extra:
            extra[turn]()
    for swap in (swaps[3], swaps[4], far[0], far[1]):
        swap.arrived()
    for copy in landed:
        copy.wait_recv()
    for copy in locals_ + small:
        copy.wait()
    for swap in swaps + far:
        swap.left()
    for copy in sent:
        copy.wait_send()


def gather_weights(shards, asked, time_weight, class_table, ada_weight, routers, width, dp, fsdp):
    ring = fsdp // 2
    dma = pltpu.SemaphoreType.DMA
    vmem = pltpu.VMEM
    f32 = jnp.float32
    steps = dma((3, ring - 1))
    pad, asking = asked.shape
    columns = ada_weight.shape[1]
    out = jax.ShapeDtypeStruct
    any_space, in_vmem = pl.BlockSpec(memory_space=pl.ANY), pl.BlockSpec(memory_space=vmem)
    return pl.pallas_call(
        partial(gather_kernel, dp, fsdp, width),
        out_shape=[out((fsdp, *s.shape), s.dtype) for s in shards]
        + [
            out((pad, width), f32),
            out((fsdp, pad, columns), f32),
            out((fsdp, *routers.shape), routers.dtype),
            out((dp, fsdp, pad, width), jnp.bfloat16),
            out((dp, fsdp, pad, asking), jnp.bfloat16),
        ],
        in_specs=[any_space] * 3 + [in_vmem] * 5,
        out_specs=[any_space] * 3 + [in_vmem] + [any_space] * 4,
        scratch_shapes=[
            vmem((fsdp, pad, asking), jnp.bfloat16),
            vmem((fsdp, pad, width), f32),
            vmem((fsdp, pad, width), f32),
            vmem((fsdp, pad, width), jnp.bfloat16),
            vmem((fsdp, pad, columns), f32),
        ]
        + [dma((3,)), dma((3, ring)), dma((3, ring))]
        + [steps] * 10
        + [dma((5, fsdp - 1))] * 2
        + [dma((2, dp - 1))] * 2
        + [dma((4,))],
        compiler_params=pltpu.CompilerParams(
            collective_id=0, has_side_effects=True, vmem_limit_bytes=32 * 2**20
        ),
        name="gather",
    )(*shards, asked, time_weight, class_table, ada_weight, routers)


def window(head, size):
    low = head * size // 128 * 128
    high = -(-(head + 1) * size // 128) * 128
    spot = low + lax.broadcasted_iota(jnp.int32, (1, high - low), 1)
    own = ((spot >= head * size) & (spot < (head + 1) * size)).astype(jnp.float32).astype(jnp.bfloat16)
    return low, high - low, own


def attend_image(joint, gates, mixed, lse, image, seq, heads):
    width = mixed.shape[1]
    size = width // heads
    scale = size ** (-0.5)
    lines = pl.ds(pl.multiple_of(image * seq, seq), seq)
    mixed[lines, :] = jnp.zeros((seq, width), mixed.dtype)
    for head in range(heads):
        low, wide, own = window(head, size)
        query = joint[lines, pl.ds(low, wide)] * own
        keys = joint[lines, pl.ds(width + low, wide)]
        values = joint[lines, pl.ds(2 * width + low, wide)] * own
        raw = times_back(keys, query) * scale
        peak = jnp.max(raw, axis=0, keepdims=True)
        expo = jnp.exp(raw - peak)
        total = jnp.sum(expo, axis=0, keepdims=True)
        lse[image, head : head + 1, :] = peak + jnp.log(total)
        probs = (expo * (1.0 / total)).astype(jnp.bfloat16)
        attended = times_rows(probs, values) * gates[image, 0, head]
        mixed[lines, pl.ds(low, wide)] = mixed[lines, pl.ds(low, wide)] + attended.astype(jnp.bfloat16)


def attend_back_image(joint, grad_mixed, gates, lse, grad_joint, grad_gates, image, seq, heads, span):
    width = grad_mixed.shape[1]
    size = width // heads
    scale = size ** (-0.5)
    if span[0] == 0:
        grad_joint[...] = jnp.zeros((seq, 3 * width), grad_joint.dtype)

    def put(column, wide, value):
        here = pl.ds(column, wide)
        grad_joint[:, here] = grad_joint[:, here] + value.astype(jnp.bfloat16)

    for head in span:
        low, wide, own = window(head, size)
        query = joint[:, pl.ds(low, wide)] * own
        keys = joint[:, pl.ds(width + low, wide)] * own
        values = joint[:, pl.ds(2 * width + low, wide)]
        grad = grad_mixed[:, pl.ds(low, wide)] * own
        gate = gates[image, 0, head]
        probs = jnp.exp(times_back(keys, query) * scale - lse[image, head : head + 1, :])
        put(2 * width + low, wide, matmul(probs.astype(jnp.bfloat16), (grad.astype(jnp.float32) * gate).astype(jnp.bfloat16)))
        grad_probs = times_back(values, grad)
        inner = jnp.sum(grad_probs * probs, axis=0, keepdims=True)
        grad_gates[image, head : head + 1, :] = inner
        grad_scores = (probs * (grad_probs - inner) * (gate * scale)).astype(jnp.bfloat16)
        put(low, wide, times_rows(grad_scores, keys))
        put(width + low, wide, matmul(grad_scores, query))


def attend(joint, gates, seq):
    images, heads = gates.shape
    def kernel(j, g, m, l):
        attend_image(j, g, m, l, 0, seq, heads)
    n = joint.shape[1]
    return pl.pallas_call(
        kernel, grid=(images,),
        out_shape=[jax.ShapeDtypeStruct((joint.shape[0], n // 3), jnp.bfloat16), jax.ShapeDtypeStruct((images, heads, seq), jnp.float32)],
        in_specs=[
            pl.BlockSpec((seq, n), lambda i: (i, 0)),
            pl.BlockSpec((1, 1, heads), lambda i: (i, 0, 0), memory_space=pltpu.SMEM),
        ],
        out_specs=[pl.BlockSpec((seq, n // 3), lambda i: (i, 0)), pl.BlockSpec((1, heads, seq), lambda i: (i, 0, 0))],
        compiler_params=pltpu.CompilerParams(vmem_limit_bytes=48*2**20),
        name="attend",
    )(joint, gates[:, None, :])
def thirds(width):
    tiles = width // 128
    a, b = tiles // 3, tiles // 3
    c = tiles - a - b
    sizes = [a, b, (c + 1) // 2, c // 2]
    starts = [sum(sizes[:i]) for i in range(4)]
    return [(128 * s, 128 * n) for s, n in zip(starts, sizes)]


OWN_SLOTS = 8
PAIR_SLOTS = 4
AHEAD = 3
LAG = 2


class Reducer:
    def __init__(self, at, piece, outs, scratch, rows, width):
        self.at, self.piece, self.outs, self.width = at, piece, outs, width
        (
            self.own, self.pair, self.first_a, self.first_b, self.second_a, self.second_b,
            self.hops, self.hops_c, self.flat_a, self.flat_b, self.last_a, self.last_b, self.done,
            self.own_in, self.core_s, self.core_r, self.fa_s, self.fa_r, self.fb_s, self.fb_r,
            self.sa_s, self.sa_r, self.sb_s, self.sb_r, self.hop_s, self.hop_r, self.hopc_s, self.hopc_r,
            self.ca_s, self.ca_r, self.cb_s, self.cb_r, self.end_s, self.end_r, self.out_sem, self.credit,
        ) = scratch
        self.ring = at.ring
        self.total = 3 * self.ring * 2
        self.spans = self.halves(rows)
        self.sent, self.flights = {}, {}
        self.loose, self.outgoing = [], []
        self.cols = [pl.ds(*part) for part in thirds(width)]
        a, b = thirds(width)[1]
        self.cols_ab = pl.ds(0, a + b)
        self.cols_c = pl.ds(a + b, width - a - b)

    @staticmethod
    def halves(rows):
        top = -(-rows // 32) * 16
        return (0, top), (top, rows - top)

    def place(self, n):
        half = n % 2
        k, j = divmod(n // 2, self.ring)
        return k, j, half, self.spans[half][1]

    @staticmethod
    def scratch(rows, width, fsdp):
        ring = fsdp // 2
        total = 3 * ring * 2
        full, rows = rows, Reducer.halves(rows)[0][1]
        low, vmem, dma = jnp.bfloat16, pltpu.VMEM, pltpu.SemaphoreType.DMA
        a, b, c, d = [size for _, size in thirds(width)]
        arrays = [
            vmem((OWN_SLOTS, QUARTERS, rows, width), low),
            vmem((PAIR_SLOTS, QUARTERS, rows, width), low),
            vmem((total, 2, rows, a), low),
            vmem((total, 2, rows, b), low),
            vmem((total, rows, a), low),
            vmem((total, rows, b), low),
            vmem((3, 2, ring - 1, rows, a + b), low),
            vmem((3, 2, ring - 1, QUARTERS, rows, c + d), low),
            vmem((3, 2, 2, rows, c), low),
            vmem((3, 2, 2, rows, d), low),
            vmem((3, 2, rows, c), low),
            vmem((3, 2, rows, d), low),
            vmem((3, QUARTERS, full, width), low),
        ]
        sems = (
            [dma((total, QUARTERS))] * 3
            + [dma((total, 2))] * 4
            + [dma((total,))] * 4
            + [dma((3, 2, ring - 1))] * 4
            + [dma((3, 2, 3))] * 4
            + [dma((3, 2, 4))] * 2
            + [dma((3, 2))]
            + [pltpu.SemaphoreType.REGULAR]
        )
        return arrays + sems

    def go(self, n, *parts):
        copy = remote(*parts)
        copy.start()
        self.sent.setdefault(n, []).append(copy)
        return copy

    def prefetch(self, n):
        at = self.at
        k, j, half, size = self.place(n)
        slot, pair_slot = n % OWN_SLOTS, n % PAIR_SLOTS
        for copy in self.sent.pop(n - OWN_SLOTS, []):
            copy.wait_send()
        mine = at.shard((j + 1) % self.ring)
        other = mine + 1 - 2 * at.c
        if n >= PAIR_SLOTS:
            pl.semaphore_wait(self.credit, 1)
        brought, pairs = [], []
        span, here = pl.ds(*self.spans[half]), pl.ds(0, size)
        for q in range(QUARTERS):
            copy = pltpu.make_async_copy(self.piece(k, mine, q, span), self.own.at[slot, q, here], self.own_in.at[n, q])
            copy.start()
            brought.append(copy)
            copy = remote(
                self.piece(k, other, q, span), self.pair.at[pair_slot, q, here], self.core_s.at[n, q], self.core_r.at[n, q], at.core
            )
            copy.start()
            pairs.append(copy)
        self.loose += pairs
        self.flights[n] = (brought, pairs)

    def plane_first(self, n, slot, here, cols_a, cols_b, land_a, land_b, sems):
        at, own = self.at, self.own
        (sa, ra), (sb, rb) = sems
        return [
            self.go(n, own.at[slot, at.qd, here, cols_a], land_a.at[1, here], sa.at[1], ra.at[1], at.x),
            self.go(n, own.at[slot, at.qd, here, cols_b], land_b.at[1, here], sb.at[1], rb.at[1], at.y),
            self.go(n, own.at[slot, at.qx, here, cols_a], land_a.at[0, here], sa.at[0], ra.at[0], at.x),
            self.go(n, own.at[slot, at.qy, here, cols_b], land_b.at[0, here], sb.at[0], rb.at[0], at.y),
        ]

    def plane_second(self, n, slot, here, copies, cols_a, cols_b, land_a, land_b, next_a, next_b, sems):
        at, own = self.at, self.own
        one_d, two_d, one, two = copies
        (sa, ra), (sb, rb) = sems
        one_d.wait_recv()
        own[slot, at.qy, here, cols_a] = own[slot, at.qy, here, cols_a] + land_a[1, here]
        on_a = self.go(n, own.at[slot, at.qy, here, cols_a], next_a.at[here], sa, ra, at.y)
        two_d.wait_recv()
        own[slot, at.qx, here, cols_b] = own[slot, at.qx, here, cols_b] + land_b[1, here]
        on_b = self.go(n, own.at[slot, at.qx, here, cols_b], next_b.at[here], sb, rb, at.x)
        one.wait_recv()
        own[slot, at.q, here, cols_a] = own[slot, at.q, here, cols_a] + land_a[0, here]
        two.wait_recv()
        own[slot, at.q, here, cols_b] = own[slot, at.q, here, cols_b] + land_b[0, here]
        return [on_a, on_b]

    def plane_third(self, slot, here, copies, cols_a, cols_b, next_a, next_b):
        at, own = self.at, self.own
        for copy in copies:
            copy.wait_recv()
        own[slot, at.q, here, cols_a] = own[slot, at.q, here, cols_a] + next_a[here, :]
        own[slot, at.q, here, cols_b] = own[slot, at.q, here, cols_b] + next_b[here, :]

    def one(self, n):
        at, own, pair = self.at, self.own, self.pair
        k, j, half, size = self.place(n)
        slot, pair_slot = n % OWN_SLOTS, n % PAIR_SLOTS
        here = pl.ds(0, size)
        brought, pairs = self.flights[n]
        for q in range(QUARTERS):
            brought[q].wait()
            pairs[q].wait_recv()

        @pl.loop(0, QUARTERS)
        def _(q):
            own[slot, q, here, :] = own[slot, q, here, :] + pair[pair_slot, q, here, :]

        if n + PAIR_SLOTS < self.total:
            pl.semaphore_signal(self.credit, inc=1, device_id=at.core, device_id_type=MESH)
        a, b, c, d = self.cols
        self.flights[n] = self.plane_first(
            n, slot, here, a, b, self.first_a.at[n], self.first_b.at[n],
            ((self.fa_s.at[n], self.fa_r.at[n]), (self.fb_s.at[n], self.fb_r.at[n])),
        )
        if j > 0:
            self.flights[k, half, "c"].wait_recv()

            @pl.loop(0, QUARTERS)
            def _(q):
                own[slot, q, here, self.cols_c] = own[slot, q, here, self.cols_c] + self.hops_c[k, half, j - 1, q, here, :]

        if j < self.ring - 1:
            self.flights[k, half, "c"] = self.go(
                n, own.at[slot, slice(None), here, self.cols_c], self.hops_c.at[k, half, j, slice(None), here],
                self.hopc_s.at[k, half, j], self.hopc_r.at[k, half, j], at.up,
            )
        else:
            self.flights[k, half, "flat"] = self.plane_first(
                n, slot, here, c, d, self.flat_a.at[k, half], self.flat_b.at[k, half],
                ((self.ca_s.at[k, half], self.ca_r.at[k, half]), (self.cb_s.at[k, half], self.cb_r.at[k, half])),
            )

    def two(self, n):
        k, j, half, size = self.place(n)
        slot, here = n % OWN_SLOTS, pl.ds(0, size)
        a, b, c, d = self.cols
        self.flights[n] = self.plane_second(
            n, slot, here, self.flights[n], a, b, self.first_a.at[n], self.first_b.at[n], self.second_a.at[n], self.second_b.at[n],
            ((self.sa_s.at[n], self.sa_r.at[n]), (self.sb_s.at[n], self.sb_r.at[n])),
        )
        if j == self.ring - 1:
            self.flights[k, half, "flat"] = self.plane_second(
                n, slot, here, self.flights[k, half, "flat"], c, d, self.flat_a.at[k, half], self.flat_b.at[k, half],
                self.last_a.at[k, half], self.last_b.at[k, half],
                ((self.ca_s.at[k, half, 2], self.ca_r.at[k, half, 2]), (self.cb_s.at[k, half, 2], self.cb_r.at[k, half, 2])),
            )

    def three(self, n):
        at, own = self.at, self.own
        k, j, half, size = self.place(n)
        slot, here = n % OWN_SLOTS, pl.ds(0, size)
        a, b, c, d = self.cols
        self.plane_third(slot, here, self.flights[n], a, b, self.second_a.at[n], self.second_b.at[n])
        if j > 0:
            self.flights[k, half, "ab"].wait_recv()
            own[slot, at.q, here, self.cols_ab] = own[slot, at.q, here, self.cols_ab] + self.hops[k, half, j - 1, here, :]
        if j < self.ring - 1:
            self.flights[k, half, "ab"] = self.go(
                n, own.at[slot, at.q, here, self.cols_ab], self.hops.at[k, half, j, here],
                self.hop_s.at[k, half, j], self.hop_r.at[k, half, j], at.up,
            )
            return
        self.plane_third(slot, here, self.flights[k, half, "flat"], c, d, self.last_a.at[k, half], self.last_b.at[k, half])
        span = pl.ds(*self.spans[half])
        self.done[k, at.q, span, :] = own[slot, at.q, here, :]
        mine = self.done.at[k, at.q, span]
        sems = self.end_s.at[k, half], self.end_r.at[k, half]
        self.flights[k, half, "end"] = [
            self.keep(remote(mine, mine, sems[0].at[0], sems[1].at[0], at.x)),
            self.keep(remote(mine, mine, sems[0].at[1], sems[1].at[1], at.y)),
        ]

    def keep(self, copy):
        copy.start()
        self.loose.append(copy)
        return copy

    def four(self, n):
        at, done = self.at, self.done
        k, _, half, _ = self.place(n)
        (start_a, size_a), (start_b, size_b) = cut(self.width)
        span = pl.ds(*self.spans[half])
        sems = self.end_s.at[k, half], self.end_r.at[k, half]
        by_x, by_y = self.flights[k, half, "end"]
        by_x.wait_recv()
        part = done.at[k, at.qx, span, pl.ds(start_a, size_a)]
        first = self.keep(remote(part, part, sems[0].at[2], sems[1].at[2], at.y))
        by_y.wait_recv()
        part = done.at[k, at.qy, span, pl.ds(start_b, size_b)]
        second = self.keep(remote(part, part, sems[0].at[3], sems[1].at[3], at.x))
        self.flights[k, half, "end"] = [first, second]

    def five(self, n):
        k, _, half, _ = self.place(n)
        for copy in self.flights[k, half, "end"]:
            copy.wait_recv()
        span = pl.ds(*self.spans[half])
        copy = pltpu.make_async_copy(self.done.at[k, :, span], self.outs[k].at[:, span], self.out_sem.at[k, half])
        copy.start()
        self.outgoing.append(copy)

    def turn(self, t):
        if t + AHEAD < self.total:
            self.prefetch(t + AHEAD)
        stages = (self.one, self.two, self.three, self.four, self.five)
        for i, stage in enumerate(stages):
            n = t - LAG * i
            if 0 <= n < self.total and (i < 3 or self.place(n)[1] == self.ring - 1):
                stage(n)

    def finish(self):
        for copy in self.outgoing:
            copy.wait()
        for copies in self.sent.values():
            for copy in copies:
                copy.wait_send()
        for copy in self.loose:
            copy.wait_send()


def back_kernel(dp, fsdp, width, images, seq, heads, *refs):
    ring = fsdp // 2
    fc2_ref, fc1_ref, proj_ref, joint_ref, mixed_ref, h1_ref, tokens_ref, middle_ref, weight_ref = refs[:9]
    lse_ref, gates_ref, vectors_ref, scales_ref, factor_ref, routers_ref, ada_ref, pre_ref, picker_ref = refs[9:18]
    refs = refs[18:]
    outs, refs = refs[:3], refs[3:]
    all_gm_ref, all_pre_ref, grad_tokens_ref, triple_ref = refs[:4]
    refs = refs[4:]
    joint, mixed, h1, middle, grad_joint, stage, total, inner, gm_row, gms, parts, mine_in, pres = refs[:13]
    in_sem, out_sem, mate_s, mate_r, cousin_s, cousin_r = refs[13:19]
    at = Place(dp, fsdp)
    at.greet()
    rows = fc1_ref.shape[1]
    count = images * seq
    pad = pre_ref.shape[0]

    def piece(k, index, q, span):
        if k == 0:
            return fc2_ref.at[index, q, span]
        if k == 1:
            return fc1_ref.at[index, span, pl.ds(q * width, width)]
        line = pl.ds(pl.multiple_of(index * rows + span.start, 8), span.size)
        if q == 3:
            return proj_ref.at[line, :]
        return triple_ref.at[q, line, :]

    work = Reducer(at, piece, outs, refs[19:], rows, width)
    moves, fetched = {}, []

    def fetch(name, src, dst):
        copy = pltpu.make_async_copy(src, dst, in_sem.at[len(fetched)])
        copy.start()
        fetched.append(copy)
        moves.setdefault(name, []).append(copy)

    def have(name):
        for copy in moves.pop(name):
            copy.wait()

    def store(name, src, dst, i):
        copy = pltpu.make_async_copy(src, dst, out_sem.at[i])
        copy.start()
        moves[name] = [copy]

    for n in range(AHEAD):
        work.prefetch(n)

    def lines(image):
        return pl.ds(image * seq, seq)

    fetch("mixed", mixed_ref, mixed)
    fetch("joint0", joint_ref.at[lines(0)], joint.at[0])
    fetch("h1", h1_ref, h1)
    inner[...] = jnp.zeros_like(inner)
    gm_row[...] = jnp.zeros_like(gm_row)

    def attention(image, half):
        slot = image % 2
        if half == 0:
            if image == 0:
                have("mixed")
            have("joint" + str(image))
            if image + 1 < images:
                fetch("joint" + str(image + 1), joint_ref.at[lines(image + 1)], joint.at[1 - slot])
        span = range(0, heads // 2) if half == 0 else range(heads // 2, heads)
        attend_back_image(
            joint.at[slot], mixed.at[lines(image)], gates_ref, lse_ref, grad_joint.at[lines(image)], inner, image, seq, heads, span
        )

    def weigh(q):
        if q == 0:
            have("h1")
            fetch("tokens", tokens_ref, mixed)
        slot = q % 2
        if q >= 2:
            have("out" + str(q - 2))

        @pl.loop(0, width // 128)
        def _(m):
            line = pl.ds(pl.multiple_of(m * 128, 128), 128)
            stage[slot, line, :] = times_rows(h1[:, line], grad_joint[:, pl.ds(q * width, width)]).astype(jnp.bfloat16)

        store("out" + str(q), stage.at[slot], triple_ref.at[q], q)

    def bring_weight(q):
        for f in range(fsdp):
            fetch("w" + str(q), weight_ref.at[f, :, pl.ds(q * width, width)], stage.at[q % 2, pl.ds(f * rows, rows), :])

    def wait_terms():
        for q in (1, 2):
            have("out" + str(q))
        bring_weight(0)
        bring_weight(1)
        fetch("middle0", middle_ref.at[lines(0)], middle.at[0])

    def spread(q):
        slot = q % 2
        have("w" + str(q))

        @pl.loop(0, images)
        def _(image):
            line = pl.ds(pl.multiple_of(image * seq, seq), seq)
            value = times_back(grad_joint[line, pl.ds(q * width, width)], stage[slot])
            if q == 0:
                total[line, :] = value
            else:
                total[line, :] = total[line, :] + value

        if q == 0:
            bring_weight(2)

    def norm(image):
        slot = image % 2
        if image == 0:
            have("tokens")
        have("middle" + str(image))
        if image + 1 < images:
            if image >= 1:
                have("done" + str(image - 1))
            fetch("middle" + str(image + 1), middle_ref.at[lines(image + 1)], middle.at[1 - slot])
        scale = 1.0 + scales_ref[image : image + 1, :]
        step = 32

        def chunk(i, sums):
            shift, gain = sums
            line = pl.ds(pl.multiple_of(image * seq + i * step, step), step)
            here = pl.ds(pl.multiple_of(i * step, step), step)
            value = mixed[line, :].astype(jnp.float32)
            grad = total[line, :]
            centered = value - jnp.mean(value, axis=-1, keepdims=True)
            inverse = lax.rsqrt(jnp.mean(centered * centered, axis=-1, keepdims=True) + EPSILON)
            normed = centered * inverse
            through = grad * scale
            back = through - jnp.mean(through, axis=-1, keepdims=True)
            back = back - normed * jnp.mean(through * normed, axis=-1, keepdims=True)
            middle[slot, here, :] = middle[slot, here, :] + inverse * back
            return (
                shift + jnp.sum(grad, axis=0, keepdims=True),
                gain + jnp.sum(grad * normed, axis=0, keepdims=True),
            )

        zero = jnp.zeros((1, width), jnp.float32)
        shift, gain = lax.fori_loop(0, seq // step, chunk, (zero, zero))
        store("done" + str(image), middle.at[slot], grad_tokens_ref.at[lines(image)], 3 + image)
        gm_row[image : image + 1, :width] = shift
        gm_row[image : image + 1, width : 2 * width] = gain

    mates, cousins = at.mates(), at.cousins()
    swaps = [Swap(mates, mate_s.at[i], mate_r.at[i]) for i in range(3)]
    far = [Swap(cousins, cousin_s.at[i], cousin_r.at[i]) for i in range(2)]
    small = []

    def keep(src, dst):
        copy = pltpu.make_async_copy(src, dst, out_sem.at[3 + images + len(small)])
        copy.start()
        small.append(copy)

    held = gms.shape[3]

    def tail_zero():
        gm_row[:, 2 * width :] = vectors_ref[...]
        for f in range(fsdp):
            gms[0, f] = gm_row[:, f * held : (f + 1) * held].astype(jnp.bfloat16)
        swaps[0].start(lambda device: gms.at[0, device[1]], gms.at[1, at.f])

    def tail_one():
        swaps[0].arrived()
        gms[1, at.f] = gms[0, at.f]
        every = gms[1].astype(jnp.float32).reshape(fsdp * pad, held).astype(jnp.bfloat16)
        parts[...] = times_back(every, ada_ref[...]).reshape(parts.shape)
        swaps[1].start(lambda device: parts.at[device[1]], mine_in.at[at.f])
        far[0].start(lambda device: gms.at[1], all_gm_ref.at[at.d])
        keep(gms.at[1], all_gm_ref.at[at.d])

    def tail_two():
        line = lax.broadcasted_iota(jnp.int32, (pad, 128), 0)
        gated = jnp.zeros((pad, 128), jnp.float32)
        for image in range(images):
            summed = lax.dot_general(
                jnp.ones((pad, seq), jnp.float32), inner[image], (((1,), (1,)), ((), ())),
                preferred_element_type=jnp.float32, precision=lax.Precision.HIGHEST,
            )
            gated = jnp.where(line == image, summed, gated)
        router = (gated * factor_ref[...]).astype(jnp.bfloat16)
        swaps[1].arrived()
        mine_in[at.f] = parts[at.f]
        grad_cond = jnp.sum(mine_in[...], axis=0) + times_back(router, routers_ref[...])
        pre_cond = pre_ref[...]
        sig = jax.nn.sigmoid(pre_cond)
        grad_pre = grad_cond * (sig * (1.0 + pre_cond * (1.0 - sig)))
        pres[at.f, :, :width] = (grad_pre + picker_ref[...]).astype(jnp.bfloat16)
        pres[at.f, :, width:] = router
        swaps[2].start(lambda device: pres.at[at.f], pres.at[at.f])

    def tail_three():
        swaps[2].arrived()
        far[1].start(lambda device: pres, all_pre_ref.at[at.d])
        keep(pres, all_pre_ref.at[at.d])

    early = [partial(attention, image, half) for image in range(images) for half in range(2)]
    early += [partial(weigh, q) for q in range(3)] + [wait_terms]
    norms = [partial(norm, image) for image in range(images)]
    late = [[partial(spread, q)] for q in range(3)] + [[step] for step in norms]
    late += [[tail_zero], [], [], [tail_one], [], [], [tail_two], [], [], [tail_three]]
    steps = [[step] for step in early] + late
    for t in range(work.total + 4 * LAG):
        work.turn(t)
        if t < len(steps):
            for step in steps[t]:
                step()
    for swap in far:
        swap.arrived()
    for copy in small:
        copy.wait()
    for image in range(max(images - 2, 0), images):
        have("done" + str(image))
    for swap in swaps + far:
        swap.left()
    work.finish()


def back_half(
    terms, joint, grad_mixed, flat_one, tokens, grad_middle, joint_full, log_total, gates, vectors, scales, factor,
    routers, ada_weight, pre_cond, picker, width, images, seq, dp, fsdp,
):
    rows = terms[1].shape[1]
    heads = gates.shape[1]
    count = images * seq
    pad = pre_cond.shape[0]
    columns = ada_weight.shape[1]
    dma, vmem = pltpu.SemaphoreType.DMA, pltpu.VMEM
    low, f32 = jnp.bfloat16, jnp.float32
    out = jax.ShapeDtypeStruct
    any_space, in_vmem = pl.BlockSpec(memory_space=pl.ANY), pl.BlockSpec(memory_space=vmem)
    in_smem = pl.BlockSpec(memory_space=pltpu.SMEM)
    return pl.pallas_call(
        partial(back_kernel, dp, fsdp, width, images, seq, heads),
        out_shape=[out((QUARTERS, rows, width), low)] * 3
        + [
            out((dp, fsdp, pad, columns), low),
            out((dp, fsdp, pad, width + 128), low),
            out((count, width), f32),
            out((3, width, width), low),
        ],
        in_specs=[any_space] * 9 + [in_vmem, in_smem] + [in_vmem] * 7,
        out_specs=[any_space] * 7,
        scratch_shapes=[
            vmem((2, seq, 3 * width), low),
            vmem((count, width), low),
            vmem((count, width), low),
            vmem((2, seq, width), f32),
            vmem((count, 3 * width), low),
            vmem((2, width, width), low),
            vmem((count, width), f32),
            vmem((images, 128, seq), f32),
            vmem((pad, 6 * width), f32),
            vmem((2, fsdp, pad, columns), low),
            vmem((fsdp, pad, width), f32),
            vmem((fsdp, pad, width), f32),
            vmem((fsdp, pad, width + 128), low),
            dma((3 * fsdp + 3 + 2 * images,)),
            dma((5 + images,)),
            dma((3, fsdp - 1)),
            dma((3, fsdp - 1)),
            dma((2, dp - 1)),
            dma((2, dp - 1)),
        ]
        + Reducer.scratch(rows, width, fsdp),
        compiler_params=pltpu.CompilerParams(
            collective_id=1, has_side_effects=True, vmem_limit_bytes=60 * 2**20
        ),
        name="back",
    )(
        *terms, joint, grad_mixed, flat_one, tokens, grad_middle, joint_full, log_total, gates[:, None, :], vectors, scales,
        factor, routers, ada_weight, pre_cond, picker,
    )


def body(
    dp,
    fsdp,
    tokens,
    timesteps,
    labels,
    head_mask,
    keep_mask,
    cotangent,
    time_weight,
    class_table,
    ada_weight,
    head_router,
    qkv_weight,
    proj_weight,
    fc1_weight,
    fc2_weight,
    token_router,
):
    images, seq, width = tokens.shape
    heads = head_mask.shape[1]
    count = images * seq
    rows = qkv_weight.shape[0]
    hidden = fc1_weight.shape[1]
    entries = time_weight.shape[0] * fsdp
    me_fsdp = lax.axis_index("fsdp")
    pad = -(-(images + 2) // 8) * 8

    def padded(array, value=0.0):
        return jnp.pad(array, ((0, pad - images), (0, 0)), constant_values=value)

    embedded = sinusoid(timesteps, entries).astype(jnp.bfloat16)
    digits = jnp.stack([labels // DIGIT, labels % DIGIT], axis=1).astype(jnp.bfloat16)
    asked = jnp.concatenate(
        [padded(embedded), jnp.pad(padded(digits, -1.0), ((0, 0), (0, 126)))], axis=1
    )
    routers = jnp.pad(
        jnp.concatenate([head_router, token_router], axis=1), ((0, 0), (0, 127 - heads))
    )
    joint_blocks, fc1_full, fc2_full, pre_cond_pad, modulation, routers_full, all_cond, all_asked = gather_weights(
        [
            jnp.concatenate([qkv_weight, proj_weight], axis=1),
            fc1_weight,
            fc2_weight.reshape(QUARTERS, rows, width),
        ],
        asked,
        time_weight,
        class_table,
        ada_weight,
        routers,
        width,
        dp,
        fsdp,
    )
    joint_full = joint_blocks.reshape(width, 4 * width)
    triple, merger = joint_full[:, : 3 * width], joint_full[:, 3 * width :]
    expand = fc1_full.reshape(width, hidden)
    shrink = fc2_full.reshape(hidden, width)
    routers_full = routers_full.reshape(width, 128)
    chooser, picker = routers_full[:, :heads], routers_full[:, heads : heads + 1]
    everyone = dp * fsdp * pad
    all_cond = all_cond.reshape(everyone, width)
    all_asked = all_asked.reshape(everyone, asked.shape[1])
    pre_cond = pre_cond_pad[:images]
    cond = jax.nn.silu(pre_cond).astype(jnp.bfloat16)
    modulation = modulation[:, :images].transpose(1, 0, 2).reshape(images, 6 * width)
    shift_one, scale_one, gate_one, shift_two, scale_two, gate_two = jnp.split(
        modulation[:, None, :], 6, axis=2
    )
    router_sig = jax.nn.sigmoid(matmul(cond, chooser))
    mask_float = head_mask.astype(jnp.float32)
    head_gates = mask_float * router_sig
    inputs = tokens.astype(jnp.float32)
    normed_one = layer_norm(inputs)
    flat_one = (
        (normed_one * (1.0 + scale_one) + shift_one).astype(jnp.bfloat16).reshape(count, width)
    )
    joint = matmul(flat_one, triple).astype(jnp.bfloat16)
    mixed, log_total = attend(joint, head_gates, seq)
    attn = matmul(mixed, merger).reshape(images, seq, width)
    middle = inputs + gate_one * attn
    normed_two = layer_norm(middle)
    flat_two = (
        (normed_two * (1.0 + scale_two) + shift_two).astype(jnp.bfloat16).reshape(count, width)
    )
    rate = jax.nn.sigmoid(matmul(flat_two, picker)).reshape(images, seq, 1)
    upward = matmul(flat_two, expand)
    active = jax.nn.gelu(upward, approximate=True).astype(jnp.bfloat16)
    downward = matmul(active, shrink).reshape(images, seq, width)
    kept = keep_mask.astype(jnp.float32)[:, :, None]
    kept_rate = kept * rate
    output = (middle + gate_two * kept_rate * downward).astype(jnp.bfloat16)
    grad_out = cotangent.astype(jnp.float32)
    grad_gate_two = jnp.sum(grad_out * kept_rate * downward, axis=1)
    grad_down = (grad_out * gate_two * kept_rate).astype(jnp.bfloat16).reshape(count, width)
    grad_rate = jnp.sum(grad_out * gate_two * downward, axis=-1, keepdims=True) * kept
    grad_logit = (grad_rate * rate * (1.0 - rate)).astype(jnp.bfloat16).reshape(count, 1)
    grad_shrink = times_rows(active, grad_down).astype(jnp.bfloat16)
    _, gelu_pull = jax.vjp(partial(jax.nn.gelu, approximate=True), upward)
    grad_up = gelu_pull(times_back(grad_down, shrink))[0].astype(jnp.bfloat16)
    grad_expand = times_rows(flat_two, grad_up).astype(jnp.bfloat16)
    grad_picker = times_rows(grad_logit, flat_two)
    grad_h_two = (times_back(grad_up, expand) + times_back(grad_logit, picker)).reshape(
        images, seq, width
    )
    grad_shift_two = jnp.sum(grad_h_two, axis=1)
    grad_scale_two = jnp.sum(grad_h_two * normed_two, axis=1)
    grad_middle = grad_out + norm_back(middle, grad_h_two * (1.0 + scale_two))
    grad_gate_one = jnp.sum(grad_middle * attn, axis=1)
    grad_attn = (grad_middle * gate_one).astype(jnp.bfloat16).reshape(count, width)
    grad_merger = times_rows(mixed, grad_attn).astype(jnp.bfloat16)
    grad_mixed = times_back(grad_attn, merger).astype(jnp.bfloat16)
    picker_high = lax.reduce_precision(grad_picker, 8, 7)
    vectors = jnp.concatenate([grad_gate_one, grad_shift_two, grad_scale_two, grad_gate_two], axis=1)
    *sums, all_grad, all_pre, grad_inputs, _ = back_half(
        [
            grad_shrink.reshape(fsdp, QUARTERS, rows, width),
            grad_expand.reshape(fsdp, rows, hidden),
            grad_merger,
        ],
        joint,
        grad_mixed,
        flat_one,
        tokens.reshape(count, width),
        grad_middle.reshape(count, width),
        joint_blocks,
        log_total,
        head_gates,
        padded(vectors),
        padded(scale_one[:, 0]),
        padded(jnp.pad(mask_float * router_sig * (1.0 - router_sig), ((0, 0), (0, 128 - heads)))),
        routers_full,
        ada_weight,
        pre_cond_pad,
        jnp.pad(jnp.concatenate([picker_high, grad_picker - picker_high], axis=0), ((pad - 2, 0), (0, 0))),
        width,
        images,
        seq,
        dp,
        fsdp,
    )
    grad_inputs = grad_inputs.reshape(images, seq, width)
    if dp > QUARTERS:
        parts = list(sums)
        for hop in range(QUARTERS, dp, QUARTERS):
            pairs = [(i, (i + hop) % dp) for i in range(dp)]
            parts = [
                part.astype(jnp.float32) + lax.ppermute(s, "dp", pairs).astype(jnp.float32)
                for part, s in zip(parts, sums)
            ]
        sums = parts
    sums = [s.astype(jnp.float32) for s in sums]
    sum_triple = jnp.concatenate([sums[2][0], sums[2][1], sums[2][2]], axis=1)
    sum_merger = sums[2][3]
    sum_expand = jnp.concatenate([sums[1][i] for i in range(QUARTERS)], axis=1)
    sum_shrink = sums[0].reshape(QUARTERS * rows, width)

    sum_ada = times_rows(all_cond, all_grad.reshape(everyone, -1))
    sum_picker = lax.dynamic_slice_in_dim(
        jnp.sum(all_pre[:, :, pad - 2 :, :width].astype(jnp.float32), axis=(0, 1, 2)), me_fsdp * rows, rows, axis=0
    )[:, None]
    is_image = (jnp.arange(pad) < images)[None, None, :, None]
    all_pre = jnp.where(is_image, all_pre, jnp.bfloat16(0.0)).reshape(everyone, -1)
    all_router = all_pre[:, width : width + heads]
    all_pre = all_pre[:, :width]
    own_entries = entries // fsdp
    all_embedded = lax.dynamic_slice_in_dim(
        all_asked[:, :entries], me_fsdp * own_entries, own_entries, axis=1
    )
    classes = jnp.arange(class_table.shape[0], dtype=jnp.float32)
    all_digits = all_asked[:, entries : entries + 2].astype(jnp.float32)
    all_labels = all_digits[:, :1] * DIGIT + all_digits[:, 1:]
    all_rows = (all_labels == classes[None, :]).astype(jnp.bfloat16)
    sum_time = times_rows(all_embedded, all_pre)
    sum_table = times_rows(
        all_rows, lax.dynamic_slice_in_dim(all_pre, me_fsdp * rows, rows, axis=1)
    )
    sum_chooser = times_rows(
        lax.dynamic_slice_in_dim(all_cond, me_fsdp * rows, rows, axis=1), all_router
    )
    return (
        output,
        grad_inputs,
        sum_time,
        sum_table,
        sum_ada,
        sum_chooser,
        sum_triple,
        sum_merger,
        sum_expand,
        sum_shrink,
        sum_picker,
    )


def solution(mesh):
    images = P(("dp", "fsdp"), None, None)
    pairs = P(("dp", "fsdp"), None)
    single = P(("dp", "fsdp"))
    by_row, by_column = P("fsdp", None), P(None, "fsdp")
    in_specs = (
        images, single, single, pairs, pairs, images,
        by_row, by_column, by_column, by_row, by_row, by_row, by_row, by_row, by_row,
    )
    out_specs = (
        images, images,
        by_row, by_column, by_column, by_row, by_row, by_row, by_row, by_row, by_row,
    )
    return jax.shard_map(
        partial(body, mesh.shape["dp"], mesh.shape["fsdp"]),
        mesh=mesh, in_specs=in_specs, out_specs=out_specs, check_vma=False,
    )
```

```python
from functools import partial
import math

import jax
import jax.numpy as jnp
from jax import lax
from jax.experimental import pallas as pl
from jax.experimental.pallas import tpu as pltpu
from jax.sharding import PartitionSpec as P

EPSILON = 1e-06
MESH = pl.DeviceIdType.MESH
QUARTERS = 4
DIGIT = 256


def sinusoid(steps, entries):
    half = entries // 2
    freqs = jnp.exp(-math.log(10000.0) * jnp.arange(half, dtype=jnp.float32) / half)
    angles = steps.astype(jnp.float32)[:, None] * freqs[None, :]
    return jnp.concatenate([jnp.cos(angles), jnp.sin(angles)], axis=1)


def layer_norm(value):
    centered = value - jnp.mean(value, axis=-1, keepdims=True)
    return centered * lax.rsqrt(jnp.mean(centered * centered, axis=-1, keepdims=True) + EPSILON)


def norm_back(value, grad):
    _, pull = jax.vjp(layer_norm, value)
    return pull(grad)[0]


def matmul(left, right):
    return jnp.dot(left, right, preferred_element_type=jnp.float32)


def times_rows(left, right):
    return lax.dot_general(
        left, right, (((0,), (0,)), ((), ())), preferred_element_type=jnp.float32
    )


def times_back(left, right):
    return lax.dot_general(
        left, right, (((1,), (1,)), ((), ())), preferred_element_type=jnp.float32
    )


class Place:
    def __init__(self, dp, fsdp):
        ring = fsdp // 2
        self.dp, self.fsdp, self.ring = dp, fsdp, ring
        d = lax.axis_index("dp")
        f = lax.axis_index("fsdp")
        self.d, self.f = d, f
        self.z = f // 2
        self.c = f % 2
        self.q = d % QUARTERS
        dx = d + 1 - 2 * (d % 2)
        dy = d + 2 - 4 * ((d // 2) % 2)
        self.qx = dx % QUARTERS
        self.qy = dy % QUARTERS
        self.qd = (self.qx + self.qy - self.q + QUARTERS) % QUARTERS
        self.core = (d, f + 1 - 2 * (f % 2))
        self.x = (dx, f)
        self.y = (dy, f)
        self.up = (d, ((self.z + 1) % ring) * 2 + self.c)
        self.down = (d, ((self.z + ring - 1) % ring) * 2 + self.c)

    def shard(self, back):
        return ((self.z + self.ring - back) % self.ring) * 2 + self.c

    def mates(self):
        return [(self.d, (self.f + offset) % self.fsdp) for offset in range(1, self.fsdp)]

    def cousins(self):
        return [((self.d + offset) % self.dp, self.f) for offset in range(1, self.dp)]

    def greet(self):
        barrier = pltpu.get_barrier_semaphore()
        near = self.mates() + self.cousins()
        for other in near:
            pl.semaphore_signal(barrier, inc=1, device_id=other, device_id_type=MESH)
        pl.semaphore_wait(barrier, len(near))


def remote(src, dst, send, recv, device):
    return pltpu.make_async_remote_copy(
        src_ref=src, dst_ref=dst, send_sem=send, recv_sem=recv, device_id=device, device_id_type=MESH
    )


class Swap:
    def __init__(self, partners, send, recv):
        self.partners, self.send, self.recv = partners, send, recv
        self.copies = []

    def start(self, source, landing):
        for i, device in enumerate(self.partners):
            copy = remote(source(device), landing, self.send.at[i], self.recv.at[i], device)
            copy.start()
            self.copies.append(copy)

    def arrived(self):
        for copy in self.copies:
            copy.wait_recv()

    def left(self):
        for copy in self.copies:
            copy.wait_send()


def cut(width):
    first = ((width // 128 + 1) // 2) * 128
    return (0, first), (first, width - first)


def view(ref, lead, q, width, part=None):
    start, size = (0, width) if part is None else part
    flat = ref.shape[-1] != width
    if flat:
        column = pl.multiple_of(q * width + start, 128)
        return ref.at[(*lead, slice(None), pl.ds(column, size))]
    return ref.at[(*lead, q, slice(None), pl.ds(start, size))]


def front_kernel(dp, fsdp, width, images, seq, heads, *refs):
    weights = 3
    ring = fsdp // 2
    shards, refs = refs[:weights], refs[weights:]
    ask_ref, time_ref, table_ref, ada_ref, router_ref, mask_ref, tokens_ref = refs[:7]
    refs = refs[7:]
    fulls, refs = refs[:weights], refs[weights:]
    pre_ref, mod_ref, routers_ref, all_cond_ref, all_ask_ref = refs[:5]
    h1_out, joint_out, lse_out, mixed_out, attn_out, middle_out, h2_out = refs[5:12]
    refs = refs[12:]
    asks, parts, mine_in, conds, columns, mods, gates = refs[:7]
    tokens, h1, joint, lse, mixed, attn, middle, h2, stage, move_sem = refs[7:17]
    refs = refs[17:]
    (own_sem, core_s, core_r, ring_s, ring_r, x_s, x_r, y_s, y_r, a_s, a_r, b_s, b_r) = refs[:13]
    mate_s, mate_r, cousin_s, cousin_r, small_sem = refs[13:]
    at = Place(dp, fsdp)
    part_a, part_b = cut(width)
    at.greet()
    sent, landed = [], []
    mates, cousins = at.mates(), at.cousins()
    swaps = [Swap(mates, mate_s.at[i], mate_r.at[i]) for i in range(5)]
    far = [Swap(cousins, cousin_s.at[i], cousin_r.at[i]) for i in range(2)]
    pad = ask_ref.shape[0]
    group = fsdp * pad
    rows = table_ref.shape[1]

    def go(copy):
        copy.start()
        sent.append(copy)
        return copy

    def ring_copy(k, step):
        index = at.shard(step - 1)
        if step == 1:
            src = view(shards[k], (), at.q, width)
        else:
            src = view(fulls[k], (index,), at.q, width)
        return remote(src, view(fulls[k], (index,), at.q, width), ring_s.at[k, step - 1], ring_r.at[k, step - 1], at.up)

    small = []

    def keep(src, dst):
        copy = pltpu.make_async_copy(src, dst, small_sem.at[len(small)])
        copy.start()
        small.append(copy)

    def cond_one():
        swaps[0].arrived()
        asks[at.f] = ask_ref[...]
        every = asks[...].astype(jnp.float32).reshape(group, asks.shape[2])
        entries = every.shape[1] - 128
        own_rows = time_ref.shape[0]
        lanes = lax.broadcasted_iota(jnp.int32, (group, entries), 1)
        held = (lanes >= at.f * own_rows) & (lanes < (at.f + 1) * own_rows)
        embedded = jnp.where(held, every[:, :entries], 0.0).astype(jnp.bfloat16)
        stacked = jnp.concatenate([time_ref[...]] * fsdp, axis=0)
        label = (every[:, entries : entries + 1] * DIGIT + every[:, entries + 1 : entries + 2]).astype(jnp.int32)
        classes = table_ref.shape[0]
        picks = (label == lax.broadcasted_iota(jnp.int32, (group, classes), 1)).astype(jnp.float32)
        picked = matmul(picks.astype(jnp.bfloat16), table_ref[...]).astype(jnp.bfloat16)
        spot = lax.broadcasted_iota(jnp.int32, (rows, width), 1)
        line = lax.broadcasted_iota(jnp.int32, (rows, width), 0)
        place = (spot == line + at.f * rows).astype(jnp.float32).astype(jnp.bfloat16)
        partial_sum = matmul(embedded, stacked) + matmul(picked, place)
        parts[...] = partial_sum.reshape(fsdp, pad, width)
        swaps[1].start(lambda device: parts.at[device[1]], mine_in.at[at.f])
        far[1].start(lambda device: asks, all_ask_ref.at[at.d])
        keep(asks, all_ask_ref.at[at.d])

    def cond_two():
        swaps[1].arrived()
        mine_in[at.f] = parts[at.f]
        pre_cond = jnp.sum(mine_in[...], axis=0)
        pre_ref[...] = pre_cond
        conds[at.f] = (pre_cond * jax.nn.sigmoid(pre_cond)).astype(jnp.bfloat16)
        swaps[2].start(lambda device: conds.at[at.f], conds.at[at.f])

    def cond_three():
        swaps[2].arrived()
        every = conds[...].astype(jnp.float32).reshape(group, width).astype(jnp.bfloat16)
        columns[...] = matmul(every, ada_ref[...]).reshape(columns.shape)
        swaps[3].start(lambda device: columns.at[device[1]], mods.at[at.f])
        far[0].start(lambda device: conds, all_cond_ref.at[at.d])
        keep(conds, all_cond_ref.at[at.d])

    def cond_four():
        swaps[3].arrived()
        swaps[4].arrived()
        mods[at.f] = columns[at.f]
        routers_ref[at.f] = router_ref[...]
        held = mods.shape[2]
        for f in range(fsdp):
            mod_ref[:, f * held : (f + 1) * held] = mods[f]
        chosen = matmul(conds[at.f], routers_ref[...].reshape(width, router_ref.shape[1]))
        gates[...] = mask_ref[...] * jax.nn.sigmoid(chosen)

    moves, moved = {}, []

    def move(name, src, dst):
        copy = pltpu.make_async_copy(src, dst, move_sem.at[len(moved)])
        copy.start()
        moved.append(copy)
        moves.setdefault(name, []).append(copy)

    def have(name):
        for copy in moves.pop(name):
            copy.wait()

    def line_of(image):
        return pl.ds(image * seq, seq)

    def bring(q):
        for f in range(fsdp):
            src = fulls[0].at[f, :, pl.ds(q * width, width)]
            move("w" + str(q), src, stage.at[q % 2, pl.ds(f * rows, rows), :])

    def modulated(image, index):
        return mod_ref[image : image + 1, index * width : (index + 1) * width]

    step = 32

    def normed(value, scale, shift):
        centered = value - jnp.mean(value, axis=-1, keepdims=True)
        inverse = lax.rsqrt(jnp.mean(centered * centered, axis=-1, keepdims=True) + EPSILON)
        return (centered * inverse * scale + shift).astype(jnp.bfloat16)

    def joint_here():
        for copy in first_landed:
            copy.wait_recv()
        locals_[0].wait()
        bring(0)
        bring(1)

    def norm_one(image):
        if image == 0:
            have("tokens")
        shift, scale = modulated(image, 0), 1.0 + modulated(image, 1)

        @pl.loop(0, seq // step)
        def _(i):
            line = pl.ds(pl.multiple_of(image * seq + i * step, step), step)
            h1[line, :] = normed(tokens[line, :].astype(jnp.float32), scale, shift)

        if image == images - 1:
            move("h1", h1, h1_out)

    def project(q):
        have("w" + str(q))

        @pl.loop(0, images)
        def _(image):
            line = pl.ds(pl.multiple_of(image * seq, seq), seq)
            joint[line, pl.ds(q * width, width)] = matmul(h1[line, :], stage[q % 2]).astype(jnp.bfloat16)

        if q + 2 < QUARTERS:
            bring(q + 2)
        if q == 2:
            move("joint", joint, joint_out)

    def attention(image, half):
        span = range(0, heads // 2) if half == 0 else range(heads // 2, heads)
        attend_image(joint.at[line_of(image)], gates, mixed.at[line_of(image)], lse, image, seq, heads, span)
        if image == images - 1 and half == 1:
            move("mixed", mixed, mixed_out)
            move("lse", lse, lse_out)

    def merge(image):
        if image == 0:
            have("w3")
        line = line_of(image)
        attn[line, :] = matmul(mixed[line, :], stage[1])
        gate, shift, scale = modulated(image, 2), modulated(image, 3), 1.0 + modulated(image, 4)

        @pl.loop(0, seq // step)
        def _(i):
            here = pl.ds(pl.multiple_of(image * seq + i * step, step), step)
            value = tokens[here, :].astype(jnp.float32) + gate * attn[here, :]
            middle[here, :] = value
            h2[here, :] = normed(value, scale, shift)

        move("attn", attn.at[line], attn_out.at[line])
        move("middle", middle.at[line], middle_out.at[line])
        move("h2", h2.at[line], h2_out.at[line])

    move("tokens", tokens_ref, tokens)
    work = [joint_here] + [partial(norm_one, image) for image in range(images)]
    work += [partial(project, q) for q in range(3)]
    work += [partial(attention, image, half) for image in range(images) for half in range(2)]
    work += [partial(merge, image) for image in range(images)]
    extra = {0: cond_one, 1: cond_two, 2: cond_three, 4: cond_four}
    swaps[0].start(lambda device: ask_ref, asks.at[at.f])
    swaps[4].start(lambda device: router_ref, routers_ref.at[at.f])

    items = [(k, step) for k in range(weights) for step in range(1, ring)]
    rings = {items[0]: go(ring_copy(*items[0]))}
    locals_ = []
    for k in range(weights):
        copy = pltpu.make_async_copy(shards[k], fulls[k].at[at.f], own_sem.at[k])
        copy.start()
        locals_.append(copy)
        landed.append(go(remote(shards[k], fulls[k].at[at.f], core_s.at[k, 0], core_r.at[k, 0], at.core)))
    flights, first_landed = {}, [landed[0]]
    begin, turns = ring + 1, len(items) + 2
    done = 0
    for turn in range(turns):
        if turn < len(items):
            k, hop = items[turn]
            rings[k, hop].wait_recv()
            if turn + 1 < len(items):
                rings[items[turn + 1]] = go(ring_copy(*items[turn + 1]))
            mine = view(fulls[k], (at.shard(hop),), at.q, width)
            flights[turn] = (
                go(remote(mine, mine, x_s.at[k, hop - 1], x_r.at[k, hop - 1], at.x)),
                go(remote(mine, mine, y_s.at[k, hop - 1], y_r.at[k, hop - 1], at.y)),
            )
        if 0 <= turn - 1 < len(items):
            k, hop = items[turn - 1]
            by_x, by_y = flights[turn - 1]
            by_x.wait_recv()
            half = view(fulls[k], (at.shard(hop),), at.qx, width, part_a)
            first = go(remote(half, half, a_s.at[k, hop - 1], a_r.at[k, hop - 1], at.y))
            by_y.wait_recv()
            half = view(fulls[k], (at.shard(hop),), at.qy, width, part_b)
            second = go(remote(half, half, b_s.at[k, hop - 1], b_r.at[k, hop - 1], at.x))
            flights[turn - 1] = (first, second)
        if 0 <= turn - 2 < len(items):
            k, hop = items[turn - 2]
            for copy in flights[turn - 2]:
                copy.wait_recv()
            whole = fulls[k].at[at.shard(hop)]
            copy = go(remote(whole, whole, core_s.at[k, hop], core_r.at[k, hop], at.core))
            (landed if k else first_landed).append(copy)
        if turn in extra:
            extra[turn]()
        if turn >= begin:
            upto = -(-len(work) * (turn + 1 - begin) // (turns - begin))
            for part in work[done:upto]:
                part()
            done = upto
    for swap in far:
        swap.arrived()
    for copy in landed[1:]:
        copy.wait_recv()
    for copy in locals_[1:] + small:
        copy.wait()
    for name in ("h1", "joint", "mixed", "lse", "attn", "middle", "h2"):
        have(name)
    for swap in swaps + far:
        swap.left()
    for copy in sent:
        copy.wait_send()


def front_half(
    shards, asked, time_weight, class_table, ada_weight, routers, mask, tokens, width, images, seq, heads, dp, fsdp
):
    ring = fsdp // 2
    dma, vmem = pltpu.SemaphoreType.DMA, pltpu.VMEM
    low, f32 = jnp.bfloat16, jnp.float32
    steps = dma((3, ring - 1))
    pad, asking = asked.shape
    columns = ada_weight.shape[1]
    count = images * seq
    out = jax.ShapeDtypeStruct
    any_space, in_vmem = pl.BlockSpec(memory_space=pl.ANY), pl.BlockSpec(memory_space=vmem)
    results = [
        out((count, width), low),
        out((count, 3 * width), low),
        out((images, heads, seq), f32),
        out((count, width), low),
        out((count, width), f32),
        out((count, width), f32),
        out((count, width), low),
    ]
    return pl.pallas_call(
        partial(front_kernel, dp, fsdp, width, images, seq, heads),
        out_shape=[out((fsdp, *s.shape), s.dtype) for s in shards]
        + [
            out((pad, width), f32),
            out((pad, 6 * width), f32),
            out((fsdp, *routers.shape), routers.dtype),
            out((dp, fsdp, pad, width), low),
            out((dp, fsdp, pad, asking), low),
        ]
        + results,
        in_specs=[any_space] * 3 + [in_vmem] * 6 + [any_space],
        out_specs=[any_space] * 3 + [in_vmem] * 3 + [any_space] * 9,
        scratch_shapes=[
            vmem((fsdp, pad, asking), low),
            vmem((fsdp, pad, width), f32),
            vmem((fsdp, pad, width), f32),
            vmem((fsdp, pad, width), low),
            vmem((fsdp, pad, columns), f32),
            vmem((fsdp, pad, columns), f32),
            vmem((pad, 128), f32),
            vmem((count, width), low),
        ]
        + [vmem(r.shape, r.dtype) for r in results]
        + [vmem((2, width, width), low), dma((4 * fsdp + 5 + 3 * images,))]
        + [dma((3,)), dma((3, ring)), dma((3, ring))]
        + [steps] * 10
        + [dma((5, fsdp - 1))] * 2
        + [dma((2, dp - 1))] * 2
        + [dma((2,))],
        compiler_params=pltpu.CompilerParams(
            collective_id=0, has_side_effects=True, vmem_limit_bytes=60 * 2**20
        ),
        name="front",
    )(*shards, asked, time_weight, class_table, ada_weight, routers, mask, tokens)


def window(head, size):
    low = head * size // 128 * 128
    high = -(-(head + 1) * size // 128) * 128
    spot = low + lax.broadcasted_iota(jnp.int32, (1, high - low), 1)
    own = ((spot >= head * size) & (spot < (head + 1) * size)).astype(jnp.float32).astype(jnp.bfloat16)
    return low, high - low, own


def attend_image(joint, gates, mixed, lse, image, seq, heads, span):
    width = mixed.shape[1]
    size = width // heads
    scale = size ** (-0.5)
    if span[0] == 0:
        mixed[...] = jnp.zeros((seq, width), mixed.dtype)
    for head in span:
        low, wide, own = window(head, size)
        query = joint[:, pl.ds(low, wide)] * own
        keys = joint[:, pl.ds(width + low, wide)]
        values = joint[:, pl.ds(2 * width + low, wide)] * own
        raw = times_back(keys, query) * scale
        peak = jnp.max(raw, axis=0, keepdims=True)
        expo = jnp.exp(raw - peak)
        total = jnp.sum(expo, axis=0, keepdims=True)
        lse[image, head : head + 1, :] = peak + jnp.log(total)
        probs = (expo * (1.0 / total)).astype(jnp.bfloat16)
        attended = times_rows(probs, values) * gates[image : image + 1, head : head + 1]
        mixed[:, pl.ds(low, wide)] = mixed[:, pl.ds(low, wide)] + attended.astype(jnp.bfloat16)


def attend_back_image(joint, grad_mixed, gates, lse, grad_joint, grad_gates, image, seq, heads, span):
    width = grad_mixed.shape[1]
    size = width // heads
    scale = size ** (-0.5)
    if span[0] == 0:
        grad_joint[...] = jnp.zeros((seq, 3 * width), grad_joint.dtype)

    def put(column, wide, value):
        here = pl.ds(column, wide)
        grad_joint[:, here] = grad_joint[:, here] + value.astype(jnp.bfloat16)

    for head in span:
        low, wide, own = window(head, size)
        query = joint[:, pl.ds(low, wide)] * own
        keys = joint[:, pl.ds(width + low, wide)] * own
        values = joint[:, pl.ds(2 * width + low, wide)]
        grad = grad_mixed[:, pl.ds(low, wide)] * own
        gate = gates[image, 0, head]
        probs = jnp.exp(times_back(keys, query) * scale - lse[image, head : head + 1, :])
        put(2 * width + low, wide, matmul(probs.astype(jnp.bfloat16), (grad.astype(jnp.float32) * gate).astype(jnp.bfloat16)))
        grad_probs = times_back(values, grad)
        inner = jnp.sum(grad_probs * probs, axis=0, keepdims=True)
        grad_gates[image, head : head + 1, :] = inner
        grad_scores = (probs * (grad_probs - inner) * (gate * scale)).astype(jnp.bfloat16)
        put(low, wide, times_rows(grad_scores, keys))
        put(width + low, wide, matmul(grad_scores, query))


def thirds(width):
    tiles = width // 128
    a, b = tiles // 3, tiles // 3
    c = tiles - a - b
    sizes = [a, b, (c + 1) // 2, c // 2]
    starts = [sum(sizes[:i]) for i in range(4)]
    return [(128 * s, 128 * n) for s, n in zip(starts, sizes)]


OWN_SLOTS = 8
PAIR_SLOTS = 4
AHEAD = 3
LAG = 2


class Reducer:
    def __init__(self, at, piece, outs, scratch, rows, width):
        self.at, self.piece, self.outs, self.width = at, piece, outs, width
        (
            self.own, self.pair, self.first_a, self.first_b, self.second_a, self.second_b,
            self.hops, self.hops_c, self.flat_a, self.flat_b, self.last_a, self.last_b, self.done,
            self.own_in, self.core_s, self.core_r, self.fa_s, self.fa_r, self.fb_s, self.fb_r,
            self.sa_s, self.sa_r, self.sb_s, self.sb_r, self.hop_s, self.hop_r, self.hopc_s, self.hopc_r,
            self.ca_s, self.ca_r, self.cb_s, self.cb_r, self.end_s, self.end_r, self.out_sem, self.credit,
        ) = scratch
        self.ring = at.ring
        self.total = 3 * self.ring * 2
        self.spans = self.halves(rows)
        self.sent, self.flights = {}, {}
        self.loose, self.outgoing = [], []
        self.cols = [pl.ds(*part) for part in thirds(width)]
        a, b = thirds(width)[1]
        self.cols_ab = pl.ds(0, a + b)
        self.cols_c = pl.ds(a + b, width - a - b)

    @staticmethod
    def halves(rows):
        top = -(-rows // 32) * 16
        return (0, top), (top, rows - top)

    def place(self, n):
        half = n % 2
        k, j = divmod(n // 2, self.ring)
        return k, j, half, self.spans[half][1]

    @staticmethod
    def scratch(rows, width, fsdp):
        ring = fsdp // 2
        total = 3 * ring * 2
        full, rows = rows, Reducer.halves(rows)[0][1]
        low, vmem, dma = jnp.bfloat16, pltpu.VMEM, pltpu.SemaphoreType.DMA
        a, b, c, d = [size for _, size in thirds(width)]
        arrays = [
            vmem((OWN_SLOTS, QUARTERS, rows, width), low),
            vmem((PAIR_SLOTS, QUARTERS, rows, width), low),
            vmem((total, 2, rows, a), low),
            vmem((total, 2, rows, b), low),
            vmem((total, rows, a), low),
            vmem((total, rows, b), low),
            vmem((3, 2, ring - 1, rows, a + b), low),
            vmem((3, 2, ring - 1, QUARTERS, rows, c + d), low),
            vmem((3, 2, 2, rows, c), low),
            vmem((3, 2, 2, rows, d), low),
            vmem((3, 2, rows, c), low),
            vmem((3, 2, rows, d), low),
            vmem((3, QUARTERS, full, width), low),
        ]
        sems = (
            [dma((total, QUARTERS))] * 3
            + [dma((total, 2))] * 4
            + [dma((total,))] * 4
            + [dma((3, 2, ring - 1))] * 4
            + [dma((3, 2, 3))] * 4
            + [dma((3, 2, 4))] * 2
            + [dma((3, 2))]
            + [pltpu.SemaphoreType.REGULAR]
        )
        return arrays + sems

    def go(self, n, *parts):
        copy = remote(*parts)
        copy.start()
        self.sent.setdefault(n, []).append(copy)
        return copy

    def prefetch(self, n):
        at = self.at
        k, j, half, size = self.place(n)
        slot, pair_slot = n % OWN_SLOTS, n % PAIR_SLOTS
        for copy in self.sent.pop(n - OWN_SLOTS, []):
            copy.wait_send()
        mine = at.shard((j + 1) % self.ring)
        other = mine + 1 - 2 * at.c
        if n >= PAIR_SLOTS:
            pl.semaphore_wait(self.credit, 1)
        brought, pairs = [], []
        span, here = pl.ds(*self.spans[half]), pl.ds(0, size)
        for q in range(QUARTERS):
            copy = pltpu.make_async_copy(self.piece(k, mine, q, span), self.own.at[slot, q, here], self.own_in.at[n, q])
            copy.start()
            brought.append(copy)
            copy = remote(
                self.piece(k, other, q, span), self.pair.at[pair_slot, q, here], self.core_s.at[n, q], self.core_r.at[n, q], at.core
            )
            copy.start()
            pairs.append(copy)
        self.loose += pairs
        self.flights[n] = (brought, pairs)

    def plane_first(self, n, slot, here, cols_a, cols_b, land_a, land_b, sems):
        at, own = self.at, self.own
        (sa, ra), (sb, rb) = sems
        return [
            self.go(n, own.at[slot, at.qd, here, cols_a], land_a.at[1, here], sa.at[1], ra.at[1], at.x),
            self.go(n, own.at[slot, at.qd, here, cols_b], land_b.at[1, here], sb.at[1], rb.at[1], at.y),
            self.go(n, own.at[slot, at.qx, here, cols_a], land_a.at[0, here], sa.at[0], ra.at[0], at.x),
            self.go(n, own.at[slot, at.qy, here, cols_b], land_b.at[0, here], sb.at[0], rb.at[0], at.y),
        ]

    def plane_second(self, n, slot, here, copies, cols_a, cols_b, land_a, land_b, next_a, next_b, sems):
        at, own = self.at, self.own
        one_d, two_d, one, two = copies
        (sa, ra), (sb, rb) = sems
        one_d.wait_recv()
        own[slot, at.qy, here, cols_a] = own[slot, at.qy, here, cols_a] + land_a[1, here]
        on_a = self.go(n, own.at[slot, at.qy, here, cols_a], next_a.at[here], sa, ra, at.y)
        two_d.wait_recv()
        own[slot, at.qx, here, cols_b] = own[slot, at.qx, here, cols_b] + land_b[1, here]
        on_b = self.go(n, own.at[slot, at.qx, here, cols_b], next_b.at[here], sb, rb, at.x)
        one.wait_recv()
        own[slot, at.q, here, cols_a] = own[slot, at.q, here, cols_a] + land_a[0, here]
        two.wait_recv()
        own[slot, at.q, here, cols_b] = own[slot, at.q, here, cols_b] + land_b[0, here]
        return [on_a, on_b]

    def plane_third(self, slot, here, copies, cols_a, cols_b, next_a, next_b):
        at, own = self.at, self.own
        for copy in copies:
            copy.wait_recv()
        own[slot, at.q, here, cols_a] = own[slot, at.q, here, cols_a] + next_a[here, :]
        own[slot, at.q, here, cols_b] = own[slot, at.q, here, cols_b] + next_b[here, :]

    def one(self, n):
        at, own, pair = self.at, self.own, self.pair
        k, j, half, size = self.place(n)
        slot, pair_slot = n % OWN_SLOTS, n % PAIR_SLOTS
        here = pl.ds(0, size)
        brought, pairs = self.flights[n]
        for q in range(QUARTERS):
            brought[q].wait()
            pairs[q].wait_recv()

        @pl.loop(0, QUARTERS)
        def _(q):
            own[slot, q, here, :] = own[slot, q, here, :] + pair[pair_slot, q, here, :]

        if n + PAIR_SLOTS < self.total:
            pl.semaphore_signal(self.credit, inc=1, device_id=at.core, device_id_type=MESH)
        a, b, c, d = self.cols
        self.flights[n] = self.plane_first(
            n, slot, here, a, b, self.first_a.at[n], self.first_b.at[n],
            ((self.fa_s.at[n], self.fa_r.at[n]), (self.fb_s.at[n], self.fb_r.at[n])),
        )
        if j > 0:
            self.flights[k, half, "c"].wait_recv()

            @pl.loop(0, QUARTERS)
            def _(q):
                own[slot, q, here, self.cols_c] = own[slot, q, here, self.cols_c] + self.hops_c[k, half, j - 1, q, here, :]

        if j < self.ring - 1:
            self.flights[k, half, "c"] = self.go(
                n, own.at[slot, slice(None), here, self.cols_c], self.hops_c.at[k, half, j, slice(None), here],
                self.hopc_s.at[k, half, j], self.hopc_r.at[k, half, j], at.up,
            )
        else:
            self.flights[k, half, "flat"] = self.plane_first(
                n, slot, here, c, d, self.flat_a.at[k, half], self.flat_b.at[k, half],
                ((self.ca_s.at[k, half], self.ca_r.at[k, half]), (self.cb_s.at[k, half], self.cb_r.at[k, half])),
            )

    def two(self, n):
        k, j, half, size = self.place(n)
        slot, here = n % OWN_SLOTS, pl.ds(0, size)
        a, b, c, d = self.cols
        self.flights[n] = self.plane_second(
            n, slot, here, self.flights[n], a, b, self.first_a.at[n], self.first_b.at[n], self.second_a.at[n], self.second_b.at[n],
            ((self.sa_s.at[n], self.sa_r.at[n]), (self.sb_s.at[n], self.sb_r.at[n])),
        )
        if j == self.ring - 1:
            self.flights[k, half, "flat"] = self.plane_second(
                n, slot, here, self.flights[k, half, "flat"], c, d, self.flat_a.at[k, half], self.flat_b.at[k, half],
                self.last_a.at[k, half], self.last_b.at[k, half],
                ((self.ca_s.at[k, half, 2], self.ca_r.at[k, half, 2]), (self.cb_s.at[k, half, 2], self.cb_r.at[k, half, 2])),
            )

    def three(self, n):
        at, own = self.at, self.own
        k, j, half, size = self.place(n)
        slot, here = n % OWN_SLOTS, pl.ds(0, size)
        a, b, c, d = self.cols
        self.plane_third(slot, here, self.flights[n], a, b, self.second_a.at[n], self.second_b.at[n])
        if j > 0:
            self.flights[k, half, "ab"].wait_recv()
            own[slot, at.q, here, self.cols_ab] = own[slot, at.q, here, self.cols_ab] + self.hops[k, half, j - 1, here, :]
        if j < self.ring - 1:
            self.flights[k, half, "ab"] = self.go(
                n, own.at[slot, at.q, here, self.cols_ab], self.hops.at[k, half, j, here],
                self.hop_s.at[k, half, j], self.hop_r.at[k, half, j], at.up,
            )
            return
        self.plane_third(slot, here, self.flights[k, half, "flat"], c, d, self.last_a.at[k, half], self.last_b.at[k, half])
        span = pl.ds(*self.spans[half])
        self.done[k, at.q, span, :] = own[slot, at.q, here, :]
        mine = self.done.at[k, at.q, span]
        sems = self.end_s.at[k, half], self.end_r.at[k, half]
        self.flights[k, half, "end"] = [
            self.keep(remote(mine, mine, sems[0].at[0], sems[1].at[0], at.x)),
            self.keep(remote(mine, mine, sems[0].at[1], sems[1].at[1], at.y)),
        ]

    def keep(self, copy):
        copy.start()
        self.loose.append(copy)
        return copy

    def four(self, n):
        at, done = self.at, self.done
        k, _, half, _ = self.place(n)
        (start_a, size_a), (start_b, size_b) = cut(self.width)
        span = pl.ds(*self.spans[half])
        sems = self.end_s.at[k, half], self.end_r.at[k, half]
        by_x, by_y = self.flights[k, half, "end"]
        by_x.wait_recv()
        part = done.at[k, at.qx, span, pl.ds(start_a, size_a)]
        first = self.keep(remote(part, part, sems[0].at[2], sems[1].at[2], at.y))
        by_y.wait_recv()
        part = done.at[k, at.qy, span, pl.ds(start_b, size_b)]
        second = self.keep(remote(part, part, sems[0].at[3], sems[1].at[3], at.x))
        self.flights[k, half, "end"] = [first, second]

    def five(self, n):
        k, _, half, _ = self.place(n)
        for copy in self.flights[k, half, "end"]:
            copy.wait_recv()
        span = pl.ds(*self.spans[half])
        copy = pltpu.make_async_copy(self.done.at[k, :, span], self.outs[k].at[:, span], self.out_sem.at[k, half])
        copy.start()
        self.outgoing.append(copy)

    def turn(self, t):
        if t + AHEAD < self.total:
            self.prefetch(t + AHEAD)
        stages = (self.one, self.two, self.three, self.four, self.five)
        for i, stage in enumerate(stages):
            n = t - LAG * i
            if 0 <= n < self.total and (i < 3 or self.place(n)[1] == self.ring - 1):
                stage(n)

    def finish(self):
        for copy in self.outgoing:
            copy.wait()
        for copies in self.sent.values():
            for copy in copies:
                copy.wait_send()
        for copy in self.loose:
            copy.wait_send()


def back_kernel(dp, fsdp, width, images, seq, heads, *refs):
    ring = fsdp // 2
    fc2_ref, fc1_ref, proj_ref, joint_ref, mixed_ref, h1_ref, tokens_ref, middle_ref, weight_ref = refs[:9]
    lse_ref, gates_ref, vectors_ref, scales_ref, factor_ref, routers_ref, ada_ref, pre_ref, picker_ref = refs[9:18]
    refs = refs[18:]
    outs, refs = refs[:3], refs[3:]
    all_gm_ref, all_pre_ref, grad_tokens_ref, triple_ref = refs[:4]
    refs = refs[4:]
    joint, mixed, h1, middle, grad_joint, stage, total, inner, gm_row, gms, parts, mine_in, pres = refs[:13]
    in_sem, out_sem, mate_s, mate_r, cousin_s, cousin_r = refs[13:19]
    at = Place(dp, fsdp)
    at.greet()
    rows = fc1_ref.shape[1]
    count = images * seq
    pad = pre_ref.shape[0]

    def piece(k, index, q, span):
        if k == 0:
            return fc2_ref.at[index, q, span]
        if k == 1:
            return fc1_ref.at[index, span, pl.ds(q * width, width)]
        line = pl.ds(pl.multiple_of(index * rows + span.start, 8), span.size)
        if q == 3:
            return proj_ref.at[line, :]
        return triple_ref.at[q, line, :]

    work = Reducer(at, piece, outs, refs[19:], rows, width)
    moves, fetched = {}, []

    def fetch(name, src, dst):
        copy = pltpu.make_async_copy(src, dst, in_sem.at[len(fetched)])
        copy.start()
        fetched.append(copy)
        moves.setdefault(name, []).append(copy)

    def have(name):
        for copy in moves.pop(name):
            copy.wait()

    def store(name, src, dst, i):
        copy = pltpu.make_async_copy(src, dst, out_sem.at[i])
        copy.start()
        moves[name] = [copy]

    for n in range(AHEAD):
        work.prefetch(n)

    def lines(image):
        return pl.ds(image * seq, seq)

    fetch("mixed", mixed_ref, mixed)
    fetch("joint0", joint_ref.at[lines(0)], joint.at[0])
    fetch("h1", h1_ref, h1)
    inner[...] = jnp.zeros_like(inner)
    gm_row[...] = jnp.zeros_like(gm_row)

    def attention(image, half):
        slot = image % 2
        if half == 0:
            if image == 0:
                have("mixed")
            have("joint" + str(image))
            if image + 1 < images:
                fetch("joint" + str(image + 1), joint_ref.at[lines(image + 1)], joint.at[1 - slot])
        span = range(0, heads // 2) if half == 0 else range(heads // 2, heads)
        attend_back_image(
            joint.at[slot], mixed.at[lines(image)], gates_ref, lse_ref, grad_joint.at[lines(image)], inner, image, seq, heads, span
        )

    def weigh(q):
        if q == 0:
            have("h1")
            fetch("tokens", tokens_ref, mixed)
        slot = q % 2
        if q >= 2:
            have("out" + str(q - 2))

        @pl.loop(0, width // 128)
        def _(m):
            line = pl.ds(pl.multiple_of(m * 128, 128), 128)
            stage[slot, line, :] = times_rows(h1[:, line], grad_joint[:, pl.ds(q * width, width)]).astype(jnp.bfloat16)

        store("out" + str(q), stage.at[slot], triple_ref.at[q], q)

    def bring_weight(q):
        for f in range(fsdp):
            fetch("w" + str(q), weight_ref.at[f, :, pl.ds(q * width, width)], stage.at[q % 2, pl.ds(f * rows, rows), :])

    def wait_terms():
        for q in (1, 2):
            have("out" + str(q))
        bring_weight(0)
        bring_weight(1)
        fetch("middle0", middle_ref.at[lines(0)], middle.at[0])

    def spread(q):
        slot = q % 2
        have("w" + str(q))

        @pl.loop(0, images)
        def _(image):
            line = pl.ds(pl.multiple_of(image * seq, seq), seq)
            value = times_back(grad_joint[line, pl.ds(q * width, width)], stage[slot])
            if q == 0:
                total[line, :] = value
            else:
                total[line, :] = total[line, :] + value

        if q == 0:
            bring_weight(2)

    def norm(image):
        slot = image % 2
        if image == 0:
            have("tokens")
        have("middle" + str(image))
        if image + 1 < images:
            if image >= 1:
                have("done" + str(image - 1))
            fetch("middle" + str(image + 1), middle_ref.at[lines(image + 1)], middle.at[1 - slot])
        scale = 1.0 + scales_ref[image : image + 1, :]
        step = 32

        def chunk(i, sums):
            shift, gain = sums
            line = pl.ds(pl.multiple_of(image * seq + i * step, step), step)
            here = pl.ds(pl.multiple_of(i * step, step), step)
            value = mixed[line, :].astype(jnp.float32)
            grad = total[line, :]
            centered = value - jnp.mean(value, axis=-1, keepdims=True)
            inverse = lax.rsqrt(jnp.mean(centered * centered, axis=-1, keepdims=True) + EPSILON)
            normed = centered * inverse
            through = grad * scale
            back = through - jnp.mean(through, axis=-1, keepdims=True)
            back = back - normed * jnp.mean(through * normed, axis=-1, keepdims=True)
            middle[slot, here, :] = middle[slot, here, :] + inverse * back
            return (
                shift + jnp.sum(grad, axis=0, keepdims=True),
                gain + jnp.sum(grad * normed, axis=0, keepdims=True),
            )

        zero = jnp.zeros((1, width), jnp.float32)
        shift, gain = lax.fori_loop(0, seq // step, chunk, (zero, zero))
        store("done" + str(image), middle.at[slot], grad_tokens_ref.at[lines(image)], 3 + image)
        gm_row[image : image + 1, :width] = shift
        gm_row[image : image + 1, width : 2 * width] = gain

    mates, cousins = at.mates(), at.cousins()
    swaps = [Swap(mates, mate_s.at[i], mate_r.at[i]) for i in range(3)]
    far = [Swap(cousins, cousin_s.at[i], cousin_r.at[i]) for i in range(2)]
    small = []

    def keep(src, dst):
        copy = pltpu.make_async_copy(src, dst, out_sem.at[3 + images + len(small)])
        copy.start()
        small.append(copy)

    held = gms.shape[3]

    def tail_zero():
        gm_row[:, 2 * width :] = vectors_ref[...]
        for f in range(fsdp):
            gms[0, f] = gm_row[:, f * held : (f + 1) * held].astype(jnp.bfloat16)
        swaps[0].start(lambda device: gms.at[0, device[1]], gms.at[1, at.f])

    def tail_one():
        swaps[0].arrived()
        gms[1, at.f] = gms[0, at.f]
        every = gms[1].astype(jnp.float32).reshape(fsdp * pad, held).astype(jnp.bfloat16)
        parts[...] = times_back(every, ada_ref[...]).reshape(parts.shape)
        swaps[1].start(lambda device: parts.at[device[1]], mine_in.at[at.f])
        far[0].start(lambda device: gms.at[1], all_gm_ref.at[at.d])
        keep(gms.at[1], all_gm_ref.at[at.d])

    def tail_two():
        line = lax.broadcasted_iota(jnp.int32, (pad, 128), 0)
        gated = jnp.zeros((pad, 128), jnp.float32)
        for image in range(images):
            summed = lax.dot_general(
                jnp.ones((pad, seq), jnp.float32), inner[image], (((1,), (1,)), ((), ())),
                preferred_element_type=jnp.float32, precision=lax.Precision.HIGHEST,
            )
            gated = jnp.where(line == image, summed, gated)
        router = (gated * factor_ref[...]).astype(jnp.bfloat16)
        swaps[1].arrived()
        mine_in[at.f] = parts[at.f]
        grad_cond = jnp.sum(mine_in[...], axis=0) + times_back(router, routers_ref[...])
        pre_cond = pre_ref[...]
        sig = jax.nn.sigmoid(pre_cond)
        grad_pre = grad_cond * (sig * (1.0 + pre_cond * (1.0 - sig)))
        pres[at.f, :, :width] = (grad_pre + picker_ref[...]).astype(jnp.bfloat16)
        pres[at.f, :, width:] = router
        swaps[2].start(lambda device: pres.at[at.f], pres.at[at.f])

    def tail_three():
        swaps[2].arrived()
        far[1].start(lambda device: pres, all_pre_ref.at[at.d])
        keep(pres, all_pre_ref.at[at.d])

    early = [partial(attention, image, half) for image in range(images) for half in range(2)]
    early += [partial(weigh, q) for q in range(3)] + [wait_terms]
    norms = [partial(norm, image) for image in range(images)]
    late = [[partial(spread, q)] for q in range(3)] + [[step] for step in norms]
    late += [[tail_zero], [], [], [tail_one], [], [], [tail_two], [], [], [tail_three]]
    steps = [[step] for step in early] + late
    for t in range(work.total + 4 * LAG):
        work.turn(t)
        if t < len(steps):
            for step in steps[t]:
                step()
    for swap in far:
        swap.arrived()
    for copy in small:
        copy.wait()
    for image in range(max(images - 2, 0), images):
        have("done" + str(image))
    for swap in swaps + far:
        swap.left()
    work.finish()


def back_half(
    terms, joint, grad_mixed, flat_one, tokens, grad_middle, joint_full, log_total, gates, vectors, scales, factor,
    routers, ada_weight, pre_cond, picker, width, images, seq, dp, fsdp,
):
    rows = terms[1].shape[1]
    heads = gates.shape[1]
    count = images * seq
    pad = pre_cond.shape[0]
    columns = ada_weight.shape[1]
    dma, vmem = pltpu.SemaphoreType.DMA, pltpu.VMEM
    low, f32 = jnp.bfloat16, jnp.float32
    out = jax.ShapeDtypeStruct
    any_space, in_vmem = pl.BlockSpec(memory_space=pl.ANY), pl.BlockSpec(memory_space=vmem)
    in_smem = pl.BlockSpec(memory_space=pltpu.SMEM)
    return pl.pallas_call(
        partial(back_kernel, dp, fsdp, width, images, seq, heads),
        out_shape=[out((QUARTERS, rows, width), low)] * 3
        + [
            out((dp, fsdp, pad, columns), low),
            out((dp, fsdp, pad, width + 128), low),
            out((count, width), f32),
            out((3, width, width), low),
        ],
        in_specs=[any_space] * 9 + [in_vmem, in_smem] + [in_vmem] * 7,
        out_specs=[any_space] * 7,
        scratch_shapes=[
            vmem((2, seq, 3 * width), low),
            vmem((count, width), low),
            vmem((count, width), low),
            vmem((2, seq, width), f32),
            vmem((count, 3 * width), low),
            vmem((2, width, width), low),
            vmem((count, width), f32),
            vmem((images, 128, seq), f32),
            vmem((pad, 6 * width), f32),
            vmem((2, fsdp, pad, columns), low),
            vmem((fsdp, pad, width), f32),
            vmem((fsdp, pad, width), f32),
            vmem((fsdp, pad, width + 128), low),
            dma((3 * fsdp + 3 + 2 * images,)),
            dma((5 + images,)),
            dma((3, fsdp - 1)),
            dma((3, fsdp - 1)),
            dma((2, dp - 1)),
            dma((2, dp - 1)),
        ]
        + Reducer.scratch(rows, width, fsdp),
        compiler_params=pltpu.CompilerParams(
            collective_id=1, has_side_effects=True, vmem_limit_bytes=60 * 2**20
        ),
        name="back",
    )(
        *terms, joint, grad_mixed, flat_one, tokens, grad_middle, joint_full, log_total, gates[:, None, :], vectors, scales,
        factor, routers, ada_weight, pre_cond, picker,
    )


def body(
    dp,
    fsdp,
    tokens,
    timesteps,
    labels,
    head_mask,
    keep_mask,
    cotangent,
    time_weight,
    class_table,
    ada_weight,
    head_router,
    qkv_weight,
    proj_weight,
    fc1_weight,
    fc2_weight,
    token_router,
):
    images, seq, width = tokens.shape
    heads = head_mask.shape[1]
    count = images * seq
    rows = qkv_weight.shape[0]
    hidden = fc1_weight.shape[1]
    entries = time_weight.shape[0] * fsdp
    me_fsdp = lax.axis_index("fsdp")
    pad = -(-(images + 2) // 8) * 8

    def padded(array, value=0.0):
        return jnp.pad(array, ((0, pad - images), (0, 0)), constant_values=value)

    embedded = sinusoid(timesteps, entries).astype(jnp.bfloat16)
    digits = jnp.stack([labels // DIGIT, labels % DIGIT], axis=1).astype(jnp.bfloat16)
    asked = jnp.concatenate(
        [padded(embedded), jnp.pad(padded(digits, -1.0), ((0, 0), (0, 126)))], axis=1
    )
    routers = jnp.pad(
        jnp.concatenate([head_router, token_router], axis=1), ((0, 0), (0, 127 - heads))
    )
    mask_float = head_mask.astype(jnp.float32)
    *gathered, flat_one, joint, log_total, mixed, attn, middle, flat_two = front_half(
        [
            jnp.concatenate([qkv_weight, proj_weight], axis=1),
            fc1_weight,
            fc2_weight.reshape(QUARTERS, rows, width),
        ],
        asked,
        time_weight,
        class_table,
        ada_weight,
        routers,
        padded(jnp.pad(mask_float, ((0, 0), (0, 128 - heads)))),
        tokens.reshape(count, width),
        width,
        images,
        seq,
        heads,
        dp,
        fsdp,
    )
    joint_blocks, fc1_full, fc2_full, pre_cond_pad, modulation, routers_full, all_cond, all_asked = gathered
    merger = joint_blocks[:, :, 3 * width :].reshape(width, width)
    expand = fc1_full.reshape(width, hidden)
    shrink = fc2_full.reshape(hidden, width)
    routers_full = routers_full.reshape(width, 128)
    chooser, picker = routers_full[:, :heads], routers_full[:, heads : heads + 1]
    everyone = dp * fsdp * pad
    all_cond = all_cond.reshape(everyone, width)
    all_asked = all_asked.reshape(everyone, asked.shape[1])
    pre_cond = pre_cond_pad[:images]
    cond = jax.nn.silu(pre_cond).astype(jnp.bfloat16)
    modulation = modulation[:images]
    shift_one, scale_one, gate_one, shift_two, scale_two, gate_two = jnp.split(
        modulation[:, None, :], 6, axis=2
    )
    router_sig = jax.nn.sigmoid(matmul(cond, chooser))
    head_gates = mask_float * router_sig
    attn = attn.reshape(images, seq, width)
    middle = middle.reshape(images, seq, width)
    normed_two = layer_norm(middle)
    rate = jax.nn.sigmoid(matmul(flat_two, picker)).reshape(images, seq, 1)
    upward = matmul(flat_two, expand)
    active = jax.nn.gelu(upward, approximate=True).astype(jnp.bfloat16)
    downward = matmul(active, shrink).reshape(images, seq, width)
    kept = keep_mask.astype(jnp.float32)[:, :, None]
    kept_rate = kept * rate
    output = (middle + gate_two * kept_rate * downward).astype(jnp.bfloat16)
    grad_out = cotangent.astype(jnp.float32)
    grad_gate_two = jnp.sum(grad_out * kept_rate * downward, axis=1)
    grad_down = (grad_out * gate_two * kept_rate).astype(jnp.bfloat16).reshape(count, width)
    grad_rate = jnp.sum(grad_out * gate_two * downward, axis=-1, keepdims=True) * kept
    grad_logit = (grad_rate * rate * (1.0 - rate)).astype(jnp.bfloat16).reshape(count, 1)
    grad_shrink = times_rows(active, grad_down).astype(jnp.bfloat16)
    _, gelu_pull = jax.vjp(partial(jax.nn.gelu, approximate=True), upward)
    grad_up = gelu_pull(times_back(grad_down, shrink))[0].astype(jnp.bfloat16)
    grad_expand = times_rows(flat_two, grad_up).astype(jnp.bfloat16)
    grad_picker = times_rows(grad_logit, flat_two)
    grad_h_two = (times_back(grad_up, expand) + times_back(grad_logit, picker)).reshape(
        images, seq, width
    )
    grad_shift_two = jnp.sum(grad_h_two, axis=1)
    grad_scale_two = jnp.sum(grad_h_two * normed_two, axis=1)
    grad_middle = grad_out + norm_back(middle, grad_h_two * (1.0 + scale_two))
    grad_gate_one = jnp.sum(grad_middle * attn, axis=1)
    grad_attn = (grad_middle * gate_one).astype(jnp.bfloat16).reshape(count, width)
    grad_merger = times_rows(mixed, grad_attn).astype(jnp.bfloat16)
    grad_mixed = times_back(grad_attn, merger).astype(jnp.bfloat16)
    picker_high = lax.reduce_precision(grad_picker, 8, 7)
    vectors = jnp.concatenate([grad_gate_one, grad_shift_two, grad_scale_two, grad_gate_two], axis=1)
    *sums, all_grad, all_pre, grad_inputs, _ = back_half(
        [
            grad_shrink.reshape(fsdp, QUARTERS, rows, width),
            grad_expand.reshape(fsdp, rows, hidden),
            grad_merger,
        ],
        joint,
        grad_mixed,
        flat_one,
        tokens.reshape(count, width),
        grad_middle.reshape(count, width),
        joint_blocks,
        log_total,
        head_gates,
        padded(vectors),
        padded(scale_one[:, 0]),
        padded(jnp.pad(mask_float * router_sig * (1.0 - router_sig), ((0, 0), (0, 128 - heads)))),
        routers_full,
        ada_weight,
        pre_cond_pad,
        jnp.pad(jnp.concatenate([picker_high, grad_picker - picker_high], axis=0), ((pad - 2, 0), (0, 0))),
        width,
        images,
        seq,
        dp,
        fsdp,
    )
    grad_inputs = grad_inputs.reshape(images, seq, width)
    if dp > QUARTERS:
        parts = list(sums)
        for hop in range(QUARTERS, dp, QUARTERS):
            pairs = [(i, (i + hop) % dp) for i in range(dp)]
            parts = [
                part.astype(jnp.float32) + lax.ppermute(s, "dp", pairs).astype(jnp.float32)
                for part, s in zip(parts, sums)
            ]
        sums = parts
    sums = [s.astype(jnp.float32) for s in sums]
    sum_triple = jnp.concatenate([sums[2][0], sums[2][1], sums[2][2]], axis=1)
    sum_merger = sums[2][3]
    sum_expand = jnp.concatenate([sums[1][i] for i in range(QUARTERS)], axis=1)
    sum_shrink = sums[0].reshape(QUARTERS * rows, width)

    sum_ada = times_rows(all_cond, all_grad.reshape(everyone, -1))
    sum_picker = lax.dynamic_slice_in_dim(
        jnp.sum(all_pre[:, :, pad - 2 :, :width].astype(jnp.float32), axis=(0, 1, 2)), me_fsdp * rows, rows, axis=0
    )[:, None]
    is_image = (jnp.arange(pad) < images)[None, None, :, None]
    all_pre = jnp.where(is_image, all_pre, jnp.bfloat16(0.0)).reshape(everyone, -1)
    all_router = all_pre[:, width : width + heads]
    all_pre = all_pre[:, :width]
    own_entries = entries // fsdp
    all_embedded = lax.dynamic_slice_in_dim(
        all_asked[:, :entries], me_fsdp * own_entries, own_entries, axis=1
    )
    classes = jnp.arange(class_table.shape[0], dtype=jnp.float32)
    all_digits = all_asked[:, entries : entries + 2].astype(jnp.float32)
    all_labels = all_digits[:, :1] * DIGIT + all_digits[:, 1:]
    all_rows = (all_labels == classes[None, :]).astype(jnp.bfloat16)
    sum_time = times_rows(all_embedded, all_pre)
    sum_table = times_rows(
        all_rows, lax.dynamic_slice_in_dim(all_pre, me_fsdp * rows, rows, axis=1)
    )
    sum_chooser = times_rows(
        lax.dynamic_slice_in_dim(all_cond, me_fsdp * rows, rows, axis=1), all_router
    )
    return (
        output,
        grad_inputs,
        sum_time,
        sum_table,
        sum_ada,
        sum_chooser,
        sum_triple,
        sum_merger,
        sum_expand,
        sum_shrink,
        sum_picker,
    )


def solution(mesh):
    images = P(("dp", "fsdp"), None, None)
    pairs = P(("dp", "fsdp"), None)
    single = P(("dp", "fsdp"))
    by_row, by_column = P("fsdp", None), P(None, "fsdp")
    in_specs = (
        images, single, single, pairs, pairs, images,
        by_row, by_column, by_column, by_row, by_row, by_row, by_row, by_row, by_row,
    )
    out_specs = (
        images, images,
        by_row, by_column, by_column, by_row, by_row, by_row, by_row, by_row, by_row,
    )
    return jax.shard_map(
        partial(body, mesh.shape["dp"], mesh.shape["fsdp"]),
        mesh=mesh, in_specs=in_specs, out_specs=out_specs, check_vma=False,
    )
```

```python
from functools import partial
import math

import jax
import jax.numpy as jnp
from jax import lax
from jax.experimental import pallas as pl
from jax.experimental.pallas import tpu as pltpu
from jax.sharding import PartitionSpec as P

EPSILON = 1e-06
MESH = pl.DeviceIdType.MESH
QUARTERS = 4
DIGIT = 256


def sinusoid(steps, entries):
    half = entries // 2
    freqs = jnp.exp(-math.log(10000.0) * jnp.arange(half, dtype=jnp.float32) / half)
    angles = steps.astype(jnp.float32)[:, None] * freqs[None, :]
    return jnp.concatenate([jnp.cos(angles), jnp.sin(angles)], axis=1)


def layer_norm(value):
    centered = value - jnp.mean(value, axis=-1, keepdims=True)
    return centered * lax.rsqrt(jnp.mean(centered * centered, axis=-1, keepdims=True) + EPSILON)


def norm_back(value, grad):
    _, pull = jax.vjp(layer_norm, value)
    return pull(grad)[0]


def matmul(left, right):
    return jnp.dot(left, right, preferred_element_type=jnp.float32)


def times_rows(left, right):
    return lax.dot_general(
        left, right, (((0,), (0,)), ((), ())), preferred_element_type=jnp.float32
    )


def times_back(left, right):
    return lax.dot_general(
        left, right, (((1,), (1,)), ((), ())), preferred_element_type=jnp.float32
    )


class Place:
    def __init__(self, dp, fsdp):
        ring = fsdp // 2
        self.dp, self.fsdp, self.ring = dp, fsdp, ring
        d = lax.axis_index("dp")
        f = lax.axis_index("fsdp")
        self.d, self.f = d, f
        self.z = f // 2
        self.c = f % 2
        self.q = d % QUARTERS
        dx = d + 1 - 2 * (d % 2)
        dy = d + 2 - 4 * ((d // 2) % 2)
        self.qx = dx % QUARTERS
        self.qy = dy % QUARTERS
        self.qd = (self.qx + self.qy - self.q + QUARTERS) % QUARTERS
        self.core = (d, f + 1 - 2 * (f % 2))
        self.x = (dx, f)
        self.y = (dy, f)
        self.up = (d, ((self.z + 1) % ring) * 2 + self.c)
        self.down = (d, ((self.z + ring - 1) % ring) * 2 + self.c)

    def shard(self, back):
        return ((self.z + self.ring - back) % self.ring) * 2 + self.c

    def mates(self):
        return [(self.d, (self.f + offset) % self.fsdp) for offset in range(1, self.fsdp)]

    def cousins(self):
        return [((self.d + offset) % self.dp, self.f) for offset in range(1, self.dp)]

    def greet(self):
        barrier = pltpu.get_barrier_semaphore()
        near = self.mates() + self.cousins()
        for other in near:
            pl.semaphore_signal(barrier, inc=1, device_id=other, device_id_type=MESH)
        pl.semaphore_wait(barrier, len(near))


def remote(src, dst, send, recv, device):
    return pltpu.make_async_remote_copy(
        src_ref=src, dst_ref=dst, send_sem=send, recv_sem=recv, device_id=device, device_id_type=MESH
    )


class Swap:
    def __init__(self, partners, send, recv):
        self.partners, self.send, self.recv = partners, send, recv
        self.copies = []

    def start(self, source, landing):
        for i, device in enumerate(self.partners):
            copy = remote(source(device), landing, self.send.at[i], self.recv.at[i], device)
            copy.start()
            self.copies.append(copy)

    def arrived(self):
        for copy in self.copies:
            copy.wait_recv()

    def left(self):
        for copy in self.copies:
            copy.wait_send()


def cut(width):
    first = ((width // 128 + 1) // 2) * 128
    return (0, first), (first, width - first)


def view(ref, lead, q, width, part=None):
    start, size = (0, width) if part is None else part
    flat = ref.shape[-1] != width
    if flat:
        column = pl.multiple_of(q * width + start, 128)
        return ref.at[(*lead, slice(None), pl.ds(column, size))]
    return ref.at[(*lead, q, slice(None), pl.ds(start, size))]


def front_kernel(dp, fsdp, width, images, seq, heads, *refs):
    weights = 3
    ring = fsdp // 2
    shards, refs = refs[:weights], refs[weights:]
    ask_ref, time_ref, table_hbm, ada_hbm, router_ref, mask_ref, tokens_ref = refs[:7]
    refs = refs[7:]
    fulls, refs = refs[:weights], refs[weights:]
    pre_ref, mod_ref, routers_ref, all_cond_ref, all_ask_ref = refs[:5]
    h1_out, joint_out, lse_out, mixed_out, attn_out, middle_out, h2_out = refs[5:12]
    refs = refs[12:]
    asks, parts, mine_in, conds, columns, mods, gates = refs[:7]
    tokens, h1, joint, lse, mixed, attn, middle, h2, stage, table_ref, ada_ref, move_sem = refs[7:19]
    refs = refs[19:]
    (own_sem, core_s, core_r, ring_s, ring_r, x_s, x_r, y_s, y_r, a_s, a_r, b_s, b_r) = refs[:13]
    mate_s, mate_r, cousin_s, cousin_r, small_sem = refs[13:]
    at = Place(dp, fsdp)
    part_a, part_b = cut(width)
    at.greet()
    sent, landed = [], []
    mates, cousins = at.mates(), at.cousins()
    swaps = [Swap(mates, mate_s.at[i], mate_r.at[i]) for i in range(5)]
    far = [Swap(cousins, cousin_s.at[i], cousin_r.at[i]) for i in range(2)]
    pad = ask_ref.shape[0]
    group = fsdp * pad
    rows = table_ref.shape[0]

    def go(copy):
        copy.start()
        sent.append(copy)
        return copy

    def ring_copy(k, step):
        index = at.shard(step - 1)
        if step == 1:
            src = view(shards[k], (), at.q, width)
        else:
            src = view(fulls[k], (index,), at.q, width)
        return remote(src, view(fulls[k], (index,), at.q, width), ring_s.at[k, step - 1], ring_r.at[k, step - 1], at.up)

    small = []

    def keep(src, dst):
        copy = pltpu.make_async_copy(src, dst, small_sem.at[len(small)])
        copy.start()
        small.append(copy)

    def cond_one():
        have("table")
        swaps[0].arrived()
        asks[at.f] = ask_ref[...]
        every = asks[...].astype(jnp.float32).reshape(group, asks.shape[2])
        entries = every.shape[1] - 128
        own_rows = time_ref.shape[0]
        lanes = lax.broadcasted_iota(jnp.int32, (group, entries), 1)
        held = (lanes >= at.f * own_rows) & (lanes < (at.f + 1) * own_rows)
        embedded = jnp.where(held, every[:, :entries], 0.0).astype(jnp.bfloat16)
        stacked = jnp.concatenate([time_ref[...]] * fsdp, axis=0)
        label = (every[:, entries : entries + 1] * DIGIT + every[:, entries + 1 : entries + 2]).astype(jnp.int32)
        classes = table_ref.shape[1]
        picks = (label == lax.broadcasted_iota(jnp.int32, (group, classes), 1)).astype(jnp.float32)
        picked = times_back(picks.astype(jnp.bfloat16), table_ref[...]).astype(jnp.bfloat16)
        spot = lax.broadcasted_iota(jnp.int32, (rows, width), 1)
        line = lax.broadcasted_iota(jnp.int32, (rows, width), 0)
        place = (spot == line + at.f * rows).astype(jnp.float32).astype(jnp.bfloat16)
        partial_sum = matmul(embedded, stacked) + matmul(picked, place)
        parts[...] = partial_sum.reshape(fsdp, pad, width)
        swaps[1].start(lambda device: parts.at[device[1]], mine_in.at[at.f])
        far[1].start(lambda device: asks, all_ask_ref.at[at.d])
        keep(asks, all_ask_ref.at[at.d])

    def cond_two():
        swaps[1].arrived()
        mine_in[at.f] = parts[at.f]
        pre_cond = jnp.sum(mine_in[...], axis=0)
        pre_ref[...] = pre_cond
        conds[at.f] = (pre_cond * jax.nn.sigmoid(pre_cond)).astype(jnp.bfloat16)
        swaps[2].start(lambda device: conds.at[at.f], conds.at[at.f])

    def cond_three():
        have("ada")
        swaps[2].arrived()
        every = conds[...].astype(jnp.float32).reshape(group, width).astype(jnp.bfloat16)
        columns[...] = times_back(every, ada_ref[...]).reshape(columns.shape)
        swaps[3].start(lambda device: columns.at[device[1]], mods.at[at.f])
        far[0].start(lambda device: conds, all_cond_ref.at[at.d])
        keep(conds, all_cond_ref.at[at.d])

    def cond_four():
        swaps[3].arrived()
        swaps[4].arrived()
        mods[at.f] = columns[at.f]
        routers_ref[at.f] = router_ref[...]
        held = mods.shape[2]
        for f in range(fsdp):
            mod_ref[:, f * held : (f + 1) * held] = mods[f]
        chosen = matmul(conds[at.f], routers_ref[...].reshape(width, router_ref.shape[1]))
        gates[...] = mask_ref[...] * jax.nn.sigmoid(chosen)

    moves, moved = {}, []

    def move(name, src, dst):
        copy = pltpu.make_async_copy(src, dst, move_sem.at[len(moved)])
        copy.start()
        moved.append(copy)
        moves.setdefault(name, []).append(copy)

    def have(name):
        for copy in moves.pop(name):
            copy.wait()

    def line_of(image):
        return pl.ds(image * seq, seq)

    def bring(q):
        for f in range(fsdp):
            src = fulls[0].at[f, :, pl.ds(q * width, width)]
            move("w" + str(q), src, stage.at[q % 2, pl.ds(f * rows, rows), :])

    def modulated(image, index):
        return mod_ref[image : image + 1, index * width : (index + 1) * width]

    step = 32

    def normed(value, scale, shift):
        centered = value - jnp.mean(value, axis=-1, keepdims=True)
        inverse = lax.rsqrt(jnp.mean(centered * centered, axis=-1, keepdims=True) + EPSILON)
        return (centered * inverse * scale + shift).astype(jnp.bfloat16)

    def joint_here():
        for copy in first_landed:
            copy.wait_recv()
        locals_[0].wait()
        bring(0)
        bring(1)

    def norm_one(image):
        if image == 0:
            have("tokens")
        shift, scale = modulated(image, 0), 1.0 + modulated(image, 1)

        @pl.loop(0, seq // step)
        def _(i):
            line = pl.ds(pl.multiple_of(image * seq + i * step, step), step)
            h1[line, :] = normed(tokens[line, :].astype(jnp.float32), scale, shift)

        if image == images - 1:
            move("h1", h1, h1_out)

    def project(q):
        have("w" + str(q))

        @pl.loop(0, images)
        def _(image):
            line = pl.ds(pl.multiple_of(image * seq, seq), seq)
            joint[line, pl.ds(q * width, width)] = matmul(h1[line, :], stage[q % 2]).astype(jnp.bfloat16)

        if q + 2 < QUARTERS:
            bring(q + 2)
        if q == 2:
            move("joint", joint, joint_out)

    def attention(image, half):
        span = range(0, heads // 2) if half == 0 else range(heads // 2, heads)
        attend_image(joint.at[line_of(image)], gates, mixed.at[line_of(image)], lse, image, seq, heads, span)
        if image == images - 1 and half == 1:
            move("mixed", mixed, mixed_out)
            move("lse", lse, lse_out)

    def merge(image):
        if image == 0:
            have("w3")
        line = line_of(image)
        attn[line, :] = matmul(mixed[line, :], stage[1])
        gate, shift, scale = modulated(image, 2), modulated(image, 3), 1.0 + modulated(image, 4)

        @pl.loop(0, seq // step)
        def _(i):
            here = pl.ds(pl.multiple_of(image * seq + i * step, step), step)
            value = tokens[here, :].astype(jnp.float32) + gate * attn[here, :]
            middle[here, :] = value
            h2[here, :] = normed(value, scale, shift)

        move("attn", attn.at[line], attn_out.at[line])
        move("middle", middle.at[line], middle_out.at[line])
        move("h2", h2.at[line], h2_out.at[line])

    move("table", table_hbm, table_ref)
    move("ada", ada_hbm, ada_ref)
    move("tokens", tokens_ref, tokens)
    work = [joint_here] + [partial(norm_one, image) for image in range(images)]
    work += [partial(project, q) for q in range(3)]
    work += [partial(attention, image, half) for image in range(images) for half in range(2)]
    work += [partial(merge, image) for image in range(images)]
    extra = {0: cond_one, 1: cond_two, 2: cond_three, 4: cond_four}
    swaps[0].start(lambda device: ask_ref, asks.at[at.f])
    swaps[4].start(lambda device: router_ref, routers_ref.at[at.f])

    items = [(k, step) for k in range(weights) for step in range(1, ring)]
    rings = {items[0]: go(ring_copy(*items[0]))}
    locals_ = []
    for k in range(weights):
        copy = pltpu.make_async_copy(shards[k], fulls[k].at[at.f], own_sem.at[k])
        copy.start()
        locals_.append(copy)
        landed.append(go(remote(shards[k], fulls[k].at[at.f], core_s.at[k, 0], core_r.at[k, 0], at.core)))
    flights, first_landed = {}, [landed[0]]
    begin, turns = ring + 1, len(items) + 2
    done = 0
    for turn in range(turns):
        if turn < len(items):
            k, hop = items[turn]
            rings[k, hop].wait_recv()
            if turn + 1 < len(items):
                rings[items[turn + 1]] = go(ring_copy(*items[turn + 1]))
            mine = view(fulls[k], (at.shard(hop),), at.q, width)
            flights[turn] = (
                go(remote(mine, mine, x_s.at[k, hop - 1], x_r.at[k, hop - 1], at.x)),
                go(remote(mine, mine, y_s.at[k, hop - 1], y_r.at[k, hop - 1], at.y)),
            )
        if 0 <= turn - 1 < len(items):
            k, hop = items[turn - 1]
            by_x, by_y = flights[turn - 1]
            by_x.wait_recv()
            half = view(fulls[k], (at.shard(hop),), at.qx, width, part_a)
            first = go(remote(half, half, a_s.at[k, hop - 1], a_r.at[k, hop - 1], at.y))
            by_y.wait_recv()
            half = view(fulls[k], (at.shard(hop),), at.qy, width, part_b)
            second = go(remote(half, half, b_s.at[k, hop - 1], b_r.at[k, hop - 1], at.x))
            flights[turn - 1] = (first, second)
        if 0 <= turn - 2 < len(items):
            k, hop = items[turn - 2]
            for copy in flights[turn - 2]:
                copy.wait_recv()
            whole = fulls[k].at[at.shard(hop)]
            copy = go(remote(whole, whole, core_s.at[k, hop], core_r.at[k, hop], at.core))
            (landed if k else first_landed).append(copy)
        if turn in extra:
            extra[turn]()
        if turn >= begin:
            upto = -(-len(work) * (turn + 1 - begin) // (turns - begin))
            for part in work[done:upto]:
                part()
            done = upto
    for swap in far:
        swap.arrived()
    for copy in landed[1:]:
        copy.wait_recv()
    for copy in locals_[1:] + small:
        copy.wait()
    for name in ("h1", "joint", "mixed", "lse", "attn", "middle", "h2"):
        have(name)
    for swap in swaps + far:
        swap.left()
    for copy in sent:
        copy.wait_send()


def front_half(
    shards, asked, time_weight, class_table, ada_weight, routers, mask, tokens, width, images, seq, heads, dp, fsdp
):
    ring = fsdp // 2
    dma, vmem = pltpu.SemaphoreType.DMA, pltpu.VMEM
    low, f32 = jnp.bfloat16, jnp.float32
    steps = dma((3, ring - 1))
    pad, asking = asked.shape
    columns = ada_weight.shape[0]
    count = images * seq
    out = jax.ShapeDtypeStruct
    any_space, in_vmem = pl.BlockSpec(memory_space=pl.ANY), pl.BlockSpec(memory_space=vmem)
    results = [
        out((count, width), low),
        out((count, 3 * width), low),
        out((images, heads, seq), f32),
        out((count, width), low),
        out((count, width), f32),
        out((count, width), f32),
        out((count, width), low),
    ]
    return pl.pallas_call(
        partial(front_kernel, dp, fsdp, width, images, seq, heads),
        out_shape=[out((fsdp, *s.shape), s.dtype) for s in shards]
        + [
            out((pad, width), f32),
            out((pad, 6 * width), f32),
            out((fsdp, *routers.shape), routers.dtype),
            out((dp, fsdp, pad, width), low),
            out((dp, fsdp, pad, asking), low),
        ]
        + results,
        in_specs=[any_space] * 3 + [in_vmem] * 2 + [any_space] * 2 + [in_vmem] * 2 + [any_space],
        out_specs=[any_space] * 3 + [in_vmem] * 3 + [any_space] * 9,
        scratch_shapes=[
            vmem((fsdp, pad, asking), low),
            vmem((fsdp, pad, width), f32),
            vmem((fsdp, pad, width), f32),
            vmem((fsdp, pad, width), low),
            vmem((fsdp, pad, columns), f32),
            vmem((fsdp, pad, columns), f32),
            vmem((pad, 128), f32),
            vmem((count, width), low),
        ]
        + [vmem(r.shape, r.dtype) for r in results]
        + [vmem((2, width, width), low), vmem(class_table.shape, low), vmem(ada_weight.shape, low)]
        + [dma((4 * fsdp + 7 + 3 * images,))]
        + [dma((3,)), dma((3, ring)), dma((3, ring))]
        + [steps] * 10
        + [dma((5, fsdp - 1))] * 2
        + [dma((2, dp - 1))] * 2
        + [dma((2,))],
        compiler_params=pltpu.CompilerParams(
            collective_id=0, has_side_effects=True, vmem_limit_bytes=60 * 2**20
        ),
        name="front",
    )(*shards, asked, time_weight, class_table, ada_weight, routers, mask, tokens)


def window(head, size):
    low = head * size // 128 * 128
    high = -(-(head + 1) * size // 128) * 128
    spot = low + lax.broadcasted_iota(jnp.int32, (1, high - low), 1)
    own = ((spot >= head * size) & (spot < (head + 1) * size)).astype(jnp.float32).astype(jnp.bfloat16)
    return low, high - low, own


def attend_image(joint, gates, mixed, lse, image, seq, heads, span):
    width = mixed.shape[1]
    size = width // heads
    scale = size ** (-0.5)
    if span[0] == 0:
        mixed[...] = jnp.zeros((seq, width), mixed.dtype)
    for head in span:
        low, wide, own = window(head, size)
        query = joint[:, pl.ds(low, wide)] * own
        keys = joint[:, pl.ds(width + low, wide)]
        values = joint[:, pl.ds(2 * width + low, wide)] * own
        raw = times_back(keys, query) * scale
        peak = jnp.max(raw, axis=0, keepdims=True)
        expo = jnp.exp(raw - peak)
        total = jnp.sum(expo, axis=0, keepdims=True)
        lse[image, head : head + 1, :] = peak + jnp.log(total)
        probs = (expo * (1.0 / total)).astype(jnp.bfloat16)
        attended = times_rows(probs, values) * gates[image : image + 1, head : head + 1]
        mixed[:, pl.ds(low, wide)] = mixed[:, pl.ds(low, wide)] + attended.astype(jnp.bfloat16)


def attend_back_image(joint, grad_mixed, gates, lse, grad_joint, grad_gates, image, seq, heads, span):
    width = grad_mixed.shape[1]
    size = width // heads
    scale = size ** (-0.5)
    if span[0] == 0:
        grad_joint[...] = jnp.zeros((seq, 3 * width), grad_joint.dtype)

    def put(column, wide, value):
        here = pl.ds(column, wide)
        grad_joint[:, here] = grad_joint[:, here] + value.astype(jnp.bfloat16)

    for head in span:
        low, wide, own = window(head, size)
        query = joint[:, pl.ds(low, wide)] * own
        keys = joint[:, pl.ds(width + low, wide)] * own
        values = joint[:, pl.ds(2 * width + low, wide)]
        grad = grad_mixed[:, pl.ds(low, wide)] * own
        gate = gates[image, 0, head]
        probs = jnp.exp(times_back(keys, query) * scale - lse[image, head : head + 1, :])
        put(2 * width + low, wide, matmul(probs.astype(jnp.bfloat16), (grad.astype(jnp.float32) * gate).astype(jnp.bfloat16)))
        grad_probs = times_back(values, grad)
        inner = jnp.sum(grad_probs * probs, axis=0, keepdims=True)
        grad_gates[image, head : head + 1, :] = inner
        grad_scores = (probs * (grad_probs - inner) * (gate * scale)).astype(jnp.bfloat16)
        put(low, wide, times_rows(grad_scores, keys))
        put(width + low, wide, matmul(grad_scores, query))


def expand_kernel(x_ref, w_ref, active_ref, slope_ref):
    depth = x_ref.shape[1]
    tile = w_ref.shape[2]
    held = w_ref[...].reshape(depth, tile)
    rows = 128
    c = math.sqrt(2.0 / math.pi)

    for i in range(x_ref.shape[0] // rows):
        line = pl.ds(i * rows, rows)
        value = matmul(x_ref[line, :], held)
        square = value * value
        bent = jnp.tanh(value * (c + c * 0.044715 * square))
        half = 0.5 + 0.5 * bent
        active_ref[line, :] = (value * half).astype(jnp.bfloat16)
        lean = value * (0.5 - 0.5 * bent * bent) * (c + 3.0 * c * 0.044715 * square)
        slope_ref[line, :] = (half + lean).astype(jnp.bfloat16)


def expand_tokens(x, blocks, tile=512):
    count, depth = x.shape
    fsdp, rows, hidden = blocks.shape
    out = jax.ShapeDtypeStruct((count, hidden), jnp.bfloat16)
    return pl.pallas_call(
        expand_kernel,
        grid=(hidden // tile,),
        out_shape=[out, out],
        in_specs=[
            pl.BlockSpec((count, depth), lambda i: (0, 0)),
            pl.BlockSpec((fsdp, rows, tile), lambda i: (0, 0, i)),
        ],
        out_specs=[pl.BlockSpec((count, tile), lambda i: (0, i))] * 2,
        compiler_params=pltpu.CompilerParams(vmem_limit_bytes=32 * 2**20),
        name="expand",
    )(x, blocks)


def thirds(width):
    tiles = width // 128
    a, b = tiles // 3, tiles // 3
    c = tiles - a - b
    sizes = [a, b, (c + 1) // 2, c // 2]
    starts = [sum(sizes[:i]) for i in range(4)]
    return [(128 * s, 128 * n) for s, n in zip(starts, sizes)]


OWN_SLOTS = 8
PAIR_SLOTS = 4
AHEAD = 3
LAG = 2


class Reducer:
    def __init__(self, at, piece, outs, scratch, rows, width):
        self.at, self.piece, self.outs, self.width = at, piece, outs, width
        (
            self.own, self.pair, self.first_a, self.first_b, self.second_a, self.second_b,
            self.hops, self.hops_c, self.flat_a, self.flat_b, self.last_a, self.last_b, self.done,
            self.own_in, self.core_s, self.core_r, self.fa_s, self.fa_r, self.fb_s, self.fb_r,
            self.sa_s, self.sa_r, self.sb_s, self.sb_r, self.hop_s, self.hop_r, self.hopc_s, self.hopc_r,
            self.ca_s, self.ca_r, self.cb_s, self.cb_r, self.end_s, self.end_r, self.out_sem, self.credit,
        ) = scratch
        self.ring = at.ring
        self.total = 3 * self.ring * 2
        self.spans = self.halves(rows)
        self.sent, self.flights = {}, {}
        self.loose, self.outgoing = [], []
        self.cols = [pl.ds(*part) for part in thirds(width)]
        a, b = thirds(width)[1]
        self.cols_ab = pl.ds(0, a + b)
        self.cols_c = pl.ds(a + b, width - a - b)

    @staticmethod
    def halves(rows):
        top = -(-rows // 32) * 16
        return (0, top), (top, rows - top)

    def place(self, n):
        half = n % 2
        k, j = divmod(n // 2, self.ring)
        return k, j, half, self.spans[half][1]

    @staticmethod
    def scratch(rows, width, fsdp):
        ring = fsdp // 2
        total = 3 * ring * 2
        full, rows = rows, Reducer.halves(rows)[0][1]
        low, vmem, dma = jnp.bfloat16, pltpu.VMEM, pltpu.SemaphoreType.DMA
        a, b, c, d = [size for _, size in thirds(width)]
        arrays = [
            vmem((OWN_SLOTS, QUARTERS, rows, width), low),
            vmem((PAIR_SLOTS, QUARTERS, rows, width), low),
            vmem((total, 2, rows, a), low),
            vmem((total, 2, rows, b), low),
            vmem((total, rows, a), low),
            vmem((total, rows, b), low),
            vmem((3, 2, ring - 1, rows, a + b), low),
            vmem((3, 2, ring - 1, QUARTERS, rows, c + d), low),
            vmem((3, 2, 2, rows, c), low),
            vmem((3, 2, 2, rows, d), low),
            vmem((3, 2, rows, c), low),
            vmem((3, 2, rows, d), low),
            vmem((3, QUARTERS, full, width), low),
        ]
        sems = (
            [dma((total, QUARTERS))] * 3
            + [dma((total, 2))] * 4
            + [dma((total,))] * 4
            + [dma((3, 2, ring - 1))] * 4
            + [dma((3, 2, 3))] * 4
            + [dma((3, 2, 4))] * 2
            + [dma((3, 2))]
            + [pltpu.SemaphoreType.REGULAR]
        )
        return arrays + sems

    def go(self, n, *parts):
        copy = remote(*parts)
        copy.start()
        self.sent.setdefault(n, []).append(copy)
        return copy

    def prefetch(self, n):
        at = self.at
        k, j, half, size = self.place(n)
        slot, pair_slot = n % OWN_SLOTS, n % PAIR_SLOTS
        for copy in self.sent.pop(n - OWN_SLOTS, []):
            copy.wait_send()
        mine = at.shard((j + 1) % self.ring)
        other = mine + 1 - 2 * at.c
        if n >= PAIR_SLOTS:
            pl.semaphore_wait(self.credit, 1)
        brought, pairs = [], []
        span, here = pl.ds(*self.spans[half]), pl.ds(0, size)
        for q in range(QUARTERS):
            copy = pltpu.make_async_copy(self.piece(k, mine, q, span), self.own.at[slot, q, here], self.own_in.at[n, q])
            copy.start()
            brought.append(copy)
            copy = remote(
                self.piece(k, other, q, span), self.pair.at[pair_slot, q, here], self.core_s.at[n, q], self.core_r.at[n, q], at.core
            )
            copy.start()
            pairs.append(copy)
        self.loose += pairs
        self.flights[n] = (brought, pairs)

    def plane_first(self, n, slot, here, cols_a, cols_b, land_a, land_b, sems):
        at, own = self.at, self.own
        (sa, ra), (sb, rb) = sems
        return [
            self.go(n, own.at[slot, at.qd, here, cols_a], land_a.at[1, here], sa.at[1], ra.at[1], at.x),
            self.go(n, own.at[slot, at.qd, here, cols_b], land_b.at[1, here], sb.at[1], rb.at[1], at.y),
            self.go(n, own.at[slot, at.qx, here, cols_a], land_a.at[0, here], sa.at[0], ra.at[0], at.x),
            self.go(n, own.at[slot, at.qy, here, cols_b], land_b.at[0, here], sb.at[0], rb.at[0], at.y),
        ]

    def plane_second(self, n, slot, here, copies, cols_a, cols_b, land_a, land_b, next_a, next_b, sems):
        at, own = self.at, self.own
        one_d, two_d, one, two = copies
        (sa, ra), (sb, rb) = sems
        one_d.wait_recv()
        own[slot, at.qy, here, cols_a] = own[slot, at.qy, here, cols_a] + land_a[1, here]
        on_a = self.go(n, own.at[slot, at.qy, here, cols_a], next_a.at[here], sa, ra, at.y)
        two_d.wait_recv()
        own[slot, at.qx, here, cols_b] = own[slot, at.qx, here, cols_b] + land_b[1, here]
        on_b = self.go(n, own.at[slot, at.qx, here, cols_b], next_b.at[here], sb, rb, at.x)
        one.wait_recv()
        own[slot, at.q, here, cols_a] = own[slot, at.q, here, cols_a] + land_a[0, here]
        two.wait_recv()
        own[slot, at.q, here, cols_b] = own[slot, at.q, here, cols_b] + land_b[0, here]
        return [on_a, on_b]

    def plane_third(self, slot, here, copies, cols_a, cols_b, next_a, next_b):
        at, own = self.at, self.own
        for copy in copies:
            copy.wait_recv()
        own[slot, at.q, here, cols_a] = own[slot, at.q, here, cols_a] + next_a[here, :]
        own[slot, at.q, here, cols_b] = own[slot, at.q, here, cols_b] + next_b[here, :]

    def one(self, n):
        at, own, pair = self.at, self.own, self.pair
        k, j, half, size = self.place(n)
        slot, pair_slot = n % OWN_SLOTS, n % PAIR_SLOTS
        here = pl.ds(0, size)
        brought, pairs = self.flights[n]
        for q in range(QUARTERS):
            brought[q].wait()
            pairs[q].wait_recv()

        @pl.loop(0, QUARTERS)
        def _(q):
            own[slot, q, here, :] = own[slot, q, here, :] + pair[pair_slot, q, here, :]

        if n + PAIR_SLOTS < self.total:
            pl.semaphore_signal(self.credit, inc=1, device_id=at.core, device_id_type=MESH)
        a, b, c, d = self.cols
        self.flights[n] = self.plane_first(
            n, slot, here, a, b, self.first_a.at[n], self.first_b.at[n],
            ((self.fa_s.at[n], self.fa_r.at[n]), (self.fb_s.at[n], self.fb_r.at[n])),
        )
        if j > 0:
            self.flights[k, half, "c"].wait_recv()

            @pl.loop(0, QUARTERS)
            def _(q):
                own[slot, q, here, self.cols_c] = own[slot, q, here, self.cols_c] + self.hops_c[k, half, j - 1, q, here, :]

        if j < self.ring - 1:
            self.flights[k, half, "c"] = self.go(
                n, own.at[slot, slice(None), here, self.cols_c], self.hops_c.at[k, half, j, slice(None), here],
                self.hopc_s.at[k, half, j], self.hopc_r.at[k, half, j], at.up,
            )
        else:
            self.flights[k, half, "flat"] = self.plane_first(
                n, slot, here, c, d, self.flat_a.at[k, half], self.flat_b.at[k, half],
                ((self.ca_s.at[k, half], self.ca_r.at[k, half]), (self.cb_s.at[k, half], self.cb_r.at[k, half])),
            )

    def two(self, n):
        k, j, half, size = self.place(n)
        slot, here = n % OWN_SLOTS, pl.ds(0, size)
        a, b, c, d = self.cols
        self.flights[n] = self.plane_second(
            n, slot, here, self.flights[n], a, b, self.first_a.at[n], self.first_b.at[n], self.second_a.at[n], self.second_b.at[n],
            ((self.sa_s.at[n], self.sa_r.at[n]), (self.sb_s.at[n], self.sb_r.at[n])),
        )
        if j == self.ring - 1:
            self.flights[k, half, "flat"] = self.plane_second(
                n, slot, here, self.flights[k, half, "flat"], c, d, self.flat_a.at[k, half], self.flat_b.at[k, half],
                self.last_a.at[k, half], self.last_b.at[k, half],
                ((self.ca_s.at[k, half, 2], self.ca_r.at[k, half, 2]), (self.cb_s.at[k, half, 2], self.cb_r.at[k, half, 2])),
            )

    def three(self, n):
        at, own = self.at, self.own
        k, j, half, size = self.place(n)
        slot, here = n % OWN_SLOTS, pl.ds(0, size)
        a, b, c, d = self.cols
        self.plane_third(slot, here, self.flights[n], a, b, self.second_a.at[n], self.second_b.at[n])
        if j > 0:
            self.flights[k, half, "ab"].wait_recv()
            own[slot, at.q, here, self.cols_ab] = own[slot, at.q, here, self.cols_ab] + self.hops[k, half, j - 1, here, :]
        if j < self.ring - 1:
            self.flights[k, half, "ab"] = self.go(
                n, own.at[slot, at.q, here, self.cols_ab], self.hops.at[k, half, j, here],
                self.hop_s.at[k, half, j], self.hop_r.at[k, half, j], at.up,
            )
            return
        self.plane_third(slot, here, self.flights[k, half, "flat"], c, d, self.last_a.at[k, half], self.last_b.at[k, half])
        span = pl.ds(*self.spans[half])
        self.done[k, at.q, span, :] = own[slot, at.q, here, :]
        mine = self.done.at[k, at.q, span]
        sems = self.end_s.at[k, half], self.end_r.at[k, half]
        self.flights[k, half, "end"] = [
            self.keep(remote(mine, mine, sems[0].at[0], sems[1].at[0], at.x)),
            self.keep(remote(mine, mine, sems[0].at[1], sems[1].at[1], at.y)),
        ]

    def keep(self, copy):
        copy.start()
        self.loose.append(copy)
        return copy

    def four(self, n):
        at, done = self.at, self.done
        k, _, half, _ = self.place(n)
        (start_a, size_a), (start_b, size_b) = cut(self.width)
        span = pl.ds(*self.spans[half])
        sems = self.end_s.at[k, half], self.end_r.at[k, half]
        by_x, by_y = self.flights[k, half, "end"]
        by_x.wait_recv()
        part = done.at[k, at.qx, span, pl.ds(start_a, size_a)]
        first = self.keep(remote(part, part, sems[0].at[2], sems[1].at[2], at.y))
        by_y.wait_recv()
        part = done.at[k, at.qy, span, pl.ds(start_b, size_b)]
        second = self.keep(remote(part, part, sems[0].at[3], sems[1].at[3], at.x))
        self.flights[k, half, "end"] = [first, second]

    def five(self, n):
        k, _, half, _ = self.place(n)
        for copy in self.flights[k, half, "end"]:
            copy.wait_recv()
        span = pl.ds(*self.spans[half])
        copy = pltpu.make_async_copy(self.done.at[k, :, span], self.outs[k].at[:, span], self.out_sem.at[k, half])
        copy.start()
        self.outgoing.append(copy)

    def turn(self, t, held):
        if t == held:
            for n in range(held, held + AHEAD):
                self.prefetch(n)
        if t + AHEAD < self.total and (t + AHEAD < held or t >= held):
            self.prefetch(t + AHEAD)
        stages = (self.one, self.two, self.three, self.four, self.five)
        for i, stage in enumerate(stages):
            n = t - LAG * i
            if 0 <= n < self.total and (i < 3 or self.place(n)[1] == self.ring - 1):
                stage(n)

    def finish(self):
        for copy in self.outgoing:
            copy.wait()
        for copies in self.sent.values():
            for copy in copies:
                copy.wait_send()
        for copy in self.loose:
            copy.wait_send()


def back_kernel(dp, fsdp, width, images, seq, heads, *refs):
    ring = fsdp // 2
    fc2_ref, fc1_ref, joint_ref, h1_ref, tokens_ref, weight_ref = refs[:6]
    up_ref, fc1_weight_ref, held_ref, attn_ref, cotangent_ref, forward_ref = refs[6:12]
    lse_ref, gates_ref, gate_two_ref, mod_ref, factor_ref, routers_ref, ada_hbm, pre_ref, picker_ref = refs[12:21]
    logit_ref, pick_ref = refs[21:23]
    refs = refs[23:]
    outs, refs = refs[:3], refs[3:]
    all_gm_ref, all_pre_ref, grad_tokens_ref, triple_ref, middle_ref, proj_ref = refs[:6]
    refs = refs[6:]
    joint, mixed, h1, middle, grad_joint, stage, total, inner, gm_row, gms, parts, mine_in, pres, ada_ref = refs[:14]
    in_sem, out_sem, mate_s, mate_r, cousin_s, cousin_r = refs[14:20]
    at = Place(dp, fsdp)
    at.greet()
    rows = fc1_ref.shape[1]
    count = images * seq
    pad = pre_ref.shape[0]

    def piece(k, index, q, span):
        if k == 0:
            return fc2_ref.at[index, q, span]
        if k == 1:
            return fc1_ref.at[index, span, pl.ds(q * width, width)]
        line = pl.ds(pl.multiple_of(index * rows + span.start, 8), span.size)
        if q == 3:
            return proj_ref.at[line, :]
        return triple_ref.at[q, line, :]

    work = Reducer(at, piece, outs, refs[20:], rows, width)
    moves, fetched = {}, []

    def fetch(name, src, dst):
        copy = pltpu.make_async_copy(src, dst, in_sem.at[len(fetched)])
        copy.start()
        fetched.append(copy)
        moves.setdefault(name, []).append(copy)

    def have(name):
        for copy in moves.pop(name):
            copy.wait()

    def store(name, src, dst, i):
        copy = pltpu.make_async_copy(src, dst, out_sem.at[i])
        copy.start()
        moves[name] = [copy]

    for n in range(AHEAD):
        work.prefetch(n)

    def lines(image):
        return pl.ds(image * seq, seq)

    def modulated(image, index):
        return mod_ref[image : image + 1, index * width : (index + 1) * width]

    chunks = fc1_weight_ref.shape[2] // width

    def bring_up(c):
        fetch("u" + str(c), up_ref.at[:, pl.ds(c * width, width)], grad_joint.at[:, pl.ds(c % 3 * width, width)])

    def bring_fc1(c):
        for f in range(fsdp):
            src = fc1_weight_ref.at[f, :, pl.ds(c * width, width)]
            fetch("f" + str(c), src, stage.at[c % 2, pl.ds(f * rows, rows), :])

    def bring_image(image):
        fetch("image" + str(image), held_ref.at[lines(image)], middle.at[0])
        fetch("image" + str(image), attn_ref.at[lines(image)], middle.at[1])
        fetch("image" + str(image), cotangent_ref.at[lines(image)], joint.at[1, :, pl.ds(0, width)])

    for c in range(2):
        bring_up(c)
        bring_fc1(c)
    bring_up(2)
    fetch("joint0", joint_ref.at[lines(0)], joint.at[0])
    bring_image(0)

    def grow(c):
        have("u" + str(c))
        have("f" + str(c))

        @pl.loop(0, images)
        def _(image):
            line = pl.ds(pl.multiple_of(image * seq, seq), seq)
            value = times_back(grad_joint[line, pl.ds(c % 3 * width, width)], stage[c % 2])
            if c == 0:
                total[line, :] = value
            else:
                total[line, :] = total[line, :] + value

        if c + 3 < chunks:
            bring_up(c + 3)
        if c + 2 < chunks:
            bring_fc1(c + 2)
        if c == chunks - 2:
            for f in range(fsdp):
                src = weight_ref.at[f, :, pl.ds(3 * width, width)]
                fetch("proj", src, stage.at[c % 2, pl.ds(f * rows, rows), :])
            fetch("forward", forward_ref, grad_joint.at[:, pl.ds(c % 3 * width, width)])

    forward_at, grad_at, proj_at = (chunks - 2) % 3, (chunks - 1) % 3, (chunks - 2) % 2

    def norm_two(image):
        have("image" + str(image))
        scale, gate = 1.0 + modulated(image, 4), modulated(image, 2)
        step = 32

        def chunk(i, sums):
            shift_sum, gain_sum, gate_sum = sums
            line = pl.ds(pl.multiple_of(image * seq + i * step, step), step)
            here = pl.ds(pl.multiple_of(i * step, step), step)
            value = middle[0, here, :]
            grad = total[line, :] + logit_ref[line, :] * pick_ref[...]
            centered = value - jnp.mean(value, axis=-1, keepdims=True)
            inverse = lax.rsqrt(jnp.mean(centered * centered, axis=-1, keepdims=True) + EPSILON)
            normed = centered * inverse
            through = grad * scale
            back = through - jnp.mean(through, axis=-1, keepdims=True)
            back = back - normed * jnp.mean(through * normed, axis=-1, keepdims=True)
            through = joint[1, here, :width].astype(jnp.float32) + inverse * back
            total[line, :] = through
            grad_joint[line, grad_at * width : (grad_at + 1) * width] = (through * gate).astype(jnp.bfloat16)
            return (
                shift_sum + jnp.sum(grad, axis=0, keepdims=True),
                gain_sum + jnp.sum(grad * normed, axis=0, keepdims=True),
                gate_sum + jnp.sum(through * middle[1, here, :], axis=0, keepdims=True),
            )

        zero = jnp.zeros((1, width), jnp.float32)
        shift, gain, gated = lax.fori_loop(0, seq // step, chunk, (zero, zero, zero))
        for index, row in ((2, gated), (3, shift), (4, gain)):
            gm_row[image : image + 1, index * width : (index + 1) * width] = row
        store("mid" + str(image), total.at[lines(image)], middle_ref.at[lines(image)], 3 + images + image)
        if image + 1 < images:
            bring_image(image + 1)

    def mix():
        have("proj")

        @pl.loop(0, images)
        def _(image):
            line = pl.ds(pl.multiple_of(image * seq, seq), seq)
            grad = grad_joint[line, grad_at * width : (grad_at + 1) * width]
            mixed[line, :] = times_back(grad, stage[proj_at]).astype(jnp.bfloat16)

    def weigh_proj():
        have("forward")

        @pl.loop(0, width // 128)
        def _(m):
            line = pl.ds(pl.multiple_of(m * 128, 128), 128)
            column = pl.ds(pl.multiple_of(forward_at * width + m * 128, 128), 128)
            value = times_rows(grad_joint[:, column], grad_joint[:, grad_at * width : (grad_at + 1) * width])
            stage[1 - proj_at, line, :] = value.astype(jnp.bfloat16)

        store("projected", stage.at[1 - proj_at], proj_ref, 3 + 2 * images)

    fetch("h1", h1_ref, h1)
    fetch("ada", ada_hbm, ada_ref)
    inner[...] = jnp.zeros_like(inner)
    gm_row[...] = jnp.zeros_like(gm_row)

    def attention(image, half):
        slot = image % 2
        if half == 0:
            have("joint" + str(image))
            if image + 1 < images:
                fetch("joint" + str(image + 1), joint_ref.at[lines(image + 1)], joint.at[1 - slot])
        span = range(0, heads // 2) if half == 0 else range(heads // 2, heads)
        attend_back_image(
            joint.at[slot], mixed.at[lines(image)], gates_ref, lse_ref, grad_joint.at[lines(image)], inner, image, seq, heads, span
        )

    def weigh(q):
        if q == 0:
            have("h1")
            have("projected")
            fetch("tokens", tokens_ref, mixed)
        slot = q % 2
        if q >= 2:
            have("out" + str(q - 2))

        @pl.loop(0, width // 128)
        def _(m):
            line = pl.ds(pl.multiple_of(m * 128, 128), 128)
            stage[slot, line, :] = times_rows(h1[:, line], grad_joint[:, pl.ds(q * width, width)]).astype(jnp.bfloat16)

        store("out" + str(q), stage.at[slot], triple_ref.at[q], q)

    def bring_weight(q):
        for f in range(fsdp):
            fetch("w" + str(q), weight_ref.at[f, :, pl.ds(q * width, width)], stage.at[q % 2, pl.ds(f * rows, rows), :])

    def wait_terms():
        for q in (1, 2):
            have("out" + str(q))
        for image in range(images):
            have("mid" + str(image))
        bring_weight(0)
        bring_weight(1)
        fetch("middle0", middle_ref.at[lines(0)], middle.at[0])

    def spread(q):
        slot = q % 2
        have("w" + str(q))

        @pl.loop(0, images)
        def _(image):
            line = pl.ds(pl.multiple_of(image * seq, seq), seq)
            value = times_back(grad_joint[line, pl.ds(q * width, width)], stage[slot])
            if q == 0:
                total[line, :] = value
            else:
                total[line, :] = total[line, :] + value

        if q == 0:
            bring_weight(2)

    def norm(image):
        slot = image % 2
        if image == 0:
            have("tokens")
        have("middle" + str(image))
        if image + 1 < images:
            if image >= 1:
                have("done" + str(image - 1))
            fetch("middle" + str(image + 1), middle_ref.at[lines(image + 1)], middle.at[1 - slot])
        scale = 1.0 + modulated(image, 1)
        step = 32

        def chunk(i, sums):
            shift, gain = sums
            line = pl.ds(pl.multiple_of(image * seq + i * step, step), step)
            here = pl.ds(pl.multiple_of(i * step, step), step)
            value = mixed[line, :].astype(jnp.float32)
            grad = total[line, :]
            centered = value - jnp.mean(value, axis=-1, keepdims=True)
            inverse = lax.rsqrt(jnp.mean(centered * centered, axis=-1, keepdims=True) + EPSILON)
            normed = centered * inverse
            through = grad * scale
            back = through - jnp.mean(through, axis=-1, keepdims=True)
            back = back - normed * jnp.mean(through * normed, axis=-1, keepdims=True)
            middle[slot, here, :] = middle[slot, here, :] + inverse * back
            return (
                shift + jnp.sum(grad, axis=0, keepdims=True),
                gain + jnp.sum(grad * normed, axis=0, keepdims=True),
            )

        zero = jnp.zeros((1, width), jnp.float32)
        shift, gain = lax.fori_loop(0, seq // step, chunk, (zero, zero))
        store("done" + str(image), middle.at[slot], grad_tokens_ref.at[lines(image)], 3 + image)
        gm_row[image : image + 1, :width] = shift
        gm_row[image : image + 1, width : 2 * width] = gain

    mates, cousins = at.mates(), at.cousins()
    swaps = [Swap(mates, mate_s.at[i], mate_r.at[i]) for i in range(3)]
    far = [Swap(cousins, cousin_s.at[i], cousin_r.at[i]) for i in range(2)]
    small = []

    def keep(src, dst):
        copy = pltpu.make_async_copy(src, dst, out_sem.at[4 + 2 * images + len(small)])
        copy.start()
        small.append(copy)

    held = gms.shape[3]

    def tail_zero():
        gm_row[:, 5 * width :] = gate_two_ref[...]
        for f in range(fsdp):
            gms[0, f] = gm_row[:, f * held : (f + 1) * held].astype(jnp.bfloat16)
        swaps[0].start(lambda device: gms.at[0, device[1]], gms.at[1, at.f])

    def tail_one():
        have("ada")
        swaps[0].arrived()
        gms[1, at.f] = gms[0, at.f]
        every = gms[1].astype(jnp.float32).reshape(fsdp * pad, held).astype(jnp.bfloat16)
        parts[...] = matmul(every, ada_ref[...]).reshape(parts.shape)
        swaps[1].start(lambda device: parts.at[device[1]], mine_in.at[at.f])
        far[0].start(lambda device: gms.at[1], all_gm_ref.at[at.d])
        keep(gms.at[1], all_gm_ref.at[at.d])

    def tail_two():
        line = lax.broadcasted_iota(jnp.int32, (pad, 128), 0)
        gated = jnp.zeros((pad, 128), jnp.float32)
        for image in range(images):
            summed = lax.dot_general(
                jnp.ones((pad, seq), jnp.float32), inner[image], (((1,), (1,)), ((), ())),
                preferred_element_type=jnp.float32, precision=lax.Precision.HIGHEST,
            )
            gated = jnp.where(line == image, summed, gated)
        router = (gated * factor_ref[...]).astype(jnp.bfloat16)
        swaps[1].arrived()
        mine_in[at.f] = parts[at.f]
        grad_cond = jnp.sum(mine_in[...], axis=0) + times_back(router, routers_ref[...])
        pre_cond = pre_ref[...]
        sig = jax.nn.sigmoid(pre_cond)
        grad_pre = grad_cond * (sig * (1.0 + pre_cond * (1.0 - sig)))
        pres[at.f, :, :width] = (grad_pre + picker_ref[...]).astype(jnp.bfloat16)
        pres[at.f, :, width:] = router
        swaps[2].start(lambda device: pres.at[at.f], pres.at[at.f])

    def tail_three():
        swaps[2].arrived()
        far[1].start(lambda device: pres, all_pre_ref.at[at.d])
        keep(pres, all_pre_ref.at[at.d])

    early = [partial(grow, c) for c in range(chunks)] + [partial(norm_two, image) for image in range(images)]
    early += [mix, weigh_proj]
    early += [partial(attention, image, half) for image in range(images) for half in range(2)]
    early += [partial(weigh, q) for q in range(3)] + [wait_terms]
    norms = [partial(norm, image) for image in range(images)]
    late = [[partial(spread, q)] for q in range(3)] + [[step] for step in norms]
    late += [[tail_zero], [], [tail_one], [], [], [tail_two], [], [], [tail_three]]
    split = 4 * ring
    done = 0
    for t in range(work.total + 4 * LAG):
        work.turn(t, split)
        if t < split:
            upto = -(-len(early) * (t + 1) // split)
            for step in early[done:upto]:
                step()
            done = upto
        elif t - split < len(late):
            for step in late[t - split]:
                step()
    for swap in far:
        swap.arrived()
    for copy in small:
        copy.wait()
    for image in range(max(images - 2, 0), images):
        have("done" + str(image))
    for swap in swaps + far:
        swap.left()
    work.finish()


def back_half(
    terms, joint, flat_one, tokens, joint_full, grad_up, fc1_full, middle, attn, cotangent, mixed, log_total, gates, gate_two,
    modulation, factor, routers, ada_weight, pre_cond, picker, logit, pick, width, images, seq, dp, fsdp,
):
    rows = terms[1].shape[1]
    heads = gates.shape[1]
    count = images * seq
    pad = pre_cond.shape[0]
    columns = ada_weight.shape[0]
    dma, vmem = pltpu.SemaphoreType.DMA, pltpu.VMEM
    low, f32 = jnp.bfloat16, jnp.float32
    out = jax.ShapeDtypeStruct
    any_space, in_vmem = pl.BlockSpec(memory_space=pl.ANY), pl.BlockSpec(memory_space=vmem)
    in_smem = pl.BlockSpec(memory_space=pltpu.SMEM)
    return pl.pallas_call(
        partial(back_kernel, dp, fsdp, width, images, seq, heads),
        out_shape=[out((QUARTERS, rows, width), low)] * 3
        + [
            out((dp, fsdp, pad, columns), low),
            out((dp, fsdp, pad, width + 128), low),
            out((count, width), f32),
            out((3, width, width), low),
            out((count, width), f32),
            out((width, width), low),
        ],
        in_specs=[any_space] * 12 + [in_vmem, in_smem] + [in_vmem] * 4 + [any_space] + [in_vmem] * 4,
        out_specs=[any_space] * 9,
        scratch_shapes=[
            vmem((2, seq, 3 * width), low),
            vmem((count, width), low),
            vmem((count, width), low),
            vmem((2, seq, width), f32),
            vmem((count, 3 * width), low),
            vmem((2, width, width), low),
            vmem((count, width), f32),
            vmem((images, 128, seq), f32),
            vmem((pad, 6 * width), f32),
            vmem((2, fsdp, pad, columns), low),
            vmem((fsdp, pad, width), f32),
            vmem((fsdp, pad, width), f32),
            vmem((fsdp, pad, width + 128), low),
            vmem(ada_weight.shape, low),
            dma((8 * fsdp + 9 + 5 * images,)),
            dma((6 + 2 * images,)),
            dma((3, fsdp - 1)),
            dma((3, fsdp - 1)),
            dma((2, dp - 1)),
            dma((2, dp - 1)),
        ]
        + Reducer.scratch(rows, width, fsdp),
        compiler_params=pltpu.CompilerParams(
            collective_id=1, has_side_effects=True, vmem_limit_bytes=60 * 2**20
        ),
        name="back",
    )(
        *terms, joint, flat_one, tokens, joint_full, grad_up, fc1_full, middle, attn, cotangent, mixed, log_total,
        gates[:, None, :], gate_two, modulation, factor, routers, ada_weight, pre_cond, picker, logit, pick,
    )


def body(
    dp,
    fsdp,
    tokens,
    timesteps,
    labels,
    head_mask,
    keep_mask,
    cotangent,
    time_weight,
    class_table,
    ada_weight,
    head_router,
    qkv_weight,
    proj_weight,
    fc1_weight,
    fc2_weight,
    token_router,
):
    images, seq, width = tokens.shape
    heads = head_mask.shape[1]
    count = images * seq
    rows = qkv_weight.shape[0]
    hidden = fc1_weight.shape[1]
    entries = time_weight.shape[0] * fsdp
    me_fsdp = lax.axis_index("fsdp")
    pad = -(-(images + 2) // 8) * 8

    def padded(array, value=0.0):
        return jnp.pad(array, ((0, pad - images), (0, 0)), constant_values=value)

    embedded = sinusoid(timesteps, entries).astype(jnp.bfloat16)
    digits = jnp.stack([labels // DIGIT, labels % DIGIT], axis=1).astype(jnp.bfloat16)
    asked = jnp.concatenate(
        [padded(embedded), jnp.pad(padded(digits, -1.0), ((0, 0), (0, 126)))], axis=1
    )
    routers = jnp.pad(
        jnp.concatenate([head_router, token_router], axis=1), ((0, 0), (0, 127 - heads))
    )
    mask_float = head_mask.astype(jnp.float32)
    *gathered, flat_one, joint, log_total, mixed, attn, middle, flat_two = front_half(
        [
            jnp.concatenate([qkv_weight, proj_weight], axis=1),
            fc1_weight,
            fc2_weight.reshape(QUARTERS, rows, width),
        ],
        asked,
        time_weight,
        class_table.T,
        ada_weight.T,
        routers,
        padded(jnp.pad(mask_float, ((0, 0), (0, 128 - heads)))),
        tokens.reshape(count, width),
        width,
        images,
        seq,
        heads,
        dp,
        fsdp,
    )
    joint_blocks, fc1_full, fc2_full, pre_cond_pad, modulation_pad, routers_full, all_cond, all_asked = gathered
    shrink = fc2_full.reshape(hidden, width)
    routers_full = routers_full.reshape(width, 128)
    chooser, picker = routers_full[:, :heads], routers_full[:, heads : heads + 1]
    everyone = dp * fsdp * pad
    all_cond = all_cond.reshape(everyone, width)
    all_asked = all_asked.reshape(everyone, asked.shape[1])
    pre_cond = pre_cond_pad[:images]
    cond = jax.nn.silu(pre_cond).astype(jnp.bfloat16)
    gate_two = modulation_pad[:images, None, 5 * width :]
    router_sig = jax.nn.sigmoid(matmul(cond, chooser))
    head_gates = mask_float * router_sig
    middle = middle.reshape(images, seq, width)
    rate = jax.nn.sigmoid(matmul(flat_two, picker)).reshape(images, seq, 1)
    active, slope = expand_tokens(flat_two, fc1_full)
    downward = matmul(active, shrink).reshape(images, seq, width)
    kept = keep_mask.astype(jnp.float32)[:, :, None]
    kept_rate = kept * rate
    output = (middle + gate_two * kept_rate * downward).astype(jnp.bfloat16)
    grad_out = cotangent.astype(jnp.float32)
    grad_gate_two = jnp.sum(grad_out * kept_rate * downward, axis=1)
    grad_down = (grad_out * gate_two * kept_rate).astype(jnp.bfloat16).reshape(count, width)
    grad_rate = jnp.sum(grad_out * gate_two * downward, axis=-1, keepdims=True) * kept
    grad_logit = (grad_rate * rate * (1.0 - rate)).astype(jnp.bfloat16).reshape(count, 1)
    grad_shrink = times_rows(active, grad_down).astype(jnp.bfloat16)
    grad_up = (times_back(grad_down, shrink) * slope.astype(jnp.float32)).astype(jnp.bfloat16)
    grad_expand = times_rows(flat_two, grad_up).astype(jnp.bfloat16)
    grad_picker = times_rows(grad_logit, flat_two)
    picker_high = lax.reduce_precision(grad_picker, 8, 7)
    *sums, all_grad, all_pre, grad_inputs, _, _, _ = back_half(
        [
            grad_shrink.reshape(fsdp, QUARTERS, rows, width),
            grad_expand.reshape(fsdp, rows, hidden),
        ],
        joint,
        flat_one,
        tokens.reshape(count, width),
        joint_blocks,
        grad_up,
        fc1_full,
        middle.reshape(count, width),
        attn,
        cotangent.reshape(count, width),
        mixed,
        log_total,
        head_gates,
        padded(grad_gate_two),
        modulation_pad,
        padded(jnp.pad(mask_float * router_sig * (1.0 - router_sig), ((0, 0), (0, 128 - heads)))),
        routers_full,
        ada_weight.T,
        pre_cond_pad,
        jnp.pad(jnp.concatenate([picker_high, grad_picker - picker_high], axis=0), ((pad - 2, 0), (0, 0))),
        grad_logit.astype(jnp.float32),
        picker.astype(jnp.float32).reshape(1, width),
        width,
        images,
        seq,
        dp,
        fsdp,
    )
    grad_inputs = grad_inputs.reshape(images, seq, width)
    if dp > QUARTERS:
        parts = list(sums)
        for hop in range(QUARTERS, dp, QUARTERS):
            pairs = [(i, (i + hop) % dp) for i in range(dp)]
            parts = [
                part.astype(jnp.float32) + lax.ppermute(s, "dp", pairs).astype(jnp.float32)
                for part, s in zip(parts, sums)
            ]
        sums = parts
    sums = [s.astype(jnp.float32) for s in sums]
    sum_triple = jnp.concatenate([sums[2][0], sums[2][1], sums[2][2]], axis=1)
    sum_merger = sums[2][3]
    sum_expand = jnp.concatenate([sums[1][i] for i in range(QUARTERS)], axis=1)
    sum_shrink = sums[0].reshape(QUARTERS * rows, width)

    sum_ada = times_rows(all_cond, all_grad.reshape(everyone, -1))
    sum_picker = lax.dynamic_slice_in_dim(
        jnp.sum(all_pre[:, :, pad - 2 :, :width].astype(jnp.float32), axis=(0, 1, 2)), me_fsdp * rows, rows, axis=0
    )[:, None]
    is_image = (jnp.arange(pad) < images)[None, None, :, None]
    all_pre = jnp.where(is_image, all_pre, jnp.bfloat16(0.0)).reshape(everyone, -1)
    all_router = all_pre[:, width : width + heads]
    all_pre = all_pre[:, :width]
    own_entries = entries // fsdp
    all_embedded = lax.dynamic_slice_in_dim(
        all_asked[:, :entries], me_fsdp * own_entries, own_entries, axis=1
    )
    classes = jnp.arange(class_table.shape[0], dtype=jnp.float32)
    all_digits = all_asked[:, entries : entries + 2].astype(jnp.float32)
    all_labels = all_digits[:, :1] * DIGIT + all_digits[:, 1:]
    all_rows = (all_labels == classes[None, :]).astype(jnp.bfloat16)
    sum_time = times_rows(all_embedded, all_pre)
    sum_table = times_rows(
        all_rows, lax.dynamic_slice_in_dim(all_pre, me_fsdp * rows, rows, axis=1)
    )
    sum_chooser = times_rows(
        lax.dynamic_slice_in_dim(all_cond, me_fsdp * rows, rows, axis=1), all_router
    )
    return (
        output,
        grad_inputs,
        sum_time,
        sum_table,
        sum_ada,
        sum_chooser,
        sum_triple,
        sum_merger,
        sum_expand,
        sum_shrink,
        sum_picker,
    )


def solution(mesh):
    images = P(("dp", "fsdp"), None, None)
    pairs = P(("dp", "fsdp"), None)
    single = P(("dp", "fsdp"))
    by_row, by_column = P("fsdp", None), P(None, "fsdp")
    in_specs = (
        images, single, single, pairs, pairs, images,
        by_row, by_column, by_column, by_row, by_row, by_row, by_row, by_row, by_row,
    )
    out_specs = (
        images, images,
        by_row, by_column, by_column, by_row, by_row, by_row, by_row, by_row, by_row,
    )
    return jax.shard_map(
        partial(body, mesh.shape["dp"], mesh.shape["fsdp"]),
        mesh=mesh, in_specs=in_specs, out_specs=out_specs, check_vma=False,
    )
```

```python
from functools import partial
import math

import jax
import jax.numpy as jnp
from jax import lax
from jax.experimental import pallas as pl
from jax.experimental.pallas import tpu as pltpu
from jax.sharding import PartitionSpec as P

EPSILON = 1e-06
MESH = pl.DeviceIdType.MESH
QUARTERS = 4
DIGIT = 256


def sinusoid(steps, entries):
    half = entries // 2
    freqs = jnp.exp(-math.log(10000.0) * jnp.arange(half, dtype=jnp.float32) / half)
    angles = steps.astype(jnp.float32)[:, None] * freqs[None, :]
    return jnp.concatenate([jnp.cos(angles), jnp.sin(angles)], axis=1)


def layer_norm(value):
    centered = value - jnp.mean(value, axis=-1, keepdims=True)
    return centered * lax.rsqrt(jnp.mean(centered * centered, axis=-1, keepdims=True) + EPSILON)


def norm_back(value, grad):
    _, pull = jax.vjp(layer_norm, value)
    return pull(grad)[0]


def matmul(left, right):
    return jnp.dot(left, right, preferred_element_type=jnp.float32)


def times_rows(left, right):
    return lax.dot_general(
        left, right, (((0,), (0,)), ((), ())), preferred_element_type=jnp.float32
    )


def times_back(left, right):
    return lax.dot_general(
        left, right, (((1,), (1,)), ((), ())), preferred_element_type=jnp.float32
    )


class Place:
    def __init__(self, dp, fsdp):
        ring = fsdp // 2
        self.dp, self.fsdp, self.ring = dp, fsdp, ring
        d = lax.axis_index("dp")
        f = lax.axis_index("fsdp")
        self.d, self.f = d, f
        self.z = f // 2
        self.c = f % 2
        self.q = d % QUARTERS
        dx = d + 1 - 2 * (d % 2)
        dy = d + 2 - 4 * ((d // 2) % 2)
        self.qx = dx % QUARTERS
        self.qy = dy % QUARTERS
        self.qd = (self.qx + self.qy - self.q + QUARTERS) % QUARTERS
        self.core = (d, f + 1 - 2 * (f % 2))
        self.x = (dx, f)
        self.y = (dy, f)
        self.up = (d, ((self.z + 1) % ring) * 2 + self.c)
        self.down = (d, ((self.z + ring - 1) % ring) * 2 + self.c)

    def shard(self, back):
        return ((self.z + self.ring - back) % self.ring) * 2 + self.c

    def mates(self):
        return [(self.d, (self.f + offset) % self.fsdp) for offset in range(1, self.fsdp)]

    def cousins(self):
        return [((self.d + offset) % self.dp, self.f) for offset in range(1, self.dp)]

    def greet(self):
        barrier = pltpu.get_barrier_semaphore()
        near = self.mates() + self.cousins()
        for other in near:
            pl.semaphore_signal(barrier, inc=1, device_id=other, device_id_type=MESH)
        pl.semaphore_wait(barrier, len(near))


def remote(src, dst, send, recv, device):
    return pltpu.make_async_remote_copy(
        src_ref=src, dst_ref=dst, send_sem=send, recv_sem=recv, device_id=device, device_id_type=MESH
    )


class Swap:
    def __init__(self, partners, send, recv):
        self.partners, self.send, self.recv = partners, send, recv
        self.copies = []

    def start(self, source, landing):
        for i, device in enumerate(self.partners):
            copy = remote(source(device), landing, self.send.at[i], self.recv.at[i], device)
            copy.start()
            self.copies.append(copy)

    def arrived(self):
        for copy in self.copies:
            copy.wait_recv()

    def left(self):
        for copy in self.copies:
            copy.wait_send()


def cut(width):
    first = ((width // 128 + 1) // 2) * 128
    return (0, first), (first, width - first)


def view(ref, lead, q, width, part=None, span=None):
    start, size = (0, width) if part is None else part
    lines = slice(None) if span is None else pl.ds(*span)
    flat = ref.shape[-1] != width
    if flat:
        column = pl.multiple_of(q * width + start, 128)
        return ref.at[(*lead, lines, pl.ds(column, size))]
    return ref.at[(*lead, q, lines, pl.ds(start, size))]


def front_kernel(dp, fsdp, width, images, seq, heads, *refs):
    weights = 3
    ring = fsdp // 2
    shards, refs = refs[:weights], refs[weights:]
    ask_ref, time_ref, table_hbm, ada_hbm, router_ref, mask_ref, tokens_ref = refs[:7]
    refs = refs[7:]
    fulls, refs = refs[:weights], refs[weights:]
    pre_ref, mod_ref, routers_ref, all_cond_ref, all_ask_ref = refs[:5]
    h1_out, joint_out, lse_out, mixed_out, attn_out, middle_out, h2_out, active_out, slope_out = refs[5:14]
    refs = refs[14:]
    asks, parts, mine_in, conds, columns, mods, gates = refs[:7]
    tokens, h1, joint, lse, mixed, attn, middle, h2, stage, table_ref, ada_ref, actives, slopes, move_sem = refs[7:21]
    refs = refs[21:]
    (own_sem, core_s, core_r, ring_s, ring_r, x_s, x_r, y_s, y_r, a_s, a_r, b_s, b_r) = refs[:13]
    mate_s, mate_r, cousin_s, cousin_r, small_sem = refs[13:]
    at = Place(dp, fsdp)
    part_a, part_b = cut(width)
    at.greet()
    sent = []
    mates, cousins = at.mates(), at.cousins()
    swaps = [Swap(mates, mate_s.at[i], mate_r.at[i]) for i in range(5)]
    far = [Swap(cousins, cousin_s.at[i], cousin_r.at[i]) for i in range(2)]
    pad = ask_ref.shape[0]
    group = fsdp * pad
    rows = table_ref.shape[0]
    spans = Reducer.halves(rows)
    chunks = shards[1].shape[1] // width

    def go(copy):
        copy.start()
        sent.append(copy)
        return copy

    def ring_copy(k, hop, half):
        index = at.shard(hop - 1)
        src = (shards[k], ()) if hop == 1 else (fulls[k], (index,))
        dst = view(fulls[k], (index,), at.q, width, span=spans[half])
        sems = ring_s.at[k, hop - 1, half], ring_r.at[k, hop - 1, half]
        return remote(view(*src, at.q, width, span=spans[half]), dst, *sems, at.up)

    small = []

    def keep(src, dst):
        copy = pltpu.make_async_copy(src, dst, small_sem.at[len(small)])
        copy.start()
        small.append(copy)

    def cond_one():
        have("table")
        swaps[0].arrived()
        asks[at.f] = ask_ref[...]
        every = asks[...].astype(jnp.float32).reshape(group, asks.shape[2])
        entries = every.shape[1] - 128
        own_rows = time_ref.shape[0]
        lanes = lax.broadcasted_iota(jnp.int32, (group, entries), 1)
        held = (lanes >= at.f * own_rows) & (lanes < (at.f + 1) * own_rows)
        embedded = jnp.where(held, every[:, :entries], 0.0).astype(jnp.bfloat16)
        stacked = jnp.concatenate([time_ref[...]] * fsdp, axis=0)
        label = (every[:, entries : entries + 1] * DIGIT + every[:, entries + 1 : entries + 2]).astype(jnp.int32)
        classes = table_ref.shape[1]
        picks = (label == lax.broadcasted_iota(jnp.int32, (group, classes), 1)).astype(jnp.float32)
        picked = times_back(picks.astype(jnp.bfloat16), table_ref[...]).astype(jnp.bfloat16)
        spot = lax.broadcasted_iota(jnp.int32, (rows, width), 1)
        line = lax.broadcasted_iota(jnp.int32, (rows, width), 0)
        place = (spot == line + at.f * rows).astype(jnp.float32).astype(jnp.bfloat16)
        partial_sum = matmul(embedded, stacked) + matmul(picked, place)
        parts[...] = partial_sum.reshape(fsdp, pad, width)
        swaps[1].start(lambda device: parts.at[device[1]], mine_in.at[at.f])
        far[1].start(lambda device: asks, all_ask_ref.at[at.d])
        keep(asks, all_ask_ref.at[at.d])

    def cond_two():
        swaps[1].arrived()
        mine_in[at.f] = parts[at.f]
        pre_cond = jnp.sum(mine_in[...], axis=0)
        pre_ref[...] = pre_cond
        conds[at.f] = (pre_cond * jax.nn.sigmoid(pre_cond)).astype(jnp.bfloat16)
        swaps[2].start(lambda device: conds.at[at.f], conds.at[at.f])

    def cond_three():
        have("ada")
        swaps[2].arrived()
        every = conds[...].astype(jnp.float32).reshape(group, width).astype(jnp.bfloat16)
        columns[...] = times_back(every, ada_ref[...]).reshape(columns.shape)
        swaps[3].start(lambda device: columns.at[device[1]], mods.at[at.f])
        far[0].start(lambda device: conds, all_cond_ref.at[at.d])
        keep(conds, all_cond_ref.at[at.d])

    def cond_four():
        swaps[3].arrived()
        swaps[4].arrived()
        mods[at.f] = columns[at.f]
        routers_ref[at.f] = router_ref[...]
        held = mods.shape[2]
        for f in range(fsdp):
            mod_ref[:, f * held : (f + 1) * held] = mods[f]
        chosen = matmul(conds[at.f], routers_ref[...].reshape(width, router_ref.shape[1]))
        gates[...] = mask_ref[...] * jax.nn.sigmoid(chosen)

    moves, moved = {}, []

    def move(name, src, dst):
        copy = pltpu.make_async_copy(src, dst, move_sem.at[len(moved)])
        copy.start()
        moved.append(copy)
        moves.setdefault(name, []).append(copy)

    def have(name):
        for copy in moves.pop(name):
            copy.wait()

    def line_of(image):
        return pl.ds(image * seq, seq)

    def bring(q):
        for f in range(fsdp):
            src = fulls[0].at[f, :, pl.ds(q * width, width)]
            move("w" + str(q), src, stage.at[q % 2, pl.ds(f * rows, rows), :])

    def modulated(image, index):
        return mod_ref[image : image + 1, index * width : (index + 1) * width]

    step = 32

    def normed(value, scale, shift):
        centered = value - jnp.mean(value, axis=-1, keepdims=True)
        inverse = lax.rsqrt(jnp.mean(centered * centered, axis=-1, keepdims=True) + EPSILON)
        return (centered * inverse * scale + shift).astype(jnp.bfloat16)

    def joint_here():
        for copy in landed[0]:
            copy.wait_recv()
        locals_[0].wait()
        bring(0)
        bring(1)

    def norm_one(image):
        if image == 0:
            have("tokens")
        shift, scale = modulated(image, 0), 1.0 + modulated(image, 1)

        @pl.loop(0, seq // step)
        def _(i):
            line = pl.ds(pl.multiple_of(image * seq + i * step, step), step)
            h1[line, :] = normed(tokens[line, :].astype(jnp.float32), scale, shift)

        if image == images - 1:
            move("h1", h1, h1_out)

    def project(q):
        have("w" + str(q))

        @pl.loop(0, images)
        def _(image):
            line = pl.ds(pl.multiple_of(image * seq, seq), seq)
            joint[line, pl.ds(q * width, width)] = matmul(h1[line, :], stage[q % 2]).astype(jnp.bfloat16)

        if q + 2 < QUARTERS:
            bring(q + 2)
        if q == 2:
            move("joint", joint, joint_out)

    def attention(image, half):
        span = range(0, heads // 2) if half == 0 else range(heads // 2, heads)
        attend_image(joint.at[line_of(image)], gates, mixed.at[line_of(image)], lse, image, seq, heads, span)
        if image == images - 1 and half == 1:
            move("mixed", mixed, mixed_out)
            move("lse", lse, lse_out)

    def merge(image):
        if image == 0:
            have("w3")
        line = line_of(image)
        attn[line, :] = matmul(mixed[line, :], stage[1])
        gate, shift, scale = modulated(image, 2), modulated(image, 3), 1.0 + modulated(image, 4)

        @pl.loop(0, seq // step)
        def _(i):
            here = pl.ds(pl.multiple_of(image * seq + i * step, step), step)
            value = tokens[here, :].astype(jnp.float32) + gate * attn[here, :]
            middle[here, :] = value
            h2[here, :] = normed(value, scale, shift)

        move("attn", attn.at[line], attn_out.at[line])
        move("middle", middle.at[line], middle_out.at[line])
        move("h2", h2.at[line], h2_out.at[line])

    def bring_fc1(c):
        for f in range(fsdp):
            src = fulls[1].at[f, :, pl.ds(c * width, width)]
            move("e" + str(c), src, stage.at[c % 2, pl.ds(f * rows, rows), :])

    def fc1_here():
        for copy in landed[1]:
            copy.wait_recv()
        locals_[1].wait()
        bring_fc1(0)
        bring_fc1(1)

    def expand(c):
        slot = c % 2
        have("e" + str(c))
        if c >= 2:
            have("active" + str(c - 2))
        bend = math.sqrt(2.0 / math.pi)
        size = 128
        pair = 2 if images * seq % (2 * size) == 0 else 1

        @pl.loop(0, images * seq // (pair * size))
        def _(i):
            for inner in range(pair):
                line = pl.ds(pl.multiple_of((i * pair + inner) * size, size), size)
                value = matmul(h2[line, :], stage[slot])
                square = value * value
                bent = jnp.tanh(value * (bend + bend * 0.044715 * square))
                half = 0.5 + 0.5 * bent
                actives[slot, line, :] = (value * half).astype(jnp.bfloat16)
                lean = value * (0.5 - 0.5 * bent * bent) * (bend + 3.0 * bend * 0.044715 * square)
                slopes[slot, line, :] = (half + lean).astype(jnp.bfloat16)

        if c + 2 < chunks:
            bring_fc1(c + 2)
        columns_of = pl.ds(c * width, width)
        move("active" + str(c), actives.at[slot], active_out.at[:, columns_of])
        move("active" + str(c), slopes.at[slot], slope_out.at[:, columns_of])

    move("table", table_hbm, table_ref)
    move("ada", ada_hbm, ada_ref)
    move("tokens", tokens_ref, tokens)
    work = [joint_here] + [partial(norm_one, image) for image in range(images)]
    work += [partial(project, q) for q in range(3)]
    work += [partial(attention, image, half) for image in range(images) for half in range(2)]
    work += [partial(merge, image) for image in range(images)]
    extra = {1: cond_one, 3: cond_two, 5: cond_three, 8: cond_four}
    swaps[0].start(lambda device: ask_ref, asks.at[at.f])
    swaps[4].start(lambda device: router_ref, routers_ref.at[at.f])

    items = [(k, hop, half) for k in range(weights) for hop in range(1, ring) for half in range(2)]
    rings = {item: go(ring_copy(*item)) for item in items[:2]}
    locals_, landed = [], [[], [], []]
    for k in range(weights):
        copy = pltpu.make_async_copy(shards[k], fulls[k].at[at.f], own_sem.at[k])
        copy.start()
        locals_.append(copy)
        landed[k].append(go(remote(shards[k], fulls[k].at[at.f], core_s.at[k, 0, 0], core_r.at[k, 0, 0], at.core)))
    flights = {}
    each = 2 * (ring - 1)
    begin, second = each + 2 * LAG - 1, 2 * each + 2 * LAG
    done = 0
    for turn in range(len(items) + 2 * LAG):
        if turn < len(items):
            k, hop, half = items[turn]
            rings[items[turn]].wait_recv()
            if turn + 2 < len(items):
                rings[items[turn + 2]] = go(ring_copy(*items[turn + 2]))
            mine = view(fulls[k], (at.shard(hop),), at.q, width, span=spans[half])
            place = (k, hop - 1, half)
            flights[turn] = (
                go(remote(mine, mine, x_s.at[place], x_r.at[place], at.x)),
                go(remote(mine, mine, y_s.at[place], y_r.at[place], at.y)),
            )
        n = turn - LAG
        if 0 <= n < len(items):
            k, hop, half = items[n]
            place = (k, hop - 1, half)
            by_x, by_y = flights[n]
            by_x.wait_recv()
            part = view(fulls[k], (at.shard(hop),), at.qx, width, part_a, spans[half])
            first = go(remote(part, part, a_s.at[place], a_r.at[place], at.y))
            by_y.wait_recv()
            part = view(fulls[k], (at.shard(hop),), at.qy, width, part_b, spans[half])
            flights[n] = (first, go(remote(part, part, b_s.at[place], b_r.at[place], at.x)))
        n = turn - 2 * LAG
        if 0 <= n < len(items):
            k, hop, half = items[n]
            for copy in flights[n]:
                copy.wait_recv()
            span = pl.ds(*spans[half])
            whole = fulls[k].at[(at.shard(hop), span) if k < 2 else (at.shard(hop), slice(None), span)]
            landed[k].append(go(remote(whole, whole, core_s.at[k, hop, half], core_r.at[k, hop, half], at.core)))
        if turn in extra:
            extra[turn]()
        if begin <= turn < second:
            upto = -(-len(work) * (turn + 1 - begin) // (second - begin))
            for part in work[done:upto]:
                part()
            done = upto
        elif turn == second:
            fc1_here()
        elif second < turn <= second + chunks:
            expand(turn - second - 1)
    for swap in far:
        swap.arrived()
    for copy in landed[2]:
        copy.wait_recv()
    for copy in locals_[2:] + small:
        copy.wait()
    for c in range(max(chunks - 2, 0), chunks):
        have("active" + str(c))
    for name in ("h1", "joint", "mixed", "lse", "attn", "middle", "h2"):
        have(name)
    for swap in swaps + far:
        swap.left()
    for copy in sent:
        copy.wait_send()


def front_half(
    shards, asked, time_weight, class_table, ada_weight, routers, mask, tokens, width, images, seq, heads, dp, fsdp
):
    ring = fsdp // 2
    dma, vmem = pltpu.SemaphoreType.DMA, pltpu.VMEM
    low, f32 = jnp.bfloat16, jnp.float32
    steps = dma((3, ring - 1, 2))
    hidden = shards[1].shape[1]
    pad, asking = asked.shape
    columns = ada_weight.shape[0]
    count = images * seq
    out = jax.ShapeDtypeStruct
    any_space, in_vmem = pl.BlockSpec(memory_space=pl.ANY), pl.BlockSpec(memory_space=vmem)
    results = [
        out((count, width), low),
        out((count, 3 * width), low),
        out((images, heads, seq), f32),
        out((count, width), low),
        out((count, width), f32),
        out((count, width), f32),
        out((count, width), low),
    ]
    return pl.pallas_call(
        partial(front_kernel, dp, fsdp, width, images, seq, heads),
        out_shape=[out((fsdp, *s.shape), s.dtype) for s in shards]
        + [
            out((pad, width), f32),
            out((pad, 6 * width), f32),
            out((fsdp, *routers.shape), routers.dtype),
            out((dp, fsdp, pad, width), low),
            out((dp, fsdp, pad, asking), low),
        ]
        + results
        + [out((count, hidden), low)] * 2,
        in_specs=[any_space] * 3 + [in_vmem] * 2 + [any_space] * 2 + [in_vmem] * 2 + [any_space],
        out_specs=[any_space] * 3 + [in_vmem] * 3 + [any_space] * 11,
        scratch_shapes=[
            vmem((fsdp, pad, asking), low),
            vmem((fsdp, pad, width), f32),
            vmem((fsdp, pad, width), f32),
            vmem((fsdp, pad, width), low),
            vmem((fsdp, pad, columns), f32),
            vmem((fsdp, pad, columns), f32),
            vmem((pad, 128), f32),
            vmem((count, width), low),
        ]
        + [vmem(r.shape, r.dtype) for r in results]
        + [vmem((2, width, width), low), vmem(class_table.shape, low), vmem(ada_weight.shape, low)]
        + [vmem((2, count, width), low)] * 2
        + [dma((8 * fsdp + 15 + 3 * images,))]
        + [dma((3,)), dma((3, ring, 2)), dma((3, ring, 2))]
        + [steps] * 10
        + [dma((5, fsdp - 1))] * 2
        + [dma((2, dp - 1))] * 2
        + [dma((2,))],
        compiler_params=pltpu.CompilerParams(
            collective_id=0, has_side_effects=True, vmem_limit_bytes=60 * 2**20
        ),
        name="front",
    )(*shards, asked, time_weight, class_table, ada_weight, routers, mask, tokens)


def window(head, size):
    low = head * size // 128 * 128
    high = -(-(head + 1) * size // 128) * 128
    spot = low + lax.broadcasted_iota(jnp.int32, (1, high - low), 1)
    own = ((spot >= head * size) & (spot < (head + 1) * size)).astype(jnp.float32).astype(jnp.bfloat16)
    return low, high - low, own


def attend_image(joint, gates, mixed, lse, image, seq, heads, span):
    width = mixed.shape[1]
    size = width // heads
    scale = size ** (-0.5)
    if span[0] == 0:
        mixed[...] = jnp.zeros((seq, width), mixed.dtype)
    for head in span:
        low, wide, own = window(head, size)
        query = joint[:, pl.ds(low, wide)] * own
        keys = joint[:, pl.ds(width + low, wide)]
        values = joint[:, pl.ds(2 * width + low, wide)] * own
        raw = times_back(keys, query) * scale
        peak = jnp.max(raw, axis=0, keepdims=True)
        expo = jnp.exp(raw - peak)
        total = jnp.sum(expo, axis=0, keepdims=True)
        lse[image, head : head + 1, :] = peak + jnp.log(total)
        probs = (expo * (1.0 / total)).astype(jnp.bfloat16)
        attended = times_rows(probs, values) * gates[image : image + 1, head : head + 1]
        mixed[:, pl.ds(low, wide)] = mixed[:, pl.ds(low, wide)] + attended.astype(jnp.bfloat16)


def attend_back_image(joint, grad_mixed, gates, lse, grad_joint, grad_gates, image, seq, heads, span):
    width = grad_mixed.shape[1]
    size = width // heads
    scale = size ** (-0.5)
    if span[0] == 0:
        grad_joint[...] = jnp.zeros((seq, 3 * width), grad_joint.dtype)

    def put(column, wide, value):
        here = pl.ds(column, wide)
        grad_joint[:, here] = grad_joint[:, here] + value.astype(jnp.bfloat16)

    for head in span:
        low, wide, own = window(head, size)
        query = joint[:, pl.ds(low, wide)] * own
        keys = joint[:, pl.ds(width + low, wide)] * own
        values = joint[:, pl.ds(2 * width + low, wide)]
        grad = grad_mixed[:, pl.ds(low, wide)] * own
        gate = gates[image, 0, head]
        probs = jnp.exp(times_back(keys, query) * scale - lse[image, head : head + 1, :])
        put(2 * width + low, wide, matmul(probs.astype(jnp.bfloat16), (grad.astype(jnp.float32) * gate).astype(jnp.bfloat16)))
        grad_probs = times_back(values, grad)
        inner = jnp.sum(grad_probs * probs, axis=0, keepdims=True)
        grad_gates[image, head : head + 1, :] = inner
        grad_scores = (probs * (grad_probs - inner) * (gate * scale)).astype(jnp.bfloat16)
        put(low, wide, times_rows(grad_scores, keys))
        put(width + low, wide, matmul(grad_scores, query))


def thirds(width):
    tiles = width // 128
    a, b = tiles // 3, tiles // 3
    c = tiles - a - b
    sizes = [a, b, (c + 1) // 2, c // 2]
    starts = [sum(sizes[:i]) for i in range(4)]
    return [(128 * s, 128 * n) for s, n in zip(starts, sizes)]


OWN_SLOTS = 8
PAIR_SLOTS = 4
AHEAD = 3
LAG = 2


class Reducer:
    def __init__(self, at, piece, outs, scratch, rows, width):
        self.at, self.piece, self.outs, self.width = at, piece, outs, width
        (
            self.own, self.pair, self.first_a, self.first_b, self.second_a, self.second_b,
            self.hops, self.hops_c, self.flat_a, self.flat_b, self.last_a, self.last_b, self.done,
            self.own_in, self.core_s, self.core_r, self.fa_s, self.fa_r, self.fb_s, self.fb_r,
            self.sa_s, self.sa_r, self.sb_s, self.sb_r, self.hop_s, self.hop_r, self.hopc_s, self.hopc_r,
            self.ca_s, self.ca_r, self.cb_s, self.cb_r, self.end_s, self.end_r, self.out_sem, self.credit,
        ) = scratch
        self.ring = at.ring
        self.total = 3 * self.ring * 2
        self.spans = self.halves(rows)
        self.sent, self.flights = {}, {}
        self.loose, self.outgoing = [], []
        self.cols = [pl.ds(*part) for part in thirds(width)]
        a, b = thirds(width)[1]
        self.cols_ab = pl.ds(0, a + b)
        self.cols_c = pl.ds(a + b, width - a - b)

    @staticmethod
    def halves(rows):
        top = -(-rows // 32) * 16
        return (0, top), (top, rows - top)

    def place(self, n):
        half = n % 2
        k, j = divmod(n // 2, self.ring)
        return k, j, half, self.spans[half][1]

    @staticmethod
    def scratch(rows, width, fsdp):
        ring = fsdp // 2
        total = 3 * ring * 2
        full, rows = rows, Reducer.halves(rows)[0][1]
        low, vmem, dma = jnp.bfloat16, pltpu.VMEM, pltpu.SemaphoreType.DMA
        a, b, c, d = [size for _, size in thirds(width)]
        arrays = [
            vmem((OWN_SLOTS, QUARTERS, rows, width), low),
            vmem((PAIR_SLOTS, QUARTERS, rows, width), low),
            vmem((total, 2, rows, a), low),
            vmem((total, 2, rows, b), low),
            vmem((total, rows, a), low),
            vmem((total, rows, b), low),
            vmem((3, 2, ring - 1, rows, a + b), low),
            vmem((3, 2, ring - 1, QUARTERS, rows, c + d), low),
            vmem((3, 2, 2, rows, c), low),
            vmem((3, 2, 2, rows, d), low),
            vmem((3, 2, rows, c), low),
            vmem((3, 2, rows, d), low),
            vmem((3, QUARTERS, full, width), low),
        ]
        sems = (
            [dma((total, QUARTERS))] * 3
            + [dma((total, 2))] * 4
            + [dma((total,))] * 4
            + [dma((3, 2, ring - 1))] * 4
            + [dma((3, 2, 3))] * 4
            + [dma((3, 2, 4))] * 2
            + [dma((3, 2))]
            + [pltpu.SemaphoreType.REGULAR]
        )
        return arrays + sems

    def go(self, n, *parts):
        copy = remote(*parts)
        copy.start()
        self.sent.setdefault(n, []).append(copy)
        return copy

    def prefetch(self, n):
        at = self.at
        k, j, half, size = self.place(n)
        slot, pair_slot = n % OWN_SLOTS, n % PAIR_SLOTS
        for copy in self.sent.pop(n - OWN_SLOTS, []):
            copy.wait_send()
        mine = at.shard((j + 1) % self.ring)
        other = mine + 1 - 2 * at.c
        if n >= PAIR_SLOTS:
            pl.semaphore_wait(self.credit, 1)
        brought, pairs = [], []
        span, here = pl.ds(*self.spans[half]), pl.ds(0, size)
        for q in range(QUARTERS):
            copy = pltpu.make_async_copy(self.piece(k, mine, q, span), self.own.at[slot, q, here], self.own_in.at[n, q])
            copy.start()
            brought.append(copy)
            copy = remote(
                self.piece(k, other, q, span), self.pair.at[pair_slot, q, here], self.core_s.at[n, q], self.core_r.at[n, q], at.core
            )
            copy.start()
            pairs.append(copy)
        self.loose += pairs
        self.flights[n] = (brought, pairs)

    def plane_first(self, n, slot, here, cols_a, cols_b, land_a, land_b, sems):
        at, own = self.at, self.own
        (sa, ra), (sb, rb) = sems
        return [
            self.go(n, own.at[slot, at.qd, here, cols_a], land_a.at[1, here], sa.at[1], ra.at[1], at.x),
            self.go(n, own.at[slot, at.qd, here, cols_b], land_b.at[1, here], sb.at[1], rb.at[1], at.y),
            self.go(n, own.at[slot, at.qx, here, cols_a], land_a.at[0, here], sa.at[0], ra.at[0], at.x),
            self.go(n, own.at[slot, at.qy, here, cols_b], land_b.at[0, here], sb.at[0], rb.at[0], at.y),
        ]

    def plane_second(self, n, slot, here, copies, cols_a, cols_b, land_a, land_b, next_a, next_b, sems):
        at, own = self.at, self.own
        one_d, two_d, one, two = copies
        (sa, ra), (sb, rb) = sems
        one_d.wait_recv()
        own[slot, at.qy, here, cols_a] = own[slot, at.qy, here, cols_a] + land_a[1, here]
        on_a = self.go(n, own.at[slot, at.qy, here, cols_a], next_a.at[here], sa, ra, at.y)
        two_d.wait_recv()
        own[slot, at.qx, here, cols_b] = own[slot, at.qx, here, cols_b] + land_b[1, here]
        on_b = self.go(n, own.at[slot, at.qx, here, cols_b], next_b.at[here], sb, rb, at.x)
        one.wait_recv()
        own[slot, at.q, here, cols_a] = own[slot, at.q, here, cols_a] + land_a[0, here]
        two.wait_recv()
        own[slot, at.q, here, cols_b] = own[slot, at.q, here, cols_b] + land_b[0, here]
        return [on_a, on_b]

    def plane_third(self, slot, here, copies, cols_a, cols_b, next_a, next_b):
        at, own = self.at, self.own
        for copy in copies:
            copy.wait_recv()
        own[slot, at.q, here, cols_a] = own[slot, at.q, here, cols_a] + next_a[here, :]
        own[slot, at.q, here, cols_b] = own[slot, at.q, here, cols_b] + next_b[here, :]

    def one(self, n):
        at, own, pair = self.at, self.own, self.pair
        k, j, half, size = self.place(n)
        slot, pair_slot = n % OWN_SLOTS, n % PAIR_SLOTS
        here = pl.ds(0, size)
        brought, pairs = self.flights[n]
        for q in range(QUARTERS):
            brought[q].wait()
            pairs[q].wait_recv()

        @pl.loop(0, QUARTERS)
        def _(q):
            own[slot, q, here, :] = own[slot, q, here, :] + pair[pair_slot, q, here, :]

        if n + PAIR_SLOTS < self.total:
            pl.semaphore_signal(self.credit, inc=1, device_id=at.core, device_id_type=MESH)
        a, b, c, d = self.cols
        self.flights[n] = self.plane_first(
            n, slot, here, a, b, self.first_a.at[n], self.first_b.at[n],
            ((self.fa_s.at[n], self.fa_r.at[n]), (self.fb_s.at[n], self.fb_r.at[n])),
        )
        if j > 0:
            self.flights[k, half, "c"].wait_recv()

            @pl.loop(0, QUARTERS)
            def _(q):
                own[slot, q, here, self.cols_c] = own[slot, q, here, self.cols_c] + self.hops_c[k, half, j - 1, q, here, :]

        if j < self.ring - 1:
            self.flights[k, half, "c"] = self.go(
                n, own.at[slot, slice(None), here, self.cols_c], self.hops_c.at[k, half, j, slice(None), here],
                self.hopc_s.at[k, half, j], self.hopc_r.at[k, half, j], at.up,
            )
        else:
            self.flights[k, half, "flat"] = self.plane_first(
                n, slot, here, c, d, self.flat_a.at[k, half], self.flat_b.at[k, half],
                ((self.ca_s.at[k, half], self.ca_r.at[k, half]), (self.cb_s.at[k, half], self.cb_r.at[k, half])),
            )

    def two(self, n):
        k, j, half, size = self.place(n)
        slot, here = n % OWN_SLOTS, pl.ds(0, size)
        a, b, c, d = self.cols
        self.flights[n] = self.plane_second(
            n, slot, here, self.flights[n], a, b, self.first_a.at[n], self.first_b.at[n], self.second_a.at[n], self.second_b.at[n],
            ((self.sa_s.at[n], self.sa_r.at[n]), (self.sb_s.at[n], self.sb_r.at[n])),
        )
        if j == self.ring - 1:
            self.flights[k, half, "flat"] = self.plane_second(
                n, slot, here, self.flights[k, half, "flat"], c, d, self.flat_a.at[k, half], self.flat_b.at[k, half],
                self.last_a.at[k, half], self.last_b.at[k, half],
                ((self.ca_s.at[k, half, 2], self.ca_r.at[k, half, 2]), (self.cb_s.at[k, half, 2], self.cb_r.at[k, half, 2])),
            )

    def three(self, n):
        at, own = self.at, self.own
        k, j, half, size = self.place(n)
        slot, here = n % OWN_SLOTS, pl.ds(0, size)
        a, b, c, d = self.cols
        self.plane_third(slot, here, self.flights[n], a, b, self.second_a.at[n], self.second_b.at[n])
        if j > 0:
            self.flights[k, half, "ab"].wait_recv()
            own[slot, at.q, here, self.cols_ab] = own[slot, at.q, here, self.cols_ab] + self.hops[k, half, j - 1, here, :]
        if j < self.ring - 1:
            self.flights[k, half, "ab"] = self.go(
                n, own.at[slot, at.q, here, self.cols_ab], self.hops.at[k, half, j, here],
                self.hop_s.at[k, half, j], self.hop_r.at[k, half, j], at.up,
            )
            return
        self.plane_third(slot, here, self.flights[k, half, "flat"], c, d, self.last_a.at[k, half], self.last_b.at[k, half])
        span = pl.ds(*self.spans[half])
        self.done[k, at.q, span, :] = own[slot, at.q, here, :]
        mine = self.done.at[k, at.q, span]
        sems = self.end_s.at[k, half], self.end_r.at[k, half]
        self.flights[k, half, "end"] = [
            self.keep(remote(mine, mine, sems[0].at[0], sems[1].at[0], at.x)),
            self.keep(remote(mine, mine, sems[0].at[1], sems[1].at[1], at.y)),
        ]

    def keep(self, copy):
        copy.start()
        self.loose.append(copy)
        return copy

    def four(self, n):
        at, done = self.at, self.done
        k, _, half, _ = self.place(n)
        (start_a, size_a), (start_b, size_b) = cut(self.width)
        span = pl.ds(*self.spans[half])
        sems = self.end_s.at[k, half], self.end_r.at[k, half]
        by_x, by_y = self.flights[k, half, "end"]
        by_x.wait_recv()
        part = done.at[k, at.qx, span, pl.ds(start_a, size_a)]
        first = self.keep(remote(part, part, sems[0].at[2], sems[1].at[2], at.y))
        by_y.wait_recv()
        part = done.at[k, at.qy, span, pl.ds(start_b, size_b)]
        second = self.keep(remote(part, part, sems[0].at[3], sems[1].at[3], at.x))
        self.flights[k, half, "end"] = [first, second]

    def five(self, n):
        k, _, half, _ = self.place(n)
        for copy in self.flights[k, half, "end"]:
            copy.wait_recv()
        span = pl.ds(*self.spans[half])
        copy = pltpu.make_async_copy(self.done.at[k, :, span], self.outs[k].at[:, span], self.out_sem.at[k, half])
        copy.start()
        self.outgoing.append(copy)

    def turn(self, t, held):
        if t == held:
            for n in range(held, held + AHEAD):
                self.prefetch(n)
        if t + AHEAD < self.total and (t + AHEAD < held or t >= held):
            self.prefetch(t + AHEAD)
        stages = (self.one, self.two, self.three, self.four, self.five)
        for i, stage in enumerate(stages):
            n = t - LAG * i
            if 0 <= n < self.total and (i < 3 or self.place(n)[1] == self.ring - 1):
                stage(n)

    def finish(self):
        for copy in self.outgoing:
            copy.wait()
        for copies in self.sent.values():
            for copy in copies:
                copy.wait_send()
        for copy in self.loose:
            copy.wait_send()


def back_kernel(dp, fsdp, width, images, seq, heads, *refs):
    ring = fsdp // 2
    fc2_ref, fc1_ref, joint_ref, h1_ref, tokens_ref, weight_ref = refs[:6]
    up_ref, fc1_weight_ref, held_ref, attn_ref, cotangent_ref, forward_ref = refs[6:12]
    lse_ref, gates_ref, gate_two_ref, mod_ref, factor_ref, routers_ref, ada_hbm, pre_ref, picker_ref = refs[12:21]
    logit_ref, pick_ref = refs[21:23]
    refs = refs[23:]
    outs, refs = refs[:3], refs[3:]
    all_gm_ref, all_pre_ref, grad_tokens_ref, triple_ref, middle_ref, proj_ref = refs[:6]
    refs = refs[6:]
    joint, mixed, h1, middle, grad_joint, stage, total, inner, gm_row, gms, parts, mine_in, pres, ada_ref = refs[:14]
    in_sem, out_sem, mate_s, mate_r, cousin_s, cousin_r = refs[14:20]
    at = Place(dp, fsdp)
    at.greet()
    rows = fc1_ref.shape[1]
    count = images * seq
    pad = pre_ref.shape[0]

    def piece(k, index, q, span):
        if k == 0:
            return fc2_ref.at[index, q, span]
        if k == 1:
            return fc1_ref.at[index, span, pl.ds(q * width, width)]
        line = pl.ds(pl.multiple_of(index * rows + span.start, 8), span.size)
        if q == 3:
            return proj_ref.at[line, :]
        return triple_ref.at[q, line, :]

    work = Reducer(at, piece, outs, refs[20:], rows, width)
    moves, fetched = {}, []

    def fetch(name, src, dst):
        copy = pltpu.make_async_copy(src, dst, in_sem.at[len(fetched)])
        copy.start()
        fetched.append(copy)
        moves.setdefault(name, []).append(copy)

    def have(name):
        for copy in moves.pop(name):
            copy.wait()

    def store(name, src, dst, i):
        copy = pltpu.make_async_copy(src, dst, out_sem.at[i])
        copy.start()
        moves[name] = [copy]

    for n in range(AHEAD):
        work.prefetch(n)

    def lines(image):
        return pl.ds(image * seq, seq)

    def modulated(image, index):
        return mod_ref[image : image + 1, index * width : (index + 1) * width]

    chunks = fc1_weight_ref.shape[2] // width

    def bring_up(c):
        fetch("u" + str(c), up_ref.at[:, pl.ds(c * width, width)], grad_joint.at[:, pl.ds(c % 3 * width, width)])

    def bring_fc1(c):
        for f in range(fsdp):
            src = fc1_weight_ref.at[f, :, pl.ds(c * width, width)]
            fetch("f" + str(c), src, stage.at[c % 2, pl.ds(f * rows, rows), :])

    def bring_image(image):
        fetch("image" + str(image), held_ref.at[lines(image)], middle.at[0])
        fetch("image" + str(image), attn_ref.at[lines(image)], middle.at[1])
        fetch("image" + str(image), cotangent_ref.at[lines(image)], joint.at[1, :, pl.ds(0, width)])

    for c in range(2):
        bring_up(c)
        bring_fc1(c)
    bring_up(2)
    fetch("joint0", joint_ref.at[lines(0)], joint.at[0])
    bring_image(0)

    def grow(c):
        have("u" + str(c))
        have("f" + str(c))

        @pl.loop(0, images)
        def _(image):
            line = pl.ds(pl.multiple_of(image * seq, seq), seq)
            value = times_back(grad_joint[line, pl.ds(c % 3 * width, width)], stage[c % 2])
            if c == 0:
                total[line, :] = value
            else:
                total[line, :] = total[line, :] + value

        if c + 3 < chunks:
            bring_up(c + 3)
        if c + 2 < chunks:
            bring_fc1(c + 2)
        if c == chunks - 2:
            for f in range(fsdp):
                src = weight_ref.at[f, :, pl.ds(3 * width, width)]
                fetch("proj", src, stage.at[c % 2, pl.ds(f * rows, rows), :])
            fetch("forward", forward_ref, grad_joint.at[:, pl.ds(c % 3 * width, width)])

    forward_at, grad_at, proj_at = (chunks - 2) % 3, (chunks - 1) % 3, (chunks - 2) % 2

    def norm_two(image):
        have("image" + str(image))
        scale, gate = 1.0 + modulated(image, 4), modulated(image, 2)
        step = 32

        def chunk(i, sums):
            shift_sum, gain_sum, gate_sum = sums
            line = pl.ds(pl.multiple_of(image * seq + i * step, step), step)
            here = pl.ds(pl.multiple_of(i * step, step), step)
            value = middle[0, here, :]
            grad = total[line, :] + logit_ref[line, :] * pick_ref[...]
            centered = value - jnp.mean(value, axis=-1, keepdims=True)
            inverse = lax.rsqrt(jnp.mean(centered * centered, axis=-1, keepdims=True) + EPSILON)
            normed = centered * inverse
            through = grad * scale
            back = through - jnp.mean(through, axis=-1, keepdims=True)
            back = back - normed * jnp.mean(through * normed, axis=-1, keepdims=True)
            through = joint[1, here, :width].astype(jnp.float32) + inverse * back
            total[line, :] = through
            grad_joint[line, grad_at * width : (grad_at + 1) * width] = (through * gate).astype(jnp.bfloat16)
            return (
                shift_sum + jnp.sum(grad, axis=0, keepdims=True),
                gain_sum + jnp.sum(grad * normed, axis=0, keepdims=True),
                gate_sum + jnp.sum(through * middle[1, here, :], axis=0, keepdims=True),
            )

        zero = jnp.zeros((1, width), jnp.float32)
        shift, gain, gated = lax.fori_loop(0, seq // step, chunk, (zero, zero, zero))
        for index, row in ((2, gated), (3, shift), (4, gain)):
            gm_row[image : image + 1, index * width : (index + 1) * width] = row
        store("mid" + str(image), total.at[lines(image)], middle_ref.at[lines(image)], 3 + images + image)
        if image + 1 < images:
            bring_image(image + 1)

    def mix():
        have("proj")

        @pl.loop(0, images)
        def _(image):
            line = pl.ds(pl.multiple_of(image * seq, seq), seq)
            grad = grad_joint[line, grad_at * width : (grad_at + 1) * width]
            mixed[line, :] = times_back(grad, stage[proj_at]).astype(jnp.bfloat16)

    def weigh_proj():
        have("forward")

        @pl.loop(0, width // 128)
        def _(m):
            line = pl.ds(pl.multiple_of(m * 128, 128), 128)
            column = pl.ds(pl.multiple_of(forward_at * width + m * 128, 128), 128)
            value = times_rows(grad_joint[:, column], grad_joint[:, grad_at * width : (grad_at + 1) * width])
            stage[1 - proj_at, line, :] = value.astype(jnp.bfloat16)

        store("projected", stage.at[1 - proj_at], proj_ref, 3 + 2 * images)

    fetch("h1", h1_ref, h1)
    fetch("ada", ada_hbm, ada_ref)
    inner[...] = jnp.zeros_like(inner)
    gm_row[...] = jnp.zeros_like(gm_row)

    def attention(image, half):
        slot = image % 2
        if half == 0:
            have("joint" + str(image))
            if image + 1 < images:
                fetch("joint" + str(image + 1), joint_ref.at[lines(image + 1)], joint.at[1 - slot])
        span = range(0, heads // 2) if half == 0 else range(heads // 2, heads)
        attend_back_image(
            joint.at[slot], mixed.at[lines(image)], gates_ref, lse_ref, grad_joint.at[lines(image)], inner, image, seq, heads, span
        )

    def weigh(q):
        if q == 0:
            have("h1")
            have("projected")
            fetch("tokens", tokens_ref, mixed)
        slot = q % 2
        if q >= 2:
            have("out" + str(q - 2))

        @pl.loop(0, width // 128)
        def _(m):
            line = pl.ds(pl.multiple_of(m * 128, 128), 128)
            stage[slot, line, :] = times_rows(h1[:, line], grad_joint[:, pl.ds(q * width, width)]).astype(jnp.bfloat16)

        store("out" + str(q), stage.at[slot], triple_ref.at[q], q)

    def bring_weight(q):
        for f in range(fsdp):
            fetch("w" + str(q), weight_ref.at[f, :, pl.ds(q * width, width)], stage.at[q % 2, pl.ds(f * rows, rows), :])

    def wait_terms():
        for q in (1, 2):
            have("out" + str(q))
        for image in range(images):
            have("mid" + str(image))
        bring_weight(0)
        bring_weight(1)
        fetch("middle0", middle_ref.at[lines(0)], middle.at[0])

    def spread(q):
        slot = q % 2
        have("w" + str(q))

        @pl.loop(0, images)
        def _(image):
            line = pl.ds(pl.multiple_of(image * seq, seq), seq)
            value = times_back(grad_joint[line, pl.ds(q * width, width)], stage[slot])
            if q == 0:
                total[line, :] = value
            else:
                total[line, :] = total[line, :] + value

        if q == 0:
            bring_weight(2)

    def norm(image):
        slot = image % 2
        if image == 0:
            have("tokens")
        have("middle" + str(image))
        if image + 1 < images:
            if image >= 1:
                have("done" + str(image - 1))
            fetch("middle" + str(image + 1), middle_ref.at[lines(image + 1)], middle.at[1 - slot])
        scale = 1.0 + modulated(image, 1)
        step = 32

        def chunk(i, sums):
            shift, gain = sums
            line = pl.ds(pl.multiple_of(image * seq + i * step, step), step)
            here = pl.ds(pl.multiple_of(i * step, step), step)
            value = mixed[line, :].astype(jnp.float32)
            grad = total[line, :]
            centered = value - jnp.mean(value, axis=-1, keepdims=True)
            inverse = lax.rsqrt(jnp.mean(centered * centered, axis=-1, keepdims=True) + EPSILON)
            normed = centered * inverse
            through = grad * scale
            back = through - jnp.mean(through, axis=-1, keepdims=True)
            back = back - normed * jnp.mean(through * normed, axis=-1, keepdims=True)
            middle[slot, here, :] = middle[slot, here, :] + inverse * back
            return (
                shift + jnp.sum(grad, axis=0, keepdims=True),
                gain + jnp.sum(grad * normed, axis=0, keepdims=True),
            )

        zero = jnp.zeros((1, width), jnp.float32)
        shift, gain = lax.fori_loop(0, seq // step, chunk, (zero, zero))
        store("done" + str(image), middle.at[slot], grad_tokens_ref.at[lines(image)], 3 + image)
        gm_row[image : image + 1, :width] = shift
        gm_row[image : image + 1, width : 2 * width] = gain

    mates, cousins = at.mates(), at.cousins()
    swaps = [Swap(mates, mate_s.at[i], mate_r.at[i]) for i in range(3)]
    far = [Swap(cousins, cousin_s.at[i], cousin_r.at[i]) for i in range(2)]
    small = []

    def keep(src, dst):
        copy = pltpu.make_async_copy(src, dst, out_sem.at[4 + 2 * images + len(small)])
        copy.start()
        small.append(copy)

    held = gms.shape[3]

    def tail_zero():
        gm_row[:, 5 * width :] = gate_two_ref[...]
        for f in range(fsdp):
            gms[0, f] = gm_row[:, f * held : (f + 1) * held].astype(jnp.bfloat16)
        swaps[0].start(lambda device: gms.at[0, device[1]], gms.at[1, at.f])

    def tail_one():
        have("ada")
        swaps[0].arrived()
        gms[1, at.f] = gms[0, at.f]
        every = gms[1].astype(jnp.float32).reshape(fsdp * pad, held).astype(jnp.bfloat16)
        parts[...] = matmul(every, ada_ref[...]).reshape(parts.shape)
        swaps[1].start(lambda device: parts.at[device[1]], mine_in.at[at.f])
        far[0].start(lambda device: gms.at[1], all_gm_ref.at[at.d])
        keep(gms.at[1], all_gm_ref.at[at.d])

    def tail_two():
        line = lax.broadcasted_iota(jnp.int32, (pad, 128), 0)
        gated = jnp.zeros((pad, 128), jnp.float32)
        for image in range(images):
            summed = lax.dot_general(
                jnp.ones((pad, seq), jnp.float32), inner[image], (((1,), (1,)), ((), ())),
                preferred_element_type=jnp.float32, precision=lax.Precision.HIGHEST,
            )
            gated = jnp.where(line == image, summed, gated)
        router = (gated * factor_ref[...]).astype(jnp.bfloat16)
        swaps[1].arrived()
        mine_in[at.f] = parts[at.f]
        grad_cond = jnp.sum(mine_in[...], axis=0) + times_back(router, routers_ref[...])
        pre_cond = pre_ref[...]
        sig = jax.nn.sigmoid(pre_cond)
        grad_pre = grad_cond * (sig * (1.0 + pre_cond * (1.0 - sig)))
        pres[at.f, :, :width] = (grad_pre + picker_ref[...]).astype(jnp.bfloat16)
        pres[at.f, :, width:] = router
        swaps[2].start(lambda device: pres.at[at.f], pres.at[at.f])

    def tail_three():
        swaps[2].arrived()
        far[1].start(lambda device: pres, all_pre_ref.at[at.d])
        keep(pres, all_pre_ref.at[at.d])

    early = [partial(grow, c) for c in range(chunks)] + [partial(norm_two, image) for image in range(images)]
    early += [mix, weigh_proj]
    early += [partial(attention, image, half) for image in range(images) for half in range(2)]
    early += [partial(weigh, q) for q in range(3)] + [wait_terms]
    norms = [partial(norm, image) for image in range(images)]
    late = [[partial(spread, q)] for q in range(3)] + [[step] for step in norms]
    late += [[tail_zero], [], [tail_one], [], [], [tail_two], [], [], [tail_three]]
    split = 4 * ring
    done = 0
    for t in range(work.total + 4 * LAG):
        work.turn(t, split)
        if t < split:
            upto = -(-len(early) * (t + 1) // split)
            for step in early[done:upto]:
                step()
            done = upto
        elif t - split < len(late):
            for step in late[t - split]:
                step()
    for swap in far:
        swap.arrived()
    for copy in small:
        copy.wait()
    for image in range(max(images - 2, 0), images):
        have("done" + str(image))
    for swap in swaps + far:
        swap.left()
    work.finish()


def back_half(
    terms, joint, flat_one, tokens, joint_full, grad_up, fc1_full, middle, attn, cotangent, mixed, log_total, gates, gate_two,
    modulation, factor, routers, ada_weight, pre_cond, picker, logit, pick, width, images, seq, dp, fsdp,
):
    rows = terms[1].shape[1]
    heads = gates.shape[1]
    count = images * seq
    pad = pre_cond.shape[0]
    columns = ada_weight.shape[0]
    dma, vmem = pltpu.SemaphoreType.DMA, pltpu.VMEM
    low, f32 = jnp.bfloat16, jnp.float32
    out = jax.ShapeDtypeStruct
    any_space, in_vmem = pl.BlockSpec(memory_space=pl.ANY), pl.BlockSpec(memory_space=vmem)
    in_smem = pl.BlockSpec(memory_space=pltpu.SMEM)
    return pl.pallas_call(
        partial(back_kernel, dp, fsdp, width, images, seq, heads),
        out_shape=[out((QUARTERS, rows, width), low)] * 3
        + [
            out((dp, fsdp, pad, columns), low),
            out((dp, fsdp, pad, width + 128), low),
            out((count, width), f32),
            out((3, width, width), low),
            out((count, width), f32),
            out((width, width), low),
        ],
        in_specs=[any_space] * 12 + [in_vmem, in_smem] + [in_vmem] * 4 + [any_space] + [in_vmem] * 4,
        out_specs=[any_space] * 9,
        scratch_shapes=[
            vmem((2, seq, 3 * width), low),
            vmem((count, width), low),
            vmem((count, width), low),
            vmem((2, seq, width), f32),
            vmem((count, 3 * width), low),
            vmem((2, width, width), low),
            vmem((count, width), f32),
            vmem((images, 128, seq), f32),
            vmem((pad, 6 * width), f32),
            vmem((2, fsdp, pad, columns), low),
            vmem((fsdp, pad, width), f32),
            vmem((fsdp, pad, width), f32),
            vmem((fsdp, pad, width + 128), low),
            vmem(ada_weight.shape, low),
            dma((8 * fsdp + 9 + 5 * images,)),
            dma((6 + 2 * images,)),
            dma((3, fsdp - 1)),
            dma((3, fsdp - 1)),
            dma((2, dp - 1)),
            dma((2, dp - 1)),
        ]
        + Reducer.scratch(rows, width, fsdp),
        compiler_params=pltpu.CompilerParams(
            collective_id=1, has_side_effects=True, vmem_limit_bytes=60 * 2**20
        ),
        name="back",
    )(
        *terms, joint, flat_one, tokens, joint_full, grad_up, fc1_full, middle, attn, cotangent, mixed, log_total,
        gates[:, None, :], gate_two, modulation, factor, routers, ada_weight, pre_cond, picker, logit, pick,
    )


def body(
    dp,
    fsdp,
    tokens,
    timesteps,
    labels,
    head_mask,
    keep_mask,
    cotangent,
    time_weight,
    class_table,
    ada_weight,
    head_router,
    qkv_weight,
    proj_weight,
    fc1_weight,
    fc2_weight,
    token_router,
):
    images, seq, width = tokens.shape
    heads = head_mask.shape[1]
    count = images * seq
    rows = qkv_weight.shape[0]
    hidden = fc1_weight.shape[1]
    entries = time_weight.shape[0] * fsdp
    me_fsdp = lax.axis_index("fsdp")
    pad = -(-(images + 2) // 8) * 8

    def padded(array, value=0.0):
        return jnp.pad(array, ((0, pad - images), (0, 0)), constant_values=value)

    embedded = sinusoid(timesteps, entries).astype(jnp.bfloat16)
    digits = jnp.stack([labels // DIGIT, labels % DIGIT], axis=1).astype(jnp.bfloat16)
    asked = jnp.concatenate(
        [padded(embedded), jnp.pad(padded(digits, -1.0), ((0, 0), (0, 126)))], axis=1
    )
    routers = jnp.pad(
        jnp.concatenate([head_router, token_router], axis=1), ((0, 0), (0, 127 - heads))
    )
    mask_float = head_mask.astype(jnp.float32)
    *gathered, flat_one, joint, log_total, mixed, attn, middle, flat_two, active, slope = front_half(
        [
            jnp.concatenate([qkv_weight, proj_weight], axis=1),
            fc1_weight,
            fc2_weight.reshape(QUARTERS, rows, width),
        ],
        asked,
        time_weight,
        class_table.T,
        ada_weight.T,
        routers,
        padded(jnp.pad(mask_float, ((0, 0), (0, 128 - heads)))),
        tokens.reshape(count, width),
        width,
        images,
        seq,
        heads,
        dp,
        fsdp,
    )
    joint_blocks, fc1_full, fc2_full, pre_cond_pad, modulation_pad, routers_full, all_cond, all_asked = gathered
    shrink = fc2_full.reshape(hidden, width)
    routers_full = routers_full.reshape(width, 128)
    chooser, picker = routers_full[:, :heads], routers_full[:, heads : heads + 1]
    everyone = dp * fsdp * pad
    all_cond = all_cond.reshape(everyone, width)
    all_asked = all_asked.reshape(everyone, asked.shape[1])
    pre_cond = pre_cond_pad[:images]
    cond = jax.nn.silu(pre_cond).astype(jnp.bfloat16)
    gate_two = modulation_pad[:images, None, 5 * width :]
    router_sig = jax.nn.sigmoid(matmul(cond, chooser))
    head_gates = mask_float * router_sig
    middle = middle.reshape(images, seq, width)
    rate = jax.nn.sigmoid(matmul(flat_two, picker)).reshape(images, seq, 1)
    downward = matmul(active, shrink).reshape(images, seq, width)
    kept = keep_mask.astype(jnp.float32)[:, :, None]
    kept_rate = kept * rate
    output = (middle + gate_two * kept_rate * downward).astype(jnp.bfloat16)
    grad_out = cotangent.astype(jnp.float32)
    grad_gate_two = jnp.sum(grad_out * kept_rate * downward, axis=1)
    grad_down = (grad_out * gate_two * kept_rate).astype(jnp.bfloat16).reshape(count, width)
    grad_rate = jnp.sum(grad_out * gate_two * downward, axis=-1, keepdims=True) * kept
    grad_logit = (grad_rate * rate * (1.0 - rate)).astype(jnp.bfloat16).reshape(count, 1)
    grad_shrink = times_rows(active, grad_down).astype(jnp.bfloat16)
    grad_up = (times_back(grad_down, shrink) * slope.astype(jnp.float32)).astype(jnp.bfloat16)
    grad_expand = times_rows(flat_two, grad_up).astype(jnp.bfloat16)
    grad_picker = times_rows(grad_logit, flat_two)
    picker_high = lax.reduce_precision(grad_picker, 8, 7)
    *sums, all_grad, all_pre, grad_inputs, _, _, _ = back_half(
        [
            grad_shrink.reshape(fsdp, QUARTERS, rows, width),
            grad_expand.reshape(fsdp, rows, hidden),
        ],
        joint,
        flat_one,
        tokens.reshape(count, width),
        joint_blocks,
        grad_up,
        fc1_full,
        middle.reshape(count, width),
        attn,
        cotangent.reshape(count, width),
        mixed,
        log_total,
        head_gates,
        padded(grad_gate_two),
        modulation_pad,
        padded(jnp.pad(mask_float * router_sig * (1.0 - router_sig), ((0, 0), (0, 128 - heads)))),
        routers_full,
        ada_weight.T,
        pre_cond_pad,
        jnp.pad(jnp.concatenate([picker_high, grad_picker - picker_high], axis=0), ((pad - 2, 0), (0, 0))),
        grad_logit.astype(jnp.float32),
        picker.astype(jnp.float32).reshape(1, width),
        width,
        images,
        seq,
        dp,
        fsdp,
    )
    grad_inputs = grad_inputs.reshape(images, seq, width)
    if dp > QUARTERS:
        parts = list(sums)
        for hop in range(QUARTERS, dp, QUARTERS):
            pairs = [(i, (i + hop) % dp) for i in range(dp)]
            parts = [
                part.astype(jnp.float32) + lax.ppermute(s, "dp", pairs).astype(jnp.float32)
                for part, s in zip(parts, sums)
            ]
        sums = parts
    sums = [s.astype(jnp.float32) for s in sums]
    sum_triple = jnp.concatenate([sums[2][0], sums[2][1], sums[2][2]], axis=1)
    sum_merger = sums[2][3]
    sum_expand = jnp.concatenate([sums[1][i] for i in range(QUARTERS)], axis=1)
    sum_shrink = sums[0].reshape(QUARTERS * rows, width)

    sum_ada = times_rows(all_cond, all_grad.reshape(everyone, -1))
    sum_picker = lax.dynamic_slice_in_dim(
        jnp.sum(all_pre[:, :, pad - 2 :, :width].astype(jnp.float32), axis=(0, 1, 2)), me_fsdp * rows, rows, axis=0
    )[:, None]
    is_image = (jnp.arange(pad) < images)[None, None, :, None]
    all_pre = jnp.where(is_image, all_pre, jnp.bfloat16(0.0)).reshape(everyone, -1)
    all_router = all_pre[:, width : width + heads]
    all_pre = all_pre[:, :width]
    own_entries = entries // fsdp
    all_embedded = lax.dynamic_slice_in_dim(
        all_asked[:, :entries], me_fsdp * own_entries, own_entries, axis=1
    )
    classes = jnp.arange(class_table.shape[0], dtype=jnp.float32)
    all_digits = all_asked[:, entries : entries + 2].astype(jnp.float32)
    all_labels = all_digits[:, :1] * DIGIT + all_digits[:, 1:]
    all_rows = (all_labels == classes[None, :]).astype(jnp.bfloat16)
    sum_time = times_rows(all_embedded, all_pre)
    sum_table = times_rows(
        all_rows, lax.dynamic_slice_in_dim(all_pre, me_fsdp * rows, rows, axis=1)
    )
    sum_chooser = times_rows(
        lax.dynamic_slice_in_dim(all_cond, me_fsdp * rows, rows, axis=1), all_router
    )
    return (
        output,
        grad_inputs,
        sum_time,
        sum_table,
        sum_ada,
        sum_chooser,
        sum_triple,
        sum_merger,
        sum_expand,
        sum_shrink,
        sum_picker,
    )


def solution(mesh):
    images = P(("dp", "fsdp"), None, None)
    pairs = P(("dp", "fsdp"), None)
    single = P(("dp", "fsdp"))
    by_row, by_column = P("fsdp", None), P(None, "fsdp")
    in_specs = (
        images, single, single, pairs, pairs, images,
        by_row, by_column, by_column, by_row, by_row, by_row, by_row, by_row, by_row,
    )
    out_specs = (
        images, images,
        by_row, by_column, by_column, by_row, by_row, by_row, by_row, by_row, by_row,
    )
    return jax.shard_map(
        partial(body, mesh.shape["dp"], mesh.shape["fsdp"]),
        mesh=mesh, in_specs=in_specs, out_specs=out_specs, check_vma=False,
    )
```

```python
from functools import partial
import math

import jax
import jax.numpy as jnp
from jax import lax
from jax.experimental import pallas as pl
from jax.experimental.pallas import tpu as pltpu
from jax.sharding import PartitionSpec as P

EPSILON = 1e-06
MESH = pl.DeviceIdType.MESH
QUARTERS = 4
DIGIT = 256


def sinusoid(steps, entries):
    half = entries // 2
    freqs = jnp.exp(-math.log(10000.0) * jnp.arange(half, dtype=jnp.float32) / half)
    angles = steps.astype(jnp.float32)[:, None] * freqs[None, :]
    return jnp.concatenate([jnp.cos(angles), jnp.sin(angles)], axis=1)


def layer_norm(value):
    centered = value - jnp.mean(value, axis=-1, keepdims=True)
    return centered * lax.rsqrt(jnp.mean(centered * centered, axis=-1, keepdims=True) + EPSILON)


def norm_back(value, grad):
    _, pull = jax.vjp(layer_norm, value)
    return pull(grad)[0]


def matmul(left, right):
    return jnp.dot(left, right, preferred_element_type=jnp.float32)


def times_rows(left, right):
    return lax.dot_general(
        left, right, (((0,), (0,)), ((), ())), preferred_element_type=jnp.float32
    )


def times_back(left, right):
    return lax.dot_general(
        left, right, (((1,), (1,)), ((), ())), preferred_element_type=jnp.float32
    )


class Place:
    def __init__(self, dp, fsdp):
        ring = fsdp // 2
        self.dp, self.fsdp, self.ring = dp, fsdp, ring
        d = lax.axis_index("dp")
        f = lax.axis_index("fsdp")
        self.d, self.f = d, f
        self.z = f // 2
        self.c = f % 2
        self.q = d % QUARTERS
        dx = d + 1 - 2 * (d % 2)
        dy = d + 2 - 4 * ((d // 2) % 2)
        self.qx = dx % QUARTERS
        self.qy = dy % QUARTERS
        self.qd = (self.qx + self.qy - self.q + QUARTERS) % QUARTERS
        self.core = (d, f + 1 - 2 * (f % 2))
        self.x = (dx, f)
        self.y = (dy, f)
        self.up = (d, ((self.z + 1) % ring) * 2 + self.c)
        self.down = (d, ((self.z + ring - 1) % ring) * 2 + self.c)

    def shard(self, back):
        return ((self.z + self.ring - back) % self.ring) * 2 + self.c

    def mates(self):
        return [(self.d, (self.f + offset) % self.fsdp) for offset in range(1, self.fsdp)]

    def cousins(self):
        return [((self.d + offset) % self.dp, self.f) for offset in range(1, self.dp)]

    def greet(self):
        barrier = pltpu.get_barrier_semaphore()
        near = self.mates() + self.cousins()
        for other in near:
            pl.semaphore_signal(barrier, inc=1, device_id=other, device_id_type=MESH)
        pl.semaphore_wait(barrier, len(near))


def remote(src, dst, send, recv, device):
    return pltpu.make_async_remote_copy(
        src_ref=src, dst_ref=dst, send_sem=send, recv_sem=recv, device_id=device, device_id_type=MESH
    )


class Swap:
    def __init__(self, partners, send, recv):
        self.partners, self.send, self.recv = partners, send, recv
        self.copies = []

    def start(self, source, landing):
        for i, device in enumerate(self.partners):
            copy = remote(source(device), landing, self.send.at[i], self.recv.at[i], device)
            copy.start()
            self.copies.append(copy)

    def arrived(self):
        for copy in self.copies:
            copy.wait_recv()

    def left(self):
        for copy in self.copies:
            copy.wait_send()


def cut(width):
    first = ((width // 128 + 1) // 2) * 128
    return (0, first), (first, width - first)


def view(ref, lead, q, width, part=None, span=None):
    start, size = (0, width) if part is None else part
    lines = slice(None) if span is None else pl.ds(*span)
    flat = ref.shape[-1] != width
    if flat:
        column = pl.multiple_of(q * width + start, 128)
        return ref.at[(*lead, lines, pl.ds(column, size))]
    return ref.at[(*lead, q, lines, pl.ds(start, size))]


def front_kernel(dp, fsdp, width, images, seq, heads, *refs):
    weights = 3
    ring = fsdp // 2
    shards, refs = refs[:weights], refs[weights:]
    ask_ref, time_ref, table_hbm, ada_hbm, router_ref, mask_ref, tokens_ref, keep_ref, cotangent_ref = refs[:9]
    refs = refs[9:]
    fulls, refs = refs[:weights], refs[weights:]
    pre_ref, mod_ref, routers_ref, all_cond_ref, all_ask_ref = refs[:5]
    h1_out, joint_out, lse_out, mixed_out, attn_out, middle_out, h2_out, active_out, slope_out = refs[5:14]
    down_out, term_out = refs[14:16]
    refs = refs[16:]
    asks, parts, mine_in, conds, columns, mods, gates = refs[:7]
    tokens, h1, joint, lse, mixed, attn, middle, h2, stage, table_ref, ada_ref, actives, slopes = refs[7:20]
    cotangent, down, term, move_sem = refs[20:24]
    refs = refs[24:]
    (own_sem, core_s, core_r, ring_s, ring_r, x_s, x_r, y_s, y_r, a_s, a_r, b_s, b_r) = refs[:13]
    mate_s, mate_r, cousin_s, cousin_r, small_sem = refs[13:]
    at = Place(dp, fsdp)
    part_a, part_b = cut(width)
    at.greet()
    sent = []
    mates, cousins = at.mates(), at.cousins()
    swaps = [Swap(mates, mate_s.at[i], mate_r.at[i]) for i in range(5)]
    far = [Swap(cousins, cousin_s.at[i], cousin_r.at[i]) for i in range(2)]
    pad = ask_ref.shape[0]
    group = fsdp * pad
    rows = table_ref.shape[0]
    spans = Reducer.halves(rows)
    chunks = shards[1].shape[1] // width

    def go(copy):
        copy.start()
        sent.append(copy)
        return copy

    def ring_copy(k, hop, half):
        index = at.shard(hop - 1)
        src = (shards[k], ()) if hop == 1 else (fulls[k], (index,))
        dst = view(fulls[k], (index,), at.q, width, span=spans[half])
        sems = ring_s.at[k, hop - 1, half], ring_r.at[k, hop - 1, half]
        return remote(view(*src, at.q, width, span=spans[half]), dst, *sems, at.up)

    small = []

    def keep(src, dst):
        copy = pltpu.make_async_copy(src, dst, small_sem.at[len(small)])
        copy.start()
        small.append(copy)

    def cond_one():
        have("table")
        swaps[0].arrived()
        asks[at.f] = ask_ref[...]
        every = asks[...].astype(jnp.float32).reshape(group, asks.shape[2])
        entries = every.shape[1] - 128
        own_rows = time_ref.shape[0]
        lanes = lax.broadcasted_iota(jnp.int32, (group, entries), 1)
        held = (lanes >= at.f * own_rows) & (lanes < (at.f + 1) * own_rows)
        embedded = jnp.where(held, every[:, :entries], 0.0).astype(jnp.bfloat16)
        stacked = jnp.concatenate([time_ref[...]] * fsdp, axis=0)
        label = (every[:, entries : entries + 1] * DIGIT + every[:, entries + 1 : entries + 2]).astype(jnp.int32)
        classes = table_ref.shape[1]
        picks = (label == lax.broadcasted_iota(jnp.int32, (group, classes), 1)).astype(jnp.float32)
        picked = times_back(picks.astype(jnp.bfloat16), table_ref[...]).astype(jnp.bfloat16)
        spot = lax.broadcasted_iota(jnp.int32, (rows, width), 1)
        line = lax.broadcasted_iota(jnp.int32, (rows, width), 0)
        place = (spot == line + at.f * rows).astype(jnp.float32).astype(jnp.bfloat16)
        partial_sum = matmul(embedded, stacked) + matmul(picked, place)
        parts[...] = partial_sum.reshape(fsdp, pad, width)
        swaps[1].start(lambda device: parts.at[device[1]], mine_in.at[at.f])

    def cond_two():
        swaps[1].arrived()
        mine_in[at.f] = parts[at.f]
        pre_cond = jnp.sum(mine_in[...], axis=0)
        pre_ref[...] = pre_cond
        conds[at.f] = (pre_cond * jax.nn.sigmoid(pre_cond)).astype(jnp.bfloat16)
        swaps[2].start(lambda device: conds.at[at.f], conds.at[at.f])

    def cond_three():
        have("ada")
        swaps[2].arrived()
        every = conds[...].astype(jnp.float32).reshape(group, width).astype(jnp.bfloat16)
        columns[...] = times_back(every, ada_ref[...]).reshape(columns.shape)
        swaps[3].start(lambda device: columns.at[device[1]], mods.at[at.f])

    def cond_four():
        swaps[3].arrived()
        swaps[4].arrived()
        mods[at.f] = columns[at.f]
        routers_ref[at.f] = router_ref[...]
        held = mods.shape[2]
        for f in range(fsdp):
            mod_ref[:, f * held : (f + 1) * held] = mods[f]
        chosen = matmul(conds[at.f], routers_ref[...].reshape(width, router_ref.shape[1]))
        gates[...] = mask_ref[...] * jax.nn.sigmoid(chosen)

    moves, moved = {}, []

    def move(name, src, dst):
        copy = pltpu.make_async_copy(src, dst, move_sem.at[len(moved)])
        copy.start()
        moved.append(copy)
        moves.setdefault(name, []).append(copy)

    def have(name):
        for copy in moves.pop(name):
            copy.wait()

    def line_of(image):
        return pl.ds(image * seq, seq)

    def bring(q):
        for f in range(fsdp):
            src = fulls[0].at[f, :, pl.ds(q * width, width)]
            move("w" + str(q), src, stage.at[q % 2, pl.ds(f * rows, rows), :])

    def modulated(image, index):
        return mod_ref[image : image + 1, index * width : (index + 1) * width]

    step = 32

    def normed(value, scale, shift):
        centered = value - jnp.mean(value, axis=-1, keepdims=True)
        inverse = lax.rsqrt(jnp.mean(centered * centered, axis=-1, keepdims=True) + EPSILON)
        return (centered * inverse * scale + shift).astype(jnp.bfloat16)

    def joint_here():
        for copy in landed[0]:
            copy.wait_recv()
        locals_[0].wait()
        bring(0)
        bring(1)

    def norm_one(image):
        if image == 0:
            have("tokens")
        shift, scale = modulated(image, 0), 1.0 + modulated(image, 1)

        @pl.loop(0, seq // step)
        def _(i):
            line = pl.ds(pl.multiple_of(image * seq + i * step, step), step)
            h1[line, :] = normed(tokens[line, :].astype(jnp.float32), scale, shift)

        if image == images - 1:
            move("h1", h1, h1_out)

    def project(q):
        have("w" + str(q))

        @pl.loop(0, images)
        def _(image):
            line = pl.ds(pl.multiple_of(image * seq, seq), seq)
            joint[line, pl.ds(q * width, width)] = matmul(h1[line, :], stage[q % 2]).astype(jnp.bfloat16)

        if q + 2 < QUARTERS:
            bring(q + 2)
        if q == 2:
            move("joint", joint, joint_out)

    def attention(image, half):
        span = range(0, heads // 2) if half == 0 else range(heads // 2, heads)
        attend_image(joint.at[line_of(image)], gates, mixed.at[line_of(image)], lse, image, seq, heads, span)
        if image == images - 1 and half == 1:
            move("mixed", mixed, mixed_out)
            move("lse", lse, lse_out)

    def merge(image):
        if image == 0:
            have("w3")
        line = line_of(image)
        attn[line, :] = matmul(mixed[line, :], stage[1])
        gate, shift, scale = modulated(image, 2), modulated(image, 3), 1.0 + modulated(image, 4)

        @pl.loop(0, seq // step)
        def _(i):
            here = pl.ds(pl.multiple_of(image * seq + i * step, step), step)
            value = tokens[here, :].astype(jnp.float32) + gate * attn[here, :]
            middle[here, :] = value
            h2[here, :] = normed(value, scale, shift)

        move("attn", attn.at[line], attn_out.at[line])
        move("middle", middle.at[line], middle_out.at[line])
        move("h2", h2.at[line], h2_out.at[line])

    def bring_fc1(c):
        for f in range(fsdp):
            src = fulls[1].at[f, :, pl.ds(c * width, width)]
            move("e" + str(c), src, stage.at[c % 2, pl.ds(f * rows, rows), :])

    def fc1_here():
        for copy in landed[1]:
            copy.wait_recv()
        locals_[1].wait()
        bring_fc1(0)
        bring_fc1(1)

    def expand(c):
        slot = c % 2
        have("e" + str(c))
        if c >= 2:
            have("active" + str(c - 2))
        bend = math.sqrt(2.0 / math.pi)
        size = 128
        pair = 2 if images * seq % (2 * size) == 0 else 1

        @pl.loop(0, images * seq // (pair * size))
        def _(i):
            for inner in range(pair):
                line = pl.ds(pl.multiple_of((i * pair + inner) * size, size), size)
                value = matmul(h2[line, :], stage[slot])
                square = value * value
                bent = jnp.tanh(value * (bend + bend * 0.044715 * square))
                half = 0.5 + 0.5 * bent
                actives[slot, line, :] = (value * half).astype(jnp.bfloat16)
                lean = value * (0.5 - 0.5 * bent * bent) * (bend + 3.0 * bend * 0.044715 * square)
                slopes[slot, line, :] = (half + lean).astype(jnp.bfloat16)

        if c + 2 < chunks:
            bring_fc1(c + 2)
        columns_of = pl.ds(c * width, width)
        move("active" + str(c), actives.at[slot], active_out.at[:, columns_of])
        move("active" + str(c), slopes.at[slot], slope_out.at[:, columns_of])

    def route(image):
        if image == 0:
            have("cotangent")
        line = line_of(image)
        chosen = matmul(h2[line, :], routers_ref[...].reshape(width, router_ref.shape[1]))
        kept = keep_ref[line, :] * jax.nn.sigmoid(chosen[:, heads : heads + 1])
        down[line, :] = (cotangent[line, :].astype(jnp.float32) * modulated(image, 5) * kept).astype(jnp.bfloat16)
        if image == images - 1:
            move("down", down, down_out)

    def weigh_fc2(c):
        if c > 0:
            have("term" + str(c - 1))

        @pl.loop(0, width // 128)
        def _(m):
            line = pl.ds(pl.multiple_of(m * 128, 128), 128)
            term[line, :] = times_rows(actives[c % 2, :, line], down[...]).astype(jnp.bfloat16)

        move("term" + str(c), term, term_out.at[pl.ds(c * width, width), :])

    move("table", table_hbm, table_ref)
    move("ada", ada_hbm, ada_ref)
    move("tokens", tokens_ref, tokens)
    move("cotangent", cotangent_ref, cotangent)
    work = [joint_here] + [partial(norm_one, image) for image in range(images)]
    work += [partial(project, q) for q in range(3)]
    work += [partial(attention, image, half) for image in range(images) for half in range(2)]
    work += [partial(merge, image) for image in range(images)] + [partial(route, image) for image in range(images)]

    def share():
        far[0].start(lambda device: conds, all_cond_ref.at[at.d])
        far[1].start(lambda device: asks, all_ask_ref.at[at.d])
        keep(conds, all_cond_ref.at[at.d])
        keep(asks, all_ask_ref.at[at.d])

    extra = {2: cond_one, 4: cond_two, 6: cond_three, 9: cond_four, 4 * (ring - 1) + 2 * LAG: share}
    swaps[0].start(lambda device: ask_ref, asks.at[at.f])
    swaps[4].start(lambda device: router_ref, routers_ref.at[at.f])

    items = [(k, hop, half) for k in range(weights) for hop in range(1, ring) for half in range(2)]
    rings = {item: go(ring_copy(*item)) for item in items[:2]}
    locals_, landed = [], [[], [], []]
    for k in range(weights):
        copy = pltpu.make_async_copy(shards[k], fulls[k].at[at.f], own_sem.at[k])
        copy.start()
        locals_.append(copy)
        landed[k].append(go(remote(shards[k], fulls[k].at[at.f], core_s.at[k, 0, 0], core_r.at[k, 0, 0], at.core)))
    flights = {}
    each = 2 * (ring - 1)
    begin, second = each + 2 * LAG - 1, 2 * each + 2 * LAG
    done = 0
    for turn in range(len(items) + 2 * LAG):
        if turn < len(items):
            k, hop, half = items[turn]
            rings[items[turn]].wait_recv()
            if turn + 2 < len(items):
                rings[items[turn + 2]] = go(ring_copy(*items[turn + 2]))
            mine = view(fulls[k], (at.shard(hop),), at.q, width, span=spans[half])
            place = (k, hop - 1, half)
            flights[turn] = (
                go(remote(mine, mine, x_s.at[place], x_r.at[place], at.x)),
                go(remote(mine, mine, y_s.at[place], y_r.at[place], at.y)),
            )
        n = turn - LAG
        if 0 <= n < len(items):
            k, hop, half = items[n]
            place = (k, hop - 1, half)
            by_x, by_y = flights[n]
            by_x.wait_recv()
            part = view(fulls[k], (at.shard(hop),), at.qx, width, part_a, spans[half])
            first = go(remote(part, part, a_s.at[place], a_r.at[place], at.y))
            by_y.wait_recv()
            part = view(fulls[k], (at.shard(hop),), at.qy, width, part_b, spans[half])
            flights[n] = (first, go(remote(part, part, b_s.at[place], b_r.at[place], at.x)))
        n = turn - 2 * LAG
        if 0 <= n < len(items):
            k, hop, half = items[n]
            for copy in flights[n]:
                copy.wait_recv()
            span = pl.ds(*spans[half])
            whole = fulls[k].at[(at.shard(hop), span) if k < 2 else (at.shard(hop), slice(None), span)]
            landed[k].append(go(remote(whole, whole, core_s.at[k, hop, half], core_r.at[k, hop, half], at.core)))
        if turn in extra:
            extra[turn]()
        if begin <= turn < second:
            upto = -(-len(work) * (turn + 1 - begin) // (second - begin))
            for part in work[done:upto]:
                part()
            done = upto
        elif turn == second:
            fc1_here()
        elif second < turn <= second + chunks:
            expand(turn - second - 1)
            weigh_fc2(turn - second - 1)
    for swap in far:
        swap.arrived()
    for copy in landed[2]:
        copy.wait_recv()
    for copy in locals_[2:] + small:
        copy.wait()
    for c in range(max(chunks - 2, 0), chunks):
        have("active" + str(c))
    have("down")
    have("term" + str(chunks - 1))
    for name in ("h1", "joint", "mixed", "lse", "attn", "middle", "h2"):
        have(name)
    for swap in swaps + far:
        swap.left()
    for copy in sent:
        copy.wait_send()


def front_half(
    shards, asked, time_weight, class_table, ada_weight, routers, mask, tokens, keep, cotangent, width, images, seq, heads,
    dp, fsdp,
):
    ring = fsdp // 2
    dma, vmem = pltpu.SemaphoreType.DMA, pltpu.VMEM
    low, f32 = jnp.bfloat16, jnp.float32
    steps = dma((3, ring - 1, 2))
    hidden = shards[1].shape[1]
    pad, asking = asked.shape
    columns = ada_weight.shape[0]
    count = images * seq
    out = jax.ShapeDtypeStruct
    any_space, in_vmem = pl.BlockSpec(memory_space=pl.ANY), pl.BlockSpec(memory_space=vmem)
    results = [
        out((count, width), low),
        out((count, 3 * width), low),
        out((images, heads, seq), f32),
        out((count, width), low),
        out((count, width), f32),
        out((count, width), f32),
        out((count, width), low),
    ]
    return pl.pallas_call(
        partial(front_kernel, dp, fsdp, width, images, seq, heads),
        out_shape=[out((fsdp, *s.shape), s.dtype) for s in shards]
        + [
            out((pad, width), f32),
            out((pad, 6 * width), f32),
            out((fsdp, *routers.shape), routers.dtype),
            out((dp, fsdp, pad, width), low),
            out((dp, fsdp, pad, asking), low),
        ]
        + results
        + [out((count, hidden), low)] * 2
        + [out((count, width), low), out((hidden, width), low)],
        in_specs=[any_space] * 3 + [in_vmem] * 2 + [any_space] * 2 + [in_vmem] * 2 + [any_space, in_vmem, any_space],
        out_specs=[any_space] * 3 + [in_vmem] * 3 + [any_space] * 13,
        scratch_shapes=[
            vmem((fsdp, pad, asking), low),
            vmem((fsdp, pad, width), f32),
            vmem((fsdp, pad, width), f32),
            vmem((fsdp, pad, width), low),
            vmem((fsdp, pad, columns), f32),
            vmem((fsdp, pad, columns), f32),
            vmem((pad, 128), f32),
            vmem((count, width), low),
        ]
        + [vmem(r.shape, r.dtype) for r in results]
        + [vmem((2, width, width), low), vmem(class_table.shape, low), vmem(ada_weight.shape, low)]
        + [vmem((2, count, width), low)] * 2
        + [vmem((count, width), low)] * 2
        + [vmem((width, width), low)]
        + [dma((8 * fsdp + 17 + 3 * images + hidden // width,))]
        + [dma((3,)), dma((3, ring, 2)), dma((3, ring, 2))]
        + [steps] * 10
        + [dma((5, fsdp - 1))] * 2
        + [dma((2, dp - 1))] * 2
        + [dma((2,))],
        compiler_params=pltpu.CompilerParams(
            collective_id=0, has_side_effects=True, vmem_limit_bytes=60 * 2**20
        ),
        name="front",
    )(*shards, asked, time_weight, class_table, ada_weight, routers, mask, tokens, keep, cotangent)


def window(head, size):
    low = head * size // 128 * 128
    high = -(-(head + 1) * size // 128) * 128
    spot = low + lax.broadcasted_iota(jnp.int32, (1, high - low), 1)
    own = ((spot >= head * size) & (spot < (head + 1) * size)).astype(jnp.float32).astype(jnp.bfloat16)
    return low, high - low, own


def attend_image(joint, gates, mixed, lse, image, seq, heads, span):
    width = mixed.shape[1]
    size = width // heads
    scale = size ** (-0.5)
    if span[0] == 0:
        mixed[...] = jnp.zeros((seq, width), mixed.dtype)
    for head in span:
        low, wide, own = window(head, size)
        query = joint[:, pl.ds(low, wide)] * own
        keys = joint[:, pl.ds(width + low, wide)]
        values = joint[:, pl.ds(2 * width + low, wide)] * own
        raw = times_back(keys, query) * scale
        peak = jnp.max(raw, axis=0, keepdims=True)
        expo = jnp.exp(raw - peak)
        total = jnp.sum(expo, axis=0, keepdims=True)
        lse[image, head : head + 1, :] = peak + jnp.log(total)
        probs = (expo * (1.0 / total)).astype(jnp.bfloat16)
        attended = times_rows(probs, values) * gates[image : image + 1, head : head + 1]
        mixed[:, pl.ds(low, wide)] = mixed[:, pl.ds(low, wide)] + attended.astype(jnp.bfloat16)


def attend_back_image(joint, grad_mixed, gates, lse, grad_joint, grad_gates, image, seq, heads, span):
    width = grad_mixed.shape[1]
    size = width // heads
    scale = size ** (-0.5)
    if span[0] == 0:
        grad_joint[...] = jnp.zeros((seq, 3 * width), grad_joint.dtype)

    def put(column, wide, value):
        here = pl.ds(column, wide)
        grad_joint[:, here] = grad_joint[:, here] + value.astype(jnp.bfloat16)

    for head in span:
        low, wide, own = window(head, size)
        query = joint[:, pl.ds(low, wide)] * own
        keys = joint[:, pl.ds(width + low, wide)] * own
        values = joint[:, pl.ds(2 * width + low, wide)]
        grad = grad_mixed[:, pl.ds(low, wide)] * own
        gate = gates[image, 0, head]
        probs = jnp.exp(times_back(keys, query) * scale - lse[image, head : head + 1, :])
        put(2 * width + low, wide, matmul(probs.astype(jnp.bfloat16), (grad.astype(jnp.float32) * gate).astype(jnp.bfloat16)))
        grad_probs = times_back(values, grad)
        inner = jnp.sum(grad_probs * probs, axis=0, keepdims=True)
        grad_gates[image, head : head + 1, :] = inner
        grad_scores = (probs * (grad_probs - inner) * (gate * scale)).astype(jnp.bfloat16)
        put(low, wide, times_rows(grad_scores, keys))
        put(width + low, wide, matmul(grad_scores, query))


def thirds(width):
    tiles = width // 128
    a, b = tiles // 3, tiles // 3
    c = tiles - a - b
    sizes = [a, b, (c + 1) // 2, c // 2]
    starts = [sum(sizes[:i]) for i in range(4)]
    return [(128 * s, 128 * n) for s, n in zip(starts, sizes)]


OWN_SLOTS = 8
PAIR_SLOTS = 4
AHEAD = 3
LAG = 2


class Reducer:
    def __init__(self, at, piece, outs, scratch, rows, width):
        self.at, self.piece, self.outs, self.width = at, piece, outs, width
        (
            self.own, self.pair, self.first_a, self.first_b, self.second_a, self.second_b,
            self.hops, self.hops_c, self.flat_a, self.flat_b, self.last_a, self.last_b, self.done,
            self.own_in, self.core_s, self.core_r, self.fa_s, self.fa_r, self.fb_s, self.fb_r,
            self.sa_s, self.sa_r, self.sb_s, self.sb_r, self.hop_s, self.hop_r, self.hopc_s, self.hopc_r,
            self.ca_s, self.ca_r, self.cb_s, self.cb_r, self.end_s, self.end_r, self.out_sem, self.credit,
        ) = scratch
        self.ring = at.ring
        self.total = 3 * self.ring * 2
        self.spans = self.halves(rows)
        self.sent, self.flights = {}, {}
        self.loose, self.outgoing = [], []
        self.cols = [pl.ds(*part) for part in thirds(width)]
        a, b = thirds(width)[1]
        self.cols_ab = pl.ds(0, a + b)
        self.cols_c = pl.ds(a + b, width - a - b)

    @staticmethod
    def halves(rows):
        top = -(-rows // 32) * 16
        return (0, top), (top, rows - top)

    def place(self, n):
        half = n % 2
        k, j = divmod(n // 2, self.ring)
        return k, j, half, self.spans[half][1]

    @staticmethod
    def scratch(rows, width, fsdp):
        ring = fsdp // 2
        total = 3 * ring * 2
        full, rows = rows, Reducer.halves(rows)[0][1]
        low, vmem, dma = jnp.bfloat16, pltpu.VMEM, pltpu.SemaphoreType.DMA
        a, b, c, d = [size for _, size in thirds(width)]
        arrays = [
            vmem((OWN_SLOTS, QUARTERS, rows, width), low),
            vmem((PAIR_SLOTS, QUARTERS, rows, width), low),
            vmem((total, 2, rows, a), low),
            vmem((total, 2, rows, b), low),
            vmem((total, rows, a), low),
            vmem((total, rows, b), low),
            vmem((3, 2, ring - 1, rows, a + b), low),
            vmem((3, 2, ring - 1, QUARTERS, rows, c + d), low),
            vmem((3, 2, 2, rows, c), low),
            vmem((3, 2, 2, rows, d), low),
            vmem((3, 2, rows, c), low),
            vmem((3, 2, rows, d), low),
            vmem((3, QUARTERS, full, width), low),
        ]
        sems = (
            [dma((total, QUARTERS))] * 3
            + [dma((total, 2))] * 4
            + [dma((total,))] * 4
            + [dma((3, 2, ring - 1))] * 4
            + [dma((3, 2, 3))] * 4
            + [dma((3, 2, 4))] * 2
            + [dma((3, 2))]
            + [pltpu.SemaphoreType.REGULAR]
        )
        return arrays + sems

    def go(self, n, *parts):
        copy = remote(*parts)
        copy.start()
        self.sent.setdefault(n, []).append(copy)
        return copy

    def prefetch(self, n):
        at = self.at
        k, j, half, size = self.place(n)
        slot, pair_slot = n % OWN_SLOTS, n % PAIR_SLOTS
        for copy in self.sent.pop(n - OWN_SLOTS, []):
            copy.wait_send()
        mine = at.shard((j + 1) % self.ring)
        other = mine + 1 - 2 * at.c
        if n >= PAIR_SLOTS:
            pl.semaphore_wait(self.credit, 1)
        brought, pairs = [], []
        span, here = pl.ds(*self.spans[half]), pl.ds(0, size)
        for q in range(QUARTERS):
            copy = pltpu.make_async_copy(self.piece(k, mine, q, span), self.own.at[slot, q, here], self.own_in.at[n, q])
            copy.start()
            brought.append(copy)
            copy = remote(
                self.piece(k, other, q, span), self.pair.at[pair_slot, q, here], self.core_s.at[n, q], self.core_r.at[n, q], at.core
            )
            copy.start()
            pairs.append(copy)
        self.loose += pairs
        self.flights[n] = (brought, pairs)

    def plane_first(self, n, slot, here, cols_a, cols_b, land_a, land_b, sems):
        at, own = self.at, self.own
        (sa, ra), (sb, rb) = sems
        return [
            self.go(n, own.at[slot, at.qd, here, cols_a], land_a.at[1, here], sa.at[1], ra.at[1], at.x),
            self.go(n, own.at[slot, at.qd, here, cols_b], land_b.at[1, here], sb.at[1], rb.at[1], at.y),
            self.go(n, own.at[slot, at.qx, here, cols_a], land_a.at[0, here], sa.at[0], ra.at[0], at.x),
            self.go(n, own.at[slot, at.qy, here, cols_b], land_b.at[0, here], sb.at[0], rb.at[0], at.y),
        ]

    def plane_second(self, n, slot, here, copies, cols_a, cols_b, land_a, land_b, next_a, next_b, sems):
        at, own = self.at, self.own
        one_d, two_d, one, two = copies
        (sa, ra), (sb, rb) = sems
        one_d.wait_recv()
        own[slot, at.qy, here, cols_a] = own[slot, at.qy, here, cols_a] + land_a[1, here]
        on_a = self.go(n, own.at[slot, at.qy, here, cols_a], next_a.at[here], sa, ra, at.y)
        two_d.wait_recv()
        own[slot, at.qx, here, cols_b] = own[slot, at.qx, here, cols_b] + land_b[1, here]
        on_b = self.go(n, own.at[slot, at.qx, here, cols_b], next_b.at[here], sb, rb, at.x)
        one.wait_recv()
        own[slot, at.q, here, cols_a] = own[slot, at.q, here, cols_a] + land_a[0, here]
        two.wait_recv()
        own[slot, at.q, here, cols_b] = own[slot, at.q, here, cols_b] + land_b[0, here]
        return [on_a, on_b]

    def plane_third(self, slot, here, copies, cols_a, cols_b, next_a, next_b):
        at, own = self.at, self.own
        for copy in copies:
            copy.wait_recv()
        own[slot, at.q, here, cols_a] = own[slot, at.q, here, cols_a] + next_a[here, :]
        own[slot, at.q, here, cols_b] = own[slot, at.q, here, cols_b] + next_b[here, :]

    def one(self, n):
        at, own, pair = self.at, self.own, self.pair
        k, j, half, size = self.place(n)
        slot, pair_slot = n % OWN_SLOTS, n % PAIR_SLOTS
        here = pl.ds(0, size)
        brought, pairs = self.flights[n]
        for q in range(QUARTERS):
            brought[q].wait()
            pairs[q].wait_recv()

        @pl.loop(0, QUARTERS)
        def _(q):
            own[slot, q, here, :] = own[slot, q, here, :] + pair[pair_slot, q, here, :]

        if n + PAIR_SLOTS < self.total:
            pl.semaphore_signal(self.credit, inc=1, device_id=at.core, device_id_type=MESH)
        a, b, c, d = self.cols
        self.flights[n] = self.plane_first(
            n, slot, here, a, b, self.first_a.at[n], self.first_b.at[n],
            ((self.fa_s.at[n], self.fa_r.at[n]), (self.fb_s.at[n], self.fb_r.at[n])),
        )
        if j > 0:
            self.flights[k, half, "c"].wait_recv()

            @pl.loop(0, QUARTERS)
            def _(q):
                own[slot, q, here, self.cols_c] = own[slot, q, here, self.cols_c] + self.hops_c[k, half, j - 1, q, here, :]

        if j < self.ring - 1:
            self.flights[k, half, "c"] = self.go(
                n, own.at[slot, slice(None), here, self.cols_c], self.hops_c.at[k, half, j, slice(None), here],
                self.hopc_s.at[k, half, j], self.hopc_r.at[k, half, j], at.up,
            )
        else:
            self.flights[k, half, "flat"] = self.plane_first(
                n, slot, here, c, d, self.flat_a.at[k, half], self.flat_b.at[k, half],
                ((self.ca_s.at[k, half], self.ca_r.at[k, half]), (self.cb_s.at[k, half], self.cb_r.at[k, half])),
            )

    def two(self, n):
        k, j, half, size = self.place(n)
        slot, here = n % OWN_SLOTS, pl.ds(0, size)
        a, b, c, d = self.cols
        self.flights[n] = self.plane_second(
            n, slot, here, self.flights[n], a, b, self.first_a.at[n], self.first_b.at[n], self.second_a.at[n], self.second_b.at[n],
            ((self.sa_s.at[n], self.sa_r.at[n]), (self.sb_s.at[n], self.sb_r.at[n])),
        )
        if j == self.ring - 1:
            self.flights[k, half, "flat"] = self.plane_second(
                n, slot, here, self.flights[k, half, "flat"], c, d, self.flat_a.at[k, half], self.flat_b.at[k, half],
                self.last_a.at[k, half], self.last_b.at[k, half],
                ((self.ca_s.at[k, half, 2], self.ca_r.at[k, half, 2]), (self.cb_s.at[k, half, 2], self.cb_r.at[k, half, 2])),
            )

    def three(self, n):
        at, own = self.at, self.own
        k, j, half, size = self.place(n)
        slot, here = n % OWN_SLOTS, pl.ds(0, size)
        a, b, c, d = self.cols
        self.plane_third(slot, here, self.flights[n], a, b, self.second_a.at[n], self.second_b.at[n])
        if j > 0:
            self.flights[k, half, "ab"].wait_recv()
            own[slot, at.q, here, self.cols_ab] = own[slot, at.q, here, self.cols_ab] + self.hops[k, half, j - 1, here, :]
        if j < self.ring - 1:
            self.flights[k, half, "ab"] = self.go(
                n, own.at[slot, at.q, here, self.cols_ab], self.hops.at[k, half, j, here],
                self.hop_s.at[k, half, j], self.hop_r.at[k, half, j], at.up,
            )
            return
        self.plane_third(slot, here, self.flights[k, half, "flat"], c, d, self.last_a.at[k, half], self.last_b.at[k, half])
        span = pl.ds(*self.spans[half])
        self.done[k, at.q, span, :] = own[slot, at.q, here, :]
        mine = self.done.at[k, at.q, span]
        sems = self.end_s.at[k, half], self.end_r.at[k, half]
        self.flights[k, half, "end"] = [
            self.keep(remote(mine, mine, sems[0].at[0], sems[1].at[0], at.x)),
            self.keep(remote(mine, mine, sems[0].at[1], sems[1].at[1], at.y)),
        ]

    def keep(self, copy):
        copy.start()
        self.loose.append(copy)
        return copy

    def four(self, n):
        at, done = self.at, self.done
        k, _, half, _ = self.place(n)
        (start_a, size_a), (start_b, size_b) = cut(self.width)
        span = pl.ds(*self.spans[half])
        sems = self.end_s.at[k, half], self.end_r.at[k, half]
        by_x, by_y = self.flights[k, half, "end"]
        by_x.wait_recv()
        part = done.at[k, at.qx, span, pl.ds(start_a, size_a)]
        first = self.keep(remote(part, part, sems[0].at[2], sems[1].at[2], at.y))
        by_y.wait_recv()
        part = done.at[k, at.qy, span, pl.ds(start_b, size_b)]
        second = self.keep(remote(part, part, sems[0].at[3], sems[1].at[3], at.x))
        self.flights[k, half, "end"] = [first, second]

    def five(self, n):
        k, _, half, _ = self.place(n)
        for copy in self.flights[k, half, "end"]:
            copy.wait_recv()
        span = pl.ds(*self.spans[half])
        copy = pltpu.make_async_copy(self.done.at[k, :, span], self.outs[k].at[:, span], self.out_sem.at[k, half])
        copy.start()
        self.outgoing.append(copy)

    def turn(self, t, starts):
        if t in starts:
            for n in range(t, t + AHEAD):
                self.prefetch(n)
        n = t + AHEAD
        if n < self.total and not any(t < start <= n for start in starts):
            self.prefetch(n)
        stages = (self.one, self.two, self.three, self.four, self.five)
        for i, stage in enumerate(stages):
            n = t - LAG * i
            if 0 <= n < self.total and (i < 3 or self.place(n)[1] == self.ring - 1):
                stage(n)

    def finish(self):
        for copy in self.outgoing:
            copy.wait()
        for copies in self.sent.values():
            for copy in copies:
                copy.wait_send()
        for copy in self.loose:
            copy.wait_send()


def back_kernel(dp, fsdp, width, images, seq, heads, *refs):
    ring = fsdp // 2
    fc2_ref, joint_ref, h1_ref, h2_ref, tokens_ref, weight_ref, down_ref, slope_ref = refs[:8]
    fc1_weight_ref, fc2_weight_ref, held_ref, attn_ref, cotangent_ref, forward_ref = refs[8:14]
    lse_ref, gates_ref, gate_two_ref, mod_ref, factor_ref, routers_ref, ada_hbm, pre_ref, picker_ref = refs[14:23]
    logit_ref, pick_ref = refs[23:25]
    refs = refs[25:]
    outs, refs = refs[:3], refs[3:]
    all_gm_ref, all_pre_ref, grad_tokens_ref, triple_ref, middle_ref, proj_ref, expand_ref = refs[:7]
    refs = refs[7:]
    joint, mixed, h1, middle, grad_joint, stage, total, inner, gm_row, gms, parts, mine_in, pres, ada_ref = refs[:14]
    in_sem, out_sem, mate_s, mate_r, cousin_s, cousin_r = refs[14:20]
    at = Place(dp, fsdp)
    at.greet()
    rows = fc1_weight_ref.shape[1]
    count = images * seq
    pad = pre_ref.shape[0]

    def piece(k, index, q, span):
        if k == 0:
            return fc2_ref.at[index, q, span]
        line = pl.ds(pl.multiple_of(index * rows + span.start, 8), span.size)
        if k == 1:
            return expand_ref.at[line, pl.ds(q * width, width)]
        if q == 3:
            return proj_ref.at[line, :]
        return triple_ref.at[q, line, :]

    work = Reducer(at, piece, outs, refs[20:], rows, width)
    moves, fetched = {}, []

    def fetch(name, src, dst):
        copy = pltpu.make_async_copy(src, dst, in_sem.at[len(fetched)])
        copy.start()
        fetched.append(copy)
        moves.setdefault(name, []).append(copy)

    def have(name):
        for copy in moves.pop(name):
            copy.wait()

    def store(name, src, dst, i):
        copy = pltpu.make_async_copy(src, dst, out_sem.at[i])
        copy.start()
        moves[name] = [copy]

    for n in range(AHEAD):
        work.prefetch(n)

    def lines(image):
        return pl.ds(image * seq, seq)

    def modulated(image, index):
        return mod_ref[image : image + 1, index * width : (index + 1) * width]

    chunks = fc1_weight_ref.shape[2] // width

    def bring_slope(c):
        fetch("s" + str(c), slope_ref.at[:, pl.ds(c * width, width)], grad_joint.at[:, pl.ds(c % 3 * width, width)])

    def bring_fc1(c):
        for f in range(fsdp):
            fetch("f" + str(c), fc1_weight_ref.at[f, :, pl.ds(c * width, width)], stage.at[0, pl.ds(f * rows, rows), :])

    def bring_fc2(c):
        for i in range(fsdp):
            f, q = c * (fsdp // chunks) + i // QUARTERS, i % QUARTERS
            fetch("d" + str(c), fc2_weight_ref.at[f, q], stage.at[2, pl.ds(i * rows, rows), :])

    def bring_image(image):
        fetch("image" + str(image), held_ref.at[lines(image)], middle.at[0])
        fetch("image" + str(image), attn_ref.at[lines(image)], middle.at[1])
        fetch("image" + str(image), cotangent_ref.at[lines(image)], joint.at[1, :, pl.ds(0, width)])

    fetch("down", down_ref, mixed)
    bring_fc2(0)
    bring_slope(0)
    fetch("h2", h2_ref, h1)
    bring_fc1(0)
    bring_slope(1)
    bring_slope(2)
    fetch("joint0", joint_ref.at[lines(0)], joint.at[0])
    bring_image(0)

    def part_of(c):
        return pl.ds(c % 3 * width, width)

    def lift(c):
        if c == 0:
            have("down")
        have("d" + str(c))
        have("s" + str(c))

        @pl.loop(0, images)
        def _(image):
            line = pl.ds(pl.multiple_of(image * seq, seq), seq)
            value = times_back(mixed[line, :], stage[2])
            grad_joint[line, part_of(c)] = (value * grad_joint[line, part_of(c)].astype(jnp.float32)).astype(jnp.bfloat16)

        if c + 1 < chunks:
            bring_fc2(c + 1)
        else:
            for f in range(fsdp):
                fetch("proj", weight_ref.at[f, :, pl.ds(3 * width, width)], stage.at[2, pl.ds(f * rows, rows), :])

    def weigh_fc1(c):
        if c == 0:
            have("h2")
        else:
            have("e" + str(c - 1))

        @pl.loop(0, width // 128)
        def _(m):
            line = pl.ds(pl.multiple_of(m * 128, 128), 128)
            stage[1, line, :] = times_rows(h1[:, line], grad_joint[:, part_of(c)]).astype(jnp.bfloat16)

        store("e" + str(c), stage.at[1], expand_ref.at[:, pl.ds(c * width, width)], 6 + 2 * images + c)

    def grow(c):
        have("f" + str(c))

        @pl.loop(0, images)
        def _(image):
            line = pl.ds(pl.multiple_of(image * seq, seq), seq)
            value = times_back(grad_joint[line, part_of(c)], stage[0])
            if c == 0:
                total[line, :] = value
            else:
                total[line, :] = total[line, :] + value

        if c + 1 < chunks:
            bring_fc1(c + 1)
        if c + 3 < chunks:
            bring_slope(c + 3)
        if c == chunks - 2:
            fetch("forward", forward_ref, grad_joint.at[:, part_of(c)])
        if c == chunks - 1:
            have("e" + str(c))
            fetch("h1", h1_ref, h1)

    forward_at, grad_at, proj_at = (chunks - 2) % 3, (chunks - 1) % 3, 2

    def norm_two(image):
        have("image" + str(image))
        scale, gate = 1.0 + modulated(image, 4), modulated(image, 2)
        step = 32

        def chunk(i, sums):
            shift_sum, gain_sum, gate_sum = sums
            line = pl.ds(pl.multiple_of(image * seq + i * step, step), step)
            here = pl.ds(pl.multiple_of(i * step, step), step)
            value = middle[0, here, :]
            grad = total[line, :] + logit_ref[line, :] * pick_ref[...]
            centered = value - jnp.mean(value, axis=-1, keepdims=True)
            inverse = lax.rsqrt(jnp.mean(centered * centered, axis=-1, keepdims=True) + EPSILON)
            normed = centered * inverse
            through = grad * scale
            back = through - jnp.mean(through, axis=-1, keepdims=True)
            back = back - normed * jnp.mean(through * normed, axis=-1, keepdims=True)
            through = joint[1, here, :width].astype(jnp.float32) + inverse * back
            total[line, :] = through
            grad_joint[line, grad_at * width : (grad_at + 1) * width] = (through * gate).astype(jnp.bfloat16)
            return (
                shift_sum + jnp.sum(grad, axis=0, keepdims=True),
                gain_sum + jnp.sum(grad * normed, axis=0, keepdims=True),
                gate_sum + jnp.sum(through * middle[1, here, :], axis=0, keepdims=True),
            )

        zero = jnp.zeros((1, width), jnp.float32)
        shift, gain, gated = lax.fori_loop(0, seq // step, chunk, (zero, zero, zero))
        for index, row in ((2, gated), (3, shift), (4, gain)):
            gm_row[image : image + 1, index * width : (index + 1) * width] = row
        store("mid" + str(image), total.at[lines(image)], middle_ref.at[lines(image)], 3 + images + image)
        if image + 1 < images:
            bring_image(image + 1)

    def mix():
        have("proj")

        @pl.loop(0, images)
        def _(image):
            line = pl.ds(pl.multiple_of(image * seq, seq), seq)
            grad = grad_joint[line, grad_at * width : (grad_at + 1) * width]
            mixed[line, :] = times_back(grad, stage[proj_at]).astype(jnp.bfloat16)

    def weigh_proj():
        have("forward")

        @pl.loop(0, width // 128)
        def _(m):
            line = pl.ds(pl.multiple_of(m * 128, 128), 128)
            column = pl.ds(pl.multiple_of(forward_at * width + m * 128, 128), 128)
            value = times_rows(grad_joint[:, column], grad_joint[:, grad_at * width : (grad_at + 1) * width])
            stage[1, line, :] = value.astype(jnp.bfloat16)

        store("projected", stage.at[1], proj_ref, 3 + 2 * images)

    fetch("ada", ada_hbm, ada_ref)
    inner[...] = jnp.zeros_like(inner)
    gm_row[...] = jnp.zeros_like(gm_row)

    def attention(image, half):
        slot = image % 2
        if half == 0:
            have("joint" + str(image))
            if image + 1 < images:
                fetch("joint" + str(image + 1), joint_ref.at[lines(image + 1)], joint.at[1 - slot])
        span = range(0, heads // 2) if half == 0 else range(heads // 2, heads)
        attend_back_image(
            joint.at[slot], mixed.at[lines(image)], gates_ref, lse_ref, grad_joint.at[lines(image)], inner, image, seq, heads, span
        )

    def weigh(q):
        if q == 0:
            have("h1")
            have("projected")
            fetch("tokens", tokens_ref, mixed)
        slot = q % 2
        if q >= 2:
            have("out" + str(q - 2))

        @pl.loop(0, width // 128)
        def _(m):
            line = pl.ds(pl.multiple_of(m * 128, 128), 128)
            stage[slot, line, :] = times_rows(h1[:, line], grad_joint[:, pl.ds(q * width, width)]).astype(jnp.bfloat16)

        store("out" + str(q), stage.at[slot], triple_ref.at[q], q)

    def bring_weight(q):
        for f in range(fsdp):
            fetch("w" + str(q), weight_ref.at[f, :, pl.ds(q * width, width)], stage.at[q % 2, pl.ds(f * rows, rows), :])

    def wait_terms():
        for q in (1, 2):
            have("out" + str(q))
        for image in range(images):
            have("mid" + str(image))
        bring_weight(0)
        bring_weight(1)
        fetch("middle0", middle_ref.at[lines(0)], middle.at[0])

    def spread(q):
        slot = q % 2
        have("w" + str(q))

        @pl.loop(0, images)
        def _(image):
            line = pl.ds(pl.multiple_of(image * seq, seq), seq)
            value = times_back(grad_joint[line, pl.ds(q * width, width)], stage[slot])
            if q == 0:
                total[line, :] = value
            else:
                total[line, :] = total[line, :] + value

        if q == 0:
            bring_weight(2)

    def norm(image):
        slot = image % 2
        if image == 0:
            have("tokens")
        have("middle" + str(image))
        if image + 1 < images:
            if image >= 1:
                have("done" + str(image - 1))
            fetch("middle" + str(image + 1), middle_ref.at[lines(image + 1)], middle.at[1 - slot])
        scale = 1.0 + modulated(image, 1)
        step = 32

        def chunk(i, sums):
            shift, gain = sums
            line = pl.ds(pl.multiple_of(image * seq + i * step, step), step)
            here = pl.ds(pl.multiple_of(i * step, step), step)
            value = mixed[line, :].astype(jnp.float32)
            grad = total[line, :]
            centered = value - jnp.mean(value, axis=-1, keepdims=True)
            inverse = lax.rsqrt(jnp.mean(centered * centered, axis=-1, keepdims=True) + EPSILON)
            normed = centered * inverse
            through = grad * scale
            back = through - jnp.mean(through, axis=-1, keepdims=True)
            back = back - normed * jnp.mean(through * normed, axis=-1, keepdims=True)
            middle[slot, here, :] = middle[slot, here, :] + inverse * back
            return (
                shift + jnp.sum(grad, axis=0, keepdims=True),
                gain + jnp.sum(grad * normed, axis=0, keepdims=True),
            )

        zero = jnp.zeros((1, width), jnp.float32)
        shift, gain = lax.fori_loop(0, seq // step, chunk, (zero, zero))
        store("done" + str(image), middle.at[slot], grad_tokens_ref.at[lines(image)], 3 + image)
        gm_row[image : image + 1, :width] = shift
        gm_row[image : image + 1, width : 2 * width] = gain

    mates, cousins = at.mates(), at.cousins()
    swaps = [Swap(mates, mate_s.at[i], mate_r.at[i]) for i in range(3)]
    far = [Swap(cousins, cousin_s.at[i], cousin_r.at[i]) for i in range(2)]
    small = []

    def keep(src, dst):
        copy = pltpu.make_async_copy(src, dst, out_sem.at[4 + 2 * images + len(small)])
        copy.start()
        small.append(copy)

    held = gms.shape[3]

    def tail_zero():
        gm_row[:, 5 * width :] = gate_two_ref[...]
        for f in range(fsdp):
            gms[0, f] = gm_row[:, f * held : (f + 1) * held].astype(jnp.bfloat16)
        swaps[0].start(lambda device: gms.at[0, device[1]], gms.at[1, at.f])

    def tail_one():
        have("ada")
        swaps[0].arrived()
        gms[1, at.f] = gms[0, at.f]
        every = gms[1].astype(jnp.float32).reshape(fsdp * pad, held).astype(jnp.bfloat16)
        parts[...] = matmul(every, ada_ref[...]).reshape(parts.shape)
        swaps[1].start(lambda device: parts.at[device[1]], mine_in.at[at.f])
        far[0].start(lambda device: gms.at[1], all_gm_ref.at[at.d])
        keep(gms.at[1], all_gm_ref.at[at.d])

    def tail_two():
        line = lax.broadcasted_iota(jnp.int32, (pad, 128), 0)
        gated = jnp.zeros((pad, 128), jnp.float32)
        for image in range(images):
            summed = lax.dot_general(
                jnp.ones((pad, seq), jnp.float32), inner[image], (((1,), (1,)), ((), ())),
                preferred_element_type=jnp.float32, precision=lax.Precision.HIGHEST,
            )
            gated = jnp.where(line == image, summed, gated)
        router = (gated * factor_ref[...]).astype(jnp.bfloat16)
        swaps[1].arrived()
        mine_in[at.f] = parts[at.f]
        grad_cond = jnp.sum(mine_in[...], axis=0) + times_back(router, routers_ref[...])
        pre_cond = pre_ref[...]
        sig = jax.nn.sigmoid(pre_cond)
        grad_pre = grad_cond * (sig * (1.0 + pre_cond * (1.0 - sig)))
        pres[at.f, :, :width] = (grad_pre + picker_ref[...]).astype(jnp.bfloat16)
        pres[at.f, :, width:] = router
        swaps[2].start(lambda device: pres.at[at.f], pres.at[at.f])

    def tail_three():
        swaps[2].arrived()
        far[1].start(lambda device: pres, all_pre_ref.at[at.d])
        keep(pres, all_pre_ref.at[at.d])

    first = [partial(step, c) for c in range(chunks) for step in (lift, weigh_fc1, grow)]
    early = [partial(norm_two, image) for image in range(images)] + [mix, weigh_proj]
    early += [partial(attention, image, half) for image in range(images) for half in range(2)]
    early += [partial(weigh, q) for q in range(3)] + [wait_terms]
    norms = [partial(norm, image) for image in range(images)]
    late = [[partial(spread, q)] for q in range(3)] + [[step] for step in norms]
    late += [[tail_zero], [], [tail_one], [], [], [tail_two], [], [], [tail_three]]
    split = 4 * ring
    starts = (split // 2, split)

    def some(steps, t, turns):
        upto = [-(-len(steps) * (t + i) // turns) for i in range(2)]
        for step in steps[upto[0] : upto[1]]:
            step()

    for t in range(work.total + 4 * LAG):
        work.turn(t, starts)
        if t < split:
            some(first + early, t, split)
        elif t - split < len(late):
            for step in late[t - split]:
                step()
    for swap in far:
        swap.arrived()
    for copy in small:
        copy.wait()
    for image in range(max(images - 2, 0), images):
        have("done" + str(image))
    for swap in swaps + far:
        swap.left()
    work.finish()


def back_half(
    term_fc2, joint, flat_one, flat_two, tokens, joint_full, grad_down, slope, fc1_full, fc2_full, middle, attn, cotangent,
    mixed, log_total, gates, gate_two,
    modulation, factor, routers, ada_weight, pre_cond, picker, logit, pick, width, images, seq, dp, fsdp,
):
    rows = fc1_full.shape[1]
    heads = gates.shape[1]
    count = images * seq
    pad = pre_cond.shape[0]
    columns = ada_weight.shape[0]
    dma, vmem = pltpu.SemaphoreType.DMA, pltpu.VMEM
    low, f32 = jnp.bfloat16, jnp.float32
    out = jax.ShapeDtypeStruct
    any_space, in_vmem = pl.BlockSpec(memory_space=pl.ANY), pl.BlockSpec(memory_space=vmem)
    in_smem = pl.BlockSpec(memory_space=pltpu.SMEM)
    return pl.pallas_call(
        partial(back_kernel, dp, fsdp, width, images, seq, heads),
        out_shape=[out((QUARTERS, rows, width), low)] * 3
        + [
            out((dp, fsdp, pad, columns), low),
            out((dp, fsdp, pad, width + 128), low),
            out((count, width), f32),
            out((3, width, width), low),
            out((count, width), f32),
            out((width, width), low),
            out((width, fc1_full.shape[2]), low),
        ],
        in_specs=[any_space] * 14 + [in_vmem, in_smem] + [in_vmem] * 4 + [any_space] + [in_vmem] * 4,
        out_specs=[any_space] * 10,
        scratch_shapes=[
            vmem((2, seq, 3 * width), low),
            vmem((count, width), low),
            vmem((count, width), low),
            vmem((2, seq, width), f32),
            vmem((count, 3 * width), low),
            vmem((3, width, width), low),
            vmem((count, width), f32),
            vmem((images, 128, seq), f32),
            vmem((pad, 6 * width), f32),
            vmem((2, fsdp, pad, columns), low),
            vmem((fsdp, pad, width), f32),
            vmem((fsdp, pad, width), f32),
            vmem((fsdp, pad, width + 128), low),
            vmem(ada_weight.shape, low),
            dma((12 * fsdp + 12 + 5 * images,)),
            dma((6 + 2 * images + fc1_full.shape[2] // width,)),
            dma((3, fsdp - 1)),
            dma((3, fsdp - 1)),
            dma((2, dp - 1)),
            dma((2, dp - 1)),
        ]
        + Reducer.scratch(rows, width, fsdp),
        compiler_params=pltpu.CompilerParams(
            collective_id=1, has_side_effects=True, vmem_limit_bytes=60 * 2**20
        ),
        name="back",
    )(
        term_fc2, joint, flat_one, flat_two, tokens, joint_full, grad_down, slope, fc1_full, fc2_full, middle, attn,
        cotangent, mixed, log_total,
        gates[:, None, :], gate_two, modulation, factor, routers, ada_weight, pre_cond, picker, logit, pick,
    )


def body(
    dp,
    fsdp,
    tokens,
    timesteps,
    labels,
    head_mask,
    keep_mask,
    cotangent,
    time_weight,
    class_table,
    ada_weight,
    head_router,
    qkv_weight,
    proj_weight,
    fc1_weight,
    fc2_weight,
    token_router,
):
    images, seq, width = tokens.shape
    heads = head_mask.shape[1]
    count = images * seq
    rows = qkv_weight.shape[0]
    hidden = fc1_weight.shape[1]
    entries = time_weight.shape[0] * fsdp
    me_fsdp = lax.axis_index("fsdp")
    pad = -(-(images + 2) // 8) * 8

    def padded(array, value=0.0):
        return jnp.pad(array, ((0, pad - images), (0, 0)), constant_values=value)

    embedded = sinusoid(timesteps, entries).astype(jnp.bfloat16)
    digits = jnp.stack([labels // DIGIT, labels % DIGIT], axis=1).astype(jnp.bfloat16)
    asked = jnp.concatenate(
        [padded(embedded), jnp.pad(padded(digits, -1.0), ((0, 0), (0, 126)))], axis=1
    )
    routers = jnp.pad(
        jnp.concatenate([head_router, token_router], axis=1), ((0, 0), (0, 127 - heads))
    )
    mask_float = head_mask.astype(jnp.float32)
    *gathered, flat_one, joint, log_total, mixed, attn, middle, flat_two, active, slope, grad_down, grad_shrink = front_half(
        [
            jnp.concatenate([qkv_weight, proj_weight], axis=1),
            fc1_weight,
            fc2_weight.reshape(QUARTERS, rows, width),
        ],
        asked,
        time_weight,
        class_table.T,
        ada_weight.T,
        routers,
        padded(jnp.pad(mask_float, ((0, 0), (0, 128 - heads)))),
        tokens.reshape(count, width),
        keep_mask.astype(jnp.float32).reshape(count, 1),
        cotangent.reshape(count, width),
        width,
        images,
        seq,
        heads,
        dp,
        fsdp,
    )
    joint_blocks, fc1_full, fc2_full, pre_cond_pad, modulation_pad, routers_full, all_cond, all_asked = gathered
    shrink = fc2_full.reshape(hidden, width)
    routers_full = routers_full.reshape(width, 128)
    chooser, picker = routers_full[:, :heads], routers_full[:, heads : heads + 1]
    everyone = dp * fsdp * pad
    all_cond = all_cond.reshape(everyone, width)
    all_asked = all_asked.reshape(everyone, asked.shape[1])
    pre_cond = pre_cond_pad[:images]
    cond = jax.nn.silu(pre_cond).astype(jnp.bfloat16)
    gate_two = modulation_pad[:images, None, 5 * width :]
    router_sig = jax.nn.sigmoid(matmul(cond, chooser))
    head_gates = mask_float * router_sig
    middle = middle.reshape(images, seq, width)
    rate = jax.nn.sigmoid(matmul(flat_two, picker)).reshape(images, seq, 1)
    downward = matmul(active, shrink).reshape(images, seq, width)
    kept = keep_mask.astype(jnp.float32)[:, :, None]
    kept_rate = kept * rate
    output = (middle + gate_two * kept_rate * downward).astype(jnp.bfloat16)
    grad_out = cotangent.astype(jnp.float32)
    grad_gate_two = jnp.sum(grad_out * kept_rate * downward, axis=1)
    grad_rate = jnp.sum(grad_out * gate_two * downward, axis=-1, keepdims=True) * kept
    grad_logit = (grad_rate * rate * (1.0 - rate)).astype(jnp.bfloat16).reshape(count, 1)
    grad_picker = times_rows(grad_logit, flat_two)
    picker_high = lax.reduce_precision(grad_picker, 8, 7)
    *sums, all_grad, all_pre, grad_inputs, _, _, _, _ = back_half(
        grad_shrink.reshape(fsdp, QUARTERS, rows, width),
        joint,
        flat_one,
        flat_two,
        tokens.reshape(count, width),
        joint_blocks,
        grad_down,
        slope,
        fc1_full,
        fc2_full,
        middle.reshape(count, width),
        attn,
        cotangent.reshape(count, width),
        mixed,
        log_total,
        head_gates,
        padded(grad_gate_two),
        modulation_pad,
        padded(jnp.pad(mask_float * router_sig * (1.0 - router_sig), ((0, 0), (0, 128 - heads)))),
        routers_full,
        ada_weight.T,
        pre_cond_pad,
        jnp.pad(jnp.concatenate([picker_high, grad_picker - picker_high], axis=0), ((pad - 2, 0), (0, 0))),
        grad_logit.astype(jnp.float32),
        picker.astype(jnp.float32).reshape(1, width),
        width,
        images,
        seq,
        dp,
        fsdp,
    )
    grad_inputs = grad_inputs.reshape(images, seq, width)
    if dp > QUARTERS:
        parts = list(sums)
        for hop in range(QUARTERS, dp, QUARTERS):
            pairs = [(i, (i + hop) % dp) for i in range(dp)]
            parts = [
                part.astype(jnp.float32) + lax.ppermute(s, "dp", pairs).astype(jnp.float32)
                for part, s in zip(parts, sums)
            ]
        sums = parts
    sums = [s.astype(jnp.float32) for s in sums]
    sum_triple = jnp.concatenate([sums[2][0], sums[2][1], sums[2][2]], axis=1)
    sum_merger = sums[2][3]
    sum_expand = jnp.concatenate([sums[1][i] for i in range(QUARTERS)], axis=1)
    sum_shrink = sums[0].reshape(QUARTERS * rows, width)

    sum_ada = times_rows(all_cond, all_grad.reshape(everyone, -1))
    sum_picker = lax.dynamic_slice_in_dim(
        jnp.sum(all_pre[:, :, pad - 2 :, :width].astype(jnp.float32), axis=(0, 1, 2)), me_fsdp * rows, rows, axis=0
    )[:, None]
    is_image = (jnp.arange(pad) < images)[None, None, :, None]
    all_pre = jnp.where(is_image, all_pre, jnp.bfloat16(0.0)).reshape(everyone, -1)
    all_router = all_pre[:, width : width + heads]
    all_pre = all_pre[:, :width]
    own_entries = entries // fsdp
    all_embedded = lax.dynamic_slice_in_dim(
        all_asked[:, :entries], me_fsdp * own_entries, own_entries, axis=1
    )
    classes = jnp.arange(class_table.shape[0], dtype=jnp.float32)
    all_digits = all_asked[:, entries : entries + 2].astype(jnp.float32)
    all_labels = all_digits[:, :1] * DIGIT + all_digits[:, 1:]
    all_rows = (all_labels == classes[None, :]).astype(jnp.bfloat16)
    sum_time = times_rows(all_embedded, all_pre)
    sum_table = times_rows(
        all_rows, lax.dynamic_slice_in_dim(all_pre, me_fsdp * rows, rows, axis=1)
    )
    sum_chooser = times_rows(
        lax.dynamic_slice_in_dim(all_cond, me_fsdp * rows, rows, axis=1), all_router
    )
    return (
        output,
        grad_inputs,
        sum_time,
        sum_table,
        sum_ada,
        sum_chooser,
        sum_triple,
        sum_merger,
        sum_expand,
        sum_shrink,
        sum_picker,
    )


def solution(mesh):
    images = P(("dp", "fsdp"), None, None)
    pairs = P(("dp", "fsdp"), None)
    single = P(("dp", "fsdp"))
    by_row, by_column = P("fsdp", None), P(None, "fsdp")
    in_specs = (
        images, single, single, pairs, pairs, images,
        by_row, by_column, by_column, by_row, by_row, by_row, by_row, by_row, by_row,
    )
    out_specs = (
        images, images,
        by_row, by_column, by_column, by_row, by_row, by_row, by_row, by_row, by_row,
    )
    return jax.shard_map(
        partial(body, mesh.shape["dp"], mesh.shape["fsdp"]),
        mesh=mesh, in_specs=in_specs, out_specs=out_specs, check_vma=False,
    )
```

```python
from functools import partial
import math

import jax
import jax.numpy as jnp
from jax import lax
from jax.experimental import pallas as pl
from jax.experimental.pallas import tpu as pltpu
from jax.sharding import PartitionSpec as P

EPSILON = 1e-06
MESH = pl.DeviceIdType.MESH
QUARTERS = 4
DIGIT = 256


def sinusoid(steps, entries):
    half = entries // 2
    freqs = jnp.exp(-math.log(10000.0) * jnp.arange(half, dtype=jnp.float32) / half)
    angles = steps.astype(jnp.float32)[:, None] * freqs[None, :]
    return jnp.concatenate([jnp.cos(angles), jnp.sin(angles)], axis=1)


def layer_norm(value):
    centered = value - jnp.mean(value, axis=-1, keepdims=True)
    return centered * lax.rsqrt(jnp.mean(centered * centered, axis=-1, keepdims=True) + EPSILON)


def norm_back(value, grad):
    _, pull = jax.vjp(layer_norm, value)
    return pull(grad)[0]


def matmul(left, right):
    return jnp.dot(left, right, preferred_element_type=jnp.float32)


def times_rows(left, right):
    return lax.dot_general(
        left, right, (((0,), (0,)), ((), ())), preferred_element_type=jnp.float32
    )


def times_back(left, right):
    return lax.dot_general(
        left, right, (((1,), (1,)), ((), ())), preferred_element_type=jnp.float32
    )


class Place:
    def __init__(self, dp, fsdp):
        ring = fsdp // 2
        self.dp, self.fsdp, self.ring = dp, fsdp, ring
        d = lax.axis_index("dp")
        f = lax.axis_index("fsdp")
        self.d, self.f = d, f
        self.z = f // 2
        self.c = f % 2
        self.q = d % QUARTERS
        dx = d + 1 - 2 * (d % 2)
        dy = d + 2 - 4 * ((d // 2) % 2)
        self.qx = dx % QUARTERS
        self.qy = dy % QUARTERS
        self.qd = (self.qx + self.qy - self.q + QUARTERS) % QUARTERS
        self.core = (d, f + 1 - 2 * (f % 2))
        self.x = (dx, f)
        self.y = (dy, f)
        self.up = (d, ((self.z + 1) % ring) * 2 + self.c)
        self.down = (d, ((self.z + ring - 1) % ring) * 2 + self.c)

    def shard(self, back):
        return ((self.z + self.ring - back) % self.ring) * 2 + self.c

    def mates(self):
        return [(self.d, (self.f + offset) % self.fsdp) for offset in range(1, self.fsdp)]

    def cousins(self):
        return [((self.d + offset) % self.dp, self.f) for offset in range(1, self.dp)]

    def greet(self):
        barrier = pltpu.get_barrier_semaphore()
        near = self.mates() + self.cousins()
        for other in near:
            pl.semaphore_signal(barrier, inc=1, device_id=other, device_id_type=MESH)
        pl.semaphore_wait(barrier, len(near))


def remote(src, dst, send, recv, device):
    return pltpu.make_async_remote_copy(
        src_ref=src, dst_ref=dst, send_sem=send, recv_sem=recv, device_id=device, device_id_type=MESH
    )


class Swap:
    def __init__(self, partners, send, recv):
        self.partners, self.send, self.recv = partners, send, recv
        self.copies = []

    def start(self, source, landing):
        for i, device in enumerate(self.partners):
            copy = remote(source(device), landing, self.send.at[i], self.recv.at[i], device)
            copy.start()
            self.copies.append(copy)

    def arrived(self):
        for copy in self.copies:
            copy.wait_recv()

    def left(self):
        for copy in self.copies:
            copy.wait_send()


def cut(width):
    first = ((width // 128 + 1) // 2) * 128
    return (0, first), (first, width - first)


def view(ref, lead, q, width, part=None, span=None):
    start, size = (0, width) if part is None else part
    lines = slice(None) if span is None else pl.ds(*span)
    flat = ref.shape[-1] != width
    if flat:
        column = pl.multiple_of(q * width + start, 128)
        return ref.at[(*lead, lines, pl.ds(column, size))]
    return ref.at[(*lead, q, lines, pl.ds(start, size))]


def front_kernel(dp, fsdp, width, images, seq, heads, *refs):
    weights = 3
    ring = fsdp // 2
    shards, refs = refs[:weights], refs[weights:]
    ask_ref, time_ref, table_hbm, ada_hbm, router_ref, mask_ref, tokens_ref, keep_ref, cotangent_ref = refs[:9]
    refs = refs[9:]
    fulls, refs = refs[:weights], refs[weights:]
    pre_ref, mod_ref, routers_ref, all_cond_ref, all_ask_ref = refs[:5]
    h1_out, joint_out, lse_out, mixed_out, attn_out, middle_out, h2_out, active_out, slope_out = refs[5:14]
    down_out, term_out = refs[14:16]
    refs = refs[16:]
    asks, parts, mine_in, conds, columns, mods, gates = refs[:7]
    tokens, h1, joint, lse, mixed, attn, middle, h2, stage, table_ref, ada_ref, actives, slopes = refs[7:20]
    cotangent, down, term, move_sem = refs[20:24]
    refs = refs[24:]
    (own_sem, core_s, core_r, ring_s, ring_r, x_s, x_r, y_s, y_r, a_s, a_r, b_s, b_r) = refs[:13]
    mate_s, mate_r, cousin_s, cousin_r, small_sem = refs[13:]
    at = Place(dp, fsdp)
    part_a, part_b = cut(width)
    at.greet()
    sent = []
    mates, cousins = at.mates(), at.cousins()
    swaps = [Swap(mates, mate_s.at[i], mate_r.at[i]) for i in range(5)]
    far = [Swap(cousins, cousin_s.at[i], cousin_r.at[i]) for i in range(2)]
    pad = ask_ref.shape[0]
    group = fsdp * pad
    rows = table_ref.shape[0]
    spans = Reducer.halves(rows)
    chunks = shards[1].shape[1] // width

    def go(copy):
        copy.start()
        sent.append(copy)
        return copy

    def ring_copy(k, hop, half):
        index = at.shard(hop - 1)
        src = (shards[k], ()) if hop == 1 else (fulls[k], (index,))
        dst = view(fulls[k], (index,), at.q, width, span=spans[half])
        sems = ring_s.at[k, hop - 1, half], ring_r.at[k, hop - 1, half]
        return remote(view(*src, at.q, width, span=spans[half]), dst, *sems, at.up)

    small = []

    def keep(src, dst):
        copy = pltpu.make_async_copy(src, dst, small_sem.at[len(small)])
        copy.start()
        small.append(copy)

    def cond_one():
        have("table")
        swaps[0].arrived()
        asks[at.f] = ask_ref[...]
        every = asks[...].astype(jnp.float32).reshape(group, asks.shape[2])
        entries = every.shape[1] - 128
        own_rows = time_ref.shape[0]
        lanes = lax.broadcasted_iota(jnp.int32, (group, entries), 1)
        held = (lanes >= at.f * own_rows) & (lanes < (at.f + 1) * own_rows)
        embedded = jnp.where(held, every[:, :entries], 0.0).astype(jnp.bfloat16)
        stacked = jnp.concatenate([time_ref[...]] * fsdp, axis=0)
        label = (every[:, entries : entries + 1] * DIGIT + every[:, entries + 1 : entries + 2]).astype(jnp.int32)
        classes = table_ref.shape[1]
        picks = (label == lax.broadcasted_iota(jnp.int32, (group, classes), 1)).astype(jnp.float32)
        picked = times_back(picks.astype(jnp.bfloat16), table_ref[...]).astype(jnp.bfloat16)
        spot = lax.broadcasted_iota(jnp.int32, (rows, width), 1)
        line = lax.broadcasted_iota(jnp.int32, (rows, width), 0)
        place = (spot == line + at.f * rows).astype(jnp.float32).astype(jnp.bfloat16)
        partial_sum = matmul(embedded, stacked) + matmul(picked, place)
        parts[...] = partial_sum.reshape(fsdp, pad, width)
        swaps[1].start(lambda device: parts.at[device[1]], mine_in.at[at.f])

    def cond_two():
        swaps[1].arrived()
        mine_in[at.f] = parts[at.f]
        pre_cond = jnp.sum(mine_in[...], axis=0)
        pre_ref[...] = pre_cond
        conds[at.f] = (pre_cond * jax.nn.sigmoid(pre_cond)).astype(jnp.bfloat16)
        swaps[2].start(lambda device: conds.at[at.f], conds.at[at.f])

    def cond_three():
        have("ada")
        swaps[2].arrived()
        every = conds[...].astype(jnp.float32).reshape(group, width).astype(jnp.bfloat16)
        columns[...] = times_back(every, ada_ref[...]).reshape(columns.shape)
        swaps[3].start(lambda device: columns.at[device[1]], mods.at[at.f])

    def cond_four():
        swaps[3].arrived()
        swaps[4].arrived()
        mods[at.f] = columns[at.f]
        routers_ref[at.f] = router_ref[...]
        held = mods.shape[2]
        for f in range(fsdp):
            mod_ref[:, f * held : (f + 1) * held] = mods[f]
        chosen = matmul(conds[at.f], routers_ref[...].reshape(width, router_ref.shape[1]))
        gates[...] = mask_ref[...] * jax.nn.sigmoid(chosen)

    moves, moved = {}, []

    def move(name, src, dst):
        copy = pltpu.make_async_copy(src, dst, move_sem.at[len(moved)])
        copy.start()
        moved.append(copy)
        moves.setdefault(name, []).append(copy)

    def have(name):
        for copy in moves.pop(name):
            copy.wait()

    def line_of(image):
        return pl.ds(image * seq, seq)

    def bring(q):
        for f in range(fsdp):
            src = fulls[0].at[f, :, pl.ds(q * width, width)]
            move("w" + str(q), src, stage.at[q % 2, pl.ds(f * rows, rows), :])

    def modulated(image, index):
        return mod_ref[image : image + 1, index * width : (index + 1) * width]

    step = 32

    def normed(value, scale, shift):
        centered = value - jnp.mean(value, axis=-1, keepdims=True)
        inverse = lax.rsqrt(jnp.mean(centered * centered, axis=-1, keepdims=True) + EPSILON)
        return (centered * inverse * scale + shift).astype(jnp.bfloat16)

    def joint_here():
        for copy in landed[0]:
            copy.wait_recv()
        locals_[0].wait()
        bring(0)
        bring(1)

    def norm_one(image):
        if image == 0:
            have("tokens")
        shift, scale = modulated(image, 0), 1.0 + modulated(image, 1)

        @pl.loop(0, seq // step)
        def _(i):
            line = pl.ds(pl.multiple_of(image * seq + i * step, step), step)
            h1[line, :] = normed(tokens[line, :].astype(jnp.float32), scale, shift)

        if image == images - 1:
            move("h1", h1, h1_out)

    def project(q):
        have("w" + str(q))

        @pl.loop(0, images)
        def _(image):
            line = pl.ds(pl.multiple_of(image * seq, seq), seq)
            joint[line, pl.ds(q * width, width)] = matmul(h1[line, :], stage[q % 2]).astype(jnp.bfloat16)

        if q + 2 < QUARTERS:
            bring(q + 2)
        if q == 2:
            move("joint", joint, joint_out)

    def attention(image, half):
        span = range(0, heads // 2) if half == 0 else range(heads // 2, heads)
        attend_image(joint.at[line_of(image)], gates, mixed.at[line_of(image)], lse, image, seq, heads, span)
        if image == images - 1 and half == 1:
            move("mixed", mixed, mixed_out)
            move("lse", lse, lse_out)

    def merge(image):
        if image == 0:
            have("w3")
        line = line_of(image)
        attn[line, :] = matmul(mixed[line, :], stage[1])
        gate, shift, scale = modulated(image, 2), modulated(image, 3), 1.0 + modulated(image, 4)

        @pl.loop(0, seq // step)
        def _(i):
            here = pl.ds(pl.multiple_of(image * seq + i * step, step), step)
            value = tokens[here, :].astype(jnp.float32) + gate * attn[here, :]
            middle[here, :] = value
            h2[here, :] = normed(value, scale, shift)

        move("attn", attn.at[line], attn_out.at[line])
        move("middle", middle.at[line], middle_out.at[line])
        move("h2", h2.at[line], h2_out.at[line])

    def bring_fc1(c):
        for f in range(fsdp):
            src = fulls[1].at[f, :, pl.ds(c * width, width)]
            move("e" + str(c), src, stage.at[c % 2, pl.ds(f * rows, rows), :])

    def fc1_here():
        for copy in landed[1]:
            copy.wait_recv()
        locals_[1].wait()
        bring_fc1(0)
        bring_fc1(1)

    def expand(c):
        slot = c % 2
        have("e" + str(c))
        if c >= 2:
            have("active" + str(c - 2))
        bend = math.sqrt(2.0 / math.pi)
        size = 128
        pair = 2 if images * seq % (2 * size) == 0 else 1

        @pl.loop(0, images * seq // (pair * size))
        def _(i):
            for inner in range(pair):
                line = pl.ds(pl.multiple_of((i * pair + inner) * size, size), size)
                value = matmul(h2[line, :], stage[slot])
                square = value * value
                bent = jnp.tanh(value * (bend + bend * 0.044715 * square))
                half = 0.5 + 0.5 * bent
                actives[slot, line, :] = (value * half).astype(jnp.bfloat16)
                lean = value * (0.5 - 0.5 * bent * bent) * (bend + 3.0 * bend * 0.044715 * square)
                slopes[slot, line, :] = (half + lean).astype(jnp.bfloat16)

        if c + 2 < chunks:
            bring_fc1(c + 2)
        columns_of = pl.ds(c * width, width)
        move("active" + str(c), actives.at[slot], active_out.at[:, columns_of])
        move("active" + str(c), slopes.at[slot], slope_out.at[:, columns_of])

    def route(image):
        if image == 0:
            have("cotangent")
        line = line_of(image)
        chosen = matmul(h2[line, :], routers_ref[...].reshape(width, router_ref.shape[1]))
        kept = keep_ref[line, :] * jax.nn.sigmoid(chosen[:, heads : heads + 1])
        down[line, :] = (cotangent[line, :].astype(jnp.float32) * modulated(image, 5) * kept).astype(jnp.bfloat16)
        if image == images - 1:
            move("down", down, down_out)

    def weigh_fc2(c):
        if c > 0:
            have("term" + str(c - 1))

        @pl.loop(0, width // 128)
        def _(m):
            line = pl.ds(pl.multiple_of(m * 128, 128), 128)
            term[line, :] = times_rows(actives[c % 2, :, line], down[...]).astype(jnp.bfloat16)

        move("term" + str(c), term, term_out.at[pl.ds(c * width, width), :])

    move("table", table_hbm, table_ref)
    move("ada", ada_hbm, ada_ref)
    move("tokens", tokens_ref, tokens)
    move("cotangent", cotangent_ref, cotangent)
    work = [joint_here] + [partial(norm_one, image) for image in range(images)]
    work += [partial(project, q) for q in range(3)]
    work += [partial(attention, image, half) for image in range(images) for half in range(2)]
    work += [partial(merge, image) for image in range(images)] + [partial(route, image) for image in range(images)]

    def share():
        far[0].start(lambda device: conds, all_cond_ref.at[at.d])
        far[1].start(lambda device: asks, all_ask_ref.at[at.d])
        keep(conds, all_cond_ref.at[at.d])
        keep(asks, all_ask_ref.at[at.d])

    extra = {2: cond_one, 4: cond_two, 6: cond_three, 9: cond_four, 4 * (ring - 1) + 2 * LAG: share}
    swaps[0].start(lambda device: ask_ref, asks.at[at.f])
    swaps[4].start(lambda device: router_ref, routers_ref.at[at.f])

    items = [(k, hop, half) for k in range(weights) for hop in range(1, ring) for half in range(2)]
    rings = {item: go(ring_copy(*item)) for item in items[:2]}
    locals_, landed = [], [[], [], []]
    for k in range(weights):
        copy = pltpu.make_async_copy(shards[k], fulls[k].at[at.f], own_sem.at[k])
        copy.start()
        locals_.append(copy)
        landed[k].append(go(remote(shards[k], fulls[k].at[at.f], core_s.at[k, 0, 0], core_r.at[k, 0, 0], at.core)))
    flights = {}
    each = 2 * (ring - 1)
    begin, second = each + 2 * LAG - 1, 2 * each + 2 * LAG - 1
    done = 0
    for turn in range(len(items) + 2 * LAG):
        if turn < len(items):
            k, hop, half = items[turn]
            rings[items[turn]].wait_recv()
            if turn + 2 < len(items):
                rings[items[turn + 2]] = go(ring_copy(*items[turn + 2]))
            mine = view(fulls[k], (at.shard(hop),), at.q, width, span=spans[half])
            place = (k, hop - 1, half)
            flights[turn] = (
                go(remote(mine, mine, x_s.at[place], x_r.at[place], at.x)),
                go(remote(mine, mine, y_s.at[place], y_r.at[place], at.y)),
            )
        n = turn - LAG
        if 0 <= n < len(items):
            k, hop, half = items[n]
            place = (k, hop - 1, half)
            by_x, by_y = flights[n]
            by_x.wait_recv()
            part = view(fulls[k], (at.shard(hop),), at.qx, width, part_a, spans[half])
            first = go(remote(part, part, a_s.at[place], a_r.at[place], at.y))
            by_y.wait_recv()
            part = view(fulls[k], (at.shard(hop),), at.qy, width, part_b, spans[half])
            flights[n] = (first, go(remote(part, part, b_s.at[place], b_r.at[place], at.x)))
        n = turn - 2 * LAG
        if 0 <= n < len(items):
            k, hop, half = items[n]
            for copy in flights[n]:
                copy.wait_recv()
            span = pl.ds(*spans[half])
            whole = fulls[k].at[(at.shard(hop), span) if k < 2 else (at.shard(hop), slice(None), span)]
            landed[k].append(go(remote(whole, whole, core_s.at[k, hop, half], core_r.at[k, hop, half], at.core)))
        if turn in extra:
            extra[turn]()
        if begin <= turn < second:
            upto = -(-len(work) * (turn + 1 - begin) // (second - begin))
            for part in work[done:upto]:
                part()
            done = upto
        elif turn == second:
            fc1_here()
        elif second < turn <= second + chunks:
            expand(turn - second - 1)
            weigh_fc2(turn - second - 1)
    for swap in far:
        swap.arrived()
    for copy in landed[2]:
        copy.wait_recv()
    for copy in locals_[2:] + small:
        copy.wait()
    for c in range(max(chunks - 2, 0), chunks):
        have("active" + str(c))
    have("down")
    have("term" + str(chunks - 1))
    for name in ("h1", "joint", "mixed", "lse", "attn", "middle", "h2"):
        have(name)
    for swap in swaps + far:
        swap.left()
    for copy in sent:
        copy.wait_send()


def front_half(
    shards, asked, time_weight, class_table, ada_weight, routers, mask, tokens, keep, cotangent, width, images, seq, heads,
    dp, fsdp,
):
    ring = fsdp // 2
    dma, vmem = pltpu.SemaphoreType.DMA, pltpu.VMEM
    low, f32 = jnp.bfloat16, jnp.float32
    steps = dma((3, ring - 1, 2))
    hidden = shards[1].shape[1]
    pad, asking = asked.shape
    columns = ada_weight.shape[0]
    count = images * seq
    out = jax.ShapeDtypeStruct
    any_space, in_vmem = pl.BlockSpec(memory_space=pl.ANY), pl.BlockSpec(memory_space=vmem)
    results = [
        out((count, width), low),
        out((count, 3 * width), low),
        out((images, heads, seq), f32),
        out((count, width), low),
        out((count, width), f32),
        out((count, width), f32),
        out((count, width), low),
    ]
    return pl.pallas_call(
        partial(front_kernel, dp, fsdp, width, images, seq, heads),
        out_shape=[out((fsdp, *s.shape), s.dtype) for s in shards]
        + [
            out((pad, width), f32),
            out((pad, 6 * width), f32),
            out((fsdp, *routers.shape), routers.dtype),
            out((dp, fsdp, pad, width), low),
            out((dp, fsdp, pad, asking), low),
        ]
        + results
        + [out((count, hidden), low)] * 2
        + [out((count, width), low), out((hidden, width), low)],
        in_specs=[any_space] * 3 + [in_vmem] * 2 + [any_space] * 2 + [in_vmem] * 2 + [any_space, in_vmem, any_space],
        out_specs=[any_space] * 3 + [in_vmem] * 3 + [any_space] * 13,
        scratch_shapes=[
            vmem((fsdp, pad, asking), low),
            vmem((fsdp, pad, width), f32),
            vmem((fsdp, pad, width), f32),
            vmem((fsdp, pad, width), low),
            vmem((fsdp, pad, columns), f32),
            vmem((fsdp, pad, columns), f32),
            vmem((pad, 128), f32),
            vmem((count, width), low),
        ]
        + [vmem(r.shape, r.dtype) for r in results]
        + [vmem((2, width, width), low), vmem(class_table.shape, low), vmem(ada_weight.shape, low)]
        + [vmem((2, count, width), low)] * 2
        + [vmem((count, width), low)] * 2
        + [vmem((width, width), low)]
        + [dma((8 * fsdp + 17 + 3 * images + hidden // width,))]
        + [dma((3,)), dma((3, ring, 2)), dma((3, ring, 2))]
        + [steps] * 10
        + [dma((5, fsdp - 1))] * 2
        + [dma((2, dp - 1))] * 2
        + [dma((2,))],
        compiler_params=pltpu.CompilerParams(
            collective_id=0, has_side_effects=True, vmem_limit_bytes=60 * 2**20
        ),
        name="front",
    )(*shards, asked, time_weight, class_table, ada_weight, routers, mask, tokens, keep, cotangent)


def window(head, size):
    low = head * size // 128 * 128
    high = -(-(head + 1) * size // 128) * 128
    spot = low + lax.broadcasted_iota(jnp.int32, (1, high - low), 1)
    own = ((spot >= head * size) & (spot < (head + 1) * size)).astype(jnp.float32).astype(jnp.bfloat16)
    return low, high - low, own


def attend_image(joint, gates, mixed, lse, image, seq, heads, span):
    width = mixed.shape[1]
    size = width // heads
    scale = size ** (-0.5)
    if span[0] == 0:
        mixed[...] = jnp.zeros((seq, width), mixed.dtype)
    for head in span:
        low, wide, own = window(head, size)
        query = joint[:, pl.ds(low, wide)] * own
        keys = joint[:, pl.ds(width + low, wide)]
        values = joint[:, pl.ds(2 * width + low, wide)] * own
        raw = times_back(keys, query) * scale
        peak = jnp.max(raw, axis=0, keepdims=True)
        expo = jnp.exp(raw - peak)
        total = jnp.sum(expo, axis=0, keepdims=True)
        lse[image, head : head + 1, :] = peak + jnp.log(total)
        probs = (expo * (1.0 / total)).astype(jnp.bfloat16)
        attended = times_rows(probs, values) * gates[image : image + 1, head : head + 1]
        mixed[:, pl.ds(low, wide)] = mixed[:, pl.ds(low, wide)] + attended.astype(jnp.bfloat16)


def attend_back_image(joint, grad_mixed, gates, lse, grad_joint, grad_gates, image, seq, heads, span):
    width = grad_mixed.shape[1]
    size = width // heads
    scale = size ** (-0.5)
    if span[0] == 0:
        grad_joint[...] = jnp.zeros((seq, 3 * width), grad_joint.dtype)

    def put(column, wide, value):
        here = pl.ds(column, wide)
        grad_joint[:, here] = grad_joint[:, here] + value.astype(jnp.bfloat16)

    for head in span:
        low, wide, own = window(head, size)
        query = joint[:, pl.ds(low, wide)] * own
        keys = joint[:, pl.ds(width + low, wide)] * own
        values = joint[:, pl.ds(2 * width + low, wide)]
        grad = grad_mixed[:, pl.ds(low, wide)] * own
        gate = gates[image, 0, head]
        probs = jnp.exp(times_back(keys, query) * scale - lse[image, head : head + 1, :])
        put(2 * width + low, wide, matmul(probs.astype(jnp.bfloat16), (grad.astype(jnp.float32) * gate).astype(jnp.bfloat16)))
        grad_probs = times_back(values, grad)
        inner = jnp.sum(grad_probs * probs, axis=0, keepdims=True)
        grad_gates[image, head : head + 1, :] = inner
        grad_scores = (probs * (grad_probs - inner) * (gate * scale)).astype(jnp.bfloat16)
        put(low, wide, times_rows(grad_scores, keys))
        put(width + low, wide, matmul(grad_scores, query))


def thirds(width):
    tiles = width // 128
    a, b = tiles // 3, tiles // 3
    c = tiles - a - b
    sizes = [a, b, (c + 1) // 2, c // 2]
    starts = [sum(sizes[:i]) for i in range(4)]
    return [(128 * s, 128 * n) for s, n in zip(starts, sizes)]


OWN_SLOTS = 8
PAIR_SLOTS = 4
AHEAD = 3
LAG = 2


class Reducer:
    def __init__(self, at, piece, outs, scratch, rows, width):
        self.at, self.piece, self.outs, self.width = at, piece, outs, width
        (
            self.own, self.pair, self.first_a, self.first_b, self.second_a, self.second_b,
            self.hops, self.hops_c, self.flat_a, self.flat_b, self.last_a, self.last_b, self.done,
            self.own_in, self.core_s, self.core_r, self.fa_s, self.fa_r, self.fb_s, self.fb_r,
            self.sa_s, self.sa_r, self.sb_s, self.sb_r, self.hop_s, self.hop_r, self.hopc_s, self.hopc_r,
            self.ca_s, self.ca_r, self.cb_s, self.cb_r, self.end_s, self.end_r, self.out_sem, self.credit,
        ) = scratch
        self.ring = at.ring
        self.total = 3 * self.ring * 2
        self.spans = self.halves(rows)
        self.sent, self.flights = {}, {}
        self.loose, self.outgoing = [], []
        self.cols = [pl.ds(*part) for part in thirds(width)]
        a, b = thirds(width)[1]
        self.cols_ab = pl.ds(0, a + b)
        self.cols_c = pl.ds(a + b, width - a - b)

    @staticmethod
    def halves(rows):
        top = -(-rows // 32) * 16
        return (0, top), (top, rows - top)

    def place(self, n):
        half = n % 2
        k, j = divmod(n // 2, self.ring)
        return k, j, half, self.spans[half][1]

    @staticmethod
    def scratch(rows, width, fsdp):
        ring = fsdp // 2
        total = 3 * ring * 2
        full, rows = rows, Reducer.halves(rows)[0][1]
        low, vmem, dma = jnp.bfloat16, pltpu.VMEM, pltpu.SemaphoreType.DMA
        a, b, c, d = [size for _, size in thirds(width)]
        arrays = [
            vmem((OWN_SLOTS, QUARTERS, rows, width), low),
            vmem((PAIR_SLOTS, QUARTERS, rows, width), low),
            vmem((total, 2, rows, a), low),
            vmem((total, 2, rows, b), low),
            vmem((total, rows, a), low),
            vmem((total, rows, b), low),
            vmem((3, 2, ring - 1, rows, a + b), low),
            vmem((3, 2, ring - 1, QUARTERS, rows, c + d), low),
            vmem((3, 2, 2, rows, c), low),
            vmem((3, 2, 2, rows, d), low),
            vmem((3, 2, rows, c), low),
            vmem((3, 2, rows, d), low),
            vmem((3, QUARTERS, full, width), low),
        ]
        sems = (
            [dma((total, QUARTERS))] * 3
            + [dma((total, 2))] * 4
            + [dma((total,))] * 4
            + [dma((3, 2, ring - 1))] * 4
            + [dma((3, 2, 3))] * 4
            + [dma((3, 2, 4))] * 2
            + [dma((3, 2))]
            + [pltpu.SemaphoreType.REGULAR]
        )
        return arrays + sems

    def go(self, n, *parts):
        copy = remote(*parts)
        copy.start()
        self.sent.setdefault(n, []).append(copy)
        return copy

    def prefetch(self, n):
        at = self.at
        k, j, half, size = self.place(n)
        slot, pair_slot = n % OWN_SLOTS, n % PAIR_SLOTS
        for copy in self.sent.pop(n - OWN_SLOTS, []):
            copy.wait_send()
        mine = at.shard((j + 1) % self.ring)
        other = mine + 1 - 2 * at.c
        if n >= PAIR_SLOTS:
            pl.semaphore_wait(self.credit, 1)
        brought, pairs = [], []
        span, here = pl.ds(*self.spans[half]), pl.ds(0, size)
        for q in range(QUARTERS):
            copy = pltpu.make_async_copy(self.piece(k, mine, q, span), self.own.at[slot, q, here], self.own_in.at[n, q])
            copy.start()
            brought.append(copy)
            copy = remote(
                self.piece(k, other, q, span), self.pair.at[pair_slot, q, here], self.core_s.at[n, q], self.core_r.at[n, q], at.core
            )
            copy.start()
            pairs.append(copy)
        self.loose += pairs
        self.flights[n] = (brought, pairs)

    def plane_first(self, n, slot, here, cols_a, cols_b, land_a, land_b, sems):
        at, own = self.at, self.own
        (sa, ra), (sb, rb) = sems
        return [
            self.go(n, own.at[slot, at.qd, here, cols_a], land_a.at[1, here], sa.at[1], ra.at[1], at.x),
            self.go(n, own.at[slot, at.qd, here, cols_b], land_b.at[1, here], sb.at[1], rb.at[1], at.y),
            self.go(n, own.at[slot, at.qx, here, cols_a], land_a.at[0, here], sa.at[0], ra.at[0], at.x),
            self.go(n, own.at[slot, at.qy, here, cols_b], land_b.at[0, here], sb.at[0], rb.at[0], at.y),
        ]

    def plane_second(self, n, slot, here, copies, cols_a, cols_b, land_a, land_b, next_a, next_b, sems):
        at, own = self.at, self.own
        one_d, two_d, one, two = copies
        (sa, ra), (sb, rb) = sems
        one_d.wait_recv()
        own[slot, at.qy, here, cols_a] = own[slot, at.qy, here, cols_a] + land_a[1, here]
        on_a = self.go(n, own.at[slot, at.qy, here, cols_a], next_a.at[here], sa, ra, at.y)
        two_d.wait_recv()
        own[slot, at.qx, here, cols_b] = own[slot, at.qx, here, cols_b] + land_b[1, here]
        on_b = self.go(n, own.at[slot, at.qx, here, cols_b], next_b.at[here], sb, rb, at.x)
        one.wait_recv()
        own[slot, at.q, here, cols_a] = own[slot, at.q, here, cols_a] + land_a[0, here]
        two.wait_recv()
        own[slot, at.q, here, cols_b] = own[slot, at.q, here, cols_b] + land_b[0, here]
        return [on_a, on_b]

    def plane_third(self, slot, here, copies, cols_a, cols_b, next_a, next_b):
        at, own = self.at, self.own
        for copy in copies:
            copy.wait_recv()
        own[slot, at.q, here, cols_a] = own[slot, at.q, here, cols_a] + next_a[here, :]
        own[slot, at.q, here, cols_b] = own[slot, at.q, here, cols_b] + next_b[here, :]

    def one(self, n):
        at, own, pair = self.at, self.own, self.pair
        k, j, half, size = self.place(n)
        slot, pair_slot = n % OWN_SLOTS, n % PAIR_SLOTS
        here = pl.ds(0, size)
        brought, pairs = self.flights[n]
        for q in range(QUARTERS):
            brought[q].wait()
            pairs[q].wait_recv()

        @pl.loop(0, QUARTERS)
        def _(q):
            own[slot, q, here, :] = own[slot, q, here, :] + pair[pair_slot, q, here, :]

        if n + PAIR_SLOTS < self.total:
            pl.semaphore_signal(self.credit, inc=1, device_id=at.core, device_id_type=MESH)
        a, b, c, d = self.cols
        self.flights[n] = self.plane_first(
            n, slot, here, a, b, self.first_a.at[n], self.first_b.at[n],
            ((self.fa_s.at[n], self.fa_r.at[n]), (self.fb_s.at[n], self.fb_r.at[n])),
        )
        if j > 0:
            self.flights[k, half, "c"].wait_recv()

            @pl.loop(0, QUARTERS)
            def _(q):
                own[slot, q, here, self.cols_c] = own[slot, q, here, self.cols_c] + self.hops_c[k, half, j - 1, q, here, :]

        if j < self.ring - 1:
            self.flights[k, half, "c"] = self.go(
                n, own.at[slot, slice(None), here, self.cols_c], self.hops_c.at[k, half, j, slice(None), here],
                self.hopc_s.at[k, half, j], self.hopc_r.at[k, half, j], at.up,
            )
        else:
            self.flights[k, half, "flat"] = self.plane_first(
                n, slot, here, c, d, self.flat_a.at[k, half], self.flat_b.at[k, half],
                ((self.ca_s.at[k, half], self.ca_r.at[k, half]), (self.cb_s.at[k, half], self.cb_r.at[k, half])),
            )

    def two(self, n):
        k, j, half, size = self.place(n)
        slot, here = n % OWN_SLOTS, pl.ds(0, size)
        a, b, c, d = self.cols
        self.flights[n] = self.plane_second(
            n, slot, here, self.flights[n], a, b, self.first_a.at[n], self.first_b.at[n], self.second_a.at[n], self.second_b.at[n],
            ((self.sa_s.at[n], self.sa_r.at[n]), (self.sb_s.at[n], self.sb_r.at[n])),
        )
        if j == self.ring - 1:
            self.flights[k, half, "flat"] = self.plane_second(
                n, slot, here, self.flights[k, half, "flat"], c, d, self.flat_a.at[k, half], self.flat_b.at[k, half],
                self.last_a.at[k, half], self.last_b.at[k, half],
                ((self.ca_s.at[k, half, 2], self.ca_r.at[k, half, 2]), (self.cb_s.at[k, half, 2], self.cb_r.at[k, half, 2])),
            )

    def three(self, n):
        at, own = self.at, self.own
        k, j, half, size = self.place(n)
        slot, here = n % OWN_SLOTS, pl.ds(0, size)
        a, b, c, d = self.cols
        self.plane_third(slot, here, self.flights[n], a, b, self.second_a.at[n], self.second_b.at[n])
        if j > 0:
            self.flights[k, half, "ab"].wait_recv()
            own[slot, at.q, here, self.cols_ab] = own[slot, at.q, here, self.cols_ab] + self.hops[k, half, j - 1, here, :]
        if j < self.ring - 1:
            self.flights[k, half, "ab"] = self.go(
                n, own.at[slot, at.q, here, self.cols_ab], self.hops.at[k, half, j, here],
                self.hop_s.at[k, half, j], self.hop_r.at[k, half, j], at.up,
            )
            return
        self.plane_third(slot, here, self.flights[k, half, "flat"], c, d, self.last_a.at[k, half], self.last_b.at[k, half])
        span = pl.ds(*self.spans[half])
        self.done[k, at.q, span, :] = own[slot, at.q, here, :]
        mine = self.done.at[k, at.q, span]
        sems = self.end_s.at[k, half], self.end_r.at[k, half]
        self.flights[k, half, "end"] = [
            self.keep(remote(mine, mine, sems[0].at[0], sems[1].at[0], at.x)),
            self.keep(remote(mine, mine, sems[0].at[1], sems[1].at[1], at.y)),
        ]

    def keep(self, copy):
        copy.start()
        self.loose.append(copy)
        return copy

    def four(self, n):
        at, done = self.at, self.done
        k, _, half, _ = self.place(n)
        (start_a, size_a), (start_b, size_b) = cut(self.width)
        span = pl.ds(*self.spans[half])
        sems = self.end_s.at[k, half], self.end_r.at[k, half]
        by_x, by_y = self.flights[k, half, "end"]
        by_x.wait_recv()
        part = done.at[k, at.qx, span, pl.ds(start_a, size_a)]
        first = self.keep(remote(part, part, sems[0].at[2], sems[1].at[2], at.y))
        by_y.wait_recv()
        part = done.at[k, at.qy, span, pl.ds(start_b, size_b)]
        second = self.keep(remote(part, part, sems[0].at[3], sems[1].at[3], at.x))
        self.flights[k, half, "end"] = [first, second]

    def five(self, n):
        k, _, half, _ = self.place(n)
        for copy in self.flights[k, half, "end"]:
            copy.wait_recv()
        span = pl.ds(*self.spans[half])
        copy = pltpu.make_async_copy(self.done.at[k, :, span], self.outs[k].at[:, span], self.out_sem.at[k, half])
        copy.start()
        self.outgoing.append(copy)

    def turn(self, t, starts):
        if t in starts:
            for n in range(t, t + AHEAD):
                self.prefetch(n)
        n = t + AHEAD
        if n < self.total and not any(t < start <= n for start in starts):
            self.prefetch(n)
        stages = (self.one, self.two, self.three, self.four, self.five)
        for i, stage in enumerate(stages):
            n = t - LAG * i
            if 0 <= n < self.total and (i < 3 or self.place(n)[1] == self.ring - 1):
                stage(n)

    def finish(self):
        for copy in self.outgoing:
            copy.wait()
        for copies in self.sent.values():
            for copy in copies:
                copy.wait_send()
        for copy in self.loose:
            copy.wait_send()


def back_kernel(dp, fsdp, width, images, seq, heads, *refs):
    ring = fsdp // 2
    fc2_ref, joint_ref, h1_ref, h2_ref, tokens_ref, weight_ref, down_ref, slope_ref = refs[:8]
    fc1_weight_ref, fc2_weight_ref, held_ref, attn_ref, cotangent_ref, forward_ref = refs[8:14]
    lse_ref, gates_ref, gate_two_ref, mod_ref, factor_ref, routers_ref, ada_hbm, pre_ref, picker_ref = refs[14:23]
    logit_ref, pick_ref = refs[23:25]
    refs = refs[25:]
    outs, refs = refs[:3], refs[3:]
    all_gm_ref, all_pre_ref, grad_tokens_ref, triple_ref, middle_ref, proj_ref, expand_ref = refs[:7]
    refs = refs[7:]
    joint, mixed, h1, middle, grad_joint, stage, total, inner, gm_row, gms, parts, mine_in, pres, ada_ref = refs[:14]
    in_sem, out_sem, mate_s, mate_r, cousin_s, cousin_r = refs[14:20]
    at = Place(dp, fsdp)
    at.greet()
    rows = fc1_weight_ref.shape[1]
    count = images * seq
    pad = pre_ref.shape[0]

    def piece(k, index, q, span):
        if k == 0:
            return fc2_ref.at[index, q, span]
        line = pl.ds(pl.multiple_of(index * rows + span.start, 8), span.size)
        if k == 1:
            return expand_ref.at[line, pl.ds(q * width, width)]
        if q == 3:
            return proj_ref.at[line, :]
        return triple_ref.at[q, line, :]

    work = Reducer(at, piece, outs, refs[20:], rows, width)
    moves, fetched = {}, []

    def fetch(name, src, dst):
        copy = pltpu.make_async_copy(src, dst, in_sem.at[len(fetched)])
        copy.start()
        fetched.append(copy)
        moves.setdefault(name, []).append(copy)

    def have(name):
        for copy in moves.pop(name):
            copy.wait()

    def store(name, src, dst, i):
        copy = pltpu.make_async_copy(src, dst, out_sem.at[i])
        copy.start()
        moves[name] = [copy]

    for n in range(AHEAD):
        work.prefetch(n)

    def lines(image):
        return pl.ds(image * seq, seq)

    def modulated(image, index):
        return mod_ref[image : image + 1, index * width : (index + 1) * width]

    chunks = fc1_weight_ref.shape[2] // width

    def bring_slope(c):
        fetch("s" + str(c), slope_ref.at[:, pl.ds(c * width, width)], grad_joint.at[:, pl.ds(c % 3 * width, width)])

    def bring_fc1(c):
        for f in range(fsdp):
            fetch("f" + str(c), fc1_weight_ref.at[f, :, pl.ds(c * width, width)], stage.at[0, pl.ds(f * rows, rows), :])

    def bring_fc2(c):
        for i in range(fsdp):
            f, q = c * (fsdp // chunks) + i // QUARTERS, i % QUARTERS
            fetch("d" + str(c), fc2_weight_ref.at[f, q], stage.at[2, pl.ds(i * rows, rows), :])

    def bring_image(image):
        fetch("image" + str(image), held_ref.at[lines(image)], middle.at[0])
        fetch("image" + str(image), attn_ref.at[lines(image)], middle.at[1])
        fetch("image" + str(image), cotangent_ref.at[lines(image)], joint.at[1, :, pl.ds(0, width)])

    fetch("down", down_ref, mixed)
    bring_fc2(0)
    bring_slope(0)
    fetch("h2", h2_ref, h1)
    bring_fc1(0)
    bring_slope(1)
    bring_slope(2)
    fetch("joint0", joint_ref.at[lines(0)], joint.at[0])
    bring_image(0)

    def part_of(c):
        return pl.ds(c % 3 * width, width)

    def lift(c):
        if c == 0:
            have("down")
        have("d" + str(c))
        have("s" + str(c))

        @pl.loop(0, images)
        def _(image):
            line = pl.ds(pl.multiple_of(image * seq, seq), seq)
            value = times_back(mixed[line, :], stage[2])
            grad_joint[line, part_of(c)] = (value * grad_joint[line, part_of(c)].astype(jnp.float32)).astype(jnp.bfloat16)

        if c + 1 < chunks:
            bring_fc2(c + 1)
        else:
            for f in range(fsdp):
                fetch("proj", weight_ref.at[f, :, pl.ds(3 * width, width)], stage.at[2, pl.ds(f * rows, rows), :])

    def weigh_fc1(c):
        if c == 0:
            have("h2")
        else:
            have("e" + str(c - 1))

        @pl.loop(0, width // 128)
        def _(m):
            line = pl.ds(pl.multiple_of(m * 128, 128), 128)
            stage[1, line, :] = times_rows(h1[:, line], grad_joint[:, part_of(c)]).astype(jnp.bfloat16)

        store("e" + str(c), stage.at[1], expand_ref.at[:, pl.ds(c * width, width)], 6 + 2 * images + c)

    def grow(c):
        have("f" + str(c))

        @pl.loop(0, images)
        def _(image):
            line = pl.ds(pl.multiple_of(image * seq, seq), seq)
            value = times_back(grad_joint[line, part_of(c)], stage[0])
            if c == 0:
                total[line, :] = value
            else:
                total[line, :] = total[line, :] + value

        if c + 1 < chunks:
            bring_fc1(c + 1)
        if c + 3 < chunks:
            bring_slope(c + 3)
        if c == chunks - 2:
            fetch("forward", forward_ref, grad_joint.at[:, part_of(c)])
        if c == chunks - 1:
            have("e" + str(c))
            fetch("h1", h1_ref, h1)

    forward_at, grad_at, proj_at = (chunks - 2) % 3, (chunks - 1) % 3, 2

    def norm_two(image):
        have("image" + str(image))
        scale, gate = 1.0 + modulated(image, 4), modulated(image, 2)
        step = 32

        def chunk(i, sums):
            shift_sum, gain_sum, gate_sum = sums
            line = pl.ds(pl.multiple_of(image * seq + i * step, step), step)
            here = pl.ds(pl.multiple_of(i * step, step), step)
            value = middle[0, here, :]
            grad = total[line, :] + logit_ref[line, :] * pick_ref[...]
            centered = value - jnp.mean(value, axis=-1, keepdims=True)
            inverse = lax.rsqrt(jnp.mean(centered * centered, axis=-1, keepdims=True) + EPSILON)
            normed = centered * inverse
            through = grad * scale
            back = through - jnp.mean(through, axis=-1, keepdims=True)
            back = back - normed * jnp.mean(through * normed, axis=-1, keepdims=True)
            through = joint[1, here, :width].astype(jnp.float32) + inverse * back
            total[line, :] = through
            grad_joint[line, grad_at * width : (grad_at + 1) * width] = (through * gate).astype(jnp.bfloat16)
            return (
                shift_sum + jnp.sum(grad, axis=0, keepdims=True),
                gain_sum + jnp.sum(grad * normed, axis=0, keepdims=True),
                gate_sum + jnp.sum(through * middle[1, here, :], axis=0, keepdims=True),
            )

        zero = jnp.zeros((1, width), jnp.float32)
        shift, gain, gated = lax.fori_loop(0, seq // step, chunk, (zero, zero, zero))
        for index, row in ((2, gated), (3, shift), (4, gain)):
            gm_row[image : image + 1, index * width : (index + 1) * width] = row
        store("mid" + str(image), total.at[lines(image)], middle_ref.at[lines(image)], 3 + images + image)
        if image + 1 < images:
            bring_image(image + 1)

    def mix():
        have("proj")

        @pl.loop(0, images)
        def _(image):
            line = pl.ds(pl.multiple_of(image * seq, seq), seq)
            grad = grad_joint[line, grad_at * width : (grad_at + 1) * width]
            mixed[line, :] = times_back(grad, stage[proj_at]).astype(jnp.bfloat16)

    def weigh_proj():
        have("forward")

        @pl.loop(0, width // 128)
        def _(m):
            line = pl.ds(pl.multiple_of(m * 128, 128), 128)
            column = pl.ds(pl.multiple_of(forward_at * width + m * 128, 128), 128)
            value = times_rows(grad_joint[:, column], grad_joint[:, grad_at * width : (grad_at + 1) * width])
            stage[1, line, :] = value.astype(jnp.bfloat16)

        store("projected", stage.at[1], proj_ref, 3 + 2 * images)

    fetch("ada", ada_hbm, ada_ref)
    inner[...] = jnp.zeros_like(inner)
    gm_row[...] = jnp.zeros_like(gm_row)

    def attention(image, half):
        slot = image % 2
        if half == 0:
            have("joint" + str(image))
            if image + 1 < images:
                fetch("joint" + str(image + 1), joint_ref.at[lines(image + 1)], joint.at[1 - slot])
        span = range(0, heads // 2) if half == 0 else range(heads // 2, heads)
        attend_back_image(
            joint.at[slot], mixed.at[lines(image)], gates_ref, lse_ref, grad_joint.at[lines(image)], inner, image, seq, heads, span
        )

    def weigh(q):
        if q == 0:
            have("h1")
            have("projected")
            fetch("tokens", tokens_ref, mixed)
        slot = q % 2
        if q >= 2:
            have("out" + str(q - 2))

        @pl.loop(0, width // 128)
        def _(m):
            line = pl.ds(pl.multiple_of(m * 128, 128), 128)
            stage[slot, line, :] = times_rows(h1[:, line], grad_joint[:, pl.ds(q * width, width)]).astype(jnp.bfloat16)

        store("out" + str(q), stage.at[slot], triple_ref.at[q], q)

    def bring_weight(q):
        for f in range(fsdp):
            fetch("w" + str(q), weight_ref.at[f, :, pl.ds(q * width, width)], stage.at[q % 2, pl.ds(f * rows, rows), :])

    def wait_terms():
        for q in (1, 2):
            have("out" + str(q))
        for image in range(images):
            have("mid" + str(image))
        bring_weight(0)
        bring_weight(1)
        fetch("middle0", middle_ref.at[lines(0)], middle.at[0])

    def spread(q):
        slot = q % 2
        have("w" + str(q))

        @pl.loop(0, images)
        def _(image):
            line = pl.ds(pl.multiple_of(image * seq, seq), seq)
            value = times_back(grad_joint[line, pl.ds(q * width, width)], stage[slot])
            if q == 0:
                total[line, :] = value
            else:
                total[line, :] = total[line, :] + value

        if q == 0:
            bring_weight(2)

    def norm(image):
        slot = image % 2
        if image == 0:
            have("tokens")
        have("middle" + str(image))
        if image + 1 < images:
            if image >= 1:
                have("done" + str(image - 1))
            fetch("middle" + str(image + 1), middle_ref.at[lines(image + 1)], middle.at[1 - slot])
        scale = 1.0 + modulated(image, 1)
        step = 32

        def chunk(i, sums):
            shift, gain = sums
            line = pl.ds(pl.multiple_of(image * seq + i * step, step), step)
            here = pl.ds(pl.multiple_of(i * step, step), step)
            value = mixed[line, :].astype(jnp.float32)
            grad = total[line, :]
            centered = value - jnp.mean(value, axis=-1, keepdims=True)
            inverse = lax.rsqrt(jnp.mean(centered * centered, axis=-1, keepdims=True) + EPSILON)
            normed = centered * inverse
            through = grad * scale
            back = through - jnp.mean(through, axis=-1, keepdims=True)
            back = back - normed * jnp.mean(through * normed, axis=-1, keepdims=True)
            middle[slot, here, :] = middle[slot, here, :] + inverse * back
            return (
                shift + jnp.sum(grad, axis=0, keepdims=True),
                gain + jnp.sum(grad * normed, axis=0, keepdims=True),
            )

        zero = jnp.zeros((1, width), jnp.float32)
        shift, gain = lax.fori_loop(0, seq // step, chunk, (zero, zero))
        store("done" + str(image), middle.at[slot], grad_tokens_ref.at[lines(image)], 3 + image)
        gm_row[image : image + 1, :width] = shift
        gm_row[image : image + 1, width : 2 * width] = gain

    mates, cousins = at.mates(), at.cousins()
    swaps = [Swap(mates, mate_s.at[i], mate_r.at[i]) for i in range(3)]
    far = [Swap(cousins, cousin_s.at[i], cousin_r.at[i]) for i in range(2)]
    small = []

    def keep(src, dst):
        copy = pltpu.make_async_copy(src, dst, out_sem.at[4 + 2 * images + len(small)])
        copy.start()
        small.append(copy)

    held = gms.shape[3]

    def tail_zero():
        gm_row[:, 5 * width :] = gate_two_ref[...]
        for f in range(fsdp):
            gms[0, f] = gm_row[:, f * held : (f + 1) * held].astype(jnp.bfloat16)
        swaps[0].start(lambda device: gms.at[0, device[1]], gms.at[1, at.f])

    def tail_one():
        have("ada")
        swaps[0].arrived()
        gms[1, at.f] = gms[0, at.f]
        every = gms[1].astype(jnp.float32).reshape(fsdp * pad, held).astype(jnp.bfloat16)
        parts[...] = matmul(every, ada_ref[...]).reshape(parts.shape)
        swaps[1].start(lambda device: parts.at[device[1]], mine_in.at[at.f])
        far[0].start(lambda device: gms.at[1], all_gm_ref.at[at.d])
        keep(gms.at[1], all_gm_ref.at[at.d])

    def tail_two():
        line = lax.broadcasted_iota(jnp.int32, (pad, 128), 0)
        gated = jnp.zeros((pad, 128), jnp.float32)
        for image in range(images):
            summed = lax.dot_general(
                jnp.ones((pad, seq), jnp.float32), inner[image], (((1,), (1,)), ((), ())),
                preferred_element_type=jnp.float32, precision=lax.Precision.HIGHEST,
            )
            gated = jnp.where(line == image, summed, gated)
        router = (gated * factor_ref[...]).astype(jnp.bfloat16)
        swaps[1].arrived()
        mine_in[at.f] = parts[at.f]
        grad_cond = jnp.sum(mine_in[...], axis=0) + times_back(router, routers_ref[...])
        pre_cond = pre_ref[...]
        sig = jax.nn.sigmoid(pre_cond)
        grad_pre = grad_cond * (sig * (1.0 + pre_cond * (1.0 - sig)))
        pres[at.f, :, :width] = (grad_pre + picker_ref[...]).astype(jnp.bfloat16)
        pres[at.f, :, width:] = router
        swaps[2].start(lambda device: pres.at[at.f], pres.at[at.f])

    def tail_three():
        swaps[2].arrived()
        far[1].start(lambda device: pres, all_pre_ref.at[at.d])
        keep(pres, all_pre_ref.at[at.d])

    first = [partial(step, c) for c in range(chunks) for step in (lift, weigh_fc1, grow)]
    early = [partial(norm_two, image) for image in range(images)] + [mix, weigh_proj]
    early += [partial(attention, image, half) for image in range(images) for half in range(2)]
    early += [partial(weigh, q) for q in range(3)] + [wait_terms]
    norms = [partial(norm, image) for image in range(images)]
    late = [[partial(spread, q)] for q in range(3)] + [[step] for step in norms]
    late += [[tail_zero], [], [tail_one], [], [], [tail_two], [], [], [tail_three]]
    split = 4 * ring
    starts = (split // 2, split)

    def some(steps, t, turns):
        upto = [-(-len(steps) * (t + i) // turns) for i in range(2)]
        for step in steps[upto[0] : upto[1]]:
            step()

    for t in range(work.total + 4 * LAG):
        work.turn(t, starts)
        if t < split:
            some(first + early, t, split)
        elif t - split < len(late):
            for step in late[t - split]:
                step()
    for swap in far:
        swap.arrived()
    for copy in small:
        copy.wait()
    for image in range(max(images - 2, 0), images):
        have("done" + str(image))
    for swap in swaps + far:
        swap.left()
    work.finish()


def back_half(
    term_fc2, joint, flat_one, flat_two, tokens, joint_full, grad_down, slope, fc1_full, fc2_full, middle, attn, cotangent,
    mixed, log_total, gates, gate_two,
    modulation, factor, routers, ada_weight, pre_cond, picker, logit, pick, width, images, seq, dp, fsdp,
):
    rows = fc1_full.shape[1]
    heads = gates.shape[1]
    count = images * seq
    pad = pre_cond.shape[0]
    columns = ada_weight.shape[0]
    dma, vmem = pltpu.SemaphoreType.DMA, pltpu.VMEM
    low, f32 = jnp.bfloat16, jnp.float32
    out = jax.ShapeDtypeStruct
    any_space, in_vmem = pl.BlockSpec(memory_space=pl.ANY), pl.BlockSpec(memory_space=vmem)
    in_smem = pl.BlockSpec(memory_space=pltpu.SMEM)
    return pl.pallas_call(
        partial(back_kernel, dp, fsdp, width, images, seq, heads),
        out_shape=[out((QUARTERS, rows, width), low)] * 3
        + [
            out((dp, fsdp, pad, columns), low),
            out((dp, fsdp, pad, width + 128), low),
            out((count, width), f32),
            out((3, width, width), low),
            out((count, width), f32),
            out((width, width), low),
            out((width, fc1_full.shape[2]), low),
        ],
        in_specs=[any_space] * 14 + [in_vmem, in_smem] + [in_vmem] * 4 + [any_space] + [in_vmem] * 4,
        out_specs=[any_space] * 10,
        scratch_shapes=[
            vmem((2, seq, 3 * width), low),
            vmem((count, width), low),
            vmem((count, width), low),
            vmem((2, seq, width), f32),
            vmem((count, 3 * width), low),
            vmem((3, width, width), low),
            vmem((count, width), f32),
            vmem((images, 128, seq), f32),
            vmem((pad, 6 * width), f32),
            vmem((2, fsdp, pad, columns), low),
            vmem((fsdp, pad, width), f32),
            vmem((fsdp, pad, width), f32),
            vmem((fsdp, pad, width + 128), low),
            vmem(ada_weight.shape, low),
            dma((12 * fsdp + 12 + 5 * images,)),
            dma((6 + 2 * images + fc1_full.shape[2] // width,)),
            dma((3, fsdp - 1)),
            dma((3, fsdp - 1)),
            dma((2, dp - 1)),
            dma((2, dp - 1)),
        ]
        + Reducer.scratch(rows, width, fsdp),
        compiler_params=pltpu.CompilerParams(
            collective_id=1, has_side_effects=True, vmem_limit_bytes=60 * 2**20
        ),
        name="back",
    )(
        term_fc2, joint, flat_one, flat_two, tokens, joint_full, grad_down, slope, fc1_full, fc2_full, middle, attn,
        cotangent, mixed, log_total,
        gates[:, None, :], gate_two, modulation, factor, routers, ada_weight, pre_cond, picker, logit, pick,
    )


def body(
    dp,
    fsdp,
    tokens,
    timesteps,
    labels,
    head_mask,
    keep_mask,
    cotangent,
    time_weight,
    class_table,
    ada_weight,
    head_router,
    qkv_weight,
    proj_weight,
    fc1_weight,
    fc2_weight,
    token_router,
):
    images, seq, width = tokens.shape
    heads = head_mask.shape[1]
    count = images * seq
    rows = qkv_weight.shape[0]
    hidden = fc1_weight.shape[1]
    entries = time_weight.shape[0] * fsdp
    me_fsdp = lax.axis_index("fsdp")
    pad = -(-(images + 2) // 8) * 8

    def padded(array, value=0.0):
        return jnp.pad(array, ((0, pad - images), (0, 0)), constant_values=value)

    embedded = sinusoid(timesteps, entries).astype(jnp.bfloat16)
    digits = jnp.stack([labels // DIGIT, labels % DIGIT], axis=1).astype(jnp.bfloat16)
    asked = jnp.concatenate(
        [padded(embedded), jnp.pad(padded(digits, -1.0), ((0, 0), (0, 126)))], axis=1
    )
    routers = jnp.pad(
        jnp.concatenate([head_router, token_router], axis=1), ((0, 0), (0, 127 - heads))
    )
    mask_float = head_mask.astype(jnp.float32)
    *gathered, flat_one, joint, log_total, mixed, attn, middle, flat_two, active, slope, grad_down, grad_shrink = front_half(
        [
            jnp.concatenate([qkv_weight, proj_weight], axis=1),
            fc1_weight,
            fc2_weight.reshape(QUARTERS, rows, width),
        ],
        asked,
        time_weight,
        class_table.T,
        ada_weight.T,
        routers,
        padded(jnp.pad(mask_float, ((0, 0), (0, 128 - heads)))),
        tokens.reshape(count, width),
        keep_mask.astype(jnp.float32).reshape(count, 1),
        cotangent.reshape(count, width),
        width,
        images,
        seq,
        heads,
        dp,
        fsdp,
    )
    joint_blocks, fc1_full, fc2_full, pre_cond_pad, modulation_pad, routers_full, all_cond, all_asked = gathered
    shrink = fc2_full.reshape(hidden, width)
    routers_full = routers_full.reshape(width, 128)
    chooser, picker = routers_full[:, :heads], routers_full[:, heads : heads + 1]
    everyone = dp * fsdp * pad
    all_cond = all_cond.reshape(everyone, width)
    all_asked = all_asked.reshape(everyone, asked.shape[1])
    pre_cond = pre_cond_pad[:images]
    cond = jax.nn.silu(pre_cond).astype(jnp.bfloat16)
    gate_two = modulation_pad[:images, None, 5 * width :]
    router_sig = jax.nn.sigmoid(matmul(cond, chooser))
    head_gates = mask_float * router_sig
    middle = middle.reshape(images, seq, width)
    rate = jax.nn.sigmoid(matmul(flat_two, picker)).reshape(images, seq, 1)
    downward = matmul(active, shrink).reshape(images, seq, width)
    kept = keep_mask.astype(jnp.float32)[:, :, None]
    kept_rate = kept * rate
    output = (middle + gate_two * kept_rate * downward).astype(jnp.bfloat16)
    grad_out = cotangent.astype(jnp.float32)
    grad_gate_two = jnp.sum(grad_out * kept_rate * downward, axis=1)
    grad_rate = jnp.sum(grad_out * gate_two * downward, axis=-1, keepdims=True) * kept
    grad_logit = (grad_rate * rate * (1.0 - rate)).astype(jnp.bfloat16).reshape(count, 1)
    grad_picker = times_rows(grad_logit, flat_two)
    picker_high = lax.reduce_precision(grad_picker, 8, 7)
    *sums, all_grad, all_pre, grad_inputs, _, _, _, _ = back_half(
        grad_shrink.reshape(fsdp, QUARTERS, rows, width),
        joint,
        flat_one,
        flat_two,
        tokens.reshape(count, width),
        joint_blocks,
        grad_down,
        slope,
        fc1_full,
        fc2_full,
        middle.reshape(count, width),
        attn,
        cotangent.reshape(count, width),
        mixed,
        log_total,
        head_gates,
        padded(grad_gate_two),
        modulation_pad,
        padded(jnp.pad(mask_float * router_sig * (1.0 - router_sig), ((0, 0), (0, 128 - heads)))),
        routers_full,
        ada_weight.T,
        pre_cond_pad,
        jnp.pad(jnp.concatenate([picker_high, grad_picker - picker_high], axis=0), ((pad - 2, 0), (0, 0))),
        grad_logit.astype(jnp.float32),
        picker.astype(jnp.float32).reshape(1, width),
        width,
        images,
        seq,
        dp,
        fsdp,
    )
    grad_inputs = grad_inputs.reshape(images, seq, width)
    if dp > QUARTERS:
        parts = list(sums)
        for hop in range(QUARTERS, dp, QUARTERS):
            pairs = [(i, (i + hop) % dp) for i in range(dp)]
            parts = [
                part.astype(jnp.float32) + lax.ppermute(s, "dp", pairs).astype(jnp.float32)
                for part, s in zip(parts, sums)
            ]
        sums = parts
    sums = [s.astype(jnp.float32) for s in sums]
    sum_triple = jnp.concatenate([sums[2][0], sums[2][1], sums[2][2]], axis=1)
    sum_merger = sums[2][3]
    sum_expand = jnp.concatenate([sums[1][i] for i in range(QUARTERS)], axis=1)
    sum_shrink = sums[0].reshape(QUARTERS * rows, width)

    sum_ada = times_rows(all_cond, all_grad.reshape(everyone, -1))
    sum_picker = lax.dynamic_slice_in_dim(
        jnp.sum(all_pre[:, :, pad - 2 :, :width].astype(jnp.float32), axis=(0, 1, 2)), me_fsdp * rows, rows, axis=0
    )[:, None]
    is_image = (jnp.arange(pad) < images)[None, None, :, None]
    all_pre = jnp.where(is_image, all_pre, jnp.bfloat16(0.0)).reshape(everyone, -1)
    all_router = all_pre[:, width : width + heads]
    all_pre = all_pre[:, :width]
    own_entries = entries // fsdp
    all_embedded = lax.dynamic_slice_in_dim(
        all_asked[:, :entries], me_fsdp * own_entries, own_entries, axis=1
    )
    classes = jnp.arange(class_table.shape[0], dtype=jnp.float32)
    all_digits = all_asked[:, entries : entries + 2].astype(jnp.float32)
    all_labels = all_digits[:, :1] * DIGIT + all_digits[:, 1:]
    all_rows = (all_labels == classes[None, :]).astype(jnp.bfloat16)
    sum_time = times_rows(all_embedded, all_pre)
    sum_table = times_rows(
        all_rows, lax.dynamic_slice_in_dim(all_pre, me_fsdp * rows, rows, axis=1)
    )
    sum_chooser = times_rows(
        lax.dynamic_slice_in_dim(all_cond, me_fsdp * rows, rows, axis=1), all_router
    )
    return (
        output,
        grad_inputs,
        sum_time,
        sum_table,
        sum_ada,
        sum_chooser,
        sum_triple,
        sum_merger,
        sum_expand,
        sum_shrink,
        sum_picker,
    )


def solution(mesh):
    images = P(("dp", "fsdp"), None, None)
    pairs = P(("dp", "fsdp"), None)
    single = P(("dp", "fsdp"))
    by_row, by_column = P("fsdp", None), P(None, "fsdp")
    in_specs = (
        images, single, single, pairs, pairs, images,
        by_row, by_column, by_column, by_row, by_row, by_row, by_row, by_row, by_row,
    )
    out_specs = (
        images, images,
        by_row, by_column, by_column, by_row, by_row, by_row, by_row, by_row, by_row,
    )
    return jax.shard_map(
        partial(body, mesh.shape["dp"], mesh.shape["fsdp"]),
        mesh=mesh, in_specs=in_specs, out_specs=out_specs, check_vma=False,
    )
```
